32 devices in a mesh: seq: 8 (over z, x), tp: 4 (over y, core).
Axes of the slice: x: 2, y: 2, z: 4, core: 2. Of those that a mesh axis runs over, the one named last changes fastest.
Arguments:
- tokens: bfloat16 [1024, 2048], P('seq'), may hold values from -6 to 6
- out_grad: bfloat16 [1024, 2048], P('seq', 'tp'), may hold values from -6 to 6
- modality: int32 [1024], P('seq'), may hold values from 0 to 2
- segment: int32 [1024], replicated, may hold values from 0 to 2, as said below
- w_in: float32 [3, 2048, 2, 4096], P(None, 'seq', None, 'tp'), may hold values from -0.125 to 0.125
- w_x: float32 [3, 4096, 160], P(None, ('tp', 'seq')), may hold values from -0.09375 to 0.09375
- w_dt: float32 [3, 128, 4096], P(None, 'seq', 'tp'), may hold values from -0.5 to 0.5
- w_out: float32 [3, 4096, 2048], P(None, 'tp', 'seq'), may hold values from -0.09375 to 0.09375
- channel: float32 [25, 4096], P(None, ('tp', 'seq'))
- norm_gain: float32 [2048], P('seq'), may hold values from 0.3 to 3.2
- moment_in: float32 [3, 2048, 2, 4096], P(None, 'seq', None, 'tp')
- moment_x: float32 [3, 4096, 160], P(None, ('tp', 'seq'))
- moment_dt: float32 [3, 128, 4096], P(None, 'seq', 'tp')
- moment_out: float32 [3, 4096, 2048], P(None, 'tp', 'seq')
- moment_channel: float32 [25, 4096], P(None, ('tp', 'seq'))
- moment_gain: float32 [2048], P('seq')
- square_in: float32 [3, 2048, 2, 4096], P(None, 'seq', None, 'tp')
- square_x: float32 [3, 4096, 160], P(None, ('tp', 'seq'))
- square_dt: float32 [3, 128, 4096], P(None, 'seq', 'tp')
- square_out: float32 [3, 4096, 2048], P(None, 'tp', 'seq')
- square_channel: float32 [25, 4096], P(None, ('tp', 'seq'))
- square_gain: float32 [2048], P('seq')
- average_in: float32 [3, 2048, 2, 4096], P(None, 'seq', None, 'tp'), may hold values from -0.125 to 0.125
- average_x: float32 [3, 4096, 160], P(None, ('tp', 'seq')), may hold values from -0.09375 to 0.09375
- average_dt: float32 [3, 128, 4096], P(None, 'seq', 'tp'), may hold values from -0.5 to 0.5
- average_out: float32 [3, 4096, 2048], P(None, 'tp', 'seq'), may hold values from -0.09375 to 0.09375
- average_channel: float32 [25, 4096], P(None, ('tp', 'seq')), may hold values from -6 to 6
- average_gain: float32 [2048], P('seq'), may hold values from 0.5 to 1.5
Outputs:
- layer_out: float32 [1024, 2048], P('seq', 'tp')
- tokens_grad: float32 [1024, 2048], P('seq', 'tp')
- new_w_in: float32 [3, 2048, 2, 4096], P(None, 'seq', None, 'tp')
- new_w_x: float32 [3, 4096, 160], P(None, ('tp', 'seq'))
- new_w_dt: float32 [3, 128, 4096], P(None, 'seq', 'tp')
- new_w_out: float32 [3, 4096, 2048], P(None, 'tp', 'seq')
- new_channel: float32 [25, 4096], P(None, ('tp', 'seq'))
- new_norm_gain: float32 [2048], P('seq')
- new_moment_in: float32 [3, 2048, 2, 4096], P(None, 'seq', None, 'tp')
- new_moment_x: float32 [3, 4096, 160], P(None, ('tp', 'seq'))
- new_moment_dt: float32 [3, 128, 4096], P(None, 'seq', 'tp')
- new_moment_out: float32 [3, 4096, 2048], P(None, 'tp', 'seq')
- new_moment_channel: float32 [25, 4096], P(None, ('tp', 'seq'))
- new_moment_gain: float32 [2048], P('seq')
- new_square_in: float32 [3, 2048, 2, 4096], P(None, 'seq', None, 'tp')
- new_square_x: float32 [3, 4096, 160], P(None, ('tp', 'seq'))
- new_square_dt: float32 [3, 128, 4096], P(None, 'seq', 'tp')
- new_square_out: float32 [3, 4096, 2048], P(None, 'tp', 'seq')
- new_square_channel: float32 [25, 4096], P(None, ('tp', 'seq'))
- new_square_gain: float32 [2048], P('seq')
- new_average_in: float32 [3, 2048, 2, 4096], P(None, 'seq', None, 'tp')
- new_average_x: float32 [3, 4096, 160], P(None, ('tp', 'seq'))
- new_average_dt: float32 [3, 128, 4096], P(None, 'seq', 'tp')
- new_average_out: float32 [3, 4096, 2048], P(None, 'tp', 'seq')
- new_average_channel: float32 [25, 4096], P(None, ('tp', 'seq'))
- new_average_gain: float32 [2048], P('seq')
The draws below stay inside these ranges and needn't reach their ends.
Inputs may be any that keep to these rules, and one draw needn't show every extreme that they name: segment never falls along the stream and starts at 0; document 1 begins within the first 128 tokens and document 2 within the last 128.
All inputs are finite; a program needn't handle non-finite values.
Results may differ from the reference program's by a relative error of at most 0.0075.
The reference program's roundings to bfloat16 on the way count: a program that leaves them out, or rounds other values in their place, can miss the bound.
Values may be sent and summed in bfloat16 or wider, within the bound.
A program may use at most 384 MiB of HBM per device.

```python
import math
from functools import partial
import jax
import jax.numpy as jnp
from jax import lax

D = 2048
E = 4096
R = 128
N = 16
K = 4
M = 3
STEP = 10
TOK_DEV = 128
TOKENS = 1024
XW = 160
CH = 25


def moment_draw(key, array_shape, spread):
    return 0.11 * spread * jax.random.normal(key, array_shape, jnp.float32)


def square_draw(key, array_shape, spread):
    factor = jnp.exp(jax.random.uniform(key, array_shape, jnp.float32, math.log(0.5), math.log(8.0)))
    return 0.001 * spread * spread * factor


def draw_segment(key, part):
    key = jax.random.fold_in(key, 1)
    first_key, second_key = jax.random.split(key)
    first_cut = jax.random.randint(first_key, (), 1, TOK_DEV)
    second_cut = jax.random.randint(second_key, (), TOKENS - TOK_DEV + 1, TOKENS)
    places = jnp.arange(TOKENS, dtype=jnp.int32)
    return (places >= first_cut).astype(jnp.int32) + (places >= second_cut).astype(jnp.int32)


def draw_channel(key, part):
    key = jax.random.fold_in(key, 2)
    subkeys = jax.random.split(key, 7)
    tap_weights = 0.5 * jax.random.normal(subkeys[0], (K, E), jnp.float32)
    conv_bias = 0.3 * jax.random.normal(subkeys[1], (1, E), jnp.float32)
    slow_share = 0.5
    skip_gain = jax.random.uniform(subkeys[2], (1, E), jnp.float32, 0.5, 1.5)
    coin_flip = jax.random.uniform(subkeys[3], (M, E), jnp.float32)
    slow_log = jax.random.uniform(subkeys[4], (M, E), jnp.float32, math.log(0.2 / TOKENS), math.log(1.0 / TOKENS))
    fast_log = jax.random.uniform(subkeys[5], (M, E), jnp.float32, math.log(0.02), math.log(0.1))
    step_target = jnp.exp(jnp.where(coin_flip < slow_share, slow_log, fast_log))
    step_bias = jnp.log(jnp.expm1(step_target))
    levels = jnp.arange(1, N + 1, dtype=jnp.float32)[:, None] * jax.random.uniform(subkeys[6], (N, E), jnp.float32, 0.7, 1.4)
    return jnp.concatenate([tap_weights, conv_bias, skip_gain, step_bias, jnp.log(levels)], axis=0)


def draw_norm_gain(key, part):
    key = jax.random.fold_in(key, 3)
    ramp_pos = jnp.arange(D, dtype=jnp.float32) / (D - 1)
    base_gain = 0.6 * 3.0 ** ramp_pos
    return base_gain * jax.random.uniform(key, (D,), jnp.float32, 0.8, 1.25)


def draw_moment_in(key, part):
    key = jax.random.fold_in(key, 11)
    return moment_draw(key, (M, D, 2, E), 0.2 * math.sqrt(TOKENS / 3))


def draw_moment_x(key, part):
    key = jax.random.fold_in(key, 12)
    return moment_draw(key, (M, E, XW), 0.2 * math.sqrt(TOKENS / 3))


def draw_moment_dt(key, part):
    key = jax.random.fold_in(key, 13)
    return moment_draw(key, (M, R, E), 0.02 * math.sqrt(TOKENS / 3))


def draw_moment_out(key, part):
    key = jax.random.fold_in(key, 14)
    return moment_draw(key, (M, E, D), 0.3 * math.sqrt(TOKENS / 3))


def draw_moment_channel(key, part):
    key = jax.random.fold_in(key, 15)
    return moment_draw(key, (CH, E), 0.1 * math.sqrt(TOKENS))


def draw_moment_gain(key, part):
    key = jax.random.fold_in(key, 16)
    return moment_draw(key, (D,), 0.4 * math.sqrt(TOKENS))


def draw_square_in(key, part):
    key = jax.random.fold_in(key, 21)
    return square_draw(key, (M, D, 2, E), 0.2 * math.sqrt(TOKENS / 3))


def draw_square_x(key, part):
    key = jax.random.fold_in(key, 22)
    return square_draw(key, (M, E, XW), 0.2 * math.sqrt(TOKENS / 3))


def draw_square_dt(key, part):
    key = jax.random.fold_in(key, 23)
    return square_draw(key, (M, R, E), 0.02 * math.sqrt(TOKENS / 3))


def draw_square_out(key, part):
    key = jax.random.fold_in(key, 24)
    return square_draw(key, (M, E, D), 0.3 * math.sqrt(TOKENS / 3))


def draw_square_channel(key, part):
    key = jax.random.fold_in(key, 25)
    return square_draw(key, (CH, E), 0.1 * math.sqrt(TOKENS))


def draw_square_gain(key, part):
    key = jax.random.fold_in(key, 26)
    return square_draw(key, (D,), 0.4 * math.sqrt(TOKENS))


def with_ends(array, own_key, low, high):
    dims = array.shape
    index_at = [jax.random.randint(jax.random.fold_in(own_key, axis), (), 0, dims[axis]) for axis in range(len(dims))]
    array = array.at[tuple(index_at)].set(low)
    longest = dims.index(max(dims))
    index_at[longest] = (index_at[longest] + 1) % dims[longest]
    return array.at[tuple(index_at)].set(high)


def block_levels(own_key, shape, pieces, smallest, high):
    factor_of, own = 1.0, jax.random.fold_in(own_key, 6)
    for dim, parts in pieces:
        steps = jnp.exp(jax.random.uniform(jax.random.fold_in(own, dim), (parts,), jnp.float32, smallest / len(pieces), high / len(pieces)))
        factor_of = factor_of * jnp.repeat(steps, shape[dim] // parts).reshape([-1 if axis == dim else 1 for axis in range(len(shape))])
    return factor_of


def centred(key, extent, width, limit, pieces=(), kind=jnp.bfloat16):
    result = width * jax.random.normal(key, extent, jnp.float32)
    if pieces:
        result = result * block_levels(key, extent, pieces, -0.22, 0.18)
    return jnp.clip(result, -limit, limit).astype(kind)


def setup_inputs(seed: int = 0) -> dict:
    arg_keys = jax.random.split(jax.random.key(seed), 29)
    tokens = centred(arg_keys[0], (TOKENS, D), 1.0, 6.0, ((0, 8),))
    out_grad = centred(arg_keys[1], (TOKENS, D), 1.0, 6.0, ((0, 8), (1, 4)))
    modality = with_ends(jax.random.randint(arg_keys[2], (TOKENS,), 0, M), jax.random.fold_in(arg_keys[2], 1), 0, M - 1).astype(jnp.int32)
    segment = draw_segment(jax.random.fold_in(arg_keys[28], 71), 0)
    w_in = centred(arg_keys[4], (M, D, 2, E), D ** -0.5, 0.125, ((1, 8), (3, 4)), jnp.float32)
    w_x = centred(arg_keys[5], (M, E, XW), E ** -0.5, 0.09375, ((1, 32),), jnp.float32)
    w_dt = centred(arg_keys[6], (M, R, E), R ** -0.5, 0.5, ((1, 8), (2, 4)), jnp.float32)
    w_out = centred(arg_keys[7], (M, E, D), E ** -0.5, 0.09375, ((1, 4), (2, 8)), jnp.float32)
    channel = draw_channel(jax.random.fold_in(arg_keys[28], 71), 0)
    norm_gain = draw_norm_gain(jax.random.fold_in(arg_keys[28], 71), 0)
    moment_in = draw_moment_in(jax.random.fold_in(arg_keys[28], 71), 0)
    moment_x = draw_moment_x(jax.random.fold_in(arg_keys[28], 71), 0)
    moment_dt = draw_moment_dt(jax.random.fold_in(arg_keys[28], 71), 0)
    moment_out = draw_moment_out(jax.random.fold_in(arg_keys[28], 71), 0)
    moment_channel = draw_moment_channel(jax.random.fold_in(arg_keys[28], 71), 0)
    moment_gain = draw_moment_gain(jax.random.fold_in(arg_keys[28], 71), 0)
    square_in = draw_square_in(jax.random.fold_in(arg_keys[28], 71), 0)
    square_x = draw_square_x(jax.random.fold_in(arg_keys[28], 71), 0)
    square_dt = draw_square_dt(jax.random.fold_in(arg_keys[28], 71), 0)
    square_out = draw_square_out(jax.random.fold_in(arg_keys[28], 71), 0)
    square_channel = draw_square_channel(jax.random.fold_in(arg_keys[28], 71), 0)
    square_gain = draw_square_gain(jax.random.fold_in(arg_keys[28], 71), 0)
    average_in = centred(arg_keys[22], (M, D, 2, E), D ** -0.5, 0.125, ((1, 8), (3, 4)), jnp.float32)
    average_x = centred(arg_keys[23], (M, E, XW), E ** -0.5, 0.09375, ((1, 32),), jnp.float32)
    average_dt = centred(arg_keys[24], (M, R, E), R ** -0.5, 0.5, ((1, 8), (2, 4)), jnp.float32)
    average_out = centred(arg_keys[25], (M, E, D), E ** -0.5, 0.09375, ((1, 4), (2, 8)), jnp.float32)
    average_channel = centred(arg_keys[26], (CH, E), 1.0, 6.0, ((1, 32),), jnp.float32)
    average_gain = jnp.clip(1.0 + 0.1 * jax.random.normal(arg_keys[27], (D,), jnp.float32), 0.5, 1.5)
    return {"tokens": tokens, "out_grad": out_grad, "modality": modality, "segment": segment, "w_in": w_in, "w_x": w_x, "w_dt": w_dt, "w_out": w_out, "channel": channel, "norm_gain": norm_gain, "moment_in": moment_in, "moment_x": moment_x, "moment_dt": moment_dt, "moment_out": moment_out, "moment_channel": moment_channel, "moment_gain": moment_gain, "square_in": square_in, "square_x": square_x, "square_dt": square_dt, "square_out": square_out, "square_channel": square_channel, "square_gain": square_gain, "average_in": average_in, "average_x": average_x, "average_dt": average_dt, "average_out": average_out, "average_channel": average_channel, "average_gain": average_gain}


@jax.custom_vjp
def low(v):
    return lax.optimization_barrier(v.astype(jnp.bfloat16)).astype(jnp.float32)

@jax.custom_vjp
def low_back(v):
    return v

def low_keep(v):
    return (low(v), None)

def low_pass(kept, grad):
    return (grad,)

def back_keep(v):
    return (v, None)

def back_low(kept, grad):
    return (low(grad),)
low.defvjp(low_keep, low_pass)
low_back.defvjp(back_keep, back_low)
EPSILON = 1e-05
BETA_ONE = 0.9
BETA_TWO = 0.999
ADAM_EPSILON = 1e-06
WEIGHT_DECAY = 0.01
MATRIX_RATE = 0.25
CHANNEL_RATE = 0.7
GAIN_RATE = 0.35
AVERAGE_KEEP = 0.8
PRECISE = lax.Precision.HIGHEST

def mixed_dot(mask_cols, operand, stacked):
    running = jnp.zeros((operand.shape[0], stacked.shape[-1]), jnp.float32)
    for modal_index in range(M):
        running = running + mask_cols[:, modal_index:modal_index + 1] * jnp.dot(operand, stacked[modal_index], precision=PRECISE)
    return running

def forward(modality, segment, tokens, w_in, w_x, w_dt, w_out, channel, norm_gain):
    mask_cols = (modality[:, None] == jnp.arange(M, dtype=jnp.int32)[None, :]).astype(jnp.float32)
    square_mean = lax.optimization_barrier(jnp.mean(tokens * tokens, axis=-1, keepdims=True))
    scaled = tokens * lax.rsqrt(square_mean + EPSILON)
    normed = low(scaled * norm_gain[None, :])
    projected = low_back(mixed_dot(mask_cols, normed, low(w_in).reshape(M, D, 2 * E)))
    inner_act = low(projected[:, :E])
    gate_pre = projected[:, E:]
    padded = jnp.concatenate([jnp.zeros((K - 1, E), jnp.float32), inner_act], axis=0)
    seg_padded = jnp.concatenate([jnp.full((K - 1,), -1, jnp.int32), segment])
    conv_pre = jnp.broadcast_to(channel[K][None, :], (TOKENS, E))
    for tap_index in range(K):
        same_doc = (seg_padded[tap_index:tap_index + TOKENS] == segment).astype(jnp.float32)
        conv_pre = conv_pre + channel[tap_index][None, :] * padded[tap_index:tap_index + TOKENS] * same_doc[:, None]
    conv_out = low_back(conv_pre)
    activated = low(jax.nn.silu(conv_out))
    params_x = low_back(mixed_dot(mask_cols, activated, low(w_x)))
    low_rank = low(params_x[:, :R])
    input_b = params_x[:, R:R + N]
    output_c = params_x[:, R + N:]
    step_pre = low_back(mixed_dot(mask_cols, low_rank, low(w_dt)) + jnp.dot(mask_cols, channel[K + 2:K + 2 + M], precision=PRECISE))
    step_size = jax.nn.softplus(step_pre)
    decay_base = -jnp.exp(channel[K + 2 + M:])
    keep_flag = jnp.concatenate([jnp.zeros((1,), jnp.float32), (segment[1:] == segment[:-1]).astype(jnp.float32)])
    block_len = math.gcd(TOKENS, 64)
    block_count = TOKENS // block_len

    def row_step(carried, row_inputs):
        step_rate, drive_b, read_c, act_row, keep_row = row_inputs
        carried = jnp.exp(step_rate[None, :] * decay_base) * keep_row * carried + (step_rate * act_row)[None, :] * drive_b[:, None]
        return (carried, lax.optimization_barrier(jnp.sum(read_c[:, None] * carried, axis=0)))

    def block_step(carried, block_inputs):
        return lax.scan(row_step, carried, block_inputs)
    block_inputs = (step_size.reshape(block_count, block_len, E), input_b.reshape(block_count, block_len, N), output_c.reshape(block_count, block_len, N), activated.reshape(block_count, block_len, E), keep_flag.reshape(block_count, block_len))
    last_state, scanned = lax.scan(jax.checkpoint(block_step), jnp.zeros((N, E), jnp.float32), block_inputs)
    mixed_out = scanned.reshape(TOKENS, E) + channel[K + 1][None, :] * activated
    gated_out = low(mixed_out * jax.nn.silu(gate_pre))
    return tokens + mixed_dot(mask_cols, gated_out, low(w_out))

def adam_parts(gradient, moment, square):
    moment_new = BETA_ONE * moment + (1.0 - BETA_ONE) * gradient
    square_new = BETA_TWO * square + (1.0 - BETA_TWO) * gradient * gradient
    adam_ratio = moment_new / (1.0 - BETA_ONE ** STEP) / (jnp.sqrt(square_new / (1.0 - BETA_TWO ** STEP)) + ADAM_EPSILON)
    return (moment_new, square_new, adam_ratio)

def reference(tokens, out_grad, modality, segment, w_in, w_x, w_dt, w_out, channel, norm_gain, moment_in, moment_x, moment_dt, moment_out, moment_channel, moment_gain, square_in, square_x, square_dt, square_out, square_channel, square_gain, average_in, average_x, average_dt, average_out, average_channel, average_gain):
    weights = (w_in, w_x, w_dt, w_out, channel, norm_gain)
    moments = (moment_in, moment_x, moment_dt, moment_out, moment_channel, moment_gain)
    squares = (square_in, square_x, square_dt, square_out, square_channel, square_gain)
    averages = (average_in, average_x, average_dt, average_out, average_channel, average_gain)
    layer_out, pullback = jax.vjp(partial(forward, modality, segment), tokens.astype(jnp.float32), *weights)
    cotangents = pullback(out_grad.astype(jnp.float32))
    tokens_grad = cotangents[0]
    new_weights = []
    new_moments = []
    new_squares = []
    new_averages = []
    for position in range(6):
        weight = weights[position]
        moment_new, square_new, adam_ratio = adam_parts(cotangents[position + 1], moments[position], squares[position])
        if position < 4:
            direction = adam_ratio + WEIGHT_DECAY * weight
            axes_rest = tuple(range(1, weight.ndim))
            trust_ratio = jnp.sqrt(lax.optimization_barrier(jnp.sum(weight * weight, axis=axes_rest))) / jnp.sqrt(lax.optimization_barrier(jnp.sum(direction * direction, axis=axes_rest)))
            updated = weight - MATRIX_RATE * trust_ratio.reshape((M,) + (1,) * (weight.ndim - 1)) * direction
        elif position == 4:
            updated = weight - CHANNEL_RATE * adam_ratio
        else:
            updated = weight - GAIN_RATE * adam_ratio
        new_weights.append(updated)
        new_moments.append(moment_new)
        new_squares.append(square_new)
        new_averages.append(AVERAGE_KEEP * averages[position] + (1.0 - AVERAGE_KEEP) * updated)
    return (layer_out, tokens_grad, new_weights[0], new_weights[1], new_weights[2], new_weights[3], new_weights[4], new_weights[5], new_moments[0], new_moments[1], new_moments[2], new_moments[3], new_moments[4], new_moments[5], new_squares[0], new_squares[1], new_squares[2], new_squares[3], new_squares[4], new_squares[5], new_averages[0], new_averages[1], new_averages[2], new_averages[3], new_averages[4], new_averages[5])
```

```python
import functools

import jax
import jax.numpy as jnp
from jax import lax
from jax.experimental import pallas as pl
from jax.experimental.pallas import tpu as pltpu
from jax.sharding import PartitionSpec as P

D = 2048
R = 128
N = 16
K = 4
M = 3
STEP = 10


EPSILON = 1e-05
BETA_ONE = 0.9
BETA_TWO = 0.999
ADAM_EPSILON = 1e-06
WEIGHT_DECAY = 0.01
MATRIX_RATE = 0.25
CHANNEL_RATE = 0.7
GAIN_RATE = 0.35
AVERAGE_KEEP = 0.8
PRECISE = lax.Precision.HIGHEST


def passed_along(value, axis, steps):
    count = lax.axis_size(axis)
    leading, last = (max(0, -steps), min(count, count - steps))
    return lax.ppermute(value, axis, [(source, source + steps) for source in range(leading, last)])


def prefix(x, axis, combine, identity, reverse):
    devices, place = (lax.axis_size(axis), lax.axis_index(axis))
    everything = jax.tree.map(lambda part: lax.all_gather(part, axis), x)
    start = jax.tree.map(
        lambda part, zero: jnp.broadcast_to(jnp.asarray(zero, part.dtype), part.shape), x, identity
    )

    def lap(k, before):
        at = devices - 1 - k if reverse else k
        reached = at > place if reverse else at < place
        new = combine(before, jax.tree.map(lambda part: part[at], everything))
        return jax.tree.map(lambda a, b: jnp.where(reached, a, b), new, before)

    return lax.fori_loop(0, devices, lap, start)


def silu_grad(operand):
    sigmoid_of = jax.nn.sigmoid(operand)
    return sigmoid_of * (1.0 + operand * (1.0 - sigmoid_of))


def combine(earlier, following):
    return (earlier[0] * following[0], following[0] * earlier[1] + following[1])


def masked_dot(mask_cols, operand, stacked):
    running = mask_cols[:, 0:1] * jnp.dot(operand, stacked[0], preferred_element_type=jnp.float32)
    for modal_index in range(1, M):
        running = running + mask_cols[:, modal_index : modal_index + 1] * jnp.dot(
            operand, stacked[modal_index], preferred_element_type=jnp.float32
        )
    return running


def masked_back(mask_cols, operand, stacked):
    contract = (((1,), (1,)), ((), ()))
    running = mask_cols[:, 0:1] * lax.dot_general(
        operand, stacked[0], contract, preferred_element_type=jnp.float32
    )
    for modal_index in range(1, M):
        running = running + mask_cols[:, modal_index : modal_index + 1] * lax.dot_general(
            operand, stacked[modal_index], contract, preferred_element_type=jnp.float32
        )
    return running


def masked_outer(mask_low, operand, cotangent):
    contract = (((0,), (0,)), ((), ()))
    return jnp.stack(
        [
            lax.dot_general(
                operand * mask_low[:, modal_index : modal_index + 1],
                cotangent,
                contract,
                preferred_element_type=jnp.float32,
            )
            for modal_index in range(M)
        ]
    )


def adam_parts(gradient, moment, square):
    moment_new = BETA_ONE * moment + (1.0 - BETA_ONE) * gradient
    square_new = BETA_TWO * square + (1.0 - BETA_TWO) * gradient * gradient
    adam_ratio = (
        moment_new
        / (1.0 - BETA_ONE**STEP)
        / (jnp.sqrt(square_new / (1.0 - BETA_TWO**STEP)) + ADAM_EPSILON)
    )
    return (moment_new, square_new, adam_ratio)


def generic_local(
    tokens,
    out_grad,
    modality,
    segment,
    w_in,
    w_x,
    w_dt,
    w_out,
    channel,
    norm_gain,
    moment_in,
    moment_x,
    moment_dt,
    moment_out,
    moment_channel,
    moment_gain,
    square_in,
    square_x,
    square_dt,
    square_out,
    square_channel,
    square_gain,
    average_in,
    average_x,
    average_dt,
    average_out,
    average_channel,
    average_gain,
):
    tok_local = tokens.shape[0]
    width_tp = out_grad.shape[1]
    lowered = (
        w_in.astype(jnp.bfloat16),
        w_x.astype(jnp.bfloat16),
        w_dt.astype(jnp.bfloat16),
        w_out.astype(jnp.bfloat16),
    )
    stack_in, stack_x, stack_dt, stack_out = (
        lax.all_gather(lowered[0], "seq", axis=1, tiled=True),
        lax.all_gather(lowered[1], "seq", axis=1, tiled=True),
        lax.all_gather(lowered[2], "seq", axis=1, tiled=True),
        lax.all_gather(lowered[3], "seq", axis=2, tiled=True),
    )
    chan_full, gain_full = (
        lax.all_gather(channel, "seq", axis=1, tiled=True),
        lax.all_gather(norm_gain, "seq", axis=0, tiled=True),
    )
    inner_width = stack_out.shape[1]
    in_flat = stack_in.reshape(M, D, 2 * inner_width)
    seq_index = lax.axis_index("seq")
    tp_index = lax.axis_index("tp")
    start_row = seq_index * tok_local
    seg_local = lax.dynamic_slice(segment, (start_row,), (tok_local,))
    seg_before = lax.dynamic_slice(
        jnp.concatenate([jnp.full((K - 1,), -1, jnp.int32), segment]),
        (start_row,),
        (tok_local + K - 1,),
    )
    seg_after = lax.dynamic_slice(
        jnp.concatenate([segment, jnp.full((K - 1,), -2, jnp.int32)]),
        (start_row,),
        (tok_local + K - 1,),
    )
    mask_cols = (modality[:, None] == jnp.arange(M, dtype=jnp.int32)[None, :]).astype(jnp.float32)
    mask_low = mask_cols.astype(jnp.bfloat16)
    tokens_wide = tokens.astype(jnp.float32)
    inv_root = lax.rsqrt(jnp.mean(tokens_wide * tokens_wide, axis=-1, keepdims=True) + EPSILON)
    scaled = tokens_wide * inv_root
    normed = (scaled * gain_full[None, :]).astype(jnp.bfloat16)
    projected = masked_dot(mask_cols, normed, in_flat)
    inner_act = projected[:, :inner_width].astype(jnp.bfloat16)
    gate_pre = projected[:, inner_width:]
    rim_rows = passed_along(inner_act[tok_local - (K - 1) :], "seq", 1)
    extended = jnp.concatenate([rim_rows, inner_act], axis=0).astype(jnp.float32)
    conv_pre = jnp.broadcast_to(chan_full[K][None, :], (tok_local, inner_width))
    same_docs = []
    for tap_index in range(K):
        same_doc = (seg_before[tap_index : tap_index + tok_local] == seg_local).astype(jnp.float32)[
            :, None
        ]
        same_docs.append(same_doc)
        conv_pre = (
            conv_pre
            + chan_full[tap_index][None, :] * extended[tap_index : tap_index + tok_local] * same_doc
        )
    activated = jax.nn.silu(conv_pre).astype(jnp.bfloat16)
    act_wide = activated.astype(jnp.float32)
    params_x = lax.psum(masked_dot(mask_cols, activated, stack_x), "tp")
    low_rank = params_x[:, :R].astype(jnp.bfloat16)
    input_b = params_x[:, R : R + N]
    output_c = params_x[:, R + N :]
    step_pre = masked_dot(mask_cols, low_rank, stack_dt) + jnp.dot(
        mask_cols, chan_full[K + 2 : K + 2 + M], precision=PRECISE
    )
    step_size = jax.nn.softplus(step_pre)
    decay_base = -jnp.exp(chan_full[K + 2 + M :])
    keep_flag = (seg_before[K - 2 : K - 2 + tok_local] == seg_local).astype(jnp.float32)
    decay_rate = jnp.exp(step_size[:, None, :] * decay_base[None]) * keep_flag[:, None, None]
    drive_term = (step_size * act_wide)[:, None, :] * input_b[:, :, None]
    decay_cum, local_state = lax.associative_scan(combine, (decay_rate, drive_term), axis=0)
    unit_pair = (jnp.ones_like(decay_base), jnp.zeros_like(decay_base))
    carry_in = prefix((decay_cum[-1], local_state[-1]), "seq", combine, unit_pair, False)[1]
    hidden_state = local_state + decay_cum * carry_in[None]
    mixed_out = (
        jnp.einsum("tn,tne->te", output_c, hidden_state, precision=PRECISE)
        + chan_full[K + 1][None, :] * act_wide
    )
    gate_act = jax.nn.silu(gate_pre)
    gated_out = (mixed_out * gate_act).astype(jnp.bfloat16)
    out_share = lax.psum_scatter(
        masked_dot(mask_cols, gated_out, stack_out), "tp", scatter_dimension=1, tiled=True
    )
    layer_out = lax.dynamic_slice_in_dim(tokens_wide, tp_index * width_tp, width_tp, 1) + out_share
    grad_full = lax.all_gather(out_grad, "tp", axis=1, tiled=True)
    d_gated = masked_back(mask_cols, grad_full, stack_out)
    grad_out = masked_outer(mask_low, gated_out, grad_full)
    d_mixed = d_gated * gate_act
    d_gate = d_gated * mixed_out * silu_grad(gate_pre)
    grad_skip = jnp.sum(d_mixed * act_wide, axis=0)
    d_out_c = jnp.einsum("te,tne->tn", d_mixed, hidden_state, precision=PRECISE)
    d_hidden = output_c[:, :, None] * d_mixed[:, None, :]
    decay_next = jnp.concatenate([decay_rate[1:], jnp.ones_like(decay_rate[:1])], axis=0)
    suffix_cum, local_back = lax.associative_scan(
        combine, (decay_next, d_hidden), reverse=True, axis=0
    )
    device_pair = (decay_rate[0] * suffix_cum[0], decay_rate[0] * local_back[0])
    carry_back = prefix(device_pair, "seq", combine, unit_pair, True)[1]
    back_state = local_back + suffix_cum * carry_back[None]
    state_prev = jnp.concatenate([carry_in[None], hidden_state[:-1]], axis=0)
    d_log = back_state * state_prev * decay_rate
    d_drive_sum = jnp.einsum("tne,tn->te", back_state, input_b, precision=PRECISE)
    d_step_size = jnp.sum(d_log * decay_base[None], axis=1) + act_wide * d_drive_sum
    grad_decay = decay_base * jnp.einsum("tne,te->ne", d_log, step_size, precision=PRECISE)
    d_in_b = jnp.einsum("tne,te->tn", back_state, step_size * act_wide, precision=PRECISE)
    d_step = (d_step_size * jax.nn.sigmoid(step_pre)).astype(jnp.bfloat16)
    d_step_wide = d_step.astype(jnp.float32)
    grad_bias = jnp.dot(mask_cols.T, d_step_wide, precision=PRECISE)
    grad_dt = masked_outer(mask_low, low_rank, d_step)
    d_low = masked_back(mask_cols, d_step, stack_dt)
    d_params = lax.psum(jnp.concatenate([d_low, d_in_b, d_out_c], axis=1), "tp").astype(
        jnp.bfloat16
    )
    grad_x = masked_outer(mask_low, activated, d_params)
    d_activ = (
        d_mixed * chan_full[K + 1][None, :]
        + step_size * d_drive_sum
        + masked_back(mask_cols, d_params, stack_x)
    )
    d_conv = (d_activ * silu_grad(conv_pre)).astype(jnp.bfloat16)
    rim_back = passed_along(d_conv[: K - 1], "seq", -1)
    d_conv_wide = d_conv.astype(jnp.float32)
    conv_after = jnp.concatenate([d_conv, rim_back], axis=0).astype(jnp.float32)
    d_inner = jnp.zeros((tok_local, inner_width), jnp.float32)
    grad_taps = []
    for tap_index in range(K):
        grad_taps.append(
            jnp.sum(
                d_conv_wide * extended[tap_index : tap_index + tok_local] * same_docs[tap_index],
                axis=0,
            )
        )
        offset = K - 1 - tap_index
        same_after = (seg_after[offset : offset + tok_local] == seg_local).astype(jnp.float32)[
            :, None
        ]
        d_inner = (
            d_inner
            + chan_full[tap_index][None, :] * conv_after[offset : offset + tok_local] * same_after
        )
    grad_conv_b = jnp.sum(d_conv_wide, axis=0)
    d_proj = jnp.concatenate([d_inner, d_gate], axis=1).astype(jnp.bfloat16)
    grad_in = masked_outer(mask_low, normed, d_proj).reshape(M, D, 2, inner_width)
    d_normed = lax.psum(masked_back(mask_cols, d_proj, in_flat), "tp")
    grad_gain = jnp.sum(d_normed * scaled, axis=0)
    d_scaled = d_normed * gain_full[None, :]
    d_tokens = inv_root * (d_scaled - scaled * jnp.mean(d_scaled * scaled, axis=-1, keepdims=True))
    tokens_grad = out_grad.astype(jnp.float32) + lax.dynamic_slice_in_dim(
        d_tokens, tp_index * width_tp, width_tp, 1
    )
    grad_channel = jnp.concatenate(
        [jnp.stack(grad_taps), grad_conv_b[None], grad_skip[None], grad_bias, grad_decay], axis=0
    )
    reduced = (
        lax.psum_scatter(grad_in, "seq", scatter_dimension=1, tiled=True),
        lax.psum_scatter(grad_x, "seq", scatter_dimension=1, tiled=True),
        lax.psum_scatter(grad_dt, "seq", scatter_dimension=1, tiled=True),
        lax.psum_scatter(grad_out, "seq", scatter_dimension=2, tiled=True),
        lax.psum_scatter(grad_channel, "seq", scatter_dimension=1, tiled=True),
        lax.psum_scatter(grad_gain, "seq", scatter_dimension=0, tiled=True),
    )
    weights = (w_in, w_x, w_dt, w_out, channel, norm_gain)
    moments = (moment_in, moment_x, moment_dt, moment_out, moment_channel, moment_gain)
    squares = (square_in, square_x, square_dt, square_out, square_channel, square_gain)
    averages = (average_in, average_x, average_dt, average_out, average_channel, average_gain)
    adam_all = [
        adam_parts(reduced[position], moments[position], squares[position]) for position in range(6)
    ]
    directions = [adam_all[position][2] + WEIGHT_DECAY * weights[position] for position in range(4)]
    weight_sums = jnp.stack(
        [
            jnp.sum(
                weights[position] * weights[position], axis=tuple(range(1, weights[position].ndim))
            )
            for position in range(4)
        ]
    )
    direction_sums = jnp.stack(
        [
            jnp.sum(
                directions[position] * directions[position],
                axis=tuple(range(1, directions[position].ndim)),
            )
            for position in range(4)
        ]
    )
    totals = lax.psum(jnp.stack([weight_sums, direction_sums]), ("seq", "tp"))
    trust_ratio = jnp.sqrt(totals[0]) / jnp.sqrt(totals[1])
    new_weights = []
    new_averages = []
    for position in range(6):
        weight = weights[position]
        if position < 4:
            updated = (
                weight
                - MATRIX_RATE
                * trust_ratio[position].reshape((M,) + (1,) * (weight.ndim - 1))
                * directions[position]
            )
        elif position == 4:
            updated = weight - CHANNEL_RATE * adam_all[position][2]
        else:
            updated = weight - GAIN_RATE * adam_all[position][2]
        new_weights.append(updated)
        new_averages.append(AVERAGE_KEEP * averages[position] + (1.0 - AVERAGE_KEEP) * updated)
    return (
        layer_out,
        tokens_grad,
        new_weights[0],
        new_weights[1],
        new_weights[2],
        new_weights[3],
        new_weights[4],
        new_weights[5],
        adam_all[0][0],
        adam_all[1][0],
        adam_all[2][0],
        adam_all[3][0],
        adam_all[4][0],
        adam_all[5][0],
        adam_all[0][1],
        adam_all[1][1],
        adam_all[2][1],
        adam_all[3][1],
        adam_all[4][1],
        adam_all[5][1],
        new_averages[0],
        new_averages[1],
        new_averages[2],
        new_averages[3],
        new_averages[4],
        new_averages[5],
    )


MESH = pl.DeviceIdType.MESH
VMEM_LIMIT = 60 * 1024 * 1024
LANES = 128
F32 = jnp.float32
BF16 = jnp.bfloat16
NT = (((1,), (1,)), ((), ()))
TN = (((0,), (0,)), ((), ()))


def dot(a, b, dims=(((1,), (0,)), ((), ()))):
    return lax.dot_general(a, b, dims, preferred_element_type=F32)


def local_call(kernel, out_shape, n_in, scratch=(), cost=None):
    return pl.pallas_call(
        kernel,
        out_shape=out_shape,
        in_specs=[pl.BlockSpec(memory_space=pltpu.VMEM)] * n_in,
        out_specs=jax.tree.map(lambda _: pl.BlockSpec(memory_space=pltpu.VMEM), out_shape),
        scratch_shapes=list(scratch),
        compiler_params=pltpu.CompilerParams(vmem_limit_bytes=VMEM_LIMIT),
        cost_estimate=cost,
    )


def remote_call(kernel, out_shape, n_in, scratch, ident):
    return pl.pallas_call(
        kernel,
        out_shape=out_shape,
        in_specs=[pl.BlockSpec(memory_space=pltpu.VMEM)] * n_in,
        out_specs=jax.tree.map(lambda _: pl.BlockSpec(memory_space=pltpu.VMEM), out_shape),
        scratch_shapes=list(scratch),
        compiler_params=pltpu.CompilerParams(
            collective_id=ident, has_side_effects=True, vmem_limit_bytes=VMEM_LIMIT
        ),
    )


def sds(shape, dtype=F32):
    return jax.ShapeDtypeStruct(shape, dtype)


def seq_copy(src, dst, send, recv, device):
    return pltpu.make_async_remote_copy(
        src_ref=src,
        dst_ref=dst,
        send_sem=send,
        recv_sem=recv,
        device_id=device,
        device_id_type=MESH,
    )


def place(S, PN):
    s, p = lax.axis_index("seq"), lax.axis_index("tp")
    return s, p, lax.div(s, 2), lax.rem(s, 2)


def greet_all(S, PN):
    s, p = lax.axis_index("seq"), lax.axis_index("tp")
    n = S * PN
    me = s * PN + p
    bar = pltpu.get_barrier_semaphore()

    def greet(k, _):
        j = lax.rem(me + k, n)
        pl.semaphore_signal(
            bar,
            inc=1,
            device_id={"seq": lax.div(j, PN), "tp": lax.rem(j, PN)},
            device_id_type=MESH,
        )
        return 0

    lax.fori_loop(1, n, greet, 0)
    pl.semaphore_wait(bar, n - 1)


class Spread:
    def __init__(self, S, PN, own, buf, zs, zr, xs, xr, ys, yr, cs, cr, ls):
        s, p, z, x = place(S, PN)
        self.zn = S // 2
        zn = self.zn
        other_x = {"seq": 2 * z + 1 - x}
        other_y = {"tp": lax.rem(p + 2, PN)}
        other_c = {"tp": p + 1 - 2 * lax.rem(p, 2)}

        def at(k, j):
            return 2 * lax.rem(z - k + zn, zn) + (x if j == 0 else 1 - x)

        self.local = pltpu.make_async_copy(own, buf.at[p, s], ls)
        self.z = [
            seq_copy(own, buf.at[p, s], zs.at[k], zr.at[k], {"seq": 2 * lax.rem(z + k, zn) + x})
            for k in range(1, zn)
        ]
        self.x = []
        self.y = {}
        for k in range(zn):
            src = own if k == 0 else buf.at[p, at(k, 0)]
            self.x.append(seq_copy(src, buf.at[p, at(k, 0)], xs.at[k], xr.at[k], other_x))
            for j in range(2):
                src = own if (k == 0 and j == 0) else buf.at[p, at(k, j)]
                self.y[k, j] = seq_copy(
                    src, buf.at[p, at(k, j)], ys.at[2 * k + j], yr.at[2 * k + j], other_y
                )
        q = lax.rem(p + 2, PN)
        self.c = [
            seq_copy(buf.at[p], buf.at[p], cs.at[0], cr.at[0], other_c),
            seq_copy(buf.at[q], buf.at[q], cs.at[1], cr.at[1], other_c),
        ]

    def start(self):
        self.local.start()
        for cp in self.z:
            cp.start()
        self.x[0].start()
        self.y[0, 0].start()

    def forward(self):
        for k in range(1, self.zn):
            self.z[k - 1].wait_recv()
            self.x[k].start()
            self.y[k, 0].start()
        for k in range(self.zn):
            self.x[k].wait_recv()
            self.y[k, 1].start()
        self.local.wait()
        self.c[0].start()

    def finish(self):
        for cp in self.y.values():
            cp.wait_recv()
        self.c[1].start()
        for cp in self.z + self.x + list(self.y.values()):
            cp.wait_send()
        for cp in self.c:
            cp.wait()

    @staticmethod
    def semaphores(S):
        dma = pltpu.SemaphoreType.DMA
        return [dma((S // 2,))] * 4 + [dma((S,))] * 2 + [dma((2,))] * 2 + [dma]


def row_copies(S, src, dst, send, recv):
    s = lax.axis_index("seq")
    out = []
    for k in range(1, S):
        d = lax.rem(s + k, S)
        out.append(seq_copy(src(d), dst(s), send.at[k], recv.at[k], {"seq": d}))
    return out


def sum_over_all(S, PN, lr, bct, LR, BCT, got_l, got_b, ssl, rsl, ssb, rsb, sgl, rgl, sgb, rgb):
    n = S * PN
    s, p = lax.axis_index("seq"), lax.axis_index("tp")
    me = s * PN + p
    rows = lr.shape[0] // n
    per = n // bct.shape[0]
    high = bct.shape[1] // per

    def device(j):
        return {"seq": lax.div(j, PN), "tp": lax.rem(j, PN)}

    def rows_of(j):
        return pl.ds(pl.multiple_of(j * rows, 16), rows)

    def slab(ref, j):
        return ref.at[lax.div(j, per), pl.ds(pl.multiple_of(lax.rem(j, per) * high, 8), high)]

    def first(k):
        j = lax.rem(me + k, n)
        return (
            seq_copy(lr.at[rows_of(j)], got_l.at[k], ssl.at[k], rsl.at[k], device(j)),
            seq_copy(slab(bct, j), got_b.at[k], ssb.at[k], rsb.at[k], device(j)),
        )

    def second(k):
        j = lax.rem(me + k, n)
        mine_l, mine_b = LR.at[rows_of(me)], slab(BCT, me)
        return (
            seq_copy(mine_l, mine_l, sgl.at[k], rgl.at[k], device(j)),
            seq_copy(mine_b, mine_b, sgb.at[k], rgb.at[k], device(j)),
        )

    def start(copies, k):
        for cp in copies(k):
            cp.start()
        return 0

    def wait(copies, k):
        for cp in copies(k):
            cp.wait()
        return 0

    lax.fori_loop(1, n, lambda k, _: start(first, k), 0)
    got_l[0] = lr[rows_of(me), :]
    got_b[0] = slab(bct, me)[...]
    lax.fori_loop(1, n, lambda k, _: wait(first, k), 0)
    LR[rows_of(me), :] = jnp.sum(got_l[...], axis=0).astype(LR.dtype)
    slab(BCT, me)[...] = jnp.sum(got_b[...], axis=0)
    lax.fori_loop(1, n, lambda k, _: start(second, k), 0)
    lax.fori_loop(1, n, lambda k, _: wait(second, k), 0)


def sum_scratch(S, PN, T):
    n = S * PN
    dma = pltpu.SemaphoreType.DMA
    slabs = (T // LANES) * 2 * N // n
    return [pltpu.VMEM((n, T // n, R), F32), pltpu.VMEM((n, slabs, LANES), F32)] + [dma((n,))] * 8


def softplus(v):
    u = jnp.exp(-jnp.abs(v))
    w = 1.0 + u
    small = jnp.where(w == 1.0, u, jnp.log(w) * (u / jnp.where(w == 1.0, 1.0, w - 1.0)))
    return jnp.maximum(v, 0.0) + small


def masked_sum(acc, aux, r, C):
    total = acc[:, 0:C] * aux[r, 0:1]
    for m in range(1, M):
        total = total + acc[:, m * C : (m + 1) * C] * aux[r, m : m + 1]
    return total


def forward_kernel(S, PN, *refs):
    (tok, og, modrow, wdt_mine, gain_mine, wi, wg, wo, segs, ch, wlr, wbc) = refs[:12]
    (act, conv, inner, low, bct, pre, H, gated, dgate, dmix, aux, X, NR, G, WD, INV) = refs[12:28]
    rest = list(refs[28:])
    take = lambda k: [rest.pop(0) for _ in range(k)]
    tile, toks, ogs, nrm, Wi, Wg, Wo, AUX, GAIN = take(9)
    step, drive, keep, Y, pad, act3, lr, bcp = take(8)
    ag1, ag2 = take(9), take(9)
    ws = take(12)
    ls = take(1)[0]
    sums = take(10)
    s, p, z, x = place(S, PN)
    TL, DD = tok.shape
    T = S * TL
    width = DD // S
    quarter = DD // PN
    C = act.shape[1]
    rows = 128

    wide = tok[...].astype(F32)
    inv = lax.rsqrt(jnp.mean(wide * wide, axis=1, keepdims=True) + EPSILON)
    row = jnp.transpose(jnp.broadcast_to(inv, (TL, LANES)))[0:8]
    tile[...] = jnp.where(
        lax.broadcasted_iota(jnp.int32, row.shape, 0) == 0, modrow[...], row
    )
    greet_all(S, PN)
    chans = lambda d: pl.ds(pl.multiple_of(d * C, LANES), C)
    block = lambda d: pl.ds(pl.multiple_of(d * width, width), width)
    tokens = Spread(
        S, PN, tok.at[:, pl.ds(pl.multiple_of(p * quarter, LANES), quarter)], toks, *ag1
    )
    small = (
        row_copies(S, lambda d: tile, lambda t: AUX.at[t], ws[0], ws[1])
        + row_copies(S, lambda d: gain_mine, lambda t: GAIN.at[t], ws[2], ws[3])
    )
    dts = row_copies(S, lambda d: wdt_mine.at[:, :, chans(d)], lambda t: WD.at[t], ws[4], ws[5])
    inners = row_copies(S, lambda d: wi.at[d], lambda t: Wi.at[block(t)], ws[6], ws[7])
    gates = row_copies(S, lambda d: wg.at[d], lambda t: Wg.at[block(t)], ws[8], ws[9])
    outs = row_copies(S, lambda d: wo.at[d], lambda t: Wo.at[t], ws[10], ws[11])
    cotangent = Spread(S, PN, og, ogs, *ag2)
    for cp in small:
        cp.start()
    tokens.start()
    for cp in inners:
        cp.start()
    own = [
        pltpu.make_async_copy(tile, AUX.at[s], ls.at[0]),
        pltpu.make_async_copy(gain_mine, GAIN.at[s], ls.at[1]),
        pltpu.make_async_copy(wdt_mine.at[:, :, chans(s)], WD.at[s], ls.at[2]),
        pltpu.make_async_copy(wi.at[s], Wi.at[block(s)], ls.at[3]),
        pltpu.make_async_copy(wg.at[s], Wg.at[block(s)], ls.at[4]),
        pltpu.make_async_copy(wo.at[s], Wo.at[s], ls.at[5]),
    ]
    for cp in own:
        cp.start()
    for cp in own:
        cp.wait()
    tokens.forward()
    for cp in small:
        cp.wait()
    lane = lax.broadcasted_iota(jnp.int32, (TL, 8), 1)

    def columns(t, _):
        r = pl.ds(pl.multiple_of(t * TL, TL), TL)
        turned = jnp.transpose(jnp.concatenate([AUX[t]] * (LANES // 8), axis=0))
        mask = (turned[:, 0:1] == lane.astype(F32)).astype(F32)
        aux[r, :] = jnp.where(
            lane < M, mask, jnp.where(lane == 7, turned[:, 1:2], segs[r, :])
        )
        return 0

    lax.fori_loop(0, S, columns, 0)
    tokens.finish()
    per = quarter // width

    def norm(t, _):
        r = pl.ds(pl.multiple_of(t * TL, TL), TL)
        scale = aux[r, 7:8]
        for q in range(PN):
            scaled = toks[q, t].astype(F32) * scale
            for j in range(per):
                part = scaled[:, j * width : (j + 1) * width] * GAIN[q * per + j, 0:1, :]
                nrm[r, q * quarter + j * width : q * quarter + (j + 1) * width] = part.astype(BF16)
        return 0

    lax.fori_loop(0, S, norm, 0)
    for cp in inners:
        cp.wait()
    for cp in gates + dts:
        cp.start()

    big = 256
    pad[0:8, :] = jnp.zeros((8, C), F32)

    def first(i, _):
        r = pl.ds(pl.multiple_of(i * big, big), big)
        value = masked_sum(dot(nrm[r, :], Wi[...]), aux, r, C).astype(BF16)
        inner[r, :] = value
        pad[pl.ds(pl.multiple_of(i * big + 8, 8), big), :] = value.astype(F32)
        return 0

    lax.fori_loop(0, T // big, first, 0)

    def convolve(i, _):
        r = pl.ds(pl.multiple_of(i * rows, rows), rows)
        window = pad[pl.ds(pl.multiple_of(i * rows, rows), rows + 8), :]
        v = jnp.broadcast_to(ch[K : K + 1, :], (rows, C))
        for k in range(K):
            term = ch[k : k + 1, :] * window[8 - (K - 1) + k : 8 - (K - 1) + k + rows]
            v = v + (term * aux[r, M + k : M + k + 1] if k < K - 1 else term)
        conv[r, :] = v
        a = (v / (1.0 + jnp.exp(-v))).astype(BF16)
        act[r, :] = a
        a_wide = a.astype(F32)
        for m in range(M):
            act3[r, m * C : (m + 1) * C] = (a_wide * aux[r, m : m + 1]).astype(BF16)
        lr[r, :] = dot(act3[r, :], wlr[...])
        bcp[i] = dot(wbc[...], act3[r, :], NT)
        return 0

    lax.fori_loop(0, T // rows, convolve, 0)
    sum_over_all(S, PN, lr, bcp, low, bct, *sums)
    for cp in dts:
        cp.wait()
    cotangent.start()
    for cp in outs:
        cp.start()

    def prepare(i, _):
        r = pl.ds(pl.multiple_of(i * rows, rows), rows)
        low_wide = low[r, :].astype(F32)
        bias = jnp.zeros((rows, C), F32)
        for m in range(M):
            mask = aux[r, m : m + 1]
            masked = (low_wide * mask).astype(BF16)
            bias = bias + mask * ch[K + 2 + m : K + 3 + m, :]
            for t in range(S):
                h = R // S
                bias = bias + dot(masked[:, t * h : (t + 1) * h], WD[t, m])
        pre[r, :] = bias
        st = softplus(bias)
        step[r, :] = st
        drive[r, :] = st * act[r, :].astype(F32)
        keep[r, :] = jnp.broadcast_to(aux[r, 6:7], (rows, C))
        return 0

    lax.fori_loop(0, T // rows, prepare, 0)
    scan_forward(T, C, bct, ch, step, drive, keep, H, Y)
    cotangent.forward()
    for cp in gates:
        cp.wait()

    def gate(i, _):
        r = pl.ds(pl.multiple_of(i * big, big), big)
        drive[r, :] = masked_sum(dot(nrm[r, :], Wg[...]), aux, r, C)
        return 0

    lax.fori_loop(0, T // big, gate, 0)
    cotangent.finish()
    for cp in outs:
        cp.wait()

    def back(i, _):
        r = pl.ds(pl.multiple_of(i * big, big), big)
        acc = jnp.zeros((big, M * C), F32)
        for q in range(PN):
            g = ogs[q, pl.ds(i * (big // TL), big // TL)].reshape(big, quarter)
            for j in range(per):
                acc = acc + dot(g[:, j * width : (j + 1) * width], Wo[q * per + j], NT)
        keep[r, :] = masked_sum(acc, aux, r, C)
        return 0

    lax.fori_loop(0, T // big, back, 0)

    def finish(i, _):
        r = pl.ds(pl.multiple_of(i * rows, rows), rows)
        mixed = Y[r, :] + ch[K + 1 : K + 2, :] * act[r, :].astype(F32)
        g, d = drive[r, :], keep[r, :]
        sig = 1.0 / (1.0 + jnp.exp(-g))
        gated[r, :] = (mixed * (g * sig)).astype(BF16)
        dmix[r, :] = d * (g * sig)
        dgate[r, :] = (d * mixed * (sig * (1.0 + g * (1.0 - sig)))).astype(BF16)
        return 0

    lax.fori_loop(0, T // rows, finish, 0)
    mine = pl.ds(pl.multiple_of(lax.rem(s, per) * width, width), width)
    NR[...] = nrm[:, pl.ds(pl.multiple_of(s * width, width), width)]

    def own_features(t, _):
        r = pl.ds(pl.multiple_of(t * TL, TL), TL)
        X[r, :] = toks[lax.div(s, per), t, :, mine]
        G[r, :] = ogs[lax.div(s, per), t, :, mine]
        return 0

    lax.fori_loop(0, S, own_features, 0)
    INV[...] = jnp.broadcast_to(inv, INV.shape)


def scan_forward(T, C, bct, ch, step, drive, keep, H, Y):
    base = -jnp.exp(ch[K + 2 + M : K + 2 + M + N, :])
    H[0] = jnp.zeros((N, C), F32)

    def chunk(c, h):
        bc = bct[c]

        def eight(i, h):
            cols = pltpu.roll(bc, lax.rem(LANES - 8 * i, LANES), 1)
            t0 = pl.multiple_of(c * LANES + i * 8, 8)
            r = pl.ds(t0, 8)
            st, dr, kp = step[r, :], drive[r, :], keep[r, :]
            ys = []
            for j in range(8):
                rate = jnp.exp(st[j : j + 1] * base) * kp[j : j + 1]
                h = rate * h + dr[j : j + 1] * cols[0:N, j : j + 1]
                H[t0 + j + 1] = h
                ys.append(jnp.sum(cols[N : 2 * N, j : j + 1] * h, axis=0, keepdims=True))
            Y[r, :] = jnp.concatenate(ys, axis=0)
            return h

        return lax.fori_loop(0, LANES // 8, eight, h)

    lax.fori_loop(0, T // LANES, chunk, jnp.zeros((N, C), F32))


def forward_call(S, PN, args, T, C, width):
    dma = pltpu.SemaphoreType.DMA
    TL, DD = args[0].shape
    chunks = T // LANES
    f = lambda *shape: sds(shape)
    b = lambda *shape: sds(shape, BF16)
    vf = lambda *shape: pltpu.VMEM(shape, F32)
    vb = lambda *shape: pltpu.VMEM(shape, BF16)
    out = (
        b(T, C), f(T, C), b(T, C), b(T, R), f(chunks, 2 * N, LANES), f(T, C), f(T + 1, N, C),
        b(T, C), b(T, C), f(T, C), f(T, 8), b(T, width), b(T, width), b(T, width),
        b(S, M, R // S, C), f(TL, LANES),
    )
    scratch = (
        [vf(8, TL), vb(PN, S, TL, DD // PN), vb(PN, S, TL, DD // PN), vb(T, DD)]
        + [vb(DD, M * C), vb(DD, M * C), vb(S, M * C, width), vf(S, 8, TL), vf(S, 8, width)]
        + [vf(T, C)] * 4
        + [vf(T + 8, C), vb(T, M * C), vf(T, R), vf(chunks, 2 * N, LANES)]
        + Spread.semaphores(S) * 2
        + [dma((S,))] * 12
        + [dma((6,))]
        + sum_scratch(S, PN, T)
    )
    return remote_call(
        functools.partial(forward_kernel, S, PN), out, len(args), scratch, 0
    )(*args)


def row_gather(S, block):
    across = [(i, i ^ 1) for i in range(S)]
    near = [block] + [
        lax.ppermute(block, "seq", [(i, (i + 2 * k) % S) for i in range(S)])
        for k in range(1, S // 2)
    ]
    out = []
    for blk in near:
        out += [blk, lax.ppermute(blk, "seq", across)]
    return jnp.stack(out)


def row_order(S):
    s = lax.axis_index("seq")
    z, x = lax.div(s, 2), lax.rem(s, 2)
    zn = S // 2
    return jnp.stack(
        [lax.rem(z - k + zn, zn) * 2 + xx for k in range(zn) for xx in (x, 1 - x)]
    ).astype(jnp.int32)


def backward_sum_kernel(S, PN, lr, bct, more, LR, BCT, MORE, sx, rx, lx, *sums):
    greet_all(S, PN)
    s = lax.axis_index("seq")
    step = more.shape[1] // S
    part = lambda d: more.at[:, pl.ds(pl.multiple_of(d * step, 8), step), :]
    copies = row_copies(S, part, lambda t: MORE.at[t], sx, rx)
    for cp in copies:
        cp.start()
    own = pltpu.make_async_copy(part(s), MORE.at[s], lx)
    own.start()
    sum_over_all(S, PN, lr, bct, LR, BCT, *sums)
    own.wait()
    for cp in copies:
        cp.wait()


def backward_sum(S, PN, lr, bct, more):
    dma = pltpu.SemaphoreType.DMA
    return remote_call(
        functools.partial(backward_sum_kernel, S, PN),
        (
            sds(lr.shape, BF16),
            sds(bct.shape),
            sds((S, more.shape[0], more.shape[1] // S, more.shape[2])),
        ),
        3,
        [dma((S,)), dma((S,)), dma] + sum_scratch(S, PN, lr.shape[0]),
        2,
    )(lr, bct, more)


def unscan_kernel(
    pre, H, dmix, act, bct, aux, ch, wdtT, low,
    dlow, dbct, gdt, gch, dact, step, drive, keep, DS, DB, dst3, low3, dst,
):
    T, C = act.shape
    rows = 128

    def prepare(i, _):
        r = pl.ds(pl.multiple_of(i * rows, rows), rows)
        sp = pre[r, :]
        st = softplus(sp)
        step[r, :] = st
        drive[r, :] = st * act[r, :].astype(F32)
        keep[r, :] = jnp.broadcast_to(aux[r, 6:7], (rows, C))
        return 0

    lax.fori_loop(0, T // rows, prepare, 0)
    base = -jnp.exp(ch[K + 2 + M : K + 2 + M + N, :])
    lane = lax.broadcasted_iota(jnp.int32, (N, LANES), 1)
    nothing = jnp.zeros((N, C), F32)
    chunks = T // LANES

    def chunk(cc, carry):
        c = chunks - 1 - cc
        bc = bct[c]

        def eight(ii, carry):
            flow, hcur, gacc, accb, accc = carry
            i = LANES // 8 - 1 - ii
            cols = pltpu.roll(bc, lax.rem(LANES - 8 * i, LANES), 1)
            t0 = pl.multiple_of(c * LANES + i * 8, 8)
            r = pl.ds(t0, 8)
            st, dr, kp, dm = step[r, :], drive[r, :], keep[r, :], dmix[r, :]
            ds, db = [None] * 8, [None] * 8
            for j in reversed(range(8)):
                bcol, ccol = cols[0:N, j : j + 1], cols[N : 2 * N, j : j + 1]
                back = ccol * dm[j : j + 1] + flow
                rate = jnp.exp(st[j : j + 1] * base) * kp[j : j + 1]
                hprev = H[t0 + j]
                here = lane == 8 * i + j
                accc = jnp.where(
                    here, jnp.sum(dm[j : j + 1] * hcur, axis=1, keepdims=True), accc
                )
                accb = jnp.where(
                    here, jnp.sum(back * dr[j : j + 1], axis=1, keepdims=True), accb
                )
                flow = rate * back
                dlog = flow * hprev
                gacc = gacc + dlog * st[j : j + 1]
                ds[j] = jnp.sum(dlog * base, axis=0, keepdims=True)
                db[j] = jnp.sum(back * bcol, axis=0, keepdims=True)
                hcur = hprev
            DS[r, :] = jnp.concatenate(ds, axis=0)
            DB[r, :] = jnp.concatenate(db, axis=0)
            return flow, hcur, gacc, accb, accc

        blank = jnp.zeros((N, LANES), F32)
        flow, hcur, gacc, accb, accc = lax.fori_loop(
            0, LANES // 8, eight, carry + (blank, blank)
        )
        dbct[c, 0:N, :] = accb
        dbct[c, N : 2 * N, :] = accc
        return flow, hcur, gacc

    _, _, gacc = lax.fori_loop(0, chunks, chunk, (nothing, H[T], nothing))

    def finish(i, carry):
        skip, bias = carry
        r = pl.ds(pl.multiple_of(i * rows, rows), rows)
        a = act[r, :].astype(F32)
        back_b = DB[r, :]
        grad = DS[r, :] + a * back_b
        d = (grad / (1.0 + jnp.exp(-pre[r, :]))).astype(BF16)
        dst[r, :] = d
        wide = d.astype(F32)
        low_wide = low[r, :].astype(F32)
        sums = []
        for m in range(M):
            mask = aux[r, m : m + 1]
            masked = wide * mask
            sums.append(jnp.sum(masked, axis=0, keepdims=True))
            dst3[r, m * C : (m + 1) * C] = masked.astype(BF16)
            low3[r, m * R : (m + 1) * R] = (low_wide * mask).astype(BF16)
        dlow[r, :] = dot(dst3[r, :], wdtT[...])
        dact[r, :] = dmix[r, :] * ch[K + 1 : K + 2, :] + step[r, :] * back_b
        skip = skip + jnp.sum(dmix[r, :] * a, axis=0, keepdims=True)
        return skip, bias + jnp.concatenate(sums, axis=0)

    skip, bias = lax.fori_loop(
        0, T // rows, finish, (jnp.zeros((1, C), F32), jnp.zeros((M, C), F32))
    )
    gch[0:1, :] = skip
    gch[1 : 1 + M, :] = bias
    gch[1 + M : 1 + M + N, :] = base * gacc
    for m in range(M):
        gdt[m] = dot(low3[:, m * R : (m + 1) * R], dst[...], TN)


def unconv_kernel(
    dpar, act, conv, inner, aux, ch, wxT, dact, dinner, gx, gtap, pad, tail, dpar3, act3,
):
    T, C = act.shape
    XWID = dpar.shape[1]
    rows = 128
    pad[0:8, :] = jnp.zeros((8, C), F32)
    tail[T : T + 8, :] = jnp.zeros((8, C), F32)

    def fill(i, _):
        r = pl.ds(pl.multiple_of(i * rows, rows), rows)
        pad[pl.ds(pl.multiple_of(i * rows + 8, 8), rows), :] = inner[r, :].astype(F32)
        wide = dpar[r, :].astype(F32)
        a = act[r, :].astype(F32)
        total = dact[r, :]
        for m in range(M):
            mask = aux[r, m : m + 1]
            total = total + dot((wide * mask).astype(BF16), wxT[m])
            act3[r, m * C : (m + 1) * C] = (a * mask).astype(BF16)
        v = conv[r, :]
        sig = 1.0 / (1.0 + jnp.exp(-v))
        tail[r, :] = (total * (sig * (1.0 + v * (1.0 - sig)))).astype(BF16).astype(F32)
        return 0

    lax.fori_loop(0, T // rows, fill, 0)

    def body(i, sums):
        r = pl.ds(pl.multiple_of(i * rows, rows), rows)
        window = pad[pl.ds(pl.multiple_of(i * rows, rows), rows + 8), :]
        d = tail[r, :]
        ahead = tail[pl.ds(pl.multiple_of(i * rows, rows), rows + 8), :]
        same = aux[pl.ds(pl.multiple_of(i * rows, rows), rows + 8), :]
        total = ch[K - 1 : K, :] * d
        new = []
        for k in range(K):
            off = K - 1 - k
            shifted = window[8 - off : 8 - off + rows]
            if k < K - 1:
                shifted = shifted * aux[r, M + k : M + k + 1]
                total = total + ch[k : k + 1, :] * (
                    ahead[off : off + rows] * same[off : off + rows, M + k : M + k + 1]
                )
            new.append(jnp.sum(d * shifted, axis=0, keepdims=True))
        new.append(jnp.sum(d, axis=0, keepdims=True))
        dinner[r, :] = total.astype(BF16)
        return sums + jnp.concatenate(new, axis=0)

    gtap[0 : K + 1, :] = lax.fori_loop(0, T // rows, body, jnp.zeros((K + 1, C), F32))
    for m in range(M):
        gx[m] = dot(act3[:, m * C : (m + 1) * C], dpar[...], TN)


def out_kernel(order, blk, G, aux, w, layer, grad, masked, acc):
    i = pl.program_id(0)
    T, C = blk.shape[1:]

    @pl.when(i == 0)
    def _():
        acc[...] = jnp.zeros(acc.shape, F32)

    wide = blk[0].astype(F32)
    for m in range(M):
        masked[:, m * C : (m + 1) * C] = (wide * aux[:, m : m + 1]).astype(BF16)
        acc[...] += dot(masked[:, m * C : (m + 1) * C], w[m])
        grad[m] = dot(masked[:, m * C : (m + 1) * C], G[...], TN)

    @pl.when(i == pl.num_programs(0) - 1)
    def _():
        layer[...] = acc[...].astype(BF16)


def out_project(S, order, blocks, G, aux, w):
    T, C = blocks.shape[1:]
    width = G.shape[1]
    whole = lambda shape: pl.BlockSpec(shape, lambda i, o: (0,) * len(shape))
    return pl.pallas_call(
        out_kernel,
        out_shape=(sds((T, width), BF16), sds((M, S * C, width))),
        grid_spec=pltpu.PrefetchScalarGridSpec(
            num_scalar_prefetch=1,
            grid=(S,),
            in_specs=[
                pl.BlockSpec((1, T, C), lambda i, o: (i, 0, 0)),
                whole((T, width)),
                whole((T, 8)),
                pl.BlockSpec((M, C, width), lambda i, o: (0, o[i], 0)),
            ],
            out_specs=[whole((T, width)), pl.BlockSpec((M, C, width), lambda i, o: (0, o[i], 0))],
            scratch_shapes=[pltpu.VMEM((T, M * C), BF16), pltpu.VMEM((T, width), F32)],
        ),
        compiler_params=pltpu.CompilerParams(vmem_limit_bytes=VMEM_LIMIT),
    )(order, blocks, G, aux, w)


def in_kernel(order, b0, b1, A3T, W0, W1, aux, gain, X, dnorm, grad0, grad1, rowdot, gg, acc):
    i = pl.program_id(0)
    T, width = X.shape

    @pl.when(i == 0)
    def _():
        acc[...] = jnp.zeros(acc.shape, F32)

    d0, d1 = b0[0], b1[0]
    grad0[...] = dot(A3T[...], d0)
    grad1[...] = dot(A3T[...], d1)
    for m in range(M):
        rows = slice(m * width, (m + 1) * width)
        acc[m] += dot(d0, W0[rows, :], NT) + dot(d1, W1[rows, :], NT)

    @pl.when(i == pl.num_programs(0) - 1)
    def _():
        rows = 128

        def body(k, total):
            r = pl.ds(pl.multiple_of(k * rows, rows), rows)
            d = acc[0, r, :] * aux[r, 0:1]
            for m in range(1, M):
                d = d + acc[m, r, :] * aux[r, m : m + 1]
            scaled = X[r, :].astype(F32) * aux[r, 7:8]
            gained = d * gain[...]
            dnorm[r, :] = gained.astype(BF16)
            along = jnp.sum(gained * scaled, axis=1, keepdims=True)
            rowdot[k] = jnp.transpose(jnp.broadcast_to(along, (rows, LANES)))[0:8]
            return total + jnp.sum(d * scaled, axis=0, keepdims=True)

        total = lax.fori_loop(0, T // rows, body, jnp.zeros((1, width), F32))
        gg[...] = jnp.broadcast_to(total, gg.shape)


def in_project_back(S, order, b0, b1, A3T, W0, W1, aux, gain, X):
    T, C = b0.shape[1:]
    width = X.shape[1]
    whole = lambda shape: pl.BlockSpec(shape, lambda i, o: (0,) * len(shape))
    piece = pl.BlockSpec((M * width, C), lambda i, o: (0, o[i]))
    return pl.pallas_call(
        in_kernel,
        out_shape=(
            sds((T, width), BF16),
            sds((M * width, S * C)),
            sds((M * width, S * C)),
            sds((T // 128, 8, 128)),
            sds((8, width)),
        ),
        grid_spec=pltpu.PrefetchScalarGridSpec(
            num_scalar_prefetch=1,
            grid=(S,),
            in_specs=[
                pl.BlockSpec((1, T, C), lambda i, o: (i, 0, 0)),
                pl.BlockSpec((1, T, C), lambda i, o: (i, 0, 0)),
                whole((M * width, T)),
                piece,
                piece,
                whole((T, 8)),
                whole((1, width)),
                whole((T, width)),
            ],
            out_specs=[
                whole((T, width)),
                piece,
                piece,
                whole((T // 128, 8, 128)),
                whole((8, width)),
            ],
            scratch_shapes=[pltpu.VMEM((M, T, width), F32)],
        ),
        compiler_params=pltpu.CompilerParams(vmem_limit_bytes=VMEM_LIMIT),
    )(order, b0, b1, A3T, W0, W1, aux, gain, X)


def last_kernel(S, PN, lo, dn, gg, tile, rowdot, LO, DN, GG, TILE, mine, los, lor, dns, dnr, gs, gr, ts, tr, ls):
    s, p = lax.axis_index("seq"), lax.axis_index("tp")
    n = S * PN
    ratio = S // PN
    me = s * PN + p
    home = lax.div(s, ratio)
    slot = lax.rem(s, ratio) * PN + p
    bar = pltpu.get_barrier_semaphore()

    def device(j):
        return {"seq": lax.div(j, PN), "tp": lax.rem(j, PN)}

    def greet(k, _):
        pl.semaphore_signal(
            bar, inc=1, device_id=device(lax.rem(me + k, n)), device_id_type=MESH
        )
        return 0

    lax.fori_loop(1, n, greet, 0)
    first = lax.broadcasted_iota(jnp.int32, tile.shape, 0)
    for b in range(S):
        mine[b] = jnp.where(first == 1, rowdot[b], tile[...])
    pl.semaphore_wait(bar, n - 1)
    TL = lo.shape[0] // S

    def block(k, start):
        rows = pl.ds(k * TL, TL)
        dev = {"seq": k, "tp": home}
        away = jnp.logical_or(s != k, home != p)

        @pl.when(away)
        def _():
            for cp in (
                seq_copy(dn.at[rows], DN.at[slot], dns.at[k], dnr.at[slot], dev),
                seq_copy(lo.at[rows], LO.at[slot], los.at[k], lor.at[slot], dev),
            ):
                if start:
                    cp.start()
                else:
                    cp.wait_send()

        if start:

            @pl.when(jnp.logical_not(away))
            def _():
                a = pltpu.make_async_copy(dn.at[rows], DN.at[slot], ls.at[0])
                b = pltpu.make_async_copy(lo.at[rows], LO.at[slot], ls.at[1])
                a.start()
                b.start()
                a.wait()
                b.wait()

    def tiles(k):
        j = lax.rem(me + k, n)
        return seq_copy(mine.at[lax.div(j, PN)], TILE.at[k], ts.at[k], tr.at[k], device(j))

    def send_tile(k, _):
        tiles(k).start()
        return 0

    def wait_tile(k, _):
        tiles(k).wait()
        return 0

    gains = [
        seq_copy(gg, GG.at[k], gs.at[k], gr.at[k], {"tp": lax.rem(p + k, PN)})
        for k in range(1, PN)
    ]
    for k in range(S):
        block(k, True)
    for cp in gains:
        cp.start()
    lax.fori_loop(1, n, send_tile, 0)
    GG[0] = gg[...]
    TILE[0] = mine[s]
    for cp in gains:
        cp.wait()
    lax.fori_loop(1, n, wait_tile, 0)
    for k in range(S):
        block(k, False)
    for h in range(ratio):
        for q in range(PN):
            t = ratio * p + h
            i = h * PN + q

            @pl.when(jnp.logical_or(t != s, p != q))
            def _():
                dev = {"seq": t, "tp": q}
                seq_copy(dn.at[0:TL], DN.at[i], dns.at[0], dnr.at[i], dev).wait_recv()
                seq_copy(lo.at[0:TL], LO.at[i], los.at[0], lor.at[i], dev).wait_recv()


def last_exchange(S, PN, lo, dn, gg, tile, rowdot):
    T, width = lo.shape
    n = S * PN
    dma = pltpu.SemaphoreType.DMA
    return remote_call(
        functools.partial(last_kernel, S, PN),
        (
            sds((S, T // S, width), BF16),
            sds((S, T // S, width), BF16),
            sds((PN,) + gg.shape),
            sds((n,) + tile.shape),
        ),
        5,
        [pltpu.VMEM((S,) + tile.shape, F32)]
        + [dma((S,))] * 4
        + [dma((PN,))] * 2
        + [dma((n,))] * 2
        + [dma((2,))],
        3,
    )(lo, dn, gg, tile, rowdot)


def local(
    tokens, out_grad, modality, segment,
    w_in, w_x, w_dt, w_out, channel, norm_gain,
    moment_in, moment_x, moment_dt, moment_out, moment_channel, moment_gain,
    square_in, square_x, square_dt, square_out, square_channel, square_gain,
    average_in, average_x, average_dt, average_out, average_channel, average_gain,
):
    S, PN = lax.axis_size("seq"), lax.axis_size("tp")
    s, p = lax.axis_index("seq"), lax.axis_index("tp")
    TL = tokens.shape[0]
    T = S * TL
    width = D // S
    inner_width = w_out.shape[1]
    C = inner_width // S
    zn = S // 2
    split = w_in.reshape(M, width, 2, S, C)
    win = jnp.transpose(w_in, (2, 0, 1, 3)).astype(BF16).reshape(2, M * width, inner_width)
    wi, wg = [
        jnp.transpose(split[:, :, h], (2, 1, 0, 3)).astype(BF16).reshape(S, width, M * C)
        for h in range(2)
    ]
    wout = w_out.astype(BF16)
    wo = jnp.transpose(wout.reshape(M, S, C, width), (1, 0, 2, 3)).reshape(S, M * C, width)
    wx = w_x.astype(BF16)
    wlr = wx[:, :, :R].reshape(M * C, R)
    wbc = jnp.transpose(wx[:, :, R:], (2, 0, 1)).reshape(2 * N, M * C)
    modrow = jnp.broadcast_to(modality.astype(F32)[None], (8, TL))
    ahead = jnp.concatenate([jnp.full((K - 1,), -1, jnp.int32), segment])
    same = [(ahead[k : k + T] == segment).astype(F32) for k in range(K - 1)]
    zero = jnp.zeros((T,), F32)
    segs = jnp.stack([zero] * M + same + [same[K - 2], zero], axis=1)
    gain = norm_gain[None, :]
    order = row_order(S)
    chunks = T // LANES

    act, conv, inner, low, bct, pre, H, gated, dgate, dmix, aux, X, NR, G, WD, INV = forward_call(
        S,
        PN,
        (
            tokens, out_grad, modrow, w_dt.astype(BF16), jnp.broadcast_to(gain, (8, width)),
            wi, wg, wo, segs, channel, wlr, wbc,
        ),
        T, C, width,
    )
    wdt = jnp.transpose(WD, (1, 0, 2, 3)).reshape(M, R, C)
    col = lambda dtype=F32: pltpu.VMEM((T, C), dtype)
    gated_all = row_gather(S, gated)
    dgate_all = row_gather(S, dgate)

    wdtT = jnp.transpose(wdt, (0, 2, 1)).reshape(M * C, R)
    dlow, dbct, gdt, gch, dact = local_call(
        unscan_kernel,
        (
            sds((T, R)),
            sds((chunks, 2 * N, LANES)),
            sds((M, R, C)),
            sds((1 + M + N, C)),
            sds((T, C)),
        ),
        9,
        [col(), col(), col(), col(), col()]
        + [pltpu.VMEM((T, M * C), BF16), pltpu.VMEM((T, M * R), BF16), col(BF16)],
    )(pre, H, dmix, act, bct, aux, channel, wdtT, low)
    dlow, dbct, gdt = backward_sum(S, PN, dlow, dbct, gdt)
    dpar = jnp.concatenate(
        [dlow, jnp.transpose(dbct, (0, 2, 1)).reshape(T, 2 * N).astype(BF16)], axis=1
    )
    grad_dt = jnp.transpose(gdt, (1, 2, 0, 3)).reshape(w_dt.shape)

    dinner, grad_x, gtap = local_call(
        unconv_kernel,
        (sds((T, C), BF16), sds((M, C, R + 2 * N)), sds((8, C))),
        8,
        [
            pltpu.VMEM((T + 8, C), F32),
            pltpu.VMEM((T + 8, C), F32),
            pltpu.VMEM((8, LANES), F32),
            pltpu.VMEM((T, M * C), BF16),
        ],
    )(
        dpar, act, conv, inner, jnp.concatenate([aux, jnp.zeros((8, 8), F32)]), channel,
        jnp.transpose(wx, (0, 2, 1)), dact,
    )
    dinner_all = row_gather(S, dinner)
    grad_channel = jnp.concatenate([gtap[: K + 1], gch], axis=0)

    layer_part, grad_out = out_project(S, order, gated_all, G, aux, wout)
    A3T = jnp.concatenate(
        [jnp.transpose(NR * aux[:, m : m + 1].astype(BF16)) for m in range(M)], axis=0
    )
    dnorm_part, gin0, gin1, rowdot, gg = in_project_back(
        S, order, dinner_all, dgate_all, A3T, win[0], win[1], aux, gain, X
    )
    grad_in = jnp.transpose(
        jnp.stack([gin0, gin1]).reshape(2, M, width, inner_width), (1, 2, 0, 3)
    )

    grads = [grad_in, grad_x, grad_dt, grad_out, grad_channel]
    weights = (w_in, w_x, w_dt, w_out, channel, norm_gain)
    moments = (moment_in, moment_x, moment_dt, moment_out, moment_channel, moment_gain)
    squares = (square_in, square_x, square_dt, square_out, square_channel, square_gain)
    averages = (average_in, average_x, average_dt, average_out, average_channel, average_gain)
    adam_all = [adam_parts(grads[i], moments[i], squares[i]) for i in range(5)]
    directions = [adam_all[i][2] + WEIGHT_DECAY * weights[i] for i in range(4)]
    squared = lambda v: jnp.sum(v * v, axis=tuple(range(1, v.ndim)))
    sums = jnp.concatenate([squared(v) for v in weights[:4]] + [squared(v) for v in directions])
    tile = jnp.broadcast_to(jnp.pad(sums, (0, LANES - sums.shape[0]))[None], (8, LANES))
    LO, DN, GG, TILE = last_exchange(S, PN, layer_part, dnorm_part, gg, tile, rowdot)

    totals = jnp.sum(TILE[:, 0, : 8 * M], axis=0).reshape(2, 4, M)
    along = jnp.sum(TILE[:, 1, :], axis=0)[:, None]
    adam_all.append(adam_parts(jnp.sum(GG[:, 0, :], axis=0), moment_gain, square_gain))

    def columns(blocks):
        b = jnp.sum(blocks.reshape(S // PN, PN, TL, width).astype(F32), axis=1)
        return jnp.concatenate([b[h] for h in range(S // PN)], axis=1)

    out_width = out_grad.shape[1]
    mine = lax.dynamic_slice_in_dim(tokens, p * out_width, out_width, 1).astype(F32)
    inv = INV[:, 0:1]
    layer_out = mine + columns(LO)
    tokens_grad = out_grad.astype(F32) + inv * (columns(DN) - mine * inv * (along / D))
    trust = jnp.sqrt(totals[0]) / jnp.sqrt(totals[1])
    new_weights, new_averages = [], []
    for i in range(6):
        w = weights[i]
        if i < 4:
            scale = MATRIX_RATE * trust[i].reshape((M,) + (1,) * (w.ndim - 1))
            new = w - scale * directions[i]
        else:
            new = w - (CHANNEL_RATE if i == 4 else GAIN_RATE) * adam_all[i][2]
        new_weights.append(new)
        new_averages.append(AVERAGE_KEEP * averages[i] + (1.0 - AVERAGE_KEEP) * new)
    return (
        layer_out,
        tokens_grad,
        *new_weights,
        *[a[0] for a in adam_all],
        *[a[1] for a in adam_all],
        *new_averages,
    )


def channels_fit(mesh):
    S, PN = mesh.shape["seq"], mesh.shape["tp"]
    n = S * PN
    return PN == 4 and S % 4 == 0 and (2 * N) % n == 0 and (D * 2 // n) % LANES == 0


def solution(mesh):
    placed = (
        P("seq", None),
        P("seq", "tp"),
        P("seq"),
        P(),
        P(None, "seq", None, "tp"),
        P(None, ("tp", "seq"), None),
        P(None, "seq", "tp"),
        P(None, "tp", "seq"),
        P(None, ("tp", "seq")),
        P("seq"),
        P(None, "seq", None, "tp"),
        P(None, ("tp", "seq"), None),
        P(None, "seq", "tp"),
        P(None, "tp", "seq"),
        P(None, ("tp", "seq")),
        P("seq"),
        P(None, "seq", None, "tp"),
        P(None, ("tp", "seq"), None),
        P(None, "seq", "tp"),
        P(None, "tp", "seq"),
        P(None, ("tp", "seq")),
        P("seq"),
        P(None, "seq", None, "tp"),
        P(None, ("tp", "seq"), None),
        P(None, "seq", "tp"),
        P(None, "tp", "seq"),
        P(None, ("tp", "seq")),
        P("seq"),
    )
    return jax.shard_map(
        local if channels_fit(mesh) else generic_local,
        mesh=mesh,
        in_specs=placed,
        out_specs=(
            P("seq", "tp"),
            P("seq", "tp"),
            P(None, "seq", None, "tp"),
            P(None, ("tp", "seq"), None),
            P(None, "seq", "tp"),
            P(None, "tp", "seq"),
            P(None, ("tp", "seq")),
            P("seq"),
            P(None, "seq", None, "tp"),
            P(None, ("tp", "seq"), None),
            P(None, "seq", "tp"),
            P(None, "tp", "seq"),
            P(None, ("tp", "seq")),
            P("seq"),
            P(None, "seq", None, "tp"),
            P(None, ("tp", "seq"), None),
            P(None, "seq", "tp"),
            P(None, "tp", "seq"),
            P(None, ("tp", "seq")),
            P("seq"),
            P(None, "seq", None, "tp"),
            P(None, ("tp", "seq"), None),
            P(None, "seq", "tp"),
            P(None, "tp", "seq"),
            P(None, ("tp", "seq")),
            P("seq"),
        ),
        check_vma=False,
    )
```

```python
import functools

import jax
import jax.numpy as jnp
from jax import lax
from jax.experimental import pallas as pl
from jax.experimental.pallas import tpu as pltpu
from jax.sharding import PartitionSpec as P

D = 2048
R = 128
N = 16
K = 4
M = 3
STEP = 10


EPSILON = 1e-05
BETA_ONE = 0.9
BETA_TWO = 0.999
ADAM_EPSILON = 1e-06
WEIGHT_DECAY = 0.01
MATRIX_RATE = 0.25
CHANNEL_RATE = 0.7
GAIN_RATE = 0.35
AVERAGE_KEEP = 0.8
PRECISE = lax.Precision.HIGHEST


def passed_along(value, axis, steps):
    count = lax.axis_size(axis)
    leading, last = (max(0, -steps), min(count, count - steps))
    return lax.ppermute(value, axis, [(source, source + steps) for source in range(leading, last)])


def prefix(x, axis, combine, identity, reverse):
    devices, place = (lax.axis_size(axis), lax.axis_index(axis))
    everything = jax.tree.map(lambda part: lax.all_gather(part, axis), x)
    start = jax.tree.map(
        lambda part, zero: jnp.broadcast_to(jnp.asarray(zero, part.dtype), part.shape), x, identity
    )

    def lap(k, before):
        at = devices - 1 - k if reverse else k
        reached = at > place if reverse else at < place
        new = combine(before, jax.tree.map(lambda part: part[at], everything))
        return jax.tree.map(lambda a, b: jnp.where(reached, a, b), new, before)

    return lax.fori_loop(0, devices, lap, start)


def silu_grad(operand):
    sigmoid_of = jax.nn.sigmoid(operand)
    return sigmoid_of * (1.0 + operand * (1.0 - sigmoid_of))


def combine(earlier, following):
    return (earlier[0] * following[0], following[0] * earlier[1] + following[1])


def masked_dot(mask_cols, operand, stacked):
    running = mask_cols[:, 0:1] * jnp.dot(operand, stacked[0], preferred_element_type=jnp.float32)
    for modal_index in range(1, M):
        running = running + mask_cols[:, modal_index : modal_index + 1] * jnp.dot(
            operand, stacked[modal_index], preferred_element_type=jnp.float32
        )
    return running


def masked_back(mask_cols, operand, stacked):
    contract = (((1,), (1,)), ((), ()))
    running = mask_cols[:, 0:1] * lax.dot_general(
        operand, stacked[0], contract, preferred_element_type=jnp.float32
    )
    for modal_index in range(1, M):
        running = running + mask_cols[:, modal_index : modal_index + 1] * lax.dot_general(
            operand, stacked[modal_index], contract, preferred_element_type=jnp.float32
        )
    return running


def masked_outer(mask_low, operand, cotangent):
    contract = (((0,), (0,)), ((), ()))
    return jnp.stack(
        [
            lax.dot_general(
                operand * mask_low[:, modal_index : modal_index + 1],
                cotangent,
                contract,
                preferred_element_type=jnp.float32,
            )
            for modal_index in range(M)
        ]
    )


def adam_parts(gradient, moment, square):
    moment_new = BETA_ONE * moment + (1.0 - BETA_ONE) * gradient
    square_new = BETA_TWO * square + (1.0 - BETA_TWO) * gradient * gradient
    adam_ratio = (
        moment_new
        / (1.0 - BETA_ONE**STEP)
        / (jnp.sqrt(square_new / (1.0 - BETA_TWO**STEP)) + ADAM_EPSILON)
    )
    return (moment_new, square_new, adam_ratio)


def generic_local(
    tokens,
    out_grad,
    modality,
    segment,
    w_in,
    w_x,
    w_dt,
    w_out,
    channel,
    norm_gain,
    moment_in,
    moment_x,
    moment_dt,
    moment_out,
    moment_channel,
    moment_gain,
    square_in,
    square_x,
    square_dt,
    square_out,
    square_channel,
    square_gain,
    average_in,
    average_x,
    average_dt,
    average_out,
    average_channel,
    average_gain,
):
    tok_local = tokens.shape[0]
    width_tp = out_grad.shape[1]
    lowered = (
        w_in.astype(jnp.bfloat16),
        w_x.astype(jnp.bfloat16),
        w_dt.astype(jnp.bfloat16),
        w_out.astype(jnp.bfloat16),
    )
    stack_in, stack_x, stack_dt, stack_out = (
        lax.all_gather(lowered[0], "seq", axis=1, tiled=True),
        lax.all_gather(lowered[1], "seq", axis=1, tiled=True),
        lax.all_gather(lowered[2], "seq", axis=1, tiled=True),
        lax.all_gather(lowered[3], "seq", axis=2, tiled=True),
    )
    chan_full, gain_full = (
        lax.all_gather(channel, "seq", axis=1, tiled=True),
        lax.all_gather(norm_gain, "seq", axis=0, tiled=True),
    )
    inner_width = stack_out.shape[1]
    in_flat = stack_in.reshape(M, D, 2 * inner_width)
    seq_index = lax.axis_index("seq")
    tp_index = lax.axis_index("tp")
    start_row = seq_index * tok_local
    seg_local = lax.dynamic_slice(segment, (start_row,), (tok_local,))
    seg_before = lax.dynamic_slice(
        jnp.concatenate([jnp.full((K - 1,), -1, jnp.int32), segment]),
        (start_row,),
        (tok_local + K - 1,),
    )
    seg_after = lax.dynamic_slice(
        jnp.concatenate([segment, jnp.full((K - 1,), -2, jnp.int32)]),
        (start_row,),
        (tok_local + K - 1,),
    )
    mask_cols = (modality[:, None] == jnp.arange(M, dtype=jnp.int32)[None, :]).astype(jnp.float32)
    mask_low = mask_cols.astype(jnp.bfloat16)
    tokens_wide = tokens.astype(jnp.float32)
    inv_root = lax.rsqrt(jnp.mean(tokens_wide * tokens_wide, axis=-1, keepdims=True) + EPSILON)
    scaled = tokens_wide * inv_root
    normed = (scaled * gain_full[None, :]).astype(jnp.bfloat16)
    projected = masked_dot(mask_cols, normed, in_flat)
    inner_act = projected[:, :inner_width].astype(jnp.bfloat16)
    gate_pre = projected[:, inner_width:]
    rim_rows = passed_along(inner_act[tok_local - (K - 1) :], "seq", 1)
    extended = jnp.concatenate([rim_rows, inner_act], axis=0).astype(jnp.float32)
    conv_pre = jnp.broadcast_to(chan_full[K][None, :], (tok_local, inner_width))
    same_docs = []
    for tap_index in range(K):
        same_doc = (seg_before[tap_index : tap_index + tok_local] == seg_local).astype(jnp.float32)[
            :, None
        ]
        same_docs.append(same_doc)
        conv_pre = (
            conv_pre
            + chan_full[tap_index][None, :] * extended[tap_index : tap_index + tok_local] * same_doc
        )
    activated = jax.nn.silu(conv_pre).astype(jnp.bfloat16)
    act_wide = activated.astype(jnp.float32)
    params_x = lax.psum(masked_dot(mask_cols, activated, stack_x), "tp")
    low_rank = params_x[:, :R].astype(jnp.bfloat16)
    input_b = params_x[:, R : R + N]
    output_c = params_x[:, R + N :]
    step_pre = masked_dot(mask_cols, low_rank, stack_dt) + jnp.dot(
        mask_cols, chan_full[K + 2 : K + 2 + M], precision=PRECISE
    )
    step_size = jax.nn.softplus(step_pre)
    decay_base = -jnp.exp(chan_full[K + 2 + M :])
    keep_flag = (seg_before[K - 2 : K - 2 + tok_local] == seg_local).astype(jnp.float32)
    decay_rate = jnp.exp(step_size[:, None, :] * decay_base[None]) * keep_flag[:, None, None]
    drive_term = (step_size * act_wide)[:, None, :] * input_b[:, :, None]
    decay_cum, local_state = lax.associative_scan(combine, (decay_rate, drive_term), axis=0)
    unit_pair = (jnp.ones_like(decay_base), jnp.zeros_like(decay_base))
    carry_in = prefix((decay_cum[-1], local_state[-1]), "seq", combine, unit_pair, False)[1]
    hidden_state = local_state + decay_cum * carry_in[None]
    mixed_out = (
        jnp.einsum("tn,tne->te", output_c, hidden_state, precision=PRECISE)
        + chan_full[K + 1][None, :] * act_wide
    )
    gate_act = jax.nn.silu(gate_pre)
    gated_out = (mixed_out * gate_act).astype(jnp.bfloat16)
    out_share = lax.psum_scatter(
        masked_dot(mask_cols, gated_out, stack_out), "tp", scatter_dimension=1, tiled=True
    )
    layer_out = lax.dynamic_slice_in_dim(tokens_wide, tp_index * width_tp, width_tp, 1) + out_share
    grad_full = lax.all_gather(out_grad, "tp", axis=1, tiled=True)
    d_gated = masked_back(mask_cols, grad_full, stack_out)
    grad_out = masked_outer(mask_low, gated_out, grad_full)
    d_mixed = d_gated * gate_act
    d_gate = d_gated * mixed_out * silu_grad(gate_pre)
    grad_skip = jnp.sum(d_mixed * act_wide, axis=0)
    d_out_c = jnp.einsum("te,tne->tn", d_mixed, hidden_state, precision=PRECISE)
    d_hidden = output_c[:, :, None] * d_mixed[:, None, :]
    decay_next = jnp.concatenate([decay_rate[1:], jnp.ones_like(decay_rate[:1])], axis=0)
    suffix_cum, local_back = lax.associative_scan(
        combine, (decay_next, d_hidden), reverse=True, axis=0
    )
    device_pair = (decay_rate[0] * suffix_cum[0], decay_rate[0] * local_back[0])
    carry_back = prefix(device_pair, "seq", combine, unit_pair, True)[1]
    back_state = local_back + suffix_cum * carry_back[None]
    state_prev = jnp.concatenate([carry_in[None], hidden_state[:-1]], axis=0)
    d_log = back_state * state_prev * decay_rate
    d_drive_sum = jnp.einsum("tne,tn->te", back_state, input_b, precision=PRECISE)
    d_step_size = jnp.sum(d_log * decay_base[None], axis=1) + act_wide * d_drive_sum
    grad_decay = decay_base * jnp.einsum("tne,te->ne", d_log, step_size, precision=PRECISE)
    d_in_b = jnp.einsum("tne,te->tn", back_state, step_size * act_wide, precision=PRECISE)
    d_step = (d_step_size * jax.nn.sigmoid(step_pre)).astype(jnp.bfloat16)
    d_step_wide = d_step.astype(jnp.float32)
    grad_bias = jnp.dot(mask_cols.T, d_step_wide, precision=PRECISE)
    grad_dt = masked_outer(mask_low, low_rank, d_step)
    d_low = masked_back(mask_cols, d_step, stack_dt)
    d_params = lax.psum(jnp.concatenate([d_low, d_in_b, d_out_c], axis=1), "tp").astype(
        jnp.bfloat16
    )
    grad_x = masked_outer(mask_low, activated, d_params)
    d_activ = (
        d_mixed * chan_full[K + 1][None, :]
        + step_size * d_drive_sum
        + masked_back(mask_cols, d_params, stack_x)
    )
    d_conv = (d_activ * silu_grad(conv_pre)).astype(jnp.bfloat16)
    rim_back = passed_along(d_conv[: K - 1], "seq", -1)
    d_conv_wide = d_conv.astype(jnp.float32)
    conv_after = jnp.concatenate([d_conv, rim_back], axis=0).astype(jnp.float32)
    d_inner = jnp.zeros((tok_local, inner_width), jnp.float32)
    grad_taps = []
    for tap_index in range(K):
        grad_taps.append(
            jnp.sum(
                d_conv_wide * extended[tap_index : tap_index + tok_local] * same_docs[tap_index],
                axis=0,
            )
        )
        offset = K - 1 - tap_index
        same_after = (seg_after[offset : offset + tok_local] == seg_local).astype(jnp.float32)[
            :, None
        ]
        d_inner = (
            d_inner
            + chan_full[tap_index][None, :] * conv_after[offset : offset + tok_local] * same_after
        )
    grad_conv_b = jnp.sum(d_conv_wide, axis=0)
    d_proj = jnp.concatenate([d_inner, d_gate], axis=1).astype(jnp.bfloat16)
    grad_in = masked_outer(mask_low, normed, d_proj).reshape(M, D, 2, inner_width)
    d_normed = lax.psum(masked_back(mask_cols, d_proj, in_flat), "tp")
    grad_gain = jnp.sum(d_normed * scaled, axis=0)
    d_scaled = d_normed * gain_full[None, :]
    d_tokens = inv_root * (d_scaled - scaled * jnp.mean(d_scaled * scaled, axis=-1, keepdims=True))
    tokens_grad = out_grad.astype(jnp.float32) + lax.dynamic_slice_in_dim(
        d_tokens, tp_index * width_tp, width_tp, 1
    )
    grad_channel = jnp.concatenate(
        [jnp.stack(grad_taps), grad_conv_b[None], grad_skip[None], grad_bias, grad_decay], axis=0
    )
    reduced = (
        lax.psum_scatter(grad_in, "seq", scatter_dimension=1, tiled=True),
        lax.psum_scatter(grad_x, "seq", scatter_dimension=1, tiled=True),
        lax.psum_scatter(grad_dt, "seq", scatter_dimension=1, tiled=True),
        lax.psum_scatter(grad_out, "seq", scatter_dimension=2, tiled=True),
        lax.psum_scatter(grad_channel, "seq", scatter_dimension=1, tiled=True),
        lax.psum_scatter(grad_gain, "seq", scatter_dimension=0, tiled=True),
    )
    weights = (w_in, w_x, w_dt, w_out, channel, norm_gain)
    moments = (moment_in, moment_x, moment_dt, moment_out, moment_channel, moment_gain)
    squares = (square_in, square_x, square_dt, square_out, square_channel, square_gain)
    averages = (average_in, average_x, average_dt, average_out, average_channel, average_gain)
    adam_all = [
        adam_parts(reduced[position], moments[position], squares[position]) for position in range(6)
    ]
    directions = [adam_all[position][2] + WEIGHT_DECAY * weights[position] for position in range(4)]
    weight_sums = jnp.stack(
        [
            jnp.sum(
                weights[position] * weights[position], axis=tuple(range(1, weights[position].ndim))
            )
            for position in range(4)
        ]
    )
    direction_sums = jnp.stack(
        [
            jnp.sum(
                directions[position] * directions[position],
                axis=tuple(range(1, directions[position].ndim)),
            )
            for position in range(4)
        ]
    )
    totals = lax.psum(jnp.stack([weight_sums, direction_sums]), ("seq", "tp"))
    trust_ratio = jnp.sqrt(totals[0]) / jnp.sqrt(totals[1])
    new_weights = []
    new_averages = []
    for position in range(6):
        weight = weights[position]
        if position < 4:
            updated = (
                weight
                - MATRIX_RATE
                * trust_ratio[position].reshape((M,) + (1,) * (weight.ndim - 1))
                * directions[position]
            )
        elif position == 4:
            updated = weight - CHANNEL_RATE * adam_all[position][2]
        else:
            updated = weight - GAIN_RATE * adam_all[position][2]
        new_weights.append(updated)
        new_averages.append(AVERAGE_KEEP * averages[position] + (1.0 - AVERAGE_KEEP) * updated)
    return (
        layer_out,
        tokens_grad,
        new_weights[0],
        new_weights[1],
        new_weights[2],
        new_weights[3],
        new_weights[4],
        new_weights[5],
        adam_all[0][0],
        adam_all[1][0],
        adam_all[2][0],
        adam_all[3][0],
        adam_all[4][0],
        adam_all[5][0],
        adam_all[0][1],
        adam_all[1][1],
        adam_all[2][1],
        adam_all[3][1],
        adam_all[4][1],
        adam_all[5][1],
        new_averages[0],
        new_averages[1],
        new_averages[2],
        new_averages[3],
        new_averages[4],
        new_averages[5],
    )


MESH = pl.DeviceIdType.MESH
VMEM_LIMIT = 60 * 1024 * 1024
LANES = 128
F32 = jnp.float32
BF16 = jnp.bfloat16
NT = (((1,), (1,)), ((), ()))
TN = (((0,), (0,)), ((), ()))


def dot(a, b, dims=(((1,), (0,)), ((), ()))):
    return lax.dot_general(a, b, dims, preferred_element_type=F32)


def local_call(kernel, out_shape, n_in, scratch=(), cost=None):
    return pl.pallas_call(
        kernel,
        out_shape=out_shape,
        in_specs=[pl.BlockSpec(memory_space=pltpu.VMEM)] * n_in,
        out_specs=jax.tree.map(lambda _: pl.BlockSpec(memory_space=pltpu.VMEM), out_shape),
        scratch_shapes=list(scratch),
        compiler_params=pltpu.CompilerParams(vmem_limit_bytes=VMEM_LIMIT),
        cost_estimate=cost,
    )


def remote_call(kernel, out_shape, n_in, scratch, ident):
    return pl.pallas_call(
        kernel,
        out_shape=out_shape,
        in_specs=[pl.BlockSpec(memory_space=pltpu.VMEM)] * n_in,
        out_specs=jax.tree.map(lambda _: pl.BlockSpec(memory_space=pltpu.VMEM), out_shape),
        scratch_shapes=list(scratch),
        compiler_params=pltpu.CompilerParams(
            collective_id=ident, has_side_effects=True, vmem_limit_bytes=VMEM_LIMIT
        ),
    )


def sds(shape, dtype=F32):
    return jax.ShapeDtypeStruct(shape, dtype)


def seq_copy(src, dst, send, recv, device):
    return pltpu.make_async_remote_copy(
        src_ref=src,
        dst_ref=dst,
        send_sem=send,
        recv_sem=recv,
        device_id=device,
        device_id_type=MESH,
    )


def place(S, PN):
    s, p = lax.axis_index("seq"), lax.axis_index("tp")
    return s, p, lax.div(s, 2), lax.rem(s, 2)


def greet_all(S, PN):
    s, p = lax.axis_index("seq"), lax.axis_index("tp")
    n = S * PN
    me = s * PN + p
    bar = pltpu.get_barrier_semaphore()

    def greet(k, _):
        j = lax.rem(me + k, n)
        pl.semaphore_signal(
            bar,
            inc=1,
            device_id={"seq": lax.div(j, PN), "tp": lax.rem(j, PN)},
            device_id_type=MESH,
        )
        return 0

    lax.fori_loop(1, n, greet, 0)
    pl.semaphore_wait(bar, n - 1)


class Spread:
    def __init__(self, S, PN, own, buf, zs, zr, xs, xr, ys, yr, cs, cr, ls):
        s, p, z, x = place(S, PN)
        self.zn = S // 2
        zn = self.zn
        other_x = {"seq": 2 * z + 1 - x}
        other_y = {"tp": lax.rem(p + 2, PN)}
        other_c = {"tp": p + 1 - 2 * lax.rem(p, 2)}

        def at(k, j):
            return 2 * lax.rem(z - k + zn, zn) + (x if j == 0 else 1 - x)

        self.local = pltpu.make_async_copy(own, buf.at[p, s], ls)
        self.z = [
            seq_copy(own, buf.at[p, s], zs.at[k], zr.at[k], {"seq": 2 * lax.rem(z + k, zn) + x})
            for k in range(1, zn)
        ]
        self.x = []
        self.y = {}
        for k in range(zn):
            src = own if k == 0 else buf.at[p, at(k, 0)]
            self.x.append(seq_copy(src, buf.at[p, at(k, 0)], xs.at[k], xr.at[k], other_x))
            for j in range(2):
                src = own if (k == 0 and j == 0) else buf.at[p, at(k, j)]
                self.y[k, j] = seq_copy(
                    src, buf.at[p, at(k, j)], ys.at[2 * k + j], yr.at[2 * k + j], other_y
                )
        q = lax.rem(p + 2, PN)
        self.c = [
            seq_copy(buf.at[p], buf.at[p], cs.at[0], cr.at[0], other_c),
            seq_copy(buf.at[q], buf.at[q], cs.at[1], cr.at[1], other_c),
        ]

    def start(self):
        self.local.start()
        for cp in self.z:
            cp.start()
        self.x[0].start()
        self.y[0, 0].start()

    def forward(self):
        for k in range(1, self.zn):
            self.z[k - 1].wait_recv()
            self.x[k].start()
            self.y[k, 0].start()
        for k in range(self.zn):
            self.x[k].wait_recv()
            self.y[k, 1].start()
        self.local.wait()
        self.c[0].start()

    def finish(self):
        for cp in self.y.values():
            cp.wait_recv()
        self.c[1].start()
        for cp in self.z + self.x + list(self.y.values()):
            cp.wait_send()
        for cp in self.c:
            cp.wait()

    @staticmethod
    def semaphores(S):
        dma = pltpu.SemaphoreType.DMA
        return [dma((S // 2,))] * 4 + [dma((S,))] * 2 + [dma((2,))] * 2 + [dma]


def row_copies(S, src, dst, send, recv):
    s = lax.axis_index("seq")
    out = []
    for k in range(1, S):
        d = lax.rem(s + k, S)
        out.append(seq_copy(src(d), dst(s), send.at[k], recv.at[k], {"seq": d}))
    return out


def sum_over_all(S, PN, lr, bct, LR, BCT, got_l, got_b, ssl, rsl, ssb, rsb, sgl, rgl, sgb, rgb):
    n = S * PN
    s, p = lax.axis_index("seq"), lax.axis_index("tp")
    me = s * PN + p
    rows = lr.shape[0] // n
    per = n // bct.shape[0]
    high = bct.shape[1] // per

    def device(j):
        return {"seq": lax.div(j, PN), "tp": lax.rem(j, PN)}

    def rows_of(j):
        return pl.ds(pl.multiple_of(j * rows, 16), rows)

    def slab(ref, j):
        return ref.at[lax.div(j, per), pl.ds(pl.multiple_of(lax.rem(j, per) * high, 8), high)]

    def first(k):
        j = lax.rem(me + k, n)
        return (
            seq_copy(lr.at[rows_of(j)], got_l.at[k], ssl.at[k], rsl.at[k], device(j)),
            seq_copy(slab(bct, j), got_b.at[k], ssb.at[k], rsb.at[k], device(j)),
        )

    def second(k):
        j = lax.rem(me + k, n)
        mine_l, mine_b = LR.at[rows_of(me)], slab(BCT, me)
        return (
            seq_copy(mine_l, mine_l, sgl.at[k], rgl.at[k], device(j)),
            seq_copy(mine_b, mine_b, sgb.at[k], rgb.at[k], device(j)),
        )

    def start(copies, k):
        for cp in copies(k):
            cp.start()
        return 0

    def wait(copies, k):
        for cp in copies(k):
            cp.wait()
        return 0

    lax.fori_loop(1, n, lambda k, _: start(first, k), 0)
    got_l[0] = lr[rows_of(me), :]
    got_b[0] = slab(bct, me)[...]
    lax.fori_loop(1, n, lambda k, _: wait(first, k), 0)
    LR[rows_of(me), :] = jnp.sum(got_l[...], axis=0).astype(LR.dtype)
    slab(BCT, me)[...] = jnp.sum(got_b[...], axis=0)
    lax.fori_loop(1, n, lambda k, _: start(second, k), 0)
    lax.fori_loop(1, n, lambda k, _: wait(second, k), 0)


def sum_scratch(S, PN, T):
    n = S * PN
    dma = pltpu.SemaphoreType.DMA
    slabs = (T // LANES) * 2 * N // n
    return [pltpu.VMEM((n, T // n, R), F32), pltpu.VMEM((n, slabs, LANES), F32)] + [dma((n,))] * 8


class RowGather:
    def __init__(self, S, own, place_of, zs, zr, xs, xr, ls):
        s, p, z, x = place(S, 1)
        self.zn = zn = S // 2
        other = {"seq": 2 * z + 1 - x}
        at = lambda k: 2 * lax.rem(z - k + zn, zn) + x
        self.local = pltpu.make_async_copy(own, place_of(s), ls)
        self.z = [
            seq_copy(own, place_of(s), zs.at[k], zr.at[k], {"seq": 2 * lax.rem(z + k, zn) + x})
            for k in range(1, zn)
        ]
        self.x = [
            seq_copy(
                own if k == 0 else place_of(at(k)), place_of(at(k)), xs.at[k], xr.at[k], other
            )
            for k in range(zn)
        ]

    def start(self):
        self.local.start()
        for cp in self.z:
            cp.start()
        self.x[0].start()

    def forward(self):
        for k in range(1, self.zn):
            self.z[k - 1].wait_recv()
            self.x[k].start()

    def finish(self):
        self.local.wait()
        for cp in self.z:
            cp.wait_send()
        for cp in self.x:
            cp.wait()

    @staticmethod
    def semaphores(S):
        dma = pltpu.SemaphoreType.DMA
        return [dma((S // 2,))] * 4 + [dma]


def softplus(v):
    u = jnp.exp(-jnp.abs(v))
    w = 1.0 + u
    small = jnp.where(w == 1.0, u, jnp.log(w) * (u / jnp.where(w == 1.0, 1.0, w - 1.0)))
    return jnp.maximum(v, 0.0) + small


def masked_sum(acc, aux, r, C):
    total = acc[:, 0:C] * aux[r, 0:1]
    for m in range(1, M):
        total = total + acc[:, m * C : (m + 1) * C] * aux[r, m : m + 1]
    return total


def block_kernel(S, PN, *refs):
    rest = list(refs)
    take = lambda k: [rest.pop(0) for _ in range(k)]
    tok, og, modrow, wdt_mine, gain_mine, wi, wg, wo, segs, ch, wlr, wbc, wxT = take(13)
    LO, DN, GG, ROW, MORE, gx, gtap, gch, NR, G, AUXC, dall_out, gall_out, INV = take(14)
    tile, toks, ogs, nrm, Wi, Wg, Wo, AUX, GAIN, WD = take(10)
    step, drive, keep, Y, pad, act3, lr, bcp = take(8)
    act, conv, inner, low, bct, pre, H, gated, dgate, dmix, aux, X = take(12)
    gall, dall, DS, DB, dst3, low3, dst, dlow, dbct, dact, gdt = take(11)
    LR2, BCT2, tail, dpar, dinner, part, rowdot, ggs = take(8)
    ag1, ag2 = take(9), take(9)
    ws = take(12)
    ls = take(1)[0]
    sums = take(10)
    rows_g, rows_d, rows_i = take(5), take(5), take(5)
    mx, mr, ml = take(3)
    last = take(8)
    s, p, z, x = place(S, PN)
    TL, DD = tok.shape
    T = S * TL
    width = DD // S
    quarter = DD // PN
    C = act.shape[1]
    rows = 128

    wide = tok[...].astype(F32)
    inv = lax.rsqrt(jnp.mean(wide * wide, axis=1, keepdims=True) + EPSILON)
    row = jnp.transpose(jnp.broadcast_to(inv, (TL, LANES)))[0:8]
    tile[...] = jnp.where(
        lax.broadcasted_iota(jnp.int32, row.shape, 0) == 0, modrow[...], row
    )
    greet_all(S, PN)
    chans = lambda d: pl.ds(pl.multiple_of(d * C, LANES), C)
    block = lambda d: pl.ds(pl.multiple_of(d * width, width), width)
    tokens = Spread(
        S, PN, tok.at[:, pl.ds(pl.multiple_of(p * quarter, LANES), quarter)], toks, *ag1
    )
    small = (
        row_copies(S, lambda d: tile, lambda t: AUX.at[t], ws[0], ws[1])
        + row_copies(S, lambda d: gain_mine, lambda t: GAIN.at[t], ws[2], ws[3])
    )
    dts = row_copies(S, lambda d: wdt_mine.at[:, :, chans(d)], lambda t: WD.at[t], ws[4], ws[5])
    inners = row_copies(S, lambda d: wi.at[d], lambda t: Wi.at[block(t)], ws[6], ws[7])
    gates = row_copies(S, lambda d: wg.at[d], lambda t: Wg.at[block(t)], ws[8], ws[9])
    outs = row_copies(S, lambda d: wo.at[d], lambda t: Wo.at[t], ws[10], ws[11])
    cotangent = Spread(S, PN, og, ogs, *ag2)
    for cp in small:
        cp.start()
    tokens.start()
    for cp in inners:
        cp.start()
    own = [
        pltpu.make_async_copy(tile, AUX.at[s], ls.at[0]),
        pltpu.make_async_copy(gain_mine, GAIN.at[s], ls.at[1]),
        pltpu.make_async_copy(wdt_mine.at[:, :, chans(s)], WD.at[s], ls.at[2]),
        pltpu.make_async_copy(wi.at[s], Wi.at[block(s)], ls.at[3]),
        pltpu.make_async_copy(wg.at[s], Wg.at[block(s)], ls.at[4]),
        pltpu.make_async_copy(wo.at[s], Wo.at[s], ls.at[5]),
    ]
    for cp in own:
        cp.start()
    for cp in own:
        cp.wait()
    tokens.forward()
    for cp in small:
        cp.wait()
    lane = lax.broadcasted_iota(jnp.int32, (TL, 8), 1)

    def columns(t, _):
        r = pl.ds(pl.multiple_of(t * TL, TL), TL)
        turned = jnp.transpose(jnp.concatenate([AUX[t]] * (LANES // 8), axis=0))
        mask = (turned[:, 0:1] == lane.astype(F32)).astype(F32)
        aux[r, :] = jnp.where(
            lane < M, mask, jnp.where(lane == 7, turned[:, 1:2], segs[r, :])
        )
        return 0

    lax.fori_loop(0, S, columns, 0)
    aux[T : T + 8, :] = jnp.zeros((8, 8), F32)
    tokens.finish()
    per = quarter // width

    def norm(t, _):
        r = pl.ds(pl.multiple_of(t * TL, TL), TL)
        scale = aux[r, 7:8]
        for q in range(PN):
            scaled = toks[q, t].astype(F32) * scale
            for j in range(per):
                part = scaled[:, j * width : (j + 1) * width] * GAIN[q * per + j, 0:1, :]
                nrm[r, q * quarter + j * width : q * quarter + (j + 1) * width] = part.astype(BF16)
        return 0

    lax.fori_loop(0, S, norm, 0)
    for cp in inners:
        cp.wait()
    for cp in gates + dts:
        cp.start()

    big = 256
    pad[0:8, :] = jnp.zeros((8, C), F32)

    def first(i, _):
        r = pl.ds(pl.multiple_of(i * big, big), big)
        value = masked_sum(dot(nrm[r, :], Wi[...]), aux, r, C).astype(BF16)
        inner[r, :] = value
        pad[pl.ds(pl.multiple_of(i * big + 8, 8), big), :] = value.astype(F32)
        return 0

    lax.fori_loop(0, T // big, first, 0)

    def convolve(i, _):
        r = pl.ds(pl.multiple_of(i * rows, rows), rows)
        window = pad[pl.ds(pl.multiple_of(i * rows, rows), rows + 8), :]
        v = jnp.broadcast_to(ch[K : K + 1, :], (rows, C))
        for k in range(K):
            term = ch[k : k + 1, :] * window[8 - (K - 1) + k : 8 - (K - 1) + k + rows]
            v = v + (term * aux[r, M + k : M + k + 1] if k < K - 1 else term)
        conv[r, :] = v
        a = (v / (1.0 + jnp.exp(-v))).astype(BF16)
        act[r, :] = a
        a_wide = a.astype(F32)
        for m in range(M):
            act3[r, m * C : (m + 1) * C] = (a_wide * aux[r, m : m + 1]).astype(BF16)
        lr[r, :] = dot(act3[r, :], wlr[...])
        bcp[i] = dot(wbc[...], act3[r, :], NT)
        return 0

    lax.fori_loop(0, T // rows, convolve, 0)
    sum_over_all(S, PN, lr, bcp, low, bct, *sums)
    for cp in dts:
        cp.wait()
    cotangent.start()
    for cp in outs:
        cp.start()

    def prepare(i, _):
        r = pl.ds(pl.multiple_of(i * rows, rows), rows)
        low_wide = low[r, :].astype(F32)
        bias = jnp.zeros((rows, C), F32)
        for m in range(M):
            mask = aux[r, m : m + 1]
            masked = (low_wide * mask).astype(BF16)
            bias = bias + mask * ch[K + 2 + m : K + 3 + m, :]
            for t in range(S):
                h = R // S
                bias = bias + dot(masked[:, t * h : (t + 1) * h], WD[t, m])
        pre[r, :] = bias
        st = softplus(bias)
        step[r, :] = st
        drive[r, :] = st * act[r, :].astype(F32)
        keep[r, :] = jnp.broadcast_to(aux[r, 6:7], (rows, C))
        return 0

    lax.fori_loop(0, T // rows, prepare, 0)
    scan_forward(T, C, bct, ch, step, drive, keep, H, Y)
    cotangent.forward()
    for cp in gates:
        cp.wait()

    def gate(i, _):
        r = pl.ds(pl.multiple_of(i * big, big), big)
        drive[r, :] = masked_sum(dot(nrm[r, :], Wg[...]), aux, r, C)
        return 0

    lax.fori_loop(0, T // big, gate, 0)
    cotangent.finish()
    for cp in outs:
        cp.wait()

    def back(i, _):
        r = pl.ds(pl.multiple_of(i * big, big), big)
        acc = jnp.zeros((big, M * C), F32)
        for q in range(PN):
            g = ogs[q, pl.ds(i * (big // TL), big // TL)].reshape(big, quarter)
            for j in range(per):
                acc = acc + dot(g[:, j * width : (j + 1) * width], Wo[q * per + j], NT)
        keep[r, :] = masked_sum(acc, aux, r, C)
        return 0

    lax.fori_loop(0, T // big, back, 0)

    def finish(i, _):
        r = pl.ds(pl.multiple_of(i * rows, rows), rows)
        mixed = Y[r, :] + ch[K + 1 : K + 2, :] * act[r, :].astype(F32)
        g, d = drive[r, :], keep[r, :]
        sig = 1.0 / (1.0 + jnp.exp(-g))
        gated[r, :] = (mixed * (g * sig)).astype(BF16)
        dmix[r, :] = d * (g * sig)
        dgate[r, :] = (d * mixed * (sig * (1.0 + g * (1.0 - sig)))).astype(BF16)
        return 0

    lax.fori_loop(0, T // rows, finish, 0)
    gathers = [
        RowGather(S, gated, lambda t: gall.at[t], *rows_g),
        RowGather(S, dgate, lambda t: dall.at[t, :, C : 2 * C], *rows_d),
        RowGather(S, dinner, lambda t: dall.at[t, :, 0:C], *rows_i),
    ]
    gathers[0].start()
    gathers[1].start()
    mine = pl.ds(pl.multiple_of(lax.rem(s, per) * width, width), width)
    NR[...] = nrm[:, pl.ds(pl.multiple_of(s * width, width), width)]

    def own_features(t, _):
        r = pl.ds(pl.multiple_of(t * TL, TL), TL)
        X[r, :] = toks[lax.div(s, per), t, :, mine]
        G[r, :] = ogs[lax.div(s, per), t, :, mine]
        drive[r, :] = step[r, :] * act[r, :].astype(F32)
        keep[r, :] = jnp.broadcast_to(aux[r, 6:7], (TL, C))
        return 0

    lax.fori_loop(0, S, own_features, 0)
    INV[...] = jnp.broadcast_to(inv, INV.shape)
    scan_backward(
        pre, H, dmix, act, bct, aux, ch, WD, low,
        dlow, dbct, gdt, gch, dact, step, drive, keep, DS, DB, dst3, low3, dst,
        [(T // LANES // 2, gathers[0].forward)],
    )
    gathers[1].forward()
    h = R // S
    part_dt = lambda d: gdt.at[:, pl.ds(pl.multiple_of(d * h, 8), h), :]
    more = row_copies(S, part_dt, lambda t: MORE.at[t], mx, mr)
    more_own = pltpu.make_async_copy(part_dt(s), MORE.at[s], ml)
    for cp in more + [more_own]:
        cp.start()
    sum_over_all(S, PN, dlow, dbct, LR2, BCT2, *sums)
    convolve_backward(
        LR2, BCT2, act, conv, aux, ch, wxT, dact, dinner, gx, gtap, pad, tail, act3, dpar
    )
    gathers[2].start()
    for cp in more + [more_own]:
        cp.wait()
    gathers[0].finish()
    out_gall = pltpu.make_async_copy(gall, gall_out, ls.at[0])
    out_gall.start()

    def layer(i, _):
        r = pl.ds(pl.multiple_of(i * big, big), big)

        def add(b, total):
            wide = gall[b, r, :].astype(F32)
            for m in range(M):
                total = total + dot(
                    (wide * aux[r, m : m + 1]).astype(BF16), wo[b, m * C : (m + 1) * C, :]
                )
            return total

        total = lax.fori_loop(0, S, add, jnp.zeros((big, width), F32))
        part[0, r, :] = total.astype(BF16)
        return 0

    lax.fori_loop(0, T // big, layer, 0)
    to_out = LastBlocks(S, PN, part.at[0], LO, last[0], last[1], ls.at[1])
    to_out.start()
    gathers[2].forward()
    gathers[1].finish()
    gathers[2].finish()
    out_dall = pltpu.make_async_copy(dall, dall_out, ls.at[2])
    out_dall.start()

    def normed_back(i, total):
        r = pl.ds(pl.multiple_of(i * big, big), big)

        def add(b, accs):
            d0, d1 = dall[b, r, 0:C], dall[b, r, C : 2 * C]
            return tuple(
                accs[m]
                + dot(d0, wi[b, :, m * C : (m + 1) * C], NT)
                + dot(d1, wg[b, :, m * C : (m + 1) * C], NT)
                for m in range(M)
            )

        accs = lax.fori_loop(0, S, add, (jnp.zeros((big, width), F32),) * M)
        d = accs[0] * aux[r, 0:1]
        for m in range(1, M):
            d = d + accs[m] * aux[r, m : m + 1]
        scaled = X[r, :].astype(F32) * aux[r, 7:8]
        gained = d * gain_mine[0:1, :]
        part[1, r, :] = gained.astype(BF16)
        along = jnp.sum(gained * scaled, axis=1, keepdims=True)
        for j in range(big // TL):
            turned = jnp.transpose(jnp.broadcast_to(along[j * TL : (j + 1) * TL], (TL, LANES)))
            rowdot[i * (big // TL) + j] = turned[0:8]
        return total + jnp.sum(d * scaled, axis=0, keepdims=True)

    total = lax.fori_loop(0, T // big, normed_back, jnp.zeros((1, width), F32))
    ggs[...] = jnp.broadcast_to(total, ggs.shape)
    to_in = LastBlocks(S, PN, part.at[1], DN, last[2], last[3], ls.at[3])
    to_in.start()
    gains = [
        seq_copy(ggs, GG.at[k], last[4].at[k], last[5].at[k], {"tp": lax.rem(p + k, PN)})
        for k in range(1, PN)
    ]
    for cp in gains:
        cp.start()
    n = S * PN
    me = s * PN + p

    def tile_copy(k):
        j = lax.rem(me + k, n)
        device = {"seq": lax.div(j, PN), "tp": lax.rem(j, PN)}
        return seq_copy(
            rowdot.at[lax.div(j, PN)], ROW.at[k], last[6].at[k], last[7].at[k], device
        )

    def send_tile(k, _):
        tile_copy(k).start()
        return 0

    def wait_tile(k, _):
        tile_copy(k).wait()
        return 0

    lax.fori_loop(1, n, send_tile, 0)
    GG[0] = ggs[...]
    ROW[0] = rowdot[s]
    AUXC[...] = aux[0:T, :]
    for cp in gains:
        cp.wait()
    lax.fori_loop(1, n, wait_tile, 0)
    to_out.finish()
    to_in.finish()
    out_gall.wait()
    out_dall.wait()


class LastBlocks:
    def __init__(self, S, PN, part, out, send, recv, ls):
        s, p = lax.axis_index("seq"), lax.axis_index("tp")
        ratio = S // PN
        self.S, self.PN, self.ratio = S, PN, ratio
        self.s, self.p, self.home = s, p, lax.div(s, ratio)
        self.slot = lax.rem(s, ratio) * PN + p
        self.part, self.out, self.send, self.recv, self.ls = part, out, send, recv, ls
        self.TL = part.shape[0] // S

    def away(self, k):
        return jnp.logical_or(self.s != k, self.home != self.p)

    def copy(self, k):
        return seq_copy(
            self.part.at[pl.ds(k * self.TL, self.TL)],
            self.out.at[self.slot],
            self.send.at[k],
            self.recv.at[self.slot],
            {"seq": k, "tp": self.home},
        )

    def own(self, k):
        return pltpu.make_async_copy(
            self.part.at[pl.ds(k * self.TL, self.TL)], self.out.at[self.slot], self.ls
        )

    def start(self):
        for k in range(self.S):

            @pl.when(self.away(k))
            def _():
                self.copy(k).start()

            @pl.when(jnp.logical_not(self.away(k)))
            def _():
                self.own(k).start()

    def finish(self):
        for k in range(self.S):

            @pl.when(self.away(k))
            def _():
                self.copy(k).wait_send()

            @pl.when(jnp.logical_not(self.away(k)))
            def _():
                self.own(k).wait()

        for h in range(self.ratio):
            for q in range(self.PN):
                t = self.ratio * self.p + h
                i = h * self.PN + q

                @pl.when(jnp.logical_or(t != self.s, self.p != q))
                def _():
                    seq_copy(
                        self.part.at[0 : self.TL],
                        self.out.at[i],
                        self.send.at[0],
                        self.recv.at[i],
                        {"seq": t, "tp": q},
                    ).wait_recv()


def scan_forward(T, C, bct, ch, step, drive, keep, H, Y):
    base = -jnp.exp(ch[K + 2 + M : K + 2 + M + N, :])
    H[0] = jnp.zeros((N, C), F32)

    def chunk(c, h):
        bc = bct[c]

        def eight(i, h):
            cols = pltpu.roll(bc, lax.rem(LANES - 8 * i, LANES), 1)
            t0 = pl.multiple_of(c * LANES + i * 8, 8)
            r = pl.ds(t0, 8)
            st, dr, kp = step[r, :], drive[r, :], keep[r, :]
            ys = []
            for j in range(8):
                rate = jnp.exp(st[j : j + 1] * base) * kp[j : j + 1]
                h = rate * h + dr[j : j + 1] * cols[0:N, j : j + 1]
                H[t0 + j + 1] = h
                ys.append(jnp.sum(cols[N : 2 * N, j : j + 1] * h, axis=0, keepdims=True))
            Y[r, :] = jnp.concatenate(ys, axis=0)
            return h

        return lax.fori_loop(0, LANES // 8, eight, h)

    lax.fori_loop(0, T // LANES, chunk, jnp.zeros((N, C), F32))


def scan_backward(
    pre, H, dmix, act, bct, aux, ch, WD, low,
    dlow, dbct, gdt, gch, dact, step, drive, keep, DS, DB, dst3, low3, dst, hooks,
):
    T, C = act.shape
    rows = 128

    base = -jnp.exp(ch[K + 2 + M : K + 2 + M + N, :])
    lane = lax.broadcasted_iota(jnp.int32, (N, LANES), 1)
    nothing = jnp.zeros((N, C), F32)
    chunks = T // LANES

    def chunk(cc, carry):
        c = chunks - 1 - cc
        bc = bct[c]

        def eight(ii, carry):
            flow, hcur, gacc, accb, accc = carry
            i = LANES // 8 - 1 - ii
            cols = pltpu.roll(bc, lax.rem(LANES - 8 * i, LANES), 1)
            t0 = pl.multiple_of(c * LANES + i * 8, 8)
            r = pl.ds(t0, 8)
            st, dr, kp, dm = step[r, :], drive[r, :], keep[r, :], dmix[r, :]
            ds, db = [None] * 8, [None] * 8
            for j in reversed(range(8)):
                bcol, ccol = cols[0:N, j : j + 1], cols[N : 2 * N, j : j + 1]
                back = ccol * dm[j : j + 1] + flow
                rate = jnp.exp(st[j : j + 1] * base) * kp[j : j + 1]
                hprev = H[t0 + j]
                here = lane == 8 * i + j
                accc = jnp.where(
                    here, jnp.sum(dm[j : j + 1] * hcur, axis=1, keepdims=True), accc
                )
                accb = jnp.where(
                    here, jnp.sum(back * dr[j : j + 1], axis=1, keepdims=True), accb
                )
                flow = rate * back
                dlog = flow * hprev
                gacc = gacc + dlog * st[j : j + 1]
                ds[j] = jnp.sum(dlog * base, axis=0, keepdims=True)
                db[j] = jnp.sum(back * bcol, axis=0, keepdims=True)
                hcur = hprev
            DS[r, :] = jnp.concatenate(ds, axis=0)
            DB[r, :] = jnp.concatenate(db, axis=0)
            return flow, hcur, gacc, accb, accc

        blank = jnp.zeros((N, LANES), F32)
        flow, hcur, gacc, accb, accc = lax.fori_loop(
            0, LANES // 8, eight, carry + (blank, blank)
        )
        dbct[c, 0:N, :] = accb
        dbct[c, N : 2 * N, :] = accc
        return flow, hcur, gacc

    carry, done = (nothing, H[T], nothing), 0
    for upto, call in hooks + [(chunks, None)]:
        carry = lax.fori_loop(done, upto, chunk, carry)
        done = upto
        if call is not None:
            call()
    gacc = carry[2]

    def finish(i, carry):
        skip, bias = carry
        r = pl.ds(pl.multiple_of(i * rows, rows), rows)
        a = act[r, :].astype(F32)
        back_b = DB[r, :]
        grad = DS[r, :] + a * back_b
        d = (grad / (1.0 + jnp.exp(-pre[r, :]))).astype(BF16)
        dst[r, :] = d
        wide = d.astype(F32)
        low_wide = low[r, :].astype(F32)
        sums = []
        for m in range(M):
            mask = aux[r, m : m + 1]
            masked = wide * mask
            sums.append(jnp.sum(masked, axis=0, keepdims=True))
            dst3[r, m * C : (m + 1) * C] = masked.astype(BF16)
            low3[r, m * R : (m + 1) * R] = (low_wide * mask).astype(BF16)
        h = R // WD.shape[0]
        for t in range(WD.shape[0]):
            total = dot(dst3[r, 0:C], WD[t, 0], NT)
            for m in range(1, M):
                total = total + dot(dst3[r, m * C : (m + 1) * C], WD[t, m], NT)
            dlow[r, t * h : (t + 1) * h] = total
        dact[r, :] = dmix[r, :] * ch[K + 1 : K + 2, :] + step[r, :] * back_b
        skip = skip + jnp.sum(dmix[r, :] * a, axis=0, keepdims=True)
        return skip, bias + jnp.concatenate(sums, axis=0)

    skip, bias = lax.fori_loop(
        0, T // rows, finish, (jnp.zeros((1, C), F32), jnp.zeros((M, C), F32))
    )
    gch[0:1, :] = skip
    gch[1 : 1 + M, :] = bias
    gch[1 + M : 1 + M + N, :] = base * gacc
    for m in range(M):
        gdt[m] = dot(low3[:, m * R : (m + 1) * R], dst[...], TN)


def convolve_backward(
    dlow, dbct, act, conv, aux, ch, wxT, dact, dinner, gx, gtap, pad, tail, act3, dpar,
):
    T, C = act.shape
    rows = 128
    tail[T : T + 8, :] = jnp.zeros((8, C), F32)
    blank = jnp.zeros((LANES - 2 * N, LANES), F32)

    def fill(i, _):
        r = pl.ds(pl.multiple_of(i * rows, rows), rows)
        turned = jnp.transpose(jnp.concatenate([dbct[i], blank], axis=0))
        dpar[r, 0:R] = dlow[r, :]
        dpar[r, R : R + 2 * N] = turned[:, 0 : 2 * N].astype(BF16)
        wide = dpar[r, :].astype(F32)
        total = dact[r, :]
        for m in range(M):
            mask = aux[r, m : m + 1]
            total = total + dot((wide * mask).astype(BF16), wxT[m])
        v = conv[r, :]
        sig = 1.0 / (1.0 + jnp.exp(-v))
        tail[r, :] = (total * (sig * (1.0 + v * (1.0 - sig)))).astype(BF16).astype(F32)
        return 0

    lax.fori_loop(0, T // rows, fill, 0)

    def body(i, sums):
        r = pl.ds(pl.multiple_of(i * rows, rows), rows)
        window = pad[pl.ds(pl.multiple_of(i * rows, rows), rows + 8), :]
        d = tail[r, :]
        ahead = tail[pl.ds(pl.multiple_of(i * rows, rows), rows + 8), :]
        same = aux[pl.ds(pl.multiple_of(i * rows, rows), rows + 8), :]
        total = ch[K - 1 : K, :] * d
        new = []
        for k in range(K):
            off = K - 1 - k
            shifted = window[8 - off : 8 - off + rows]
            if k < K - 1:
                shifted = shifted * aux[r, M + k : M + k + 1]
                total = total + ch[k : k + 1, :] * (
                    ahead[off : off + rows] * same[off : off + rows, M + k : M + k + 1]
                )
            new.append(jnp.sum(d * shifted, axis=0, keepdims=True))
        new.append(jnp.sum(d, axis=0, keepdims=True))
        dinner[r, :] = total.astype(BF16)
        return sums + jnp.concatenate(new, axis=0)

    gtap[0 : K + 1, :] = lax.fori_loop(0, T // rows, body, jnp.zeros((K + 1, C), F32))
    for m in range(M):
        gx[m] = dot(act3[:, m * C : (m + 1) * C], dpar[...], TN)


def block_call(S, PN, args, T, C, width):
    dma = pltpu.SemaphoreType.DMA
    TL, DD = args[0].shape
    chunks = T // LANES
    f = lambda *shape: sds(shape)
    b = lambda *shape: sds(shape, BF16)
    vf = lambda *shape: pltpu.VMEM(shape, F32)
    vb = lambda *shape: pltpu.VMEM(shape, BF16)
    n = S * PN
    out = (
        b(S, TL, width), b(S, TL, width), f(PN, 8, width), f(n, 8, LANES),
        f(S, M, R // S, C), f(M, C, R + 2 * N), f(8, C), f(1 + M + N, C),
        b(T, width), b(T, width), f(T, 8), b(S, T, 2 * C), b(S, T, C), f(TL, LANES),
    )
    scratch = (
        [vf(8, TL), vb(PN, S, TL, DD // PN), vb(PN, S, TL, DD // PN), vb(T, DD)]
        + [vb(DD, M * C), vb(DD, M * C), vb(S, M * C, width), vf(S, 8, TL), vf(S, 8, width)]
        + [vb(S, M, R // S, C)]
        + [vf(T, C)] * 4
        + [vf(T + 8, C), vb(T, M * C), vf(T, R), vf(chunks, 2 * N, LANES)]
        + [vb(T, C), vf(T, C), vb(T, C), vb(T, R), vf(chunks, 2 * N, LANES), vf(T, C)]
        + [vf(T + 1, N, C), vb(T, C), vb(T, C), vf(T, C), vf(T + 8, 8), vb(T, width)]
        + [vb(S, T, C), vb(S, T, 2 * C), vf(T, C), vf(T, C), vb(T, M * C), vb(T, M * R)]
        + [vb(T, C), vf(T, R), vf(chunks, 2 * N, LANES), vf(T, C), vf(M, R, C)]
        + [vb(T, R), vf(chunks, 2 * N, LANES), vf(T + 8, C), vb(T, R + 2 * N), vb(T, C)]
        + [vb(2, T, width), vf(S, 8, LANES), vf(8, width)]
        + Spread.semaphores(S) * 2
        + [dma((S,))] * 12
        + [dma((6,))]
        + sum_scratch(S, PN, T)
        + RowGather.semaphores(S) * 3
        + [dma((S,)), dma((S,)), dma]
        + [dma((S,))] * 4 + [dma((PN,))] * 2 + [dma((n,))] * 2
    )
    vm, hb = pl.BlockSpec(memory_space=pltpu.VMEM), pl.BlockSpec(memory_space=pl.ANY)
    return pl.pallas_call(
        functools.partial(block_kernel, S, PN),
        out_shape=out,
        in_specs=[vm] * len(args),
        out_specs=[hb if i in (11, 12) else vm for i in range(len(out))],
        scratch_shapes=scratch,
        compiler_params=pltpu.CompilerParams(
            collective_id=0, has_side_effects=True, vmem_limit_bytes=VMEM_LIMIT
        ),
    )(*args)


def cast_kernel(w_in, w_out, wi, wg, wo):
    S, width, C = wi.shape
    stride = 2 * S
    for b in range(S):
        wi[b] = w_in[pl.ds(2 * b, width, stride=stride), :].astype(BF16)
        wg[b] = w_in[pl.ds(2 * b + 1, width, stride=stride), :].astype(BF16)
        wo[b] = w_out[0, b * C : (b + 1) * C, :].astype(BF16)


def cast_weights(S, flat, w_out):
    _, inner_width, width = w_out.shape
    C = inner_width // S
    return pl.pallas_call(
        cast_kernel,
        out_shape=(
            sds((S, width, M * C), BF16),
            sds((S, width, M * C), BF16),
            sds((S, M * C, width), BF16),
        ),
        grid=(M,),
        in_specs=[
            pl.BlockSpec((width * 2 * S, C), lambda m: (m, 0)),
            pl.BlockSpec((1, inner_width, width), lambda m: (m, 0, 0)),
        ],
        out_specs=[
            pl.BlockSpec((S, width, C), lambda m: (0, 0, m)),
            pl.BlockSpec((S, width, C), lambda m: (0, 0, m)),
            pl.BlockSpec((S, C, width), lambda m: (0, m, 0)),
        ],
        compiler_params=pltpu.CompilerParams(vmem_limit_bytes=VMEM_LIMIT),
    )(flat, w_out)


def to_rows(w, S):
    m, width, two, channels = w.shape
    c = channels // S
    return w.reshape(m, width, two, S, c).transpose(0, 1, 3, 2, 4).reshape(-1, c)


def from_rows(rows, S, shape):
    m, width, two, channels = shape
    c = channels // S
    return rows.reshape(m, width, S, two, c).transpose(0, 1, 3, 2, 4).reshape(shape)


def adam_terms(g, m, s):
    new_m = BETA_ONE * m + (1.0 - BETA_ONE) * g
    new_s = BETA_TWO * s + (1.0 - BETA_TWO) * (g * g)
    root = jnp.sqrt(new_s * (1.0 / (1.0 - BETA_TWO**STEP))) + ADAM_EPSILON
    return new_m, new_s, (new_m * (1.0 / (1.0 - BETA_ONE**STEP))) / root


def corner(shape, row, value):
    at = lambda k: lax.broadcasted_iota(jnp.int32, shape, k)
    return jnp.where(jnp.logical_and(at(0) == row, at(1) == 0), value, 0.0)


def adam_in_kernel(NR, aux, dall, w, m, s, nm, ns, dr, norms, turned, gs):
    i = pl.program_id(0)
    T, width = NR.shape
    S = dall.shape[0]
    C = dall.shape[2] // 2
    mask = aux[:, 0:1]
    for k in range(1, M):
        mask = jnp.where(i == k, aux[:, k : k + 1], mask)
    turned[...] = jnp.transpose((NR[...].astype(F32) * mask).astype(BF16))
    for b in range(S):
        g = dot(turned[...], dall[b])
        gs[pl.ds(2 * b, width, stride=2 * S), :] = g[:, 0:C]
        gs[pl.ds(2 * b + 1, width, stride=2 * S), :] = g[:, C : 2 * C]
    rows = 256

    def body(k, sums):
        r = pl.ds(pl.multiple_of(k * rows, rows), rows)
        weight = w[r, :]
        new_m, new_s, ratio = adam_terms(gs[r, :], m[r, :], s[r, :])
        direction = ratio + WEIGHT_DECAY * weight
        nm[r, :] = new_m
        ns[r, :] = new_s
        dr[r, :] = direction
        fold = lambda v: jnp.sum((v * v).reshape(rows // 8, 8, C), axis=0)
        return sums[0] + fold(weight), sums[1] + fold(direction)

    zero = jnp.zeros((8, C), F32)
    a, b = lax.fori_loop(0, w.shape[0] // rows, body, (zero, zero))
    norms[0, 0] = a
    norms[0, 1] = b


def adam_in(NR, aux, dall, w, m, s):
    T, width = NR.shape
    S, _, two = dall.shape
    C = two // 2
    piece = pl.BlockSpec((width * 2 * S, C), lambda i: (i, 0))
    whole = lambda shape: pl.BlockSpec(shape, lambda i: (0,) * len(shape))
    return pl.pallas_call(
        adam_in_kernel,
        out_shape=(sds(w.shape), sds(w.shape), sds(w.shape), sds((M, 2, 8, C))),
        grid=(M,),
        in_specs=[whole((T, width)), whole((T, 8)), whole(dall.shape), piece, piece, piece],
        out_specs=[piece, piece, piece, pl.BlockSpec((1, 2, 8, C), lambda i: (i, 0, 0, 0))],
        scratch_shapes=[pltpu.VMEM((width, T), BF16), pltpu.VMEM((width * 2 * S, C), F32)],
        compiler_params=pltpu.CompilerParams(vmem_limit_bytes=VMEM_LIMIT),
    )(NR, aux, dall, w, m, s)


def adam_out_kernel(gall, G, aux, w, m, s, nm, ns, dr, norms, turned):
    i = pl.program_id(0)
    T, C = gall.shape[1:]
    wide = gall[0].astype(F32)

    @pl.when(i == 0)
    def _():
        norms[...] = jnp.zeros(norms.shape, F32)

    for k in range(M):
        turned[...] = jnp.transpose((wide * aux[:, k : k + 1]).astype(BF16))
        weight = w[k]
        new_m, new_s, ratio = adam_terms(dot(turned[...], G[...]), m[k], s[k])
        direction = ratio + WEIGHT_DECAY * weight
        nm[k] = new_m
        ns[k] = new_s
        dr[k] = direction
        fold = lambda v: jnp.sum((v * v).reshape(C // 8, 8, v.shape[1]), axis=0)
        norms[k, 0] += fold(weight)
        norms[k, 1] += fold(direction)


def adam_out(gall, G, aux, w, m, s):
    S, T, C = gall.shape
    width = G.shape[1]
    piece = pl.BlockSpec((M, C, width), lambda i: (0, i, 0))
    whole = lambda shape: pl.BlockSpec(shape, lambda i: (0,) * len(shape))
    return pl.pallas_call(
        adam_out_kernel,
        out_shape=(sds(w.shape), sds(w.shape), sds(w.shape), sds((M, 2, 8, width))),
        grid=(S,),
        in_specs=[
            pl.BlockSpec((1, T, C), lambda i: (i, 0, 0)),
            whole((T, width)),
            whole((T, 8)),
            piece,
            piece,
            piece,
        ],
        out_specs=[piece, piece, piece, whole((M, 2, 8, width))],
        scratch_shapes=[pltpu.VMEM((C, T), BF16)],
        compiler_params=pltpu.CompilerParams(vmem_limit_bytes=VMEM_LIMIT),
    )(gall, G, aux, w, m, s)


def adam_small_kernel(
    gx, more, gtap, gch, GG, wx, mx, sx, ax, wd, md, sd, ch, mc, sc, ac, gn, mg, sg, ag, nin, nout,
    nmx, nsx, dx, nmd, nsd, dd, nwc, nmc, nsc, nac, nwg, nmg, nsg, nag, tile, gc, gd,
):
    S = more.shape[0]
    C = more.shape[3]
    total = jnp.zeros((8, LANES), F32)
    lane = lax.broadcasted_iota(jnp.int32, total.shape, 1)

    def put(total, k, value):
        return jnp.where(lane == k, value, total)

    square = lambda v: jnp.sum(v * v)
    for t in range(S):
        gd[:, :, t * C : (t + 1) * C] = more[t]
    for m in range(M):
        total = put(total, m, jnp.sum(nin[m, 0]))
        total = put(total, 4 * M + m, jnp.sum(nin[m, 1]))
        total = put(total, 3 * M + m, jnp.sum(nout[m, 0]))
        total = put(total, 7 * M + m, jnp.sum(nout[m, 1]))
        new_m, new_s, ratio = adam_terms(gx[m], mx[m], sx[m])
        direction = ratio + WEIGHT_DECAY * wx[m]
        nmx[m] = new_m
        nsx[m] = new_s
        dx[m] = direction
        total = put(total, M + m, square(wx[m]))
        total = put(total, 5 * M + m, square(direction))
        new_m, new_s, ratio = adam_terms(gd[m], md[m], sd[m])
        direction = ratio + WEIGHT_DECAY * wd[m]
        nmd[m] = new_m
        nsd[m] = new_s
        dd[m] = direction
        total = put(total, 2 * M + m, square(wd[m]))
        total = put(total, 6 * M + m, square(direction))
    tile[...] = total
    gc[0 : K + 1, :] = gtap[0 : K + 1, :]
    gc[K + 1 :, :] = gch[...]
    new_m, new_s, ratio = adam_terms(gc[...], mc[...], sc[...])
    new = ch[...] - CHANNEL_RATE * ratio
    nwc[...] = new
    nmc[...] = new_m
    nsc[...] = new_s
    nac[...] = AVERAGE_KEEP * ac[...] + (1.0 - AVERAGE_KEEP) * new
    g = GG[0, 0:1, :]
    for q in range(1, GG.shape[0]):
        g = g + GG[q, 0:1, :]
    new_m, new_s, ratio = adam_terms(g, mg[...], sg[...])
    new = gn[...] - GAIN_RATE * ratio
    nwg[...] = new
    nmg[...] = new_m
    nsg[...] = new_s
    nag[...] = AVERAGE_KEEP * ag[...] + (1.0 - AVERAGE_KEEP) * new


def norms_kernel(S, PN, tile, TILE, ts, tr):
    greet_all(S, PN)
    s, p = lax.axis_index("seq"), lax.axis_index("tp")
    n = S * PN
    me = s * PN + p

    def copy(k):
        j = lax.rem(me + k, n)
        device = {"seq": lax.div(j, PN), "tp": lax.rem(j, PN)}
        return seq_copy(tile, TILE.at[k], ts.at[k], tr.at[k], device)

    def send(k, _):
        copy(k).start()
        return 0

    def wait(k, _):
        copy(k).wait()
        return 0

    lax.fori_loop(1, n, send, 0)
    TILE[0] = tile[...]
    lax.fori_loop(1, n, wait, 0)


def norms_over_all(S, PN, tile):
    n = S * PN
    dma = pltpu.SemaphoreType.DMA
    return remote_call(
        functools.partial(norms_kernel, S, PN), sds((n,) + tile.shape), 1, [dma((n,))] * 2, 1
    )(tile)


def final_rows_kernel(scale, w, dr, avg, nw, na):
    k = scale[pl.program_id(0)]
    new = w[...] - k * dr[...]
    nw[...] = new
    na[...] = AVERAGE_KEEP * avg[...] + (1.0 - AVERAGE_KEEP) * new


def final_rows(scale, w, dr, avg, pieces):
    shape = w.shape
    rows = lambda v: v.reshape(M * pieces, -1, shape[-1])
    block = pl.BlockSpec((1, w.size // shape[-1] // M // pieces, shape[-1]), lambda i: (i, 0, 0))
    nw, na = pl.pallas_call(
        final_rows_kernel,
        out_shape=(sds(rows(w).shape), sds(rows(w).shape)),
        grid=(M * pieces,),
        in_specs=[pl.BlockSpec(memory_space=pltpu.SMEM), block, block, block],
        out_specs=[block, block],
        compiler_params=pltpu.CompilerParams(vmem_limit_bytes=VMEM_LIMIT),
    )(jnp.repeat(scale, pieces), rows(w), rows(dr), rows(avg))
    return nw.reshape(shape), na.reshape(shape)


def local(
    tokens, out_grad, modality, segment,
    w_in, w_x, w_dt, w_out, channel, norm_gain,
    moment_in, moment_x, moment_dt, moment_out, moment_channel, moment_gain,
    square_in, square_x, square_dt, square_out, square_channel, square_gain,
    average_in, average_x, average_dt, average_out, average_channel, average_gain,
):
    S, PN = lax.axis_size("seq"), lax.axis_size("tp")
    p = lax.axis_index("tp")
    TL = tokens.shape[0]
    T = S * TL
    width = D // S
    inner_width = w_out.shape[1]
    C = inner_width // S
    flat_in = to_rows(w_in, S)
    wi, wg, wo = cast_weights(S, flat_in, w_out)
    wx = w_x.astype(BF16)
    wlr = wx[:, :, :R].reshape(M * C, R)
    wbc = jnp.transpose(wx[:, :, R:], (2, 0, 1)).reshape(2 * N, M * C)
    modrow = jnp.broadcast_to(modality.astype(F32)[None], (8, TL))
    ahead = jnp.concatenate([jnp.full((K - 1,), -1, jnp.int32), segment])
    same = [(ahead[k : k + T] == segment).astype(F32) for k in range(K - 1)]
    zero = jnp.zeros((T,), F32)
    segs = jnp.stack([zero] * M + same + [same[K - 2], zero], axis=1)
    gain = norm_gain[None, :]
    LO, DN, GG, ROW, MORE, gx, gtap, gch, NR, G, aux, dall, gall, INV = block_call(
        S,
        PN,
        (
            tokens, out_grad, modrow, w_dt.astype(BF16), jnp.broadcast_to(gain, (8, width)),
            wi, wg, wo, segs, channel, wlr, wbc, jnp.transpose(wx, (0, 2, 1)),
        ),
        T, C, width,
    )
    nm_in, ns_in, dir_in, norm_in = adam_in(
        NR, aux, dall, flat_in, to_rows(moment_in, S), to_rows(square_in, S)
    )
    nm_out, ns_out, dir_out, norm_out = adam_out(gall, G, aux, w_out, moment_out, square_out)
    like = lambda v: sds(v.shape)
    row = lambda v: v[None, :]
    vec = sds((1, width))
    (
        nm_x, ns_x, dir_x, nm_dt, ns_dt, dir_dt, nw_ch, nm_ch, ns_ch, na_ch,
        nw_g, nm_g, ns_g, na_g, tile,
    ) = local_call(
        adam_small_kernel,
        (like(w_x),) * 3 + (like(w_dt),) * 3 + (like(channel),) * 4 + (vec,) * 4
        + (sds((8, LANES)),),
        22,
        [pltpu.VMEM(channel.shape, F32), pltpu.VMEM(w_dt.shape, F32)],
    )(
        gx, MORE, gtap, gch, GG, w_x, moment_x, square_x, average_x,
        w_dt, moment_dt, square_dt, channel, moment_channel, square_channel, average_channel,
        gain, row(moment_gain), row(square_gain), row(average_gain), norm_in, norm_out,
    )
    TILE = norms_over_all(S, PN, tile)
    totals = jnp.sum(TILE[:, 0, : 8 * M], axis=0).reshape(2, 4, M)
    scales = MATRIX_RATE * (jnp.sqrt(totals[0]) / jnp.sqrt(totals[1]))
    nw_in, na_in = final_rows(scales[0], flat_in, dir_in, to_rows(average_in, S), 2)
    nw_out, na_out = final_rows(scales[3], w_out, dir_out, average_out, 1)
    nw_x = w_x - scales[1][:, None, None] * dir_x
    nw_dt = w_dt - scales[2][:, None, None] * dir_dt
    na_x = AVERAGE_KEEP * average_x + (1.0 - AVERAGE_KEEP) * nw_x
    na_dt = AVERAGE_KEEP * average_dt + (1.0 - AVERAGE_KEEP) * nw_dt

    def columns(blocks):
        b = jnp.sum(blocks.reshape(S // PN, PN, TL, width).astype(F32), axis=1)
        return jnp.concatenate([b[h] for h in range(S // PN)], axis=1)

    along = jnp.sum(ROW[:, 0, :], axis=0)[:, None]
    out_width = out_grad.shape[1]
    mine = lax.dynamic_slice_in_dim(tokens, p * out_width, out_width, 1).astype(F32)
    inv = INV[:, 0:1]
    layer_out = mine + columns(LO)
    tokens_grad = out_grad.astype(F32) + inv * (columns(DN) - mine * inv * (along / D))
    back = lambda v: from_rows(v, S, w_in.shape)
    return (
        layer_out, tokens_grad,
        back(nw_in), nw_x, nw_dt, nw_out, nw_ch, nw_g[0],
        back(nm_in), nm_x, nm_dt, nm_out, nm_ch, nm_g[0],
        back(ns_in), ns_x, ns_dt, ns_out, ns_ch, ns_g[0],
        back(na_in), na_x, na_dt, na_out, na_ch, na_g[0],
    )


def channels_fit(mesh):
    S, PN = mesh.shape["seq"], mesh.shape["tp"]
    n = S * PN
    return PN == 4 and S % 4 == 0 and (2 * N) % n == 0 and D * 2 // n == LANES


def solution(mesh):
    placed = (
        P("seq", None),
        P("seq", "tp"),
        P("seq"),
        P(),
        P(None, "seq", None, "tp"),
        P(None, ("tp", "seq"), None),
        P(None, "seq", "tp"),
        P(None, "tp", "seq"),
        P(None, ("tp", "seq")),
        P("seq"),
        P(None, "seq", None, "tp"),
        P(None, ("tp", "seq"), None),
        P(None, "seq", "tp"),
        P(None, "tp", "seq"),
        P(None, ("tp", "seq")),
        P("seq"),
        P(None, "seq", None, "tp"),
        P(None, ("tp", "seq"), None),
        P(None, "seq", "tp"),
        P(None, "tp", "seq"),
        P(None, ("tp", "seq")),
        P("seq"),
        P(None, "seq", None, "tp"),
        P(None, ("tp", "seq"), None),
        P(None, "seq", "tp"),
        P(None, "tp", "seq"),
        P(None, ("tp", "seq")),
        P("seq"),
    )
    return jax.shard_map(
        local if channels_fit(mesh) else generic_local,
        mesh=mesh,
        in_specs=placed,
        out_specs=(
            P("seq", "tp"),
            P("seq", "tp"),
            P(None, "seq", None, "tp"),
            P(None, ("tp", "seq"), None),
            P(None, "seq", "tp"),
            P(None, "tp", "seq"),
            P(None, ("tp", "seq")),
            P("seq"),
            P(None, "seq", None, "tp"),
            P(None, ("tp", "seq"), None),
            P(None, "seq", "tp"),
            P(None, "tp", "seq"),
            P(None, ("tp", "seq")),
            P("seq"),
            P(None, "seq", None, "tp"),
            P(None, ("tp", "seq"), None),
            P(None, "seq", "tp"),
            P(None, "tp", "seq"),
            P(None, ("tp", "seq")),
            P("seq"),
            P(None, "seq", None, "tp"),
            P(None, ("tp", "seq"), None),
            P(None, "seq", "tp"),
            P(None, "tp", "seq"),
            P(None, ("tp", "seq")),
            P("seq"),
        ),
        check_vma=False,
    )
```

```python
import functools

import jax
import jax.numpy as jnp
from jax import lax
from jax.experimental import pallas as pl
from jax.experimental.pallas import tpu as pltpu
from jax.sharding import PartitionSpec as P

D = 2048
R = 128
N = 16
K = 4
M = 3
STEP = 10


EPSILON = 1e-05
BETA_ONE = 0.9
BETA_TWO = 0.999
ADAM_EPSILON = 1e-06
WEIGHT_DECAY = 0.01
MATRIX_RATE = 0.25
CHANNEL_RATE = 0.7
GAIN_RATE = 0.35
AVERAGE_KEEP = 0.8
PRECISE = lax.Precision.HIGHEST


def passed_along(value, axis, steps):
    count = lax.axis_size(axis)
    leading, last = (max(0, -steps), min(count, count - steps))
    return lax.ppermute(value, axis, [(source, source + steps) for source in range(leading, last)])


def prefix(x, axis, combine, identity, reverse):
    devices, place = (lax.axis_size(axis), lax.axis_index(axis))
    everything = jax.tree.map(lambda part: lax.all_gather(part, axis), x)
    start = jax.tree.map(
        lambda part, zero: jnp.broadcast_to(jnp.asarray(zero, part.dtype), part.shape), x, identity
    )

    def lap(k, before):
        at = devices - 1 - k if reverse else k
        reached = at > place if reverse else at < place
        new = combine(before, jax.tree.map(lambda part: part[at], everything))
        return jax.tree.map(lambda a, b: jnp.where(reached, a, b), new, before)

    return lax.fori_loop(0, devices, lap, start)


def silu_grad(operand):
    sigmoid_of = jax.nn.sigmoid(operand)
    return sigmoid_of * (1.0 + operand * (1.0 - sigmoid_of))


def combine(earlier, following):
    return (earlier[0] * following[0], following[0] * earlier[1] + following[1])


def masked_dot(mask_cols, operand, stacked):
    running = mask_cols[:, 0:1] * jnp.dot(operand, stacked[0], preferred_element_type=jnp.float32)
    for modal_index in range(1, M):
        running = running + mask_cols[:, modal_index : modal_index + 1] * jnp.dot(
            operand, stacked[modal_index], preferred_element_type=jnp.float32
        )
    return running


def masked_back(mask_cols, operand, stacked):
    contract = (((1,), (1,)), ((), ()))
    running = mask_cols[:, 0:1] * lax.dot_general(
        operand, stacked[0], contract, preferred_element_type=jnp.float32
    )
    for modal_index in range(1, M):
        running = running + mask_cols[:, modal_index : modal_index + 1] * lax.dot_general(
            operand, stacked[modal_index], contract, preferred_element_type=jnp.float32
        )
    return running


def masked_outer(mask_low, operand, cotangent):
    contract = (((0,), (0,)), ((), ()))
    return jnp.stack(
        [
            lax.dot_general(
                operand * mask_low[:, modal_index : modal_index + 1],
                cotangent,
                contract,
                preferred_element_type=jnp.float32,
            )
            for modal_index in range(M)
        ]
    )


def adam_parts(gradient, moment, square):
    moment_new = BETA_ONE * moment + (1.0 - BETA_ONE) * gradient
    square_new = BETA_TWO * square + (1.0 - BETA_TWO) * gradient * gradient
    adam_ratio = (
        moment_new
        / (1.0 - BETA_ONE**STEP)
        / (jnp.sqrt(square_new / (1.0 - BETA_TWO**STEP)) + ADAM_EPSILON)
    )
    return (moment_new, square_new, adam_ratio)


def generic_local(
    tokens,
    out_grad,
    modality,
    segment,
    w_in,
    w_x,
    w_dt,
    w_out,
    channel,
    norm_gain,
    moment_in,
    moment_x,
    moment_dt,
    moment_out,
    moment_channel,
    moment_gain,
    square_in,
    square_x,
    square_dt,
    square_out,
    square_channel,
    square_gain,
    average_in,
    average_x,
    average_dt,
    average_out,
    average_channel,
    average_gain,
):
    tok_local = tokens.shape[0]
    width_tp = out_grad.shape[1]
    lowered = (
        w_in.astype(jnp.bfloat16),
        w_x.astype(jnp.bfloat16),
        w_dt.astype(jnp.bfloat16),
        w_out.astype(jnp.bfloat16),
    )
    stack_in, stack_x, stack_dt, stack_out = (
        lax.all_gather(lowered[0], "seq", axis=1, tiled=True),
        lax.all_gather(lowered[1], "seq", axis=1, tiled=True),
        lax.all_gather(lowered[2], "seq", axis=1, tiled=True),
        lax.all_gather(lowered[3], "seq", axis=2, tiled=True),
    )
    chan_full, gain_full = (
        lax.all_gather(channel, "seq", axis=1, tiled=True),
        lax.all_gather(norm_gain, "seq", axis=0, tiled=True),
    )
    inner_width = stack_out.shape[1]
    in_flat = stack_in.reshape(M, D, 2 * inner_width)
    seq_index = lax.axis_index("seq")
    tp_index = lax.axis_index("tp")
    start_row = seq_index * tok_local
    seg_local = lax.dynamic_slice(segment, (start_row,), (tok_local,))
    seg_before = lax.dynamic_slice(
        jnp.concatenate([jnp.full((K - 1,), -1, jnp.int32), segment]),
        (start_row,),
        (tok_local + K - 1,),
    )
    seg_after = lax.dynamic_slice(
        jnp.concatenate([segment, jnp.full((K - 1,), -2, jnp.int32)]),
        (start_row,),
        (tok_local + K - 1,),
    )
    mask_cols = (modality[:, None] == jnp.arange(M, dtype=jnp.int32)[None, :]).astype(jnp.float32)
    mask_low = mask_cols.astype(jnp.bfloat16)
    tokens_wide = tokens.astype(jnp.float32)
    inv_root = lax.rsqrt(jnp.mean(tokens_wide * tokens_wide, axis=-1, keepdims=True) + EPSILON)
    scaled = tokens_wide * inv_root
    normed = (scaled * gain_full[None, :]).astype(jnp.bfloat16)
    projected = masked_dot(mask_cols, normed, in_flat)
    inner_act = projected[:, :inner_width].astype(jnp.bfloat16)
    gate_pre = projected[:, inner_width:]
    rim_rows = passed_along(inner_act[tok_local - (K - 1) :], "seq", 1)
    extended = jnp.concatenate([rim_rows, inner_act], axis=0).astype(jnp.float32)
    conv_pre = jnp.broadcast_to(chan_full[K][None, :], (tok_local, inner_width))
    same_docs = []
    for tap_index in range(K):
        same_doc = (seg_before[tap_index : tap_index + tok_local] == seg_local).astype(jnp.float32)[
            :, None
        ]
        same_docs.append(same_doc)
        conv_pre = (
            conv_pre
            + chan_full[tap_index][None, :] * extended[tap_index : tap_index + tok_local] * same_doc
        )
    activated = jax.nn.silu(conv_pre).astype(jnp.bfloat16)
    act_wide = activated.astype(jnp.float32)
    params_x = lax.psum(masked_dot(mask_cols, activated, stack_x), "tp")
    low_rank = params_x[:, :R].astype(jnp.bfloat16)
    input_b = params_x[:, R : R + N]
    output_c = params_x[:, R + N :]
    step_pre = masked_dot(mask_cols, low_rank, stack_dt) + jnp.dot(
        mask_cols, chan_full[K + 2 : K + 2 + M], precision=PRECISE
    )
    step_size = jax.nn.softplus(step_pre)
    decay_base = -jnp.exp(chan_full[K + 2 + M :])
    keep_flag = (seg_before[K - 2 : K - 2 + tok_local] == seg_local).astype(jnp.float32)
    decay_rate = jnp.exp(step_size[:, None, :] * decay_base[None]) * keep_flag[:, None, None]
    drive_term = (step_size * act_wide)[:, None, :] * input_b[:, :, None]
    decay_cum, local_state = lax.associative_scan(combine, (decay_rate, drive_term), axis=0)
    unit_pair = (jnp.ones_like(decay_base), jnp.zeros_like(decay_base))
    carry_in = prefix((decay_cum[-1], local_state[-1]), "seq", combine, unit_pair, False)[1]
    hidden_state = local_state + decay_cum * carry_in[None]
    mixed_out = (
        jnp.einsum("tn,tne->te", output_c, hidden_state, precision=PRECISE)
        + chan_full[K + 1][None, :] * act_wide
    )
    gate_act = jax.nn.silu(gate_pre)
    gated_out = (mixed_out * gate_act).astype(jnp.bfloat16)
    out_share = lax.psum_scatter(
        masked_dot(mask_cols, gated_out, stack_out), "tp", scatter_dimension=1, tiled=True
    )
    layer_out = lax.dynamic_slice_in_dim(tokens_wide, tp_index * width_tp, width_tp, 1) + out_share
    grad_full = lax.all_gather(out_grad, "tp", axis=1, tiled=True)
    d_gated = masked_back(mask_cols, grad_full, stack_out)
    grad_out = masked_outer(mask_low, gated_out, grad_full)
    d_mixed = d_gated * gate_act
    d_gate = d_gated * mixed_out * silu_grad(gate_pre)
    grad_skip = jnp.sum(d_mixed * act_wide, axis=0)
    d_out_c = jnp.einsum("te,tne->tn", d_mixed, hidden_state, precision=PRECISE)
    d_hidden = output_c[:, :, None] * d_mixed[:, None, :]
    decay_next = jnp.concatenate([decay_rate[1:], jnp.ones_like(decay_rate[:1])], axis=0)
    suffix_cum, local_back = lax.associative_scan(
        combine, (decay_next, d_hidden), reverse=True, axis=0
    )
    device_pair = (decay_rate[0] * suffix_cum[0], decay_rate[0] * local_back[0])
    carry_back = prefix(device_pair, "seq", combine, unit_pair, True)[1]
    back_state = local_back + suffix_cum * carry_back[None]
    state_prev = jnp.concatenate([carry_in[None], hidden_state[:-1]], axis=0)
    d_log = back_state * state_prev * decay_rate
    d_drive_sum = jnp.einsum("tne,tn->te", back_state, input_b, precision=PRECISE)
    d_step_size = jnp.sum(d_log * decay_base[None], axis=1) + act_wide * d_drive_sum
    grad_decay = decay_base * jnp.einsum("tne,te->ne", d_log, step_size, precision=PRECISE)
    d_in_b = jnp.einsum("tne,te->tn", back_state, step_size * act_wide, precision=PRECISE)
    d_step = (d_step_size * jax.nn.sigmoid(step_pre)).astype(jnp.bfloat16)
    d_step_wide = d_step.astype(jnp.float32)
    grad_bias = jnp.dot(mask_cols.T, d_step_wide, precision=PRECISE)
    grad_dt = masked_outer(mask_low, low_rank, d_step)
    d_low = masked_back(mask_cols, d_step, stack_dt)
    d_params = lax.psum(jnp.concatenate([d_low, d_in_b, d_out_c], axis=1), "tp").astype(
        jnp.bfloat16
    )
    grad_x = masked_outer(mask_low, activated, d_params)
    d_activ = (
        d_mixed * chan_full[K + 1][None, :]
        + step_size * d_drive_sum
        + masked_back(mask_cols, d_params, stack_x)
    )
    d_conv = (d_activ * silu_grad(conv_pre)).astype(jnp.bfloat16)
    rim_back = passed_along(d_conv[: K - 1], "seq", -1)
    d_conv_wide = d_conv.astype(jnp.float32)
    conv_after = jnp.concatenate([d_conv, rim_back], axis=0).astype(jnp.float32)
    d_inner = jnp.zeros((tok_local, inner_width), jnp.float32)
    grad_taps = []
    for tap_index in range(K):
        grad_taps.append(
            jnp.sum(
                d_conv_wide * extended[tap_index : tap_index + tok_local] * same_docs[tap_index],
                axis=0,
            )
        )
        offset = K - 1 - tap_index
        same_after = (seg_after[offset : offset + tok_local] == seg_local).astype(jnp.float32)[
            :, None
        ]
        d_inner = (
            d_inner
            + chan_full[tap_index][None, :] * conv_after[offset : offset + tok_local] * same_after
        )
    grad_conv_b = jnp.sum(d_conv_wide, axis=0)
    d_proj = jnp.concatenate([d_inner, d_gate], axis=1).astype(jnp.bfloat16)
    grad_in = masked_outer(mask_low, normed, d_proj).reshape(M, D, 2, inner_width)
    d_normed = lax.psum(masked_back(mask_cols, d_proj, in_flat), "tp")
    grad_gain = jnp.sum(d_normed * scaled, axis=0)
    d_scaled = d_normed * gain_full[None, :]
    d_tokens = inv_root * (d_scaled - scaled * jnp.mean(d_scaled * scaled, axis=-1, keepdims=True))
    tokens_grad = out_grad.astype(jnp.float32) + lax.dynamic_slice_in_dim(
        d_tokens, tp_index * width_tp, width_tp, 1
    )
    grad_channel = jnp.concatenate(
        [jnp.stack(grad_taps), grad_conv_b[None], grad_skip[None], grad_bias, grad_decay], axis=0
    )
    reduced = (
        lax.psum_scatter(grad_in, "seq", scatter_dimension=1, tiled=True),
        lax.psum_scatter(grad_x, "seq", scatter_dimension=1, tiled=True),
        lax.psum_scatter(grad_dt, "seq", scatter_dimension=1, tiled=True),
        lax.psum_scatter(grad_out, "seq", scatter_dimension=2, tiled=True),
        lax.psum_scatter(grad_channel, "seq", scatter_dimension=1, tiled=True),
        lax.psum_scatter(grad_gain, "seq", scatter_dimension=0, tiled=True),
    )
    weights = (w_in, w_x, w_dt, w_out, channel, norm_gain)
    moments = (moment_in, moment_x, moment_dt, moment_out, moment_channel, moment_gain)
    squares = (square_in, square_x, square_dt, square_out, square_channel, square_gain)
    averages = (average_in, average_x, average_dt, average_out, average_channel, average_gain)
    adam_all = [
        adam_parts(reduced[position], moments[position], squares[position]) for position in range(6)
    ]
    directions = [adam_all[position][2] + WEIGHT_DECAY * weights[position] for position in range(4)]
    weight_sums = jnp.stack(
        [
            jnp.sum(
                weights[position] * weights[position], axis=tuple(range(1, weights[position].ndim))
            )
            for position in range(4)
        ]
    )
    direction_sums = jnp.stack(
        [
            jnp.sum(
                directions[position] * directions[position],
                axis=tuple(range(1, directions[position].ndim)),
            )
            for position in range(4)
        ]
    )
    totals = lax.psum(jnp.stack([weight_sums, direction_sums]), ("seq", "tp"))
    trust_ratio = jnp.sqrt(totals[0]) / jnp.sqrt(totals[1])
    new_weights = []
    new_averages = []
    for position in range(6):
        weight = weights[position]
        if position < 4:
            updated = (
                weight
                - MATRIX_RATE
                * trust_ratio[position].reshape((M,) + (1,) * (weight.ndim - 1))
                * directions[position]
            )
        elif position == 4:
            updated = weight - CHANNEL_RATE * adam_all[position][2]
        else:
            updated = weight - GAIN_RATE * adam_all[position][2]
        new_weights.append(updated)
        new_averages.append(AVERAGE_KEEP * averages[position] + (1.0 - AVERAGE_KEEP) * updated)
    return (
        layer_out,
        tokens_grad,
        new_weights[0],
        new_weights[1],
        new_weights[2],
        new_weights[3],
        new_weights[4],
        new_weights[5],
        adam_all[0][0],
        adam_all[1][0],
        adam_all[2][0],
        adam_all[3][0],
        adam_all[4][0],
        adam_all[5][0],
        adam_all[0][1],
        adam_all[1][1],
        adam_all[2][1],
        adam_all[3][1],
        adam_all[4][1],
        adam_all[5][1],
        new_averages[0],
        new_averages[1],
        new_averages[2],
        new_averages[3],
        new_averages[4],
        new_averages[5],
    )


MESH = pl.DeviceIdType.MESH
VMEM_LIMIT = 62 * 1024 * 1024
LANES = 128
F32 = jnp.float32
BF16 = jnp.bfloat16
NT = (((1,), (1,)), ((), ()))
TN = (((0,), (0,)), ((), ()))


def dot(a, b, dims=(((1,), (0,)), ((), ()))):
    return lax.dot_general(a, b, dims, preferred_element_type=F32)


def local_call(kernel, out_shape, n_in, scratch=(), cost=None):
    return pl.pallas_call(
        kernel,
        out_shape=out_shape,
        in_specs=[pl.BlockSpec(memory_space=pltpu.VMEM)] * n_in,
        out_specs=jax.tree.map(lambda _: pl.BlockSpec(memory_space=pltpu.VMEM), out_shape),
        scratch_shapes=list(scratch),
        compiler_params=pltpu.CompilerParams(vmem_limit_bytes=VMEM_LIMIT),
        cost_estimate=cost,
    )


def remote_call(kernel, out_shape, n_in, scratch, ident):
    return pl.pallas_call(
        kernel,
        out_shape=out_shape,
        in_specs=[pl.BlockSpec(memory_space=pltpu.VMEM)] * n_in,
        out_specs=jax.tree.map(lambda _: pl.BlockSpec(memory_space=pltpu.VMEM), out_shape),
        scratch_shapes=list(scratch),
        compiler_params=pltpu.CompilerParams(
            collective_id=ident, has_side_effects=True, vmem_limit_bytes=VMEM_LIMIT
        ),
    )


def sds(shape, dtype=F32):
    return jax.ShapeDtypeStruct(shape, dtype)


def seq_copy(src, dst, send, recv, device):
    return pltpu.make_async_remote_copy(
        src_ref=src,
        dst_ref=dst,
        send_sem=send,
        recv_sem=recv,
        device_id=device,
        device_id_type=MESH,
    )


def place(S, PN):
    s, p = lax.axis_index("seq"), lax.axis_index("tp")
    return s, p, lax.div(s, 2), lax.rem(s, 2)


def greet_all(S, PN):
    s, p = lax.axis_index("seq"), lax.axis_index("tp")
    n = S * PN
    me = s * PN + p
    bar = pltpu.get_barrier_semaphore()

    def greet(k, _):
        j = lax.rem(me + k, n)
        pl.semaphore_signal(
            bar,
            inc=1,
            device_id={"seq": lax.div(j, PN), "tp": lax.rem(j, PN)},
            device_id_type=MESH,
        )
        return 0

    lax.fori_loop(1, n, greet, 0)
    pl.semaphore_wait(bar, n - 1)


class Spread:
    def __init__(self, S, PN, own, buf, zs, zr, xs, xr, ys, yr, cs, cr, ls):
        s, p, z, x = place(S, PN)
        self.zn = S // 2
        zn = self.zn
        other_x = {"seq": 2 * z + 1 - x}
        other_y = {"tp": lax.rem(p + 2, PN)}
        other_c = {"tp": p + 1 - 2 * lax.rem(p, 2)}

        def at(k, j):
            return 2 * lax.rem(z - k + zn, zn) + (x if j == 0 else 1 - x)

        self.local = pltpu.make_async_copy(own, buf.at[p, s], ls)
        self.z = [
            seq_copy(own, buf.at[p, s], zs.at[k], zr.at[k], {"seq": 2 * lax.rem(z + k, zn) + x})
            for k in range(1, zn)
        ]
        self.x = []
        self.y = {}
        for k in range(zn):
            src = own if k == 0 else buf.at[p, at(k, 0)]
            self.x.append(seq_copy(src, buf.at[p, at(k, 0)], xs.at[k], xr.at[k], other_x))
            for j in range(2):
                src = own if (k == 0 and j == 0) else buf.at[p, at(k, j)]
                self.y[k, j] = seq_copy(
                    src, buf.at[p, at(k, j)], ys.at[2 * k + j], yr.at[2 * k + j], other_y
                )
        q = lax.rem(p + 2, PN)
        self.c = [
            seq_copy(buf.at[p], buf.at[p], cs.at[0], cr.at[0], other_c),
            seq_copy(buf.at[q], buf.at[q], cs.at[1], cr.at[1], other_c),
        ]

    def start(self):
        self.local.start()
        for cp in self.z:
            cp.start()
        self.x[0].start()
        self.y[0, 0].start()

    def forward(self):
        for k in range(1, self.zn):
            self.z[k - 1].wait_recv()
            self.x[k].start()
            self.y[k, 0].start()
        for k in range(self.zn):
            self.x[k].wait_recv()
            self.y[k, 1].start()
        self.local.wait()
        self.c[0].start()

    def finish(self):
        for cp in self.y.values():
            cp.wait_recv()
        self.c[1].start()
        for cp in self.z + self.x + list(self.y.values()):
            cp.wait_send()
        for cp in self.c:
            cp.wait()

    @staticmethod
    def semaphores(S):
        dma = pltpu.SemaphoreType.DMA
        return [dma((S // 2,))] * 4 + [dma((S,))] * 2 + [dma((2,))] * 2 + [dma]


def row_copies(S, src, dst, send, recv):
    s = lax.axis_index("seq")
    out = []
    for k in range(1, S):
        d = lax.rem(s + k, S)
        out.append(seq_copy(src(d), dst(s), send.at[k], recv.at[k], {"seq": d}))
    return out


def sum_over_all(
    S, PN, lr, bct, LR, BCT, got_l, got_b, core_l, core_b,
    c1s, c1r, ssl, rsl, ssb, rsb, sgl, rgl, sgb, rgb, c2s, c2r, between=(),
):
    n = S * PN // 2
    s, p = lax.axis_index("seq"), lax.axis_index("tp")
    y, c = lax.div(p, 2), lax.rem(p, 2)
    me = s * (PN // 2) + y
    T = lr.shape[0]
    half, rows = T // 2, T // 2 // n
    chunks = bct.shape[0]
    per = n // (chunks // 2)
    high = bct.shape[1] // per
    twin = {"tp": p + 1 - 2 * c}

    def device(j):
        return {"seq": lax.div(j, PN // 2), "tp": 2 * lax.rem(j, PN // 2) + c}

    def half_l(k):
        return pl.ds(pl.multiple_of(k * half, half), half)

    def half_b(k):
        return pl.ds(k * (chunks // 2), chunks // 2)

    def rows_of(j):
        return pl.ds(pl.multiple_of(c * half + j * rows, rows), rows)

    def slab(ref, j):
        at = c * (chunks // 2) + lax.div(j, per)
        return ref.at[at, pl.ds(pl.multiple_of(lax.rem(j, per) * high, 8), high)]

    swap = [
        seq_copy(lr.at[half_l(1 - c)], core_l, c1s.at[0], c1r.at[0], twin),
        seq_copy(bct.at[half_b(1 - c)], core_b, c1s.at[1], c1r.at[1], twin),
    ]
    for cp in swap:
        cp.start()
    for cp in swap:
        cp.wait()
    lr[half_l(c), :] = lr[half_l(c), :] + core_l[...]
    bct[half_b(c)] = bct[half_b(c)] + core_b[...]

    def first(k):
        j = lax.rem(me + k, n)
        return (
            seq_copy(lr.at[rows_of(j)], got_l.at[k], ssl.at[k], rsl.at[k], device(j)),
            seq_copy(slab(bct, j), got_b.at[k], ssb.at[k], rsb.at[k], device(j)),
        )

    def second(k):
        j = lax.rem(me + k, n)
        mine_l, mine_b = LR.at[rows_of(me)], slab(BCT, me)
        return (
            seq_copy(mine_l, mine_l, sgl.at[k], rgl.at[k], device(j)),
            seq_copy(mine_b, mine_b, sgb.at[k], rgb.at[k], device(j)),
        )

    def start(copies, k):
        for cp in copies(k):
            cp.start()
        return 0

    def wait(copies, k):
        for cp in copies(k):
            cp.wait()
        return 0

    lax.fori_loop(1, n, lambda k, _: start(first, k), 0)
    for cp in between[0:1]:
        cp()
    got_l[0] = lr[rows_of(me), :]
    got_b[0] = slab(bct, me)[...]
    lax.fori_loop(1, n, lambda k, _: wait(first, k), 0)
    LR[rows_of(me), :] = jnp.sum(got_l[...], axis=0).astype(LR.dtype)
    slab(BCT, me)[...] = jnp.sum(got_b[...], axis=0)
    lax.fori_loop(1, n, lambda k, _: start(second, k), 0)
    for cp in between[1:2]:
        cp()
    lax.fori_loop(1, n, lambda k, _: wait(second, k), 0)
    swap = [
        seq_copy(LR.at[half_l(c)], LR.at[half_l(c)], c2s.at[0], c2r.at[0], twin),
        seq_copy(BCT.at[half_b(c)], BCT.at[half_b(c)], c2s.at[1], c2r.at[1], twin),
    ]
    for cp in swap:
        cp.start()
    for cp in swap:
        cp.wait()


def sum_scratch(S, PN, T):
    n = S * PN // 2
    dma = pltpu.SemaphoreType.DMA
    chunks = T // LANES
    slabs = chunks * N // n
    return (
        [pltpu.VMEM((n, T // 2 // n, R), F32), pltpu.VMEM((n, slabs, LANES), F32)]
        + [pltpu.VMEM((T // 2, R), F32), pltpu.VMEM((chunks // 2, 2 * N, LANES), F32)]
        + [dma((2,))] * 2 + [dma((n,))] * 8 + [dma((2,))] * 2
    )


class RowGather:
    def __init__(self, S, own, place_of, zs, zr, xs, xr, ls):
        s, p, z, x = place(S, 1)
        self.zn = zn = S // 2
        other = {"seq": 2 * z + 1 - x}
        at = lambda k: 2 * lax.rem(z - k + zn, zn) + x
        self.local = pltpu.make_async_copy(own, place_of(s), ls)
        self.z = [
            seq_copy(own, place_of(s), zs.at[k], zr.at[k], {"seq": 2 * lax.rem(z + k, zn) + x})
            for k in range(1, zn)
        ]
        self.x = [
            seq_copy(
                own if k == 0 else place_of(at(k)), place_of(at(k)), xs.at[k], xr.at[k], other
            )
            for k in range(zn)
        ]

    def start(self, *which):
        for k in which:
            if k == 0:
                self.local.start()
                self.x[0].start()
            elif k < self.zn:
                self.z[k - 1].start()

    def start_from(self, first):
        self.start(*range(first, self.zn))

    def forward(self, k):
        if k < self.zn:
            self.z[k - 1].wait_recv()
            self.x[k].start()

    def forward_from(self, first):
        for k in range(first, self.zn):
            self.forward(k)

    def finish(self):
        self.local.wait()
        for cp in self.z:
            cp.wait_send()
        for cp in self.x:
            cp.wait()

    @staticmethod
    def semaphores(S):
        dma = pltpu.SemaphoreType.DMA
        return [dma((S // 2,))] * 4 + [dma]


def adam_terms(g, m, s):
    new_m = BETA_ONE * m + (1.0 - BETA_ONE) * g
    new_s = BETA_TWO * s + (1.0 - BETA_TWO) * (g * g)
    root = jnp.sqrt(new_s * (1.0 / (1.0 - BETA_TWO**STEP))) + ADAM_EPSILON
    return new_m, new_s, (new_m * (1.0 / (1.0 - BETA_ONE**STEP))) / root


def softplus(v):
    u = jnp.exp(-jnp.abs(v))
    w = 1.0 + u
    small = jnp.where(w == 1.0, u, jnp.log(w) * (u / jnp.where(w == 1.0, 1.0, w - 1.0)))
    return jnp.maximum(v, 0.0) + small


def masked_sum(acc, aux, r, C):
    total = acc[:, 0:C] * aux[r, 0:1]
    for m in range(1, M):
        total = total + acc[:, m * C : (m + 1) * C] * aux[r, m : m + 1]
    return total


def block_kernel(S, PN, *refs):
    rest = list(refs)
    take = lambda k: [rest.pop(0) for _ in range(k)]
    tok, og, modrow, gain, segs, ch, w_x, m_x, s_x, w_dt, m_dt, s_dt = take(12)
    w_in, m_in, s_in, w_out, m_out, s_out = take(6)
    LO, DN, GG, ROW, MORE, gx, gtap, gch, INV, SCALE, g_in, g_out = take(12)
    tile, toks, ogs, nrm, Wi, Wg, Wo, AUX, GAIN, WD = take(10)
    step, drive, keep, Y, pad, act3, lr, bcp = take(8)
    act, conv, inner, low, bct, pre, H, gated, dgate, dmix, aux, X = take(12)
    gall, dall, DS, DB, dst3, low3, dst, dlow, dbct, dact, gdt = take(11)
    LR2, BCT2, tail, dpar, dinner, part, rowdot, ggs, wdt = take(9)
    wi, wg, wo, wdt_mine, gain_mine, wlr, wbc, wxT, NR, G = take(10)
    gdt_mine, turned, sums_ref, TILE, total_tile = take(5)
    stage, load, store, pair, swaps = take(5)
    ag1, ag2 = take(9), take(9)
    ws = take(12)
    ls = take(1)[0]
    sums = take(16)
    rows_g, rows_d, rows_i = take(5), take(5), take(5)
    mx, mr, ml = take(3)
    last = take(10)
    s, p, z, x = place(S, PN)
    TL, DD = tok.shape
    T = S * TL
    width = DD // S
    quarter = DD // PN
    C = act.shape[1]
    rows = 128

    load_in = pltpu.make_async_copy(w_in, H.at[0 : w_in.shape[0]], stage.at[0])
    load_in.start()
    wide = tok[...].astype(F32)
    inv = lax.rsqrt(jnp.mean(wide * wide, axis=1, keepdims=True) + EPSILON)
    row = jnp.transpose(jnp.broadcast_to(inv, (TL, LANES)))[0:8]
    tile[...] = jnp.where(
        lax.broadcasted_iota(jnp.int32, row.shape, 0) == 0, modrow[...], row
    )
    gain_mine[...] = jnp.broadcast_to(gain[...], gain_mine.shape)
    wdt_mine[...] = w_dt[...].astype(BF16)
    greet_all(S, PN)
    chans = lambda d: pl.ds(pl.multiple_of(d * C, LANES), C)
    block = lambda d: pl.ds(pl.multiple_of(d * width, width), width)
    tokens = Spread(
        S, PN, tok.at[:, pl.ds(pl.multiple_of(p * quarter, LANES), quarter)], toks, *ag1
    )
    small = (
        row_copies(S, lambda d: tile, lambda t: AUX.at[t], ws[0], ws[1])
        + row_copies(S, lambda d: gain_mine, lambda t: GAIN.at[t], ws[2], ws[3])
    )
    dts = row_copies(S, lambda d: wdt_mine.at[:, :, chans(d)], lambda t: WD.at[t], ws[4], ws[5])
    inners = row_copies(S, lambda d: wi.at[d], lambda t: Wi.at[block(t)], ws[6], ws[7])
    gates = row_copies(S, lambda d: wg.at[d], lambda t: Wg.at[block(t)], ws[8], ws[9])
    outs = row_copies(S, lambda d: wo.at[d], lambda t: Wo.at[t], ws[10], ws[11])
    cotangent = Spread(S, PN, og, ogs, *ag2)
    for cp in small:
        cp.start()
    tokens.start()
    load_in.wait()
    stride = 2 * S
    for m in range(M):
        for b in range(S):
            r = pl.ds(m * width * stride + 2 * b, width, stride=stride)
            wi[b, :, m * C : (m + 1) * C] = H[r, :].astype(BF16)
    for cp in inners + dts:
        cp.start()
    for m in range(M):
        for b in range(S):
            r = pl.ds(m * width * stride + 2 * b + 1, width, stride=stride)
            wg[b, :, m * C : (m + 1) * C] = H[r, :].astype(BF16)
    load_out = pltpu.make_async_copy(w_out, H.at[0 : w_out.shape[0]], stage.at[1])
    load_out.start()
    own = [
        pltpu.make_async_copy(tile, AUX.at[s], ls.at[0]),
        pltpu.make_async_copy(gain_mine, GAIN.at[s], ls.at[1]),
        pltpu.make_async_copy(wdt_mine.at[:, :, chans(s)], WD.at[s], ls.at[2]),
        pltpu.make_async_copy(wi.at[s], Wi.at[block(s)], ls.at[3]),
        pltpu.make_async_copy(wg.at[s], Wg.at[block(s)], ls.at[4]),
    ]
    for cp in own:
        cp.start()
    for m in range(M):
        wlr[m * C : (m + 1) * C, :] = jnp.transpose(w_x[m, 0:R, :]).astype(BF16)
        wbc[:, m * C : (m + 1) * C] = w_x[m, R : R + 2 * N, :].astype(BF16)
        wxT[m] = w_x[m].astype(BF16)
    load_out.wait()
    tiles = width // LANES
    for m in range(M):
        for b in range(S):
            rows_b = H[(m * S + b) * C * tiles : (m * S + b + 1) * C * tiles, :]
            pieces = rows_b.reshape(C // 8, tiles, 8, LANES)
            for t in range(tiles):
                wo[b, m * C : (m + 1) * C, t * LANES : (t + 1) * LANES] = (
                    pieces[:, t].reshape(C, LANES).astype(BF16)
                )
    own.append(pltpu.make_async_copy(wo.at[s], Wo.at[s], ls.at[5]))
    own[-1].start()
    for cp in own:
        cp.wait()
    tokens.forward()
    for cp in small:
        cp.wait()
    lane = lax.broadcasted_iota(jnp.int32, (TL, 8), 1)

    def columns(t, _):
        r = pl.ds(pl.multiple_of(t * TL, TL), TL)
        turned = jnp.transpose(jnp.concatenate([AUX[t]] * (LANES // 8), axis=0))
        mask = (turned[:, 0:1] == lane.astype(F32)).astype(F32)
        aux[r, :] = jnp.where(
            lane < M, mask, jnp.where(lane == 7, turned[:, 1:2], segs[r, :])
        )
        return 0

    lax.fori_loop(0, S, columns, 0)
    aux[T : T + 8, :] = jnp.zeros((8, 8), F32)
    tokens.finish()
    per = quarter // width

    def norm(t, _):
        r = pl.ds(pl.multiple_of(t * TL, TL), TL)
        scale = aux[r, 7:8]
        for q in range(PN):
            scaled = toks[q, t].astype(F32) * scale
            for j in range(per):
                part = scaled[:, j * width : (j + 1) * width] * GAIN[q * per + j, 0:1, :]
                nrm[r, q * quarter + j * width : q * quarter + (j + 1) * width] = part.astype(BF16)
        return 0

    lax.fori_loop(0, S, norm, 0)
    for cp in inners:
        cp.wait()
    for cp in gates[0:1]:
        cp.start()

    big = 256
    pad[0:8, :] = jnp.zeros((8, C), F32)

    def first(i, _):
        r = pl.ds(pl.multiple_of(i * big, big), big)
        value = masked_sum(dot(nrm[r, :], Wi[...]), aux, r, C).astype(BF16)
        inner[r, :] = value
        pad[pl.ds(pl.multiple_of(i * big + 8, 8), big), :] = value.astype(F32)
        return 0

    lax.fori_loop(0, T // big, first, 0)

    def convolve(i, _):
        r = pl.ds(pl.multiple_of(i * rows, rows), rows)
        window = pad[pl.ds(pl.multiple_of(i * rows, rows), rows + 8), :]
        v = jnp.broadcast_to(ch[K : K + 1, :], (rows, C))
        for k in range(K):
            term = ch[k : k + 1, :] * window[8 - (K - 1) + k : 8 - (K - 1) + k + rows]
            v = v + (term * aux[r, M + k : M + k + 1] if k < K - 1 else term)
        conv[r, :] = v
        a = (v / (1.0 + jnp.exp(-v))).astype(BF16)
        act[r, :] = a
        a_wide = a.astype(F32)
        for m in range(M):
            act3[r, m * C : (m + 1) * C] = (a_wide * aux[r, m : m + 1]).astype(BF16)
        lr[r, :] = dot(act3[r, :], wlr[...])
        bcp[i] = dot(wbc[...], act3[r, :], NT)
        return 0

    lax.fori_loop(0, T // rows, convolve, 0)
    def start_all(copies):
        for cp in copies:
            cp.start()

    sum_over_all(
        S, PN, lr, bcp, low, bct, *sums,
        between=(lambda: start_all(gates[1:3]), lambda: start_all(gates[3:5])),
    )
    start_all(gates[5:])
    for cp in dts:
        cp.wait()
    cotangent.start()
    for cp in outs:
        cp.start()

    for m in range(M):
        for t in range(S):
            h = R // S
            wdt[m * R + t * h : m * R + (t + 1) * h, :] = WD[t, m]

    def prepare(i, _):
        r = pl.ds(pl.multiple_of(i * rows, rows), rows)
        low_wide = low[r, :].astype(F32)
        bias = jnp.zeros((rows, C), F32)
        for m in range(M):
            mask = aux[r, m : m + 1]
            masked = (low_wide * mask).astype(BF16)
            bias = bias + mask * ch[K + 2 + m : K + 3 + m, :]
            low3[r, m * R : (m + 1) * R] = masked
        bias = bias + dot(low3[r, :], wdt[...])
        pre[r, :] = bias
        st = softplus(bias)
        step[r, :] = st
        drive[r, :] = st * act[r, :].astype(F32)
        keep[r, :] = jnp.broadcast_to(aux[r, 6:7], (rows, C))
        return 0

    lax.fori_loop(0, T // rows, prepare, 0)
    scan_forward(T, C, bct, ch, step, drive, keep, H, Y)
    cotangent.forward()
    for cp in gates:
        cp.wait()

    def gate(i, _):
        r = pl.ds(pl.multiple_of(i * big, big), big)
        drive[r, :] = masked_sum(dot(nrm[r, :], Wg[...]), aux, r, C)
        return 0

    lax.fori_loop(0, T // big, gate, 0)
    cotangent.finish()
    for cp in outs:
        cp.wait()

    def back(i, _):
        r = pl.ds(pl.multiple_of(i * big, big), big)
        acc = jnp.zeros((big, M * C), F32)
        for q in range(PN):
            g = ogs[q, pl.ds(i * (big // TL), big // TL)].reshape(big, quarter)
            for j in range(per):
                acc = acc + dot(g[:, j * width : (j + 1) * width], Wo[q * per + j], NT)
        keep[r, :] = masked_sum(acc, aux, r, C)
        return 0

    lax.fori_loop(0, T // big, back, 0)

    def finish(i, _):
        r = pl.ds(pl.multiple_of(i * rows, rows), rows)
        mixed = Y[r, :] + ch[K + 1 : K + 2, :] * act[r, :].astype(F32)
        g, d = drive[r, :], keep[r, :]
        sig = 1.0 / (1.0 + jnp.exp(-g))
        gated[r, :] = (mixed * (g * sig)).astype(BF16)
        dmix[r, :] = d * (g * sig)
        dgate[r, :] = (d * mixed * (sig * (1.0 + g * (1.0 - sig)))).astype(BF16)
        return 0

    lax.fori_loop(0, T // rows, finish, 0)
    half = lambda t, k: pl.ds(pl.multiple_of((2 * t + k) * C, LANES), C)
    gathers = [
        RowGather(S, gated, lambda t: gall.at[:, chans(t)], *rows_g),
        RowGather(S, dgate, lambda t: dall.at[:, half(t, 1)], *rows_d),
        RowGather(S, dinner, lambda t: dall.at[:, half(t, 0)], *rows_i),
    ]
    gathers[0].start(0, 1, 2)
    mine = pl.ds(pl.multiple_of(lax.rem(s, per) * width, width), width)
    NR[...] = nrm[:, pl.ds(pl.multiple_of(s * width, width), width)]

    def own_features(t, _):
        r = pl.ds(pl.multiple_of(t * TL, TL), TL)
        X[r, :] = toks[lax.div(s, per), t, :, mine]
        G[r, :] = ogs[lax.div(s, per), t, :, mine]
        drive[r, :] = step[r, :] * act[r, :].astype(F32)
        keep[r, :] = jnp.broadcast_to(aux[r, 6:7], (TL, C))
        return 0

    lax.fori_loop(0, S, own_features, 0)
    INV[...] = jnp.broadcast_to(inv, INV.shape)
    scan_backward(
        pre, H, dmix, act, bct, aux, ch, wdt, low,
        dlow, dbct, gdt, gch, dact, step, drive, keep, DS, DB, dst3, low3, dst,
        [],
    )
    h = R // S
    part_dt = lambda d: gdt.at[:, pl.ds(pl.multiple_of(d * h, 8), h), :]
    more = row_copies(S, part_dt, lambda t: MORE.at[t], mx, mr)
    more_own = pltpu.make_async_copy(part_dt(s), MORE.at[s], ml)
    for cp in more + [more_own]:
        cp.start()
    sum_over_all(
        S, PN, dlow, dbct, LR2, BCT2, *sums,
        between=(lambda: gathers[0].start_from(3), lambda: gathers[1].start(0, 1)),
    )
    gathers[1].start(2)
    gathers[0].forward(1)
    gathers[0].forward(2)
    convolve_backward(
        LR2, BCT2, act, conv, aux, ch, wxT, dact, dinner, gx, gtap, pad, tail, act3, dpar
    )
    gathers[1].start_from(3)
    gathers[2].start_from(0)
    for cp in more + [more_own]:
        cp.wait()
    gathers[0].forward_from(3)
    gathers[1].forward(1)
    gathers[0].finish()

    large = 512

    def layer(i, _):
        r = pl.ds(pl.multiple_of(i * large, large), large)

        total = jnp.zeros((large, width), F32)
        for m in range(M):
            w = jnp.concatenate([wo[b, m * C : (m + 1) * C, :] for b in range(S)], axis=0)
            total = total + dot(gall[r, :], w) * aux[r, m : m + 1]
        part[0, r, :] = total.astype(BF16)
        return 0

    lax.fori_loop(0, T // large, layer, 0)
    stream = Stream(H, load, (w_out, m_out, s_out), 6, sums_ref.at[1])
    stream.start(0)

    def out_gradient(i, rows_of):
        m, k = i // 2, i % 2
        wide = gall[:, k * (S // 2) * C : (k + 1) * (S // 2) * C].astype(F32)
        turned[...] = jnp.transpose((wide * aux[0:T, m : m + 1]).astype(BF16))
        g = dot(turned[...], G[...])
        parts = [
            g[:, t * LANES : (t + 1) * LANES].reshape(-1, 8, LANES) for t in range(tiles)
        ]
        H[rows_of, :] = jnp.stack(parts, axis=1).reshape(-1, LANES)

    to_out = LastBlocks(
        S, PN, part.at[0], LO, pair.at[0], pair.at[1], last[0], last[1], swaps.at[0], ls.at[1]
    )
    to_out.start()
    gathers[1].forward(2)
    stores = [None, None]
    for i in range(6):
        k = i % 2
        if stores[k] is not None:
            stores[k].wait()
        rows_of = pl.ds((6 + k) * 1024, 1024)
        out_gradient(i, rows_of)
        stores[k] = pltpu.make_async_copy(
            H.at[rows_of], g_out.at[i * 1024 : (i + 1) * 1024], store.at[k]
        )
        stores[k].start()
        stream.norms(i, i // 2, (6 + k) * 1024)
        if i == 1:
            gathers[1].forward_from(3)
        elif i == 3:
            gathers[2].forward(1)
        elif i == 4:
            gathers[2].forward(2)
    gathers[2].forward_from(3)
    for cp in stores:
        cp.wait()
    stream = Stream(H, load, (w_in, m_in, s_in), 12, sums_ref.at[0])
    stream.start(0)
    gathers[1].finish()
    gathers[2].finish()

    def normed_back(i, total):
        r = pl.ds(pl.multiple_of(i * large, large), large)

        d = jnp.zeros((large, width), F32)
        for m in range(M):
            cols = slice(m * C, (m + 1) * C)
            w = jnp.concatenate([v[b, :, cols] for b in range(S) for v in (wi, wg)], axis=1)
            d = d + dot(dall[r, :], w, NT) * aux[r, m : m + 1]
        scaled = X[r, :].astype(F32) * aux[r, 7:8]
        gained = d * gain_mine[0:1, :]
        part[1, r, :] = gained.astype(BF16)
        along = jnp.sum(gained * scaled, axis=1, keepdims=True)
        for j in range(large // TL):
            turned = jnp.transpose(jnp.broadcast_to(along[j * TL : (j + 1) * TL], (TL, LANES)))
            rowdot[i * (large // TL) + j] = turned[0:8]
        return total + jnp.sum(d * scaled, axis=0, keepdims=True)

    total = lax.fori_loop(0, T // large, normed_back, jnp.zeros((1, width), F32))
    ggs[...] = jnp.broadcast_to(total, ggs.shape)
    to_in = LastBlocks(
        S, PN, part.at[1], DN, pair.at[2], pair.at[3], last[2], last[3], swaps.at[1], ls.at[3]
    )
    to_in.start()
    gains = [
        seq_copy(ggs, GG.at[k], last[4].at[k], last[5].at[k], {"tp": lax.rem(p + k, PN)})
        for k in range(1, PN)
    ]
    for cp in gains:
        cp.start()
    n = S * PN
    me = s * PN + p

    def to_all(src, dst, send, recv):
        def copy(k):
            j = lax.rem(me + k, n)
            device = {"seq": lax.div(j, PN), "tp": lax.rem(j, PN)}
            return seq_copy(src(lax.div(j, PN)), dst.at[k], send.at[k], recv.at[k], device)

        def start(k, _):
            copy(k).start()
            return 0

        def wait(k, _):
            copy(k).wait()
            return 0

        return (
            lambda: lax.fori_loop(1, n, start, 0),
            lambda: lax.fori_loop(1, n, wait, 0),
        )

    send_row, wait_row = to_all(lambda t: rowdot.at[t], ROW, last[6], last[7])
    send_row()
    GG[0] = ggs[...]
    ROW[0] = rowdot[s]

    stores = [None, None]
    per_m = width * stride
    for m in range(M):
        k = m % 2
        if stores[k] is not None:
            stores[k].wait()
        first_row = 6 * 1024 + k * per_m
        turned[0:width, :] = jnp.transpose(
            (NR[...].astype(F32) * aux[0:T, m : m + 1]).astype(BF16)
        )
        for b in range(S):
            g = dot(turned[0:width, :], dall[:, 2 * b * C : 2 * (b + 1) * C])
            H[pl.ds(first_row + 2 * b, width, stride=stride), :] = g[:, 0:C]
            H[pl.ds(first_row + 2 * b + 1, width, stride=stride), :] = g[:, C : 2 * C]
        stores[k] = pltpu.make_async_copy(
            H.at[first_row : first_row + per_m], g_in.at[m * per_m : (m + 1) * per_m], store.at[k]
        )
        stores[k].start()
        for q in range(per_m // 1024):
            stream.norms(m * (per_m // 1024) + q, m, first_row + q * 1024)
    lane = lax.broadcasted_iota(jnp.int32, (8, LANES), 1)
    total = jnp.zeros((8, LANES), F32)
    square = lambda v: jnp.sum(v * v)
    for t in range(S):
        gdt_mine[:, :, t * C : (t + 1) * C] = MORE[t]
    for m in range(M):
        x = adam_terms(gx[m], m_x[m], s_x[m])[2] + WEIGHT_DECAY * w_x[m]
        d = adam_terms(gdt_mine[m], m_dt[m], s_dt[m])[2] + WEIGHT_DECAY * w_dt[m]
        for k, value in enumerate((
            jnp.sum(sums_ref[0, m, 0]), square(w_x[m]), square(w_dt[m]), jnp.sum(sums_ref[1, m, 0]),
            jnp.sum(sums_ref[0, m, 1]), square(x), square(d), jnp.sum(sums_ref[1, m, 1]),
        )):
            total = jnp.where(lane == k * M + m, value, total)
    total_tile[...] = total
    send_tile, wait_tile = to_all(lambda t: total_tile, TILE, last[8], last[9])
    send_tile()
    TILE[0] = total
    for cp in gains:
        cp.wait()
    wait_row()
    wait_tile()
    total = jnp.sum(TILE[...], axis=0)
    below = pltpu.roll(total, LANES - 4 * M, 1)
    SCALE[...] = MATRIX_RATE * (jnp.sqrt(total) / jnp.sqrt(below))
    for cp in stores:
        cp.wait()
    to_out.finish()
    to_in.finish()


class Stream:
    def __init__(self, H, sems, refs, steps, sums):
        self.H, self.sems, self.refs, self.steps, self.sums = H, sems, refs, steps, sums
        sums[...] = jnp.zeros(sums.shape, F32)

    def copies(self, i):
        k = i % 2
        return [
            pltpu.make_async_copy(
                ref.at[i * 1024 : (i + 1) * 1024],
                self.H.at[pl.ds((3 * k + a) * 1024, 1024)],
                self.sems.at[k, a],
            )
            for a, ref in enumerate(self.refs)
        ]

    def start(self, i):
        for cp in self.copies(i):
            cp.start()

    def norms(self, i, m, g_row):
        for cp in self.copies(i):
            cp.wait()
        if i + 1 < self.steps:
            self.start(i + 1)
        H, k, rows = self.H, i % 2, 128

        def body(t, sums):
            at = lambda first: pl.ds(pl.multiple_of(first + t * rows, rows), rows)
            weight = H[at(3 * k * 1024), :]
            ratio = adam_terms(
                H[at(g_row), :], H[at((3 * k + 1) * 1024), :], H[at((3 * k + 2) * 1024), :]
            )[2]
            direction = ratio + WEIGHT_DECAY * weight
            fold = lambda v: jnp.sum((v * v).reshape(rows // 8, 8, LANES), axis=0)
            return sums[0] + fold(weight), sums[1] + fold(direction)

        a, b = lax.fori_loop(0, 1024 // rows, body, (self.sums[m, 0], self.sums[m, 1]))
        self.sums[m, 0] = a
        self.sums[m, 1] = b


class LastBlocks:
    def __init__(self, S, PN, part, out, other, both, send, recv, swap, ls):
        s, p = lax.axis_index("seq"), lax.axis_index("tp")
        ratio = S // PN
        self.S, self.PN, self.ratio = S, PN, ratio
        self.s, self.p, self.home = s, p, lax.div(s, ratio)
        self.y, self.c = lax.div(p, 2), lax.rem(p, 2)
        self.slot = lax.rem(s, ratio) * (PN // 2) + self.y
        self.part, self.out, self.other, self.both = part, out, other, both
        self.send, self.recv, self.ls = send, recv, ls
        self.half = part.shape[0] // 2
        self.TL = part.shape[0] // S
        self.swap = seq_copy(
            part.at[self.rows(1 - self.c)],
            other,
            swap.at[0],
            swap.at[1],
            {"tp": p + 1 - 2 * self.c},
        )

    def rows(self, c):
        return pl.ds(pl.multiple_of(c * self.half, self.half), self.half)

    def seq(self, k):
        return self.c * (self.S // 2) + k

    def away(self, k):
        return jnp.logical_or(self.s != self.seq(k), self.home != self.p)

    def copy(self, k):
        return seq_copy(
            self.both.at[k * self.TL : (k + 1) * self.TL],
            self.out.at[self.slot],
            self.send.at[k],
            self.recv.at[self.slot],
            {"seq": self.seq(k), "tp": self.home},
        )

    def own(self, k):
        return pltpu.make_async_copy(
            self.both.at[k * self.TL : (k + 1) * self.TL], self.out.at[self.slot], self.ls
        )

    def start(self):
        self.swap.start()
        self.swap.wait()
        mine = self.part[self.rows(self.c), :].astype(F32)
        self.both[...] = (mine + self.other[...].astype(F32)).astype(BF16)
        for k in range(self.S // 2):

            @pl.when(self.away(k))
            def _():
                self.copy(k).start()

            @pl.when(jnp.logical_not(self.away(k)))
            def _():
                self.own(k).start()

    def finish(self):
        for k in range(self.S // 2):

            @pl.when(self.away(k))
            def _():
                self.copy(k).wait_send()

            @pl.when(jnp.logical_not(self.away(k)))
            def _():
                self.own(k).wait()

        core = lax.div(self.s, self.S // 2)
        for h in range(self.ratio):
            for y in range(self.PN // 2):
                t, q = self.ratio * self.p + h, 2 * y + core
                i = h * (self.PN // 2) + y

                @pl.when(jnp.logical_or(t != self.s, self.p != q))
                def _():
                    seq_copy(
                        self.both.at[0 : self.TL],
                        self.out.at[i],
                        self.send.at[0],
                        self.recv.at[i],
                        {"seq": t, "tp": q},
                    ).wait_recv()


def scan_forward(T, C, bct, ch, step, drive, keep, H, Y):
    base = -jnp.exp(ch[K + 2 + M : K + 2 + M + N, :])
    H[0:N, :] = jnp.zeros((N, C), F32)

    def chunk(c, h):
        cols = bct[c]
        for i in range(LANES // 8):
            t0 = pl.multiple_of(c * LANES + 8 * i, 8)
            r = pl.ds(t0, 8)
            st, dr, kp = step[r, :], drive[r, :], keep[r, :]
            ys = []
            for j in range(8):
                k = 8 * i + j
                rate = jnp.exp(st[j : j + 1] * base) * kp[j : j + 1]
                h = rate * h + dr[j : j + 1] * cols[0:N, k : k + 1]
                H[pl.ds(pl.multiple_of((t0 + j + 1) * N, N), N), :] = h
                ys.append(jnp.sum(cols[N : 2 * N, k : k + 1] * h, axis=0, keepdims=True))
            Y[r, :] = jnp.concatenate(ys, axis=0)
        return h

    lax.fori_loop(0, T // LANES, chunk, jnp.zeros((N, C), F32))


def lane_sums(values):
    v = jnp.concatenate(values, axis=0)
    high = v.astype(BF16)
    low = (v - high.astype(F32)).astype(BF16)
    sums = dot(jnp.concatenate([high, low], axis=1), jnp.ones((2 * v.shape[1], LANES), BF16))
    return [sums[k * N : (k + 1) * N] for k in range(len(values))]


def scan_backward(
    pre, H, dmix, act, bct, aux, ch, wdt, low,
    dlow, dbct, gdt, gch, dact, step, drive, keep, DS, DB, dst3, low3, dst, hooks,
):
    T, C = act.shape
    rows = 128

    base = -jnp.exp(ch[K + 2 + M : K + 2 + M + N, :])
    lane = lax.broadcasted_iota(jnp.int32, (N, LANES), 1)
    nothing = jnp.zeros((N, C), F32)
    chunks = T // LANES

    def chunk(cc, carry):
        c = chunks - 1 - cc
        cols = bct[c]
        flow, hcur, gacc = carry
        accb = accc = jnp.zeros((N, LANES), F32)
        for i in reversed(range(LANES // 8)):
            t0 = pl.multiple_of(c * LANES + 8 * i, 8)
            r = pl.ds(t0, 8)
            st, dr, kp, dm = step[r, :], drive[r, :], keep[r, :], dmix[r, :]
            ds, db, ub, uc = [None] * 8, [None] * 8, [None] * 8, [None] * 8
            for j in reversed(range(8)):
                k = 8 * i + j
                back = cols[N : 2 * N, k : k + 1] * dm[j : j + 1] + flow
                rate = jnp.exp(st[j : j + 1] * base) * kp[j : j + 1]
                hprev = H[pl.ds(pl.multiple_of((t0 + j) * N, N), N), :]
                uc[j] = dm[j : j + 1] * hcur
                ub[j] = back * dr[j : j + 1]
                flow = rate * back
                dlog = flow * hprev
                gacc = gacc + dlog * st[j : j + 1]
                ds[j] = jnp.sum(dlog * base, axis=0, keepdims=True)
                db[j] = jnp.sum(back * cols[0:N, k : k + 1], axis=0, keepdims=True)
                hcur = hprev
            DS[r, :] = jnp.concatenate(ds, axis=0)
            DB[r, :] = jnp.concatenate(db, axis=0)
            sb, sc = lane_sums(ub), lane_sums(uc)
            for j in range(8):
                here = lane == 8 * i + j
                accb = jnp.where(here, sb[j], accb)
                accc = jnp.where(here, sc[j], accc)
        dbct[c, 0:N, :] = accb
        dbct[c, N : 2 * N, :] = accc
        return flow, hcur, gacc

    carry, done = (nothing, H[T * N : (T + 1) * N, :], nothing), 0
    for upto, call in hooks + [(chunks, None)]:
        carry = lax.fori_loop(done, upto, chunk, carry)
        done = upto
        if call is not None:
            call()
    gacc = carry[2]

    def finish(i, carry):
        skip, bias = carry
        r = pl.ds(pl.multiple_of(i * rows, rows), rows)
        a = act[r, :].astype(F32)
        back_b = DB[r, :]
        grad = DS[r, :] + a * back_b
        d = (grad / (1.0 + jnp.exp(-pre[r, :]))).astype(BF16)
        dst[r, :] = d
        wide = d.astype(F32)
        sums = []
        for m in range(M):
            mask = aux[r, m : m + 1]
            masked = wide * mask
            sums.append(jnp.sum(masked, axis=0, keepdims=True))
            dst3[r, m * C : (m + 1) * C] = masked.astype(BF16)
        total = dot(dst3[r, 0:C], wdt[0:R, :], NT)
        for m in range(1, M):
            total = total + dot(dst3[r, m * C : (m + 1) * C], wdt[m * R : (m + 1) * R, :], NT)
        dlow[r, :] = total
        dact[r, :] = dmix[r, :] * ch[K + 1 : K + 2, :] + step[r, :] * back_b
        skip = skip + jnp.sum(dmix[r, :] * a, axis=0, keepdims=True)
        return skip, bias + jnp.concatenate(sums, axis=0)

    skip, bias = lax.fori_loop(
        0, T // rows, finish, (jnp.zeros((1, C), F32), jnp.zeros((M, C), F32))
    )
    gch[0:1, :] = skip
    gch[1 : 1 + M, :] = bias
    gch[1 + M : 1 + M + N, :] = base * gacc
    for m in range(M):
        gdt[m] = dot(low3[:, m * R : (m + 1) * R], dst[...], TN)


def convolve_backward(
    dlow, dbct, act, conv, aux, ch, wxT, dact, dinner, gx, gtap, pad, tail, act3, dpar,
):
    T, C = act.shape
    rows = 128
    tail[T : T + 8, :] = jnp.zeros((8, C), F32)
    blank = jnp.zeros((LANES - 2 * N, LANES), F32)

    def fill(i, _):
        r = pl.ds(pl.multiple_of(i * rows, rows), rows)
        turned = jnp.transpose(jnp.concatenate([dbct[i], blank], axis=0))
        dpar[r, 0:R] = dlow[r, :]
        dpar[r, R : R + 2 * N] = turned[:, 0 : 2 * N].astype(BF16)
        wide = dpar[r, :].astype(F32)
        total = dact[r, :]
        for m in range(M):
            mask = aux[r, m : m + 1]
            total = total + dot((wide * mask).astype(BF16), wxT[m])
        v = conv[r, :]
        sig = 1.0 / (1.0 + jnp.exp(-v))
        tail[r, :] = (total * (sig * (1.0 + v * (1.0 - sig)))).astype(BF16).astype(F32)
        return 0

    lax.fori_loop(0, T // rows, fill, 0)

    def body(i, sums):
        r = pl.ds(pl.multiple_of(i * rows, rows), rows)
        window = pad[pl.ds(pl.multiple_of(i * rows, rows), rows + 8), :]
        d = tail[r, :]
        ahead = tail[pl.ds(pl.multiple_of(i * rows, rows), rows + 8), :]
        same = aux[pl.ds(pl.multiple_of(i * rows, rows), rows + 8), :]
        total = ch[K - 1 : K, :] * d
        new = []
        for k in range(K):
            off = K - 1 - k
            shifted = window[8 - off : 8 - off + rows]
            if k < K - 1:
                shifted = shifted * aux[r, M + k : M + k + 1]
                total = total + ch[k : k + 1, :] * (
                    ahead[off : off + rows] * same[off : off + rows, M + k : M + k + 1]
                )
            new.append(jnp.sum(d * shifted, axis=0, keepdims=True))
        new.append(jnp.sum(d, axis=0, keepdims=True))
        dinner[r, :] = total.astype(BF16)
        return sums + jnp.concatenate(new, axis=0)

    gtap[0 : K + 1, :] = lax.fori_loop(0, T // rows, body, jnp.zeros((K + 1, C), F32))
    for m in range(M):
        gx[m] = dot(dpar[...], act3[:, m * C : (m + 1) * C], TN)


def block_call(S, PN, args, T, C, width):
    dma = pltpu.SemaphoreType.DMA
    TL, DD = args[0].shape
    chunks = T // LANES
    f = lambda *shape: sds(shape)
    b = lambda *shape: sds(shape, BF16)
    vf = lambda *shape: pltpu.VMEM(shape, F32)
    vb = lambda *shape: pltpu.VMEM(shape, BF16)
    n = S * PN
    out = (
        b(S // 2, TL, width), b(S // 2, TL, width), f(PN, 8, width), f(n, 8, LANES),
        f(S, M, R // S, C), f(M, R + 2 * N, C), f(8, C), f(1 + M + N, C),
        f(TL, LANES), f(8, LANES), f(M * width * 2 * S, C), f(M * S * width, C),
    )
    scratch = (
        [vf(8, TL), vb(PN, S, TL, DD // PN), vb(PN, S, TL, DD // PN), vb(T, DD)]
        + [vb(DD, M * C), vb(DD, M * C), vb(S, M * C, width), vf(S, 8, TL), vf(S, 8, width)]
        + [vb(S, M, R // S, C)]
        + [vf(T, C)] * 4
        + [vf(T + 8, C), vb(T, M * C), vf(T, R), vf(chunks, 2 * N, LANES)]
        + [vb(T, C), vf(T, C), vb(T, C), vb(T, R), vf(chunks, 2 * N, LANES), vf(T, C)]
        + [vf((T + 1) * N, C), vb(T, C), vb(T, C), vf(T, C), vf(T + 8, 8), vb(T, width)]
        + [vb(T, S * C), vb(T, 2 * S * C), vf(T, C), vf(T, C), vb(T, M * C), vb(T, M * R)]
        + [vb(T, C), vf(T, R), vf(chunks, 2 * N, LANES), vf(T, C), vf(M, R, C)]
        + [vb(T, R), vf(chunks, 2 * N, LANES), vf(T + 8, C), vb(T, R + 2 * N), vb(T, C)]
        + [vb(2, T, width), vf(S, 8, LANES), vf(8, width), vb(M * R, C)]
        + [vb(S, width, M * C), vb(S, width, M * C), vb(S, M * C, width), vb(M, R // S, S * C)]
        + [vf(8, width), vb(M * C, R), vb(2 * N, M * C), vb(M, R + 2 * N, C), vb(T, width)]
        + [vb(T, width), vf(M, R // S, S * C), vb(S * C // 2, T), vf(2, M, 2, 8, LANES)]
        + [vf(n, 8, LANES), vf(8, LANES), dma((2,)), dma((2, 3)), dma((2,))]
        + [vb(4, T // 2, width), dma((2, 2))]
        + Spread.semaphores(S) * 2
        + [dma((S,))] * 12
        + [dma((6,))]
        + sum_scratch(S, PN, T)
        + RowGather.semaphores(S) * 3
        + [dma((S,)), dma((S,)), dma]
        + [dma((S,))] * 4 + [dma((PN,))] * 2 + [dma((n,))] * 4
    )
    vm, hb = pl.BlockSpec(memory_space=pltpu.VMEM), pl.BlockSpec(memory_space=pl.ANY)
    return pl.pallas_call(
        functools.partial(block_kernel, S, PN),
        out_shape=out,
        in_specs=[vm] * (len(args) - 6) + [hb] * 6,
        out_specs=[vm] * (len(out) - 2) + [hb] * 2,
        scratch_shapes=scratch,
        compiler_params=pltpu.CompilerParams(
            collective_id=0, has_side_effects=True, vmem_limit_bytes=VMEM_LIMIT
        ),
    )(*args)


def update_kernel(steps, scale, g, w, m, s, avg, nw, nm, ns, na, which):
    k = lax.div(pl.program_id(0), steps)
    factor = scale[0:1, M * which : M * which + 1]
    for i in range(1, M):
        lane = M * which + i
        factor = jnp.where(k == i, scale[0:1, lane : lane + 1], factor)
    rows = 256

    def body(t, _):
        r = pl.ds(pl.multiple_of(t * rows, rows), rows)
        weight = w[r, :]
        new_m, new_s, ratio = adam_terms(g[r, :], m[r, :], s[r, :])
        new = weight - factor * (ratio + WEIGHT_DECAY * weight)
        nw[r, :] = new
        nm[r, :] = new_m
        ns[r, :] = new_s
        na[r, :] = AVERAGE_KEEP * avg[r, :] + (1.0 - AVERAGE_KEEP) * new
        return 0

    lax.fori_loop(0, w.shape[0] // rows, body, 0)


def update(which, rows, scale, *arrays):
    total, C = arrays[0].shape
    block = pl.BlockSpec((rows, C), lambda i: (i, 0))

    def kernel(*refs):
        update_kernel(total // M // rows, *refs, which)

    return pl.pallas_call(
        kernel,
        out_shape=(sds((total, C)),) * 4,
        grid=(total // rows,),
        in_specs=[pl.BlockSpec((8, LANES), lambda i: (0, 0))] + [block] * 5,
        out_specs=[block] * 4,
        compiler_params=pltpu.CompilerParams(vmem_limit_bytes=VMEM_LIMIT),
    )(scale, *arrays)


def rest_kernel(
    S, PN, tok, og, LO, DN, ROW, INV, scale, gx, more, gtap, gch, GG, wx, mx, sx, ax, wd, md, sd, ad,
    ch, mc, sc, ac, gn, mg, sg, ag,
    layer, grad, nwx, nmx, nsx, nax, nwd, nmd, nsd, nad, nwc, nmc, nsc, nac, nwg, nmg, nsg, nag, gc, gd,
):
    p = lax.axis_index("tp")
    C = more.shape[3]
    width = LO.shape[2]
    out_width = og.shape[1]

    def average(old, new):
        return AVERAGE_KEEP * old + (1.0 - AVERAGE_KEEP) * new

    along = ROW[0, 0:1, :]
    for k in range(1, ROW.shape[0]):
        along = along + ROW[k, 0:1, :]
    column = jnp.transpose(jnp.broadcast_to(along, (LANES, LANES)))[:, 0:1]
    inv = INV[:, 0:1]
    for h in range(out_width // width):
        cols = pl.ds(pl.multiple_of(p * out_width + h * width, LANES), width)
        here = slice(h * width, (h + 1) * width)
        mine = tok[:, cols].astype(F32)
        chips = PN // 2
        total = LO[h * chips].astype(F32)
        back = DN[h * chips].astype(F32)
        for q in range(1, chips):
            total = total + LO[h * chips + q].astype(F32)
            back = back + DN[h * chips + q].astype(F32)
        layer[:, here] = mine + total
        grad[:, here] = og[:, here].astype(F32) + inv * (back - mine * inv * (column / D))
    for t in range(S):
        gd[:, :, t * C : (t + 1) * C] = more[t]
    for m in range(M):
        for k, g, w, mo, sq, av, nw, nm, ns, na in (
            (1, gx, wx, mx, sx, ax, nwx, nmx, nsx, nax),
            (2, gd, wd, md, sd, ad, nwd, nmd, nsd, nad),
        ):
            factor = scale[0:1, M * k + m : M * k + m + 1]
            new_m, new_s, ratio = adam_terms(g[m], mo[m], sq[m])
            new = w[m] - factor * (ratio + WEIGHT_DECAY * w[m])
            nw[m] = new
            nm[m] = new_m
            ns[m] = new_s
            na[m] = average(av[m], new)
    gc[0 : K + 1, :] = gtap[0 : K + 1, :]
    gc[K + 1 :, :] = gch[...]
    new_m, new_s, ratio = adam_terms(gc[...], mc[...], sc[...])
    new = ch[...] - CHANNEL_RATE * ratio
    nwc[...] = new
    nmc[...] = new_m
    nsc[...] = new_s
    nac[...] = average(ac[...], new)
    g = GG[0, 0:1, :]
    for q in range(1, PN):
        g = g + GG[q, 0:1, :]
    new_m, new_s, ratio = adam_terms(g, mg[...], sg[...])
    new = gn[...] - GAIN_RATE * ratio
    nwg[...] = new
    nmg[...] = new_m
    nsg[...] = new_s
    nag[...] = average(ag[...], new)


def to_rows(w, S):
    m, width, two, channels = w.shape
    c = channels // S
    return w.reshape(m, width, two, S, c).transpose(0, 1, 3, 2, 4).reshape(-1, c)


def from_rows(rows, S, shape):
    m, width, two, channels = shape
    c = channels // S
    return rows.reshape(m, width, S, two, c).transpose(0, 1, 3, 2, 4).reshape(shape)


def to_tiles(w):
    m, rows, columns = w.shape
    return w.reshape(m, rows // 8, 8, columns // LANES, LANES).transpose(0, 1, 3, 2, 4).reshape(
        -1, LANES
    )


def from_tiles(flat, shape):
    m, rows, columns = shape
    return flat.reshape(m, rows // 8, columns // LANES, 8, LANES).transpose(0, 1, 3, 2, 4).reshape(
        shape
    )


def local(
    tokens, out_grad, modality, segment,
    w_in, w_x, w_dt, w_out, channel, norm_gain,
    moment_in, moment_x, moment_dt, moment_out, moment_channel, moment_gain,
    square_in, square_x, square_dt, square_out, square_channel, square_gain,
    average_in, average_x, average_dt, average_out, average_channel, average_gain,
):
    S, PN = lax.axis_size("seq"), lax.axis_size("tp")
    TL = tokens.shape[0]
    T = S * TL
    width = D // S
    inner_width = w_out.shape[1]
    C = inner_width // S
    ins = [to_rows(v, S) for v in (w_in, moment_in, square_in, average_in)]
    outs = [to_tiles(v) for v in (w_out, moment_out, square_out, average_out)]
    modrow = jnp.broadcast_to(modality.astype(F32)[None], (8, TL))
    ahead = jnp.concatenate([jnp.full((K - 1,), -1, jnp.int32), segment])
    same = [(ahead[k : k + T] == segment).astype(F32) for k in range(K - 1)]
    zero = jnp.zeros((T,), F32)
    segs = jnp.stack([zero] * M + same + [same[K - 2], zero], axis=1)
    row = lambda v: v[None, :]
    xs = [jnp.transpose(v, (0, 2, 1)) for v in (w_x, moment_x, square_x, average_x)]
    LO, DN, GG, ROW, MORE, gx, gtap, gch, INV, scale, g_in, g_out = block_call(
        S,
        PN,
        (
            tokens, out_grad, modrow, row(norm_gain), segs, channel,
            *xs[:3], w_dt, moment_dt, square_dt, *ins[:3], *outs[:3],
        ),
        T, C, width,
    )
    new_in = [from_rows(v, S, w_in.shape) for v in update(0, 4096, scale, g_in, *ins)]
    new_out = [from_tiles(v, w_out.shape) for v in update(3, 1024, scale, g_out, *outs)]
    like = lambda v: sds(v.shape)
    vec = sds((1, width))
    rest = local_call(
        functools.partial(rest_kernel, S, PN),
        (sds(out_grad.shape),) * 2 + (like(xs[0]),) * 4 + (like(w_dt),) * 4 + (like(channel),) * 4
        + (vec,) * 4,
        28,
        [pltpu.VMEM(channel.shape, F32), pltpu.VMEM(w_dt.shape, F32)],
    )(
        tokens, out_grad, LO, DN, ROW, INV, scale, gx, MORE, gtap, gch, GG,
        *xs, w_dt, moment_dt, square_dt, average_dt,
        channel, moment_channel, square_channel, average_channel,
        row(norm_gain), row(moment_gain), row(square_gain), row(average_gain),
    )
    new_x, new_dt, new_ch, new_g = [rest[2 + 4 * k : 6 + 4 * k] for k in range(4)]
    new_x = [jnp.transpose(v, (0, 2, 1)) for v in new_x]
    groups = [(new_in[k], new_x[k], new_dt[k], new_out[k], new_ch[k], new_g[k][0]) for k in range(4)]
    return (*rest[:2], *groups[0], *groups[1], *groups[2], *groups[3])


def channels_fit(mesh):
    S, PN = mesh.shape["seq"], mesh.shape["tp"]
    n = S * PN
    return PN == 4 and S % 4 == 0 and (2 * N) % n == 0 and D * 2 // n == LANES


def solution(mesh):
    placed = (
        P("seq", None),
        P("seq", "tp"),
        P("seq"),
        P(),
        P(None, "seq", None, "tp"),
        P(None, ("tp", "seq"), None),
        P(None, "seq", "tp"),
        P(None, "tp", "seq"),
        P(None, ("tp", "seq")),
        P("seq"),
        P(None, "seq", None, "tp"),
        P(None, ("tp", "seq"), None),
        P(None, "seq", "tp"),
        P(None, "tp", "seq"),
        P(None, ("tp", "seq")),
        P("seq"),
        P(None, "seq", None, "tp"),
        P(None, ("tp", "seq"), None),
        P(None, "seq", "tp"),
        P(None, "tp", "seq"),
        P(None, ("tp", "seq")),
        P("seq"),
        P(None, "seq", None, "tp"),
        P(None, ("tp", "seq"), None),
        P(None, "seq", "tp"),
        P(None, "tp", "seq"),
        P(None, ("tp", "seq")),
        P("seq"),
    )
    return jax.shard_map(
        local if channels_fit(mesh) else generic_local,
        mesh=mesh,
        in_specs=placed,
        out_specs=(
            P("seq", "tp"),
            P("seq", "tp"),
            P(None, "seq", None, "tp"),
            P(None, ("tp", "seq"), None),
            P(None, "seq", "tp"),
            P(None, "tp", "seq"),
            P(None, ("tp", "seq")),
            P("seq"),
            P(None, "seq", None, "tp"),
            P(None, ("tp", "seq"), None),
            P(None, "seq", "tp"),
            P(None, "tp", "seq"),
            P(None, ("tp", "seq")),
            P("seq"),
            P(None, "seq", None, "tp"),
            P(None, ("tp", "seq"), None),
            P(None, "seq", "tp"),
            P(None, "tp", "seq"),
            P(None, ("tp", "seq")),
            P("seq"),
            P(None, "seq", None, "tp"),
            P(None, ("tp", "seq"), None),
            P(None, "seq", "tp"),
            P(None, "tp", "seq"),
            P(None, ("tp", "seq")),
            P("seq"),
        ),
        check_vma=False,
    )
```

```python
import functools

import jax
import jax.numpy as jnp
from jax import lax
from jax.experimental import pallas as pl
from jax.experimental.pallas import tpu as pltpu
from jax.sharding import PartitionSpec as P

D = 2048
R = 128
N = 16
K = 4
M = 3
STEP = 10


EPSILON = 1e-05
BETA_ONE = 0.9
BETA_TWO = 0.999
ADAM_EPSILON = 1e-06
WEIGHT_DECAY = 0.01
MATRIX_RATE = 0.25
CHANNEL_RATE = 0.7
GAIN_RATE = 0.35
AVERAGE_KEEP = 0.8
PRECISE = lax.Precision.HIGHEST


def passed_along(value, axis, steps):
    count = lax.axis_size(axis)
    leading, last = (max(0, -steps), min(count, count - steps))
    return lax.ppermute(value, axis, [(source, source + steps) for source in range(leading, last)])


def prefix(x, axis, combine, identity, reverse):
    devices, place = (lax.axis_size(axis), lax.axis_index(axis))
    everything = jax.tree.map(lambda part: lax.all_gather(part, axis), x)
    start = jax.tree.map(
        lambda part, zero: jnp.broadcast_to(jnp.asarray(zero, part.dtype), part.shape), x, identity
    )

    def lap(k, before):
        at = devices - 1 - k if reverse else k
        reached = at > place if reverse else at < place
        new = combine(before, jax.tree.map(lambda part: part[at], everything))
        return jax.tree.map(lambda a, b: jnp.where(reached, a, b), new, before)

    return lax.fori_loop(0, devices, lap, start)


def silu_grad(operand):
    sigmoid_of = jax.nn.sigmoid(operand)
    return sigmoid_of * (1.0 + operand * (1.0 - sigmoid_of))


def combine(earlier, following):
    return (earlier[0] * following[0], following[0] * earlier[1] + following[1])


def masked_dot(mask_cols, operand, stacked):
    running = mask_cols[:, 0:1] * jnp.dot(operand, stacked[0], preferred_element_type=jnp.float32)
    for modal_index in range(1, M):
        running = running + mask_cols[:, modal_index : modal_index + 1] * jnp.dot(
            operand, stacked[modal_index], preferred_element_type=jnp.float32
        )
    return running


def masked_back(mask_cols, operand, stacked):
    contract = (((1,), (1,)), ((), ()))
    running = mask_cols[:, 0:1] * lax.dot_general(
        operand, stacked[0], contract, preferred_element_type=jnp.float32
    )
    for modal_index in range(1, M):
        running = running + mask_cols[:, modal_index : modal_index + 1] * lax.dot_general(
            operand, stacked[modal_index], contract, preferred_element_type=jnp.float32
        )
    return running


def masked_outer(mask_low, operand, cotangent):
    contract = (((0,), (0,)), ((), ()))
    return jnp.stack(
        [
            lax.dot_general(
                operand * mask_low[:, modal_index : modal_index + 1],
                cotangent,
                contract,
                preferred_element_type=jnp.float32,
            )
            for modal_index in range(M)
        ]
    )


def adam_parts(gradient, moment, square):
    moment_new = BETA_ONE * moment + (1.0 - BETA_ONE) * gradient
    square_new = BETA_TWO * square + (1.0 - BETA_TWO) * gradient * gradient
    adam_ratio = (
        moment_new
        / (1.0 - BETA_ONE**STEP)
        / (jnp.sqrt(square_new / (1.0 - BETA_TWO**STEP)) + ADAM_EPSILON)
    )
    return (moment_new, square_new, adam_ratio)


def generic_local(
    tokens,
    out_grad,
    modality,
    segment,
    w_in,
    w_x,
    w_dt,
    w_out,
    channel,
    norm_gain,
    moment_in,
    moment_x,
    moment_dt,
    moment_out,
    moment_channel,
    moment_gain,
    square_in,
    square_x,
    square_dt,
    square_out,
    square_channel,
    square_gain,
    average_in,
    average_x,
    average_dt,
    average_out,
    average_channel,
    average_gain,
):
    tok_local = tokens.shape[0]
    width_tp = out_grad.shape[1]
    lowered = (
        w_in.astype(jnp.bfloat16),
        w_x.astype(jnp.bfloat16),
        w_dt.astype(jnp.bfloat16),
        w_out.astype(jnp.bfloat16),
    )
    stack_in, stack_x, stack_dt, stack_out = (
        lax.all_gather(lowered[0], "seq", axis=1, tiled=True),
        lax.all_gather(lowered[1], "seq", axis=1, tiled=True),
        lax.all_gather(lowered[2], "seq", axis=1, tiled=True),
        lax.all_gather(lowered[3], "seq", axis=2, tiled=True),
    )
    chan_full, gain_full = (
        lax.all_gather(channel, "seq", axis=1, tiled=True),
        lax.all_gather(norm_gain, "seq", axis=0, tiled=True),
    )
    inner_width = stack_out.shape[1]
    in_flat = stack_in.reshape(M, D, 2 * inner_width)
    seq_index = lax.axis_index("seq")
    tp_index = lax.axis_index("tp")
    start_row = seq_index * tok_local
    seg_local = lax.dynamic_slice(segment, (start_row,), (tok_local,))
    seg_before = lax.dynamic_slice(
        jnp.concatenate([jnp.full((K - 1,), -1, jnp.int32), segment]),
        (start_row,),
        (tok_local + K - 1,),
    )
    seg_after = lax.dynamic_slice(
        jnp.concatenate([segment, jnp.full((K - 1,), -2, jnp.int32)]),
        (start_row,),
        (tok_local + K - 1,),
    )
    mask_cols = (modality[:, None] == jnp.arange(M, dtype=jnp.int32)[None, :]).astype(jnp.float32)
    mask_low = mask_cols.astype(jnp.bfloat16)
    tokens_wide = tokens.astype(jnp.float32)
    inv_root = lax.rsqrt(jnp.mean(tokens_wide * tokens_wide, axis=-1, keepdims=True) + EPSILON)
    scaled = tokens_wide * inv_root
    normed = (scaled * gain_full[None, :]).astype(jnp.bfloat16)
    projected = masked_dot(mask_cols, normed, in_flat)
    inner_act = projected[:, :inner_width].astype(jnp.bfloat16)
    gate_pre = projected[:, inner_width:]
    rim_rows = passed_along(inner_act[tok_local - (K - 1) :], "seq", 1)
    extended = jnp.concatenate([rim_rows, inner_act], axis=0).astype(jnp.float32)
    conv_pre = jnp.broadcast_to(chan_full[K][None, :], (tok_local, inner_width))
    same_docs = []
    for tap_index in range(K):
        same_doc = (seg_before[tap_index : tap_index + tok_local] == seg_local).astype(jnp.float32)[
            :, None
        ]
        same_docs.append(same_doc)
        conv_pre = (
            conv_pre
            + chan_full[tap_index][None, :] * extended[tap_index : tap_index + tok_local] * same_doc
        )
    activated = jax.nn.silu(conv_pre).astype(jnp.bfloat16)
    act_wide = activated.astype(jnp.float32)
    params_x = lax.psum(masked_dot(mask_cols, activated, stack_x), "tp")
    low_rank = params_x[:, :R].astype(jnp.bfloat16)
    input_b = params_x[:, R : R + N]
    output_c = params_x[:, R + N :]
    step_pre = masked_dot(mask_cols, low_rank, stack_dt) + jnp.dot(
        mask_cols, chan_full[K + 2 : K + 2 + M], precision=PRECISE
    )
    step_size = jax.nn.softplus(step_pre)
    decay_base = -jnp.exp(chan_full[K + 2 + M :])
    keep_flag = (seg_before[K - 2 : K - 2 + tok_local] == seg_local).astype(jnp.float32)
    decay_rate = jnp.exp(step_size[:, None, :] * decay_base[None]) * keep_flag[:, None, None]
    drive_term = (step_size * act_wide)[:, None, :] * input_b[:, :, None]
    decay_cum, local_state = lax.associative_scan(combine, (decay_rate, drive_term), axis=0)
    unit_pair = (jnp.ones_like(decay_base), jnp.zeros_like(decay_base))
    carry_in = prefix((decay_cum[-1], local_state[-1]), "seq", combine, unit_pair, False)[1]
    hidden_state = local_state + decay_cum * carry_in[None]
    mixed_out = (
        jnp.einsum("tn,tne->te", output_c, hidden_state, precision=PRECISE)
        + chan_full[K + 1][None, :] * act_wide
    )
    gate_act = jax.nn.silu(gate_pre)
    gated_out = (mixed_out * gate_act).astype(jnp.bfloat16)
    out_share = lax.psum_scatter(
        masked_dot(mask_cols, gated_out, stack_out), "tp", scatter_dimension=1, tiled=True
    )
    layer_out = lax.dynamic_slice_in_dim(tokens_wide, tp_index * width_tp, width_tp, 1) + out_share
    grad_full = lax.all_gather(out_grad, "tp", axis=1, tiled=True)
    d_gated = masked_back(mask_cols, grad_full, stack_out)
    grad_out = masked_outer(mask_low, gated_out, grad_full)
    d_mixed = d_gated * gate_act
    d_gate = d_gated * mixed_out * silu_grad(gate_pre)
    grad_skip = jnp.sum(d_mixed * act_wide, axis=0)
    d_out_c = jnp.einsum("te,tne->tn", d_mixed, hidden_state, precision=PRECISE)
    d_hidden = output_c[:, :, None] * d_mixed[:, None, :]
    decay_next = jnp.concatenate([decay_rate[1:], jnp.ones_like(decay_rate[:1])], axis=0)
    suffix_cum, local_back = lax.associative_scan(
        combine, (decay_next, d_hidden), reverse=True, axis=0
    )
    device_pair = (decay_rate[0] * suffix_cum[0], decay_rate[0] * local_back[0])
    carry_back = prefix(device_pair, "seq", combine, unit_pair, True)[1]
    back_state = local_back + suffix_cum * carry_back[None]
    state_prev = jnp.concatenate([carry_in[None], hidden_state[:-1]], axis=0)
    d_log = back_state * state_prev * decay_rate
    d_drive_sum = jnp.einsum("tne,tn->te", back_state, input_b, precision=PRECISE)
    d_step_size = jnp.sum(d_log * decay_base[None], axis=1) + act_wide * d_drive_sum
    grad_decay = decay_base * jnp.einsum("tne,te->ne", d_log, step_size, precision=PRECISE)
    d_in_b = jnp.einsum("tne,te->tn", back_state, step_size * act_wide, precision=PRECISE)
    d_step = (d_step_size * jax.nn.sigmoid(step_pre)).astype(jnp.bfloat16)
    d_step_wide = d_step.astype(jnp.float32)
    grad_bias = jnp.dot(mask_cols.T, d_step_wide, precision=PRECISE)
    grad_dt = masked_outer(mask_low, low_rank, d_step)
    d_low = masked_back(mask_cols, d_step, stack_dt)
    d_params = lax.psum(jnp.concatenate([d_low, d_in_b, d_out_c], axis=1), "tp").astype(
        jnp.bfloat16
    )
    grad_x = masked_outer(mask_low, activated, d_params)
    d_activ = (
        d_mixed * chan_full[K + 1][None, :]
        + step_size * d_drive_sum
        + masked_back(mask_cols, d_params, stack_x)
    )
    d_conv = (d_activ * silu_grad(conv_pre)).astype(jnp.bfloat16)
    rim_back = passed_along(d_conv[: K - 1], "seq", -1)
    d_conv_wide = d_conv.astype(jnp.float32)
    conv_after = jnp.concatenate([d_conv, rim_back], axis=0).astype(jnp.float32)
    d_inner = jnp.zeros((tok_local, inner_width), jnp.float32)
    grad_taps = []
    for tap_index in range(K):
        grad_taps.append(
            jnp.sum(
                d_conv_wide * extended[tap_index : tap_index + tok_local] * same_docs[tap_index],
                axis=0,
            )
        )
        offset = K - 1 - tap_index
        same_after = (seg_after[offset : offset + tok_local] == seg_local).astype(jnp.float32)[
            :, None
        ]
        d_inner = (
            d_inner
            + chan_full[tap_index][None, :] * conv_after[offset : offset + tok_local] * same_after
        )
    grad_conv_b = jnp.sum(d_conv_wide, axis=0)
    d_proj = jnp.concatenate([d_inner, d_gate], axis=1).astype(jnp.bfloat16)
    grad_in = masked_outer(mask_low, normed, d_proj).reshape(M, D, 2, inner_width)
    d_normed = lax.psum(masked_back(mask_cols, d_proj, in_flat), "tp")
    grad_gain = jnp.sum(d_normed * scaled, axis=0)
    d_scaled = d_normed * gain_full[None, :]
    d_tokens = inv_root * (d_scaled - scaled * jnp.mean(d_scaled * scaled, axis=-1, keepdims=True))
    tokens_grad = out_grad.astype(jnp.float32) + lax.dynamic_slice_in_dim(
        d_tokens, tp_index * width_tp, width_tp, 1
    )
    grad_channel = jnp.concatenate(
        [jnp.stack(grad_taps), grad_conv_b[None], grad_skip[None], grad_bias, grad_decay], axis=0
    )
    reduced = (
        lax.psum_scatter(grad_in, "seq", scatter_dimension=1, tiled=True),
        lax.psum_scatter(grad_x, "seq", scatter_dimension=1, tiled=True),
        lax.psum_scatter(grad_dt, "seq", scatter_dimension=1, tiled=True),
        lax.psum_scatter(grad_out, "seq", scatter_dimension=2, tiled=True),
        lax.psum_scatter(grad_channel, "seq", scatter_dimension=1, tiled=True),
        lax.psum_scatter(grad_gain, "seq", scatter_dimension=0, tiled=True),
    )
    weights = (w_in, w_x, w_dt, w_out, channel, norm_gain)
    moments = (moment_in, moment_x, moment_dt, moment_out, moment_channel, moment_gain)
    squares = (square_in, square_x, square_dt, square_out, square_channel, square_gain)
    averages = (average_in, average_x, average_dt, average_out, average_channel, average_gain)
    adam_all = [
        adam_parts(reduced[position], moments[position], squares[position]) for position in range(6)
    ]
    directions = [adam_all[position][2] + WEIGHT_DECAY * weights[position] for position in range(4)]
    weight_sums = jnp.stack(
        [
            jnp.sum(
                weights[position] * weights[position], axis=tuple(range(1, weights[position].ndim))
            )
            for position in range(4)
        ]
    )
    direction_sums = jnp.stack(
        [
            jnp.sum(
                directions[position] * directions[position],
                axis=tuple(range(1, directions[position].ndim)),
            )
            for position in range(4)
        ]
    )
    totals = lax.psum(jnp.stack([weight_sums, direction_sums]), ("seq", "tp"))
    trust_ratio = jnp.sqrt(totals[0]) / jnp.sqrt(totals[1])
    new_weights = []
    new_averages = []
    for position in range(6):
        weight = weights[position]
        if position < 4:
            updated = (
                weight
                - MATRIX_RATE
                * trust_ratio[position].reshape((M,) + (1,) * (weight.ndim - 1))
                * directions[position]
            )
        elif position == 4:
            updated = weight - CHANNEL_RATE * adam_all[position][2]
        else:
            updated = weight - GAIN_RATE * adam_all[position][2]
        new_weights.append(updated)
        new_averages.append(AVERAGE_KEEP * averages[position] + (1.0 - AVERAGE_KEEP) * updated)
    return (
        layer_out,
        tokens_grad,
        new_weights[0],
        new_weights[1],
        new_weights[2],
        new_weights[3],
        new_weights[4],
        new_weights[5],
        adam_all[0][0],
        adam_all[1][0],
        adam_all[2][0],
        adam_all[3][0],
        adam_all[4][0],
        adam_all[5][0],
        adam_all[0][1],
        adam_all[1][1],
        adam_all[2][1],
        adam_all[3][1],
        adam_all[4][1],
        adam_all[5][1],
        new_averages[0],
        new_averages[1],
        new_averages[2],
        new_averages[3],
        new_averages[4],
        new_averages[5],
    )


MESH = pl.DeviceIdType.MESH
VMEM_LIMIT = 62 * 1024 * 1024
LANES = 128
F32 = jnp.float32
BF16 = jnp.bfloat16
NT = (((1,), (1,)), ((), ()))
TN = (((0,), (0,)), ((), ()))


def dot(a, b, dims=(((1,), (0,)), ((), ()))):
    return lax.dot_general(a, b, dims, preferred_element_type=F32)


def local_call(kernel, out_shape, n_in, scratch=(), cost=None):
    return pl.pallas_call(
        kernel,
        out_shape=out_shape,
        in_specs=[pl.BlockSpec(memory_space=pltpu.VMEM)] * n_in,
        out_specs=jax.tree.map(lambda _: pl.BlockSpec(memory_space=pltpu.VMEM), out_shape),
        scratch_shapes=list(scratch),
        compiler_params=pltpu.CompilerParams(vmem_limit_bytes=VMEM_LIMIT),
        cost_estimate=cost,
    )


def remote_call(kernel, out_shape, n_in, scratch, ident):
    return pl.pallas_call(
        kernel,
        out_shape=out_shape,
        in_specs=[pl.BlockSpec(memory_space=pltpu.VMEM)] * n_in,
        out_specs=jax.tree.map(lambda _: pl.BlockSpec(memory_space=pltpu.VMEM), out_shape),
        scratch_shapes=list(scratch),
        compiler_params=pltpu.CompilerParams(
            collective_id=ident, has_side_effects=True, vmem_limit_bytes=VMEM_LIMIT
        ),
    )


def sds(shape, dtype=F32):
    return jax.ShapeDtypeStruct(shape, dtype)


def seq_copy(src, dst, send, recv, device):
    return pltpu.make_async_remote_copy(
        src_ref=src,
        dst_ref=dst,
        send_sem=send,
        recv_sem=recv,
        device_id=device,
        device_id_type=MESH,
    )


def place(S, PN):
    s, p = lax.axis_index("seq"), lax.axis_index("tp")
    return s, p, lax.div(s, 2), lax.rem(s, 2)


def greet_all(S, PN):
    s, p = lax.axis_index("seq"), lax.axis_index("tp")
    n = S * PN
    me = s * PN + p
    bar = pltpu.get_barrier_semaphore()

    def greet(k, _):
        j = lax.rem(me + k, n)
        pl.semaphore_signal(
            bar,
            inc=1,
            device_id={"seq": lax.div(j, PN), "tp": lax.rem(j, PN)},
            device_id_type=MESH,
        )
        return 0

    lax.fori_loop(1, n, greet, 0)
    pl.semaphore_wait(bar, n - 1)


class Spread:
    def __init__(self, S, PN, own, buf, zs, zr, xs, xr, ys, yr, cs, cr, ls):
        s, p, z, x = place(S, PN)
        self.zn = S // 2
        zn = self.zn
        other_x = {"seq": 2 * z + 1 - x}
        other_y = {"tp": lax.rem(p + 2, PN)}
        other_c = {"tp": p + 1 - 2 * lax.rem(p, 2)}

        def at(k, j):
            return 2 * lax.rem(z - k + zn, zn) + (x if j == 0 else 1 - x)

        self.local = pltpu.make_async_copy(own, buf.at[p, s], ls)
        self.z = [
            seq_copy(own, buf.at[p, s], zs.at[k], zr.at[k], {"seq": 2 * lax.rem(z + k, zn) + x})
            for k in range(1, zn)
        ]
        self.x = []
        self.y = {}
        for k in range(zn):
            src = own if k == 0 else buf.at[p, at(k, 0)]
            self.x.append(seq_copy(src, buf.at[p, at(k, 0)], xs.at[k], xr.at[k], other_x))
            for j in range(2):
                src = own if (k == 0 and j == 0) else buf.at[p, at(k, j)]
                self.y[k, j] = seq_copy(
                    src, buf.at[p, at(k, j)], ys.at[2 * k + j], yr.at[2 * k + j], other_y
                )
        q = lax.rem(p + 2, PN)
        self.c = [
            seq_copy(buf.at[p], buf.at[p], cs.at[0], cr.at[0], other_c),
            seq_copy(buf.at[q], buf.at[q], cs.at[1], cr.at[1], other_c),
        ]

    def start(self):
        self.local.start()
        for cp in self.z:
            cp.start()
        self.x[0].start()
        self.y[0, 0].start()

    def forward(self):
        for k in range(1, self.zn):
            self.z[k - 1].wait_recv()
            self.x[k].start()
            self.y[k, 0].start()
        for k in range(self.zn):
            self.x[k].wait_recv()
            self.y[k, 1].start()
        self.local.wait()
        self.c[0].start()

    def finish(self):
        for cp in self.y.values():
            cp.wait_recv()
        self.c[1].start()
        for cp in self.z + self.x + list(self.y.values()):
            cp.wait_send()
        for cp in self.c:
            cp.wait()

    @staticmethod
    def semaphores(S):
        dma = pltpu.SemaphoreType.DMA
        return [dma((S // 2,))] * 4 + [dma((S,))] * 2 + [dma((2,))] * 2 + [dma]


def row_copies(S, src, dst, send, recv):
    s = lax.axis_index("seq")
    out = []
    for k in range(1, S):
        d = lax.rem(s + k, S)
        out.append(seq_copy(src(d), dst(s), send.at[k], recv.at[k], {"seq": d}))
    return out


def sum_over_all(
    S, PN, lr, bct, LR, BCT, got_l, got_b, core_l, core_b,
    c1s, c1r, ssl, rsl, ssb, rsb, sgl, rgl, sgb, rgb, c2s, c2r, between=(),
):
    n = S * PN // 2
    s, p = lax.axis_index("seq"), lax.axis_index("tp")
    y, c = lax.div(p, 2), lax.rem(p, 2)
    me = s * (PN // 2) + y
    T = lr.shape[0]
    half, rows = T // 2, T // 2 // n
    chunks = bct.shape[0]
    per = n // (chunks // 2)
    high = bct.shape[1] // per
    twin = {"tp": p + 1 - 2 * c}

    def device(j):
        return {"seq": lax.div(j, PN // 2), "tp": 2 * lax.rem(j, PN // 2) + c}

    def half_l(k):
        return pl.ds(pl.multiple_of(k * half, half), half)

    def half_b(k):
        return pl.ds(k * (chunks // 2), chunks // 2)

    def rows_of(j):
        return pl.ds(pl.multiple_of(c * half + j * rows, rows), rows)

    def slab(ref, j):
        at = c * (chunks // 2) + lax.div(j, per)
        return ref.at[at, pl.ds(pl.multiple_of(lax.rem(j, per) * high, 8), high)]

    swap = [
        seq_copy(lr.at[half_l(1 - c)], core_l, c1s.at[0], c1r.at[0], twin),
        seq_copy(bct.at[half_b(1 - c)], core_b, c1s.at[1], c1r.at[1], twin),
    ]
    for cp in swap:
        cp.start()
    for cp in swap:
        cp.wait()
    lr[half_l(c), :] = lr[half_l(c), :] + core_l[...]
    bct[half_b(c)] = bct[half_b(c)] + core_b[...]

    def first(k):
        j = lax.rem(me + k, n)
        return (
            seq_copy(lr.at[rows_of(j)], got_l.at[k], ssl.at[k], rsl.at[k], device(j)),
            seq_copy(slab(bct, j), got_b.at[k], ssb.at[k], rsb.at[k], device(j)),
        )

    def second(k):
        j = lax.rem(me + k, n)
        mine_l, mine_b = LR.at[rows_of(me)], slab(BCT, me)
        return (
            seq_copy(mine_l, mine_l, sgl.at[k], rgl.at[k], device(j)),
            seq_copy(mine_b, mine_b, sgb.at[k], rgb.at[k], device(j)),
        )

    def start(copies, k):
        for cp in copies(k):
            cp.start()
        return 0

    def wait(copies, k):
        for cp in copies(k):
            cp.wait()
        return 0

    lax.fori_loop(1, n, lambda k, _: start(first, k), 0)
    for cp in between[0:1]:
        cp()
    got_l[0] = lr[rows_of(me), :]
    got_b[0] = slab(bct, me)[...]
    lax.fori_loop(1, n, lambda k, _: wait(first, k), 0)
    LR[rows_of(me), :] = jnp.sum(got_l[...], axis=0).astype(LR.dtype)
    slab(BCT, me)[...] = jnp.sum(got_b[...], axis=0)
    lax.fori_loop(1, n, lambda k, _: start(second, k), 0)
    for cp in between[1:2]:
        cp()
    lax.fori_loop(1, n, lambda k, _: wait(second, k), 0)
    swap = [
        seq_copy(LR.at[half_l(c)], LR.at[half_l(c)], c2s.at[0], c2r.at[0], twin),
        seq_copy(BCT.at[half_b(c)], BCT.at[half_b(c)], c2s.at[1], c2r.at[1], twin),
    ]
    for cp in swap:
        cp.start()
    for cp in swap:
        cp.wait()


def sum_scratch(S, PN, T):
    n = S * PN // 2
    dma = pltpu.SemaphoreType.DMA
    chunks = T // LANES
    slabs = chunks * N // n
    return (
        [pltpu.VMEM((n, T // 2 // n, R), F32), pltpu.VMEM((n, slabs, LANES), F32)]
        + [pltpu.VMEM((T // 2, R), F32), pltpu.VMEM((chunks // 2, 2 * N, LANES), F32)]
        + [dma((2,))] * 2 + [dma((n,))] * 8 + [dma((2,))] * 2
    )


class FeatureGather:
    def __init__(self, S, PN, own, buf, s1, r1, s2, r2, cs, cr, ys, yr, ls):
        s, p, z, x = place(S, PN)
        self.zn = zn = S // 2
        self.root = p == z
        self.relay = lax.rem(p + 2, PN) == z
        self.twin_of_root = p + 1 - 2 * lax.rem(p, 2) == z
        self.z = z
        self.moves = z != p
        self.local = pltpu.make_async_copy(own, buf.at[z, x], ls)
        self.first = seq_copy(own, buf.at[z, x], s1, r1.at[z], {"seq": 2 * p + x})
        self.arrive = [
            seq_copy(own, buf.at[t, x], s1, r1.at[t], {"seq": 2 * lax.rem(z + 1, zn) + x})
            for t in range(zn)
        ]
        halves = [buf.at[:, x], buf.at[:, 1 - x]]
        twin = {"tp": p + 1 - 2 * lax.rem(p, 2)}
        far = {"tp": lax.rem(p + 2, PN)}
        self.across = seq_copy(halves[0], halves[0], s2, r2, {"seq": 2 * z + 1 - x})
        self.core = [seq_copy(h, h, cs.at[j], cr.at[j], twin) for j, h in enumerate(halves)]
        self.y = [seq_copy(h, h, ys.at[j], yr.at[j], far) for j, h in enumerate(halves)]

    def start(self):
        @pl.when(self.moves)
        def _():
            self.first.start()

        @pl.when(jnp.logical_not(self.moves))
        def _():
            self.local.start()
            self.local.wait()

    def near(self):
        @pl.when(self.root)
        def _():
            for t in range(self.zn):

                @pl.when(self.z != t)
                def _():
                    self.arrive[t].wait_recv()

            self.across.start()
            self.core[0].start()
            self.y[0].start()

    def far(self):
        @pl.when(self.root)
        def _():
            self.across.wait_recv()
            self.core[1].start()
            self.y[1].start()

        self.pass_on(0)

    def pass_on(self, j):
        @pl.when(self.relay)
        def _():
            self.y[j].wait_recv()
            self.core[j].start()

    def finish(self):
        self.pass_on(1)

        @pl.when(self.moves)
        def _():
            self.first.wait_send()

        @pl.when(self.root)
        def _():
            self.across.wait_send()
            for cp in self.core + self.y:
                cp.wait_send()

        @pl.when(self.relay)
        def _():
            for cp in self.core:
                cp.wait_send()

        @pl.when(jnp.logical_not(jnp.logical_or(self.root, self.relay)))
        def _():
            for cp in self.core:
                cp.wait_recv()

    @staticmethod
    def semaphores(S):
        dma = pltpu.SemaphoreType.DMA
        return [dma, dma((S // 2,)), dma, dma] + [dma((2,))] * 4 + [dma]


class RowGather:
    PARTS = 2

    def __init__(self, S, own, place_of, us, ur, ds, dr, xs, xr, ls):
        s, p, z, x = place(S, 1)
        self.zn, self.z, self.x, self.own, self.place_of = S // 2, z, x, own, place_of
        self.up_sems, self.down_sems, self.x_sems = (us, ur), (ds, dr), (xs, xr)
        self.every = pl.ds(0, own.shape[0])
        self.local = pltpu.make_async_copy(own, place_of(self.every, s), ls)

    def hop(self, t, d, h, up, toward=1):
        size = self.own.shape[0] // self.PARTS
        r = pl.ds(h * size, size)
        there = self.place_of(r, 2 * t + self.x)
        send, recv = self.up_sems if up else self.down_sems
        chip = self.z + (toward if up else -toward)
        src = self.own.at[r] if d == 1 else there
        return seq_copy(src, there, send.at[d, h], recv.at[d, h], {"seq": 2 * chip + self.x})

    def across(self, t):
        block = self.place_of(self.every, 2 * t + self.x)
        send, recv = self.x_sems
        other = {"seq": 2 * self.z + 1 - self.x}
        return seq_copy(block, block, send.at[t], recv.at[t], other)

    def can(self, d, up):
        z, last = self.z, self.zn - 1
        if up:
            return jnp.logical_and(z >= d - 1, z < last)
        return jnp.logical_and(z + d - 1 <= last, z > 0)

    def start(self):
        self.local.start()
        for h in range(self.PARTS):
            for up in (True, False):

                @pl.when(self.can(1, up))
                def _():
                    self.hop(self.z, 1, h, up).start()

        self.local.wait()
        self.across(self.z).start()

    def step(self, d):
        if d >= self.zn:
            return
        for up in (True, False):
            t = self.z - d if up else self.z + d
            there = self.z >= d if up else self.z + d < self.zn

            @pl.when(there)
            def _():
                for h in range(self.PARTS):
                    self.hop(t, d, h, up, -1).wait_recv()
                    if d + 1 < self.zn:

                        @pl.when(self.can(d + 1, up))
                        def _():
                            self.hop(t, d + 1, h, up).start()

                self.across(t).start()

    def finish(self):
        for d in range(1, self.zn):
            for h in range(self.PARTS):
                for up in (True, False):

                    @pl.when(self.can(d, up))
                    def _():
                        t = self.z - (d - 1) if up else self.z + (d - 1)
                        self.hop(t, d, h, up).wait_send()

        for t in range(self.zn):
            self.across(t).wait()

    @staticmethod
    def semaphores(S):
        dma = pltpu.SemaphoreType.DMA
        return [dma((S // 2, RowGather.PARTS))] * 4 + [dma((S // 2,))] * 2 + [dma]


def adam_terms(g, m, s):
    new_m = BETA_ONE * m + (1.0 - BETA_ONE) * g
    new_s = BETA_TWO * s + (1.0 - BETA_TWO) * (g * g)
    root = jnp.sqrt(new_s * (1.0 / (1.0 - BETA_TWO**STEP))) + ADAM_EPSILON
    return new_m, new_s, (new_m * (1.0 / (1.0 - BETA_ONE**STEP))) / root


def softplus(v):
    u = jnp.exp(-jnp.abs(v))
    w = 1.0 + u
    small = jnp.where(w == 1.0, u, jnp.log(w) * (u / jnp.where(w == 1.0, 1.0, w - 1.0)))
    return jnp.maximum(v, 0.0) + small


def masked_sum(acc, aux, r, C):
    total = acc[:, 0:C] * aux[r, 0:1]
    for m in range(1, M):
        total = total + acc[:, m * C : (m + 1) * C] * aux[r, m : m + 1]
    return total


def block_kernel(S, PN, *refs):
    rest = list(refs)
    take = lambda k: [rest.pop(0) for _ in range(k)]
    tok, og, modrow, gain, segs, ch, w_x, m_x, s_x, w_dt, m_dt, s_dt = take(12)
    w_in, m_in, s_in, w_out, m_out, s_out = take(6)
    LO, DN, GG, ROW, MORE, gx, gtap, gch, INV, SCALE, g_in, g_out = take(12)
    tile, toks, ogz, nrm, Wi, Wg, Wo, AUX, GAIN, WD = take(10)
    gsend, grecv, osend, orecv = take(4)
    step, drive, keep, Y, pad, act3, lr, bcp = take(8)
    act, conv, inner, low, bct, pre, H, gated, dgate, dmix, aux, X = take(12)
    gall, dall, DS, DB, dst3, low3, dst, dlow, dbct, dact, gdt = take(11)
    LR2, BCT2, tail, dpar, dinner, part, rowdot, ggs, wdt = take(9)
    wi, wg, wo, wdt_mine, gain_mine, wlr, wbc, wxT, NR, G = take(10)
    gdt_mine, turned, sums_ref, TILE, total_tile = take(5)
    stage, load, store, pair, swaps = take(5)
    ag1, ag2 = take(9), take(9)
    parts_sems = take(4)
    ws = take(12)
    ls = take(1)[0]
    sums = take(16)
    rows_g, rows_d, rows_i = take(7), take(7), take(7)
    mx, mr, ml = take(3)
    last = take(10)
    s, p, z, x = place(S, PN)
    TL, DD = tok.shape
    T = S * TL
    width = DD // S
    quarter = DD // PN
    C = act.shape[1]
    rows = 128

    load_in = pltpu.make_async_copy(w_in, H.at[0 : w_in.shape[0]], stage.at[0])
    load_in.start()
    wide = tok[...].astype(F32)
    inv = lax.rsqrt(jnp.mean(wide * wide, axis=1, keepdims=True) + EPSILON)
    row = jnp.transpose(jnp.broadcast_to(inv, (TL, LANES)))[0:8]
    tile[...] = jnp.where(
        lax.broadcasted_iota(jnp.int32, row.shape, 0) == 0, modrow[...], row
    )
    gain_mine[...] = jnp.broadcast_to(gain[...], gain_mine.shape)
    wdt_mine[...] = w_dt[...].astype(BF16)
    greet_all(S, PN)
    chans = lambda d: pl.ds(pl.multiple_of(d * C, LANES), C)
    block = lambda d: pl.ds(pl.multiple_of(d * width, width), width)
    tokens = Spread(
        S, PN, tok.at[:, pl.ds(pl.multiple_of(p * quarter, LANES), quarter)], toks, *ag1
    )
    small = (
        row_copies(S, lambda d: tile, lambda t: AUX.at[t], ws[0], ws[1])
        + row_copies(S, lambda d: gain_mine, lambda t: GAIN.at[t], ws[2], ws[3])
    )
    dts = row_copies(S, lambda d: wdt_mine.at[:, :, chans(d)], lambda t: WD.at[t], ws[4], ws[5])
    inners = row_copies(S, lambda d: wi.at[d], lambda t: Wi.at[block(t)], ws[6], ws[7])
    zn = S // 2
    across = {"seq": 2 * z + 1 - x}
    pair_rows = pl.ds(pl.multiple_of(x * width, width), width)
    gate_swap = seq_copy(wg.at[:, 1 - x], Wg.at[:, pair_rows], ws[8].at[0], ws[9].at[0], across)
    out_swap = seq_copy(
        wo.at[:, 1 - x], Wo.at[:, :, pair_rows], ws[10].at[0], ws[11].at[0], across
    )

    def along(k, send, recv, sems):
        return seq_copy(
            send.at[k - 1],
            recv.at[k - 1],
            sems[0].at[k],
            sems[1].at[k],
            {"seq": 2 * lax.rem(z + k, zn) + x},
        )

    gates = [along(k, gsend, grecv, parts_sems[0:2]) for k in range(1, zn)]
    backs = [along(k, osend, orecv, parts_sems[2:4]) for k in range(1, zn)]
    cotangent = FeatureGather(S, PN, og, ogz, *ag2)
    for cp in small:
        cp.start()
    tokens.start()
    load_in.wait()
    stride = 2 * S
    for m in range(M):
        for b in range(S):
            r = pl.ds(m * width * stride + 2 * b, width, stride=stride)
            wi[b, :, m * C : (m + 1) * C] = H[r, :].astype(BF16)
    for cp in inners + dts:
        cp.start()
    cotangent.start()
    for m in range(M):
        for b in range(S):
            r = pl.ds(m * width * stride + 2 * b + 1, width, stride=stride)
            wg[b // 2, b % 2, :, m * C : (m + 1) * C] = H[r, :].astype(BF16)
    gate_swap.start()
    load_out = pltpu.make_async_copy(w_out, H.at[0 : w_out.shape[0]], stage.at[1])
    load_out.start()
    own = [
        pltpu.make_async_copy(tile, AUX.at[s], ls.at[0]),
        pltpu.make_async_copy(gain_mine, GAIN.at[s], ls.at[1]),
        pltpu.make_async_copy(wdt_mine.at[:, :, chans(s)], WD.at[s], ls.at[2]),
        pltpu.make_async_copy(wi.at[s], Wi.at[block(s)], ls.at[3]),
        pltpu.make_async_copy(wg.at[:, x], Wg.at[:, pair_rows], ls.at[4]),
    ]
    for cp in own:
        cp.start()
    for m in range(M):
        wlr[m * C : (m + 1) * C, :] = jnp.transpose(w_x[m, 0:R, :]).astype(BF16)
        wbc[:, m * C : (m + 1) * C] = w_x[m, R : R + 2 * N, :].astype(BF16)
        wxT[m] = w_x[m].astype(BF16)
    load_out.wait()
    tiles = width // LANES
    for m in range(M):
        for b in range(S):
            rows_b = H[(m * S + b) * C * tiles : (m * S + b + 1) * C * tiles, :]
            pieces = rows_b.reshape(C // 8, tiles, 8, LANES)
            for t in range(tiles):
                wo[b // 2, b % 2, m * C : (m + 1) * C, t * LANES : (t + 1) * LANES] = (
                    pieces[:, t].reshape(C, LANES).astype(BF16)
                )
    out_swap.start()
    own.append(pltpu.make_async_copy(wo.at[:, x], Wo.at[:, :, pair_rows], ls.at[5]))
    own[-1].start()
    for cp in own:
        cp.wait()
    tokens.forward()
    cotangent.near()
    for cp in small:
        cp.wait()
    lane = lax.broadcasted_iota(jnp.int32, (TL, 8), 1)

    def columns(t, _):
        r = pl.ds(pl.multiple_of(t * TL, TL), TL)
        turned = jnp.transpose(jnp.concatenate([AUX[t]] * (LANES // 8), axis=0))
        mask = (turned[:, 0:1] == lane.astype(F32)).astype(F32)
        aux[r, :] = jnp.where(
            lane < M, mask, jnp.where(lane == 7, turned[:, 1:2], segs[r, :])
        )
        return 0

    lax.fori_loop(0, S, columns, 0)
    aux[T : T + 8, :] = jnp.zeros((8, 8), F32)
    tokens.finish()
    per = quarter // width

    def norm(t, _):
        r = pl.ds(pl.multiple_of(t * TL, TL), TL)
        scale = aux[r, 7:8]
        for q in range(PN):
            scaled = toks[q, t].astype(F32) * scale
            for j in range(per):
                part = scaled[:, j * width : (j + 1) * width] * GAIN[q * per + j, 0:1, :]
                nrm[r, q * quarter + j * width : q * quarter + (j + 1) * width] = part.astype(BF16)
        return 0

    lax.fori_loop(0, S, norm, 0)
    for cp in inners:
        cp.wait()

    big = 256
    features = pl.ds(pl.multiple_of(z * 2 * width, 2 * width), 2 * width)

    def gate_part(k):
        def body(i, _):
            r = pl.ds(pl.multiple_of(i * big, big), big)
            w = Wg[lax.rem(z + k, zn)]
            value = masked_sum(dot(nrm[r, features], w), aux, r, C)
            if k == 0:
                DS[r, :] = value
            else:
                gsend[k - 1, r, :] = value.astype(BF16)
            return 0

        lax.fori_loop(0, T // big, body, 0)

    def back_part(k):
        def body(i, _):
            r = pl.ds(pl.multiple_of(i * big, big), big)
            w = Wo[lax.rem(z + k, zn)]
            chips = big // TL // 2
            g = ogz[pl.ds(i * chips, chips)].reshape(big, 2 * width)
            value = masked_sum(dot(g, w, NT), aux, r, C)
            if k == 0:
                DB[r, :] = value
            else:
                osend[k - 1, r, :] = value.astype(BF16)
            return 0

        lax.fori_loop(0, T // big, body, 0)

    pad[0:8, :] = jnp.zeros((8, C), F32)

    def first(i, _):
        r = pl.ds(pl.multiple_of(i * big, big), big)
        value = masked_sum(dot(nrm[r, :], Wi[...]), aux, r, C).astype(BF16)
        inner[r, :] = value
        pad[pl.ds(pl.multiple_of(i * big + 8, 8), big), :] = value.astype(F32)
        return 0

    lax.fori_loop(0, T // big, first, 0)

    def convolve(i, _):
        r = pl.ds(pl.multiple_of(i * rows, rows), rows)
        window = pad[pl.ds(pl.multiple_of(i * rows, rows), rows + 8), :]
        v = jnp.broadcast_to(ch[K : K + 1, :], (rows, C))
        for k in range(K):
            term = ch[k : k + 1, :] * window[8 - (K - 1) + k : 8 - (K - 1) + k + rows]
            v = v + (term * aux[r, M + k : M + k + 1] if k < K - 1 else term)
        conv[r, :] = v
        a = (v / (1.0 + jnp.exp(-v))).astype(BF16)
        act[r, :] = a
        a_wide = a.astype(F32)
        for m in range(M):
            act3[r, m * C : (m + 1) * C] = (a_wide * aux[r, m : m + 1]).astype(BF16)
        lr[r, :] = dot(act3[r, :], wlr[...])
        bcp[i] = dot(wbc[...], act3[r, :], NT)
        return 0

    lax.fori_loop(0, T // rows, convolve, 0)
    cotangent.far()

    def during_first():
        gate_swap.wait()
        gate_part(1)
        gates[0].start()
        gate_part(2)
        gates[1].start()
        gate_part(3)
        gate_part(0)

    def during_second():
        gates[2].start()
        cotangent.finish()
        out_swap.wait()
        back_part(1)
        backs[0].start()

    sum_over_all(
        S, PN, lr, bcp, low, bct, *sums, between=(during_first, during_second)
    )
    back_part(2)
    backs[1].start()
    back_part(3)
    backs[2].start()
    back_part(0)
    for cp in dts:
        cp.wait()
    for m in range(M):
        for t in range(S):
            h = R // S
            wdt[m * R + t * h : m * R + (t + 1) * h, :] = WD[t, m]

    def prepare(i, _):
        r = pl.ds(pl.multiple_of(i * rows, rows), rows)
        low_wide = low[r, :].astype(F32)
        bias = jnp.zeros((rows, C), F32)
        for m in range(M):
            mask = aux[r, m : m + 1]
            masked = (low_wide * mask).astype(BF16)
            bias = bias + mask * ch[K + 2 + m : K + 3 + m, :]
            low3[r, m * R : (m + 1) * R] = masked
        bias = bias + dot(low3[r, :], wdt[...])
        pre[r, :] = bias
        st = softplus(bias)
        step[r, :] = st
        drive[r, :] = st * act[r, :].astype(F32)
        keep[r, :] = jnp.broadcast_to(aux[r, 6:7], (rows, C))
        return 0

    lax.fori_loop(0, T // rows, prepare, 0)
    scan_forward(T, C, bct, ch, step, drive, keep, H, Y)
    for cp in gates + backs:
        cp.wait()

    def finish(i, _):
        r = pl.ds(pl.multiple_of(i * rows, rows), rows)
        mixed = Y[r, :] + ch[K + 1 : K + 2, :] * act[r, :].astype(F32)
        g, d = DS[r, :], DB[r, :]
        for k in range(zn - 1):
            g = g + grecv[k, r, :].astype(F32)
            d = d + orecv[k, r, :].astype(F32)
        sig = 1.0 / (1.0 + jnp.exp(-g))
        gated[r, :] = (mixed * (g * sig)).astype(BF16)
        dmix[r, :] = d * (g * sig)
        dgate[r, :] = (d * mixed * (sig * (1.0 + g * (1.0 - sig)))).astype(BF16)
        return 0

    lax.fori_loop(0, T // rows, finish, 0)
    half = lambda t, k: pl.ds(pl.multiple_of((2 * t + k) * C, LANES), C)
    gathers = [
        RowGather(S, gated, lambda r, t: gall.at[r, chans(t)], *rows_g),
        RowGather(S, dgate, lambda r, t: dall.at[r, half(t, 1)], *rows_d),
        RowGather(S, dinner, lambda r, t: dall.at[r, half(t, 0)], *rows_i),
    ]
    gathers[0].start()
    gathers[1].start()
    mine = pl.ds(pl.multiple_of(lax.rem(s, per) * width, width), width)
    NR[...] = nrm[:, pl.ds(pl.multiple_of(s * width, width), width)]

    def own_features(t, _):
        r = pl.ds(pl.multiple_of(t * TL, TL), TL)
        X[r, :] = toks[lax.div(s, per), t, :, mine]
        G[r, :] = ogz[lax.div(t, 2), lax.rem(t, 2), :, mine]
        return 0

    lax.fori_loop(0, S, own_features, 0)
    INV[...] = jnp.broadcast_to(inv, INV.shape)
    scan_backward(
        pre, H, dmix, act, bct, aux, ch, wdt, low,
        dlow, dbct, gdt, gch, dact, step, drive, keep, DS, DB, dst3, low3, dst,
        [(T // LANES * 3 // 4, lambda: gathers[0].step(1))],
    )
    h = R // S
    part_dt = lambda d: gdt.at[:, pl.ds(pl.multiple_of(d * h, 8), h), :]
    more = row_copies(S, part_dt, lambda t: MORE.at[t], mx, mr)
    more_own = pltpu.make_async_copy(part_dt(s), MORE.at[s], ml)
    for cp in more + [more_own]:
        cp.start()
    def during_second_sum():
        gathers[1].step(1)
        gathers[0].step(3)

    sum_over_all(
        S, PN, dlow, dbct, LR2, BCT2, *sums,
        between=(lambda: gathers[0].step(2), during_second_sum),
    )
    convolve_backward(
        LR2, BCT2, act, conv, aux, ch, wxT, dact, dinner, gx, gtap, pad, tail, act3, dpar
    )
    gathers[2].start()
    for cp in more + [more_own]:
        cp.wait()
    gathers[0].finish()

    large = 512

    def layer(i, _):
        r = pl.ds(pl.multiple_of(i * large, large), large)

        total = jnp.zeros((large, width), F32)
        for m in range(M):
            w = jnp.concatenate(
                [wo[b // 2, b % 2, m * C : (m + 1) * C, :] for b in range(S)], axis=0
            )
            total = total + dot(gall[r, :], w) * aux[r, m : m + 1]
        part[0, r, :] = total.astype(BF16)
        return 0

    lax.fori_loop(0, T // large, layer, 0)
    stream = Stream(H, load, (w_out, m_out, s_out), 6, sums_ref.at[1])
    stream.start(0)

    def out_gradient(i, rows_of):
        m, k = i // 2, i % 2
        wide = gall[:, k * (S // 2) * C : (k + 1) * (S // 2) * C].astype(F32)
        turned[...] = jnp.transpose((wide * aux[0:T, m : m + 1]).astype(BF16))
        g = dot(turned[...], G[...])
        parts = [
            g[:, t * LANES : (t + 1) * LANES].reshape(-1, 8, LANES) for t in range(tiles)
        ]
        H[rows_of, :] = jnp.stack(parts, axis=1).reshape(-1, LANES)

    to_out = LastBlocks(
        S, PN, part.at[0], LO, pair.at[0], pair.at[1], last[0], last[1], swaps.at[0], ls.at[1]
    )
    to_out.start()
    gathers[1].step(2)
    stores = [None, None]
    for i in range(6):
        k = i % 2
        if stores[k] is not None:
            stores[k].wait()
        rows_of = pl.ds((6 + k) * 1024, 1024)
        out_gradient(i, rows_of)
        stores[k] = pltpu.make_async_copy(
            H.at[rows_of], g_out.at[i * 1024 : (i + 1) * 1024], store.at[k]
        )
        stores[k].start()
        stream.norms(i, i // 2, (6 + k) * 1024)
        if i == 0:
            gathers[2].step(1)
        elif i == 1:
            gathers[1].step(3)
        elif i == 3:
            gathers[2].step(2)
        elif i == 5:
            gathers[2].step(3)
    for cp in stores:
        cp.wait()
    stream = Stream(H, load, (w_in, m_in, s_in), 12, sums_ref.at[0])
    stream.start(0)
    gathers[1].finish()
    gathers[2].finish()

    def normed_back(i, total):
        r = pl.ds(pl.multiple_of(i * large, large), large)

        d = jnp.zeros((large, width), F32)
        for m in range(M):
            cols = slice(m * C, (m + 1) * C)
            w = jnp.concatenate(
                [v for b in range(S) for v in (wi[b, :, cols], wg[b // 2, b % 2, :, cols])], axis=1
            )
            d = d + dot(dall[r, :], w, NT) * aux[r, m : m + 1]
        scaled = X[r, :].astype(F32) * aux[r, 7:8]
        gained = d * gain_mine[0:1, :]
        part[1, r, :] = gained.astype(BF16)
        along = jnp.sum(gained * scaled, axis=1, keepdims=True)
        for j in range(large // TL):
            turned = jnp.transpose(jnp.broadcast_to(along[j * TL : (j + 1) * TL], (TL, LANES)))
            rowdot[i * (large // TL) + j] = turned[0:8]
        return total + jnp.sum(d * scaled, axis=0, keepdims=True)

    total = lax.fori_loop(0, T // large, normed_back, jnp.zeros((1, width), F32))
    ggs[...] = jnp.broadcast_to(total, ggs.shape)
    to_in = LastBlocks(
        S, PN, part.at[1], DN, pair.at[2], pair.at[3], last[2], last[3], swaps.at[1], ls.at[3]
    )
    to_in.start()
    gains = [
        seq_copy(ggs, GG.at[k], last[4].at[k], last[5].at[k], {"tp": lax.rem(p + k, PN)})
        for k in range(1, PN)
    ]
    for cp in gains:
        cp.start()
    n = S * PN
    me = s * PN + p

    def to_all(src, dst, send, recv):
        def copy(k):
            j = lax.rem(me + k, n)
            device = {"seq": lax.div(j, PN), "tp": lax.rem(j, PN)}
            return seq_copy(src(lax.div(j, PN)), dst.at[k], send.at[k], recv.at[k], device)

        def start(k, _):
            copy(k).start()
            return 0

        def wait(k, _):
            copy(k).wait()
            return 0

        return (
            lambda: lax.fori_loop(1, n, start, 0),
            lambda: lax.fori_loop(1, n, wait, 0),
        )

    send_row, wait_row = to_all(lambda t: rowdot.at[t], ROW, last[6], last[7])
    send_row()
    GG[0] = ggs[...]
    ROW[0] = rowdot[s]

    stores = [None, None]
    per_m = width * stride
    for m in range(M):
        k = m % 2
        if stores[k] is not None:
            stores[k].wait()
        first_row = 6 * 1024 + k * per_m
        turned[0:width, :] = jnp.transpose(
            (NR[...].astype(F32) * aux[0:T, m : m + 1]).astype(BF16)
        )
        for b in range(S):
            g = dot(turned[0:width, :], dall[:, 2 * b * C : 2 * (b + 1) * C])
            H[pl.ds(first_row + 2 * b, width, stride=stride), :] = g[:, 0:C]
            H[pl.ds(first_row + 2 * b + 1, width, stride=stride), :] = g[:, C : 2 * C]
        stores[k] = pltpu.make_async_copy(
            H.at[first_row : first_row + per_m], g_in.at[m * per_m : (m + 1) * per_m], store.at[k]
        )
        stores[k].start()
        for q in range(per_m // 1024):
            stream.norms(m * (per_m // 1024) + q, m, first_row + q * 1024)
    lane = lax.broadcasted_iota(jnp.int32, (8, LANES), 1)
    total = jnp.zeros((8, LANES), F32)
    square = lambda v: jnp.sum(v * v)
    for t in range(S):
        gdt_mine[:, :, t * C : (t + 1) * C] = MORE[t]
    for m in range(M):
        x = adam_terms(gx[m], m_x[m], s_x[m])[2] + WEIGHT_DECAY * w_x[m]
        d = adam_terms(gdt_mine[m], m_dt[m], s_dt[m])[2] + WEIGHT_DECAY * w_dt[m]
        for k, value in enumerate((
            jnp.sum(sums_ref[0, m, 0]), square(w_x[m]), square(w_dt[m]), jnp.sum(sums_ref[1, m, 0]),
            jnp.sum(sums_ref[0, m, 1]), square(x), square(d), jnp.sum(sums_ref[1, m, 1]),
        )):
            total = jnp.where(lane == k * M + m, value, total)
    total_tile[...] = total
    send_tile, wait_tile = to_all(lambda t: total_tile, TILE, last[8], last[9])
    send_tile()
    TILE[0] = total
    for cp in gains:
        cp.wait()
    wait_row()
    wait_tile()
    total = jnp.sum(TILE[...], axis=0)
    below = pltpu.roll(total, LANES - 4 * M, 1)
    SCALE[...] = MATRIX_RATE * (jnp.sqrt(total) / jnp.sqrt(below))
    for cp in stores:
        cp.wait()
    to_out.finish()
    to_in.finish()


class Stream:
    def __init__(self, H, sems, refs, steps, sums):
        self.H, self.sems, self.refs, self.steps, self.sums = H, sems, refs, steps, sums
        sums[...] = jnp.zeros(sums.shape, F32)

    def copies(self, i):
        k = i % 2
        return [
            pltpu.make_async_copy(
                ref.at[i * 1024 : (i + 1) * 1024],
                self.H.at[pl.ds((3 * k + a) * 1024, 1024)],
                self.sems.at[k, a],
            )
            for a, ref in enumerate(self.refs)
        ]

    def start(self, i):
        for cp in self.copies(i):
            cp.start()

    def norms(self, i, m, g_row):
        for cp in self.copies(i):
            cp.wait()
        if i + 1 < self.steps:
            self.start(i + 1)
        H, k, rows = self.H, i % 2, 128

        def body(t, sums):
            at = lambda first: pl.ds(pl.multiple_of(first + t * rows, rows), rows)
            weight = H[at(3 * k * 1024), :]
            ratio = adam_terms(
                H[at(g_row), :], H[at((3 * k + 1) * 1024), :], H[at((3 * k + 2) * 1024), :]
            )[2]
            direction = ratio + WEIGHT_DECAY * weight
            fold = lambda v: jnp.sum((v * v).reshape(rows // 8, 8, LANES), axis=0)
            return sums[0] + fold(weight), sums[1] + fold(direction)

        a, b = lax.fori_loop(0, 1024 // rows, body, (self.sums[m, 0], self.sums[m, 1]))
        self.sums[m, 0] = a
        self.sums[m, 1] = b


class LastBlocks:
    def __init__(self, S, PN, part, out, other, both, send, recv, swap, ls):
        s, p = lax.axis_index("seq"), lax.axis_index("tp")
        ratio = S // PN
        self.S, self.PN, self.ratio = S, PN, ratio
        self.s, self.p, self.home = s, p, lax.div(s, ratio)
        self.y, self.c = lax.div(p, 2), lax.rem(p, 2)
        self.slot = lax.rem(s, ratio) * (PN // 2) + self.y
        self.part, self.out, self.other, self.both = part, out, other, both
        self.send, self.recv, self.ls = send, recv, ls
        self.half = part.shape[0] // 2
        self.TL = part.shape[0] // S
        self.swap = seq_copy(
            part.at[self.rows(1 - self.c)],
            other,
            swap.at[0],
            swap.at[1],
            {"tp": p + 1 - 2 * self.c},
        )

    def rows(self, c):
        return pl.ds(pl.multiple_of(c * self.half, self.half), self.half)

    def seq(self, k):
        return self.c * (self.S // 2) + k

    def away(self, k):
        return jnp.logical_or(self.s != self.seq(k), self.home != self.p)

    def copy(self, k):
        return seq_copy(
            self.both.at[k * self.TL : (k + 1) * self.TL],
            self.out.at[self.slot],
            self.send.at[k],
            self.recv.at[self.slot],
            {"seq": self.seq(k), "tp": self.home},
        )

    def own(self, k):
        return pltpu.make_async_copy(
            self.both.at[k * self.TL : (k + 1) * self.TL], self.out.at[self.slot], self.ls
        )

    def start(self):
        self.swap.start()
        self.swap.wait()
        mine = self.part[self.rows(self.c), :].astype(F32)
        self.both[...] = (mine + self.other[...].astype(F32)).astype(BF16)
        for k in range(self.S // 2):

            @pl.when(self.away(k))
            def _():
                self.copy(k).start()

            @pl.when(jnp.logical_not(self.away(k)))
            def _():
                self.own(k).start()

    def finish(self):
        for k in range(self.S // 2):

            @pl.when(self.away(k))
            def _():
                self.copy(k).wait_send()

            @pl.when(jnp.logical_not(self.away(k)))
            def _():
                self.own(k).wait()

        core = lax.div(self.s, self.S // 2)
        for h in range(self.ratio):
            for y in range(self.PN // 2):
                t, q = self.ratio * self.p + h, 2 * y + core
                i = h * (self.PN // 2) + y

                @pl.when(jnp.logical_or(t != self.s, self.p != q))
                def _():
                    seq_copy(
                        self.both.at[0 : self.TL],
                        self.out.at[i],
                        self.send.at[0],
                        self.recv.at[i],
                        {"seq": t, "tp": q},
                    ).wait_recv()


def scan_forward(T, C, bct, ch, step, drive, keep, H, Y):
    base = -jnp.exp(ch[K + 2 + M : K + 2 + M + N, :])
    H[0:N, :] = jnp.zeros((N, C), F32)

    def chunk(c, h):
        cols = bct[c]
        for i in range(LANES // 8):
            t0 = pl.multiple_of(c * LANES + 8 * i, 8)
            r = pl.ds(t0, 8)
            st, dr, kp = step[r, :], drive[r, :], keep[r, :]
            ys = []
            for j in range(8):
                k = 8 * i + j
                rate = jnp.exp(st[j : j + 1] * base) * kp[j : j + 1]
                h = rate * h + dr[j : j + 1] * cols[0:N, k : k + 1]
                H[pl.ds(pl.multiple_of((t0 + j + 1) * N, N), N), :] = h
                ys.append(jnp.sum(cols[N : 2 * N, k : k + 1] * h, axis=0, keepdims=True))
            Y[r, :] = jnp.concatenate(ys, axis=0)
        return h

    lax.fori_loop(0, T // LANES, chunk, jnp.zeros((N, C), F32))


def lane_sums(values):
    v = jnp.concatenate(values, axis=0)
    high = v.astype(BF16)
    low = (v - high.astype(F32)).astype(BF16)
    sums = dot(jnp.concatenate([high, low], axis=1), jnp.ones((2 * v.shape[1], LANES), BF16))
    return [sums[k * N : (k + 1) * N] for k in range(len(values))]


def scan_backward(
    pre, H, dmix, act, bct, aux, ch, wdt, low,
    dlow, dbct, gdt, gch, dact, step, drive, keep, DS, DB, dst3, low3, dst, hooks,
):
    T, C = act.shape
    rows = 128

    base = -jnp.exp(ch[K + 2 + M : K + 2 + M + N, :])
    lane = lax.broadcasted_iota(jnp.int32, (N, LANES), 1)
    nothing = jnp.zeros((N, C), F32)
    chunks = T // LANES

    def chunk(cc, carry):
        c = chunks - 1 - cc
        cols = bct[c]
        flow, hcur, gacc = carry
        accb = accc = jnp.zeros((N, LANES), F32)
        for i in reversed(range(LANES // 8)):
            t0 = pl.multiple_of(c * LANES + 8 * i, 8)
            r = pl.ds(t0, 8)
            st, dr, kp, dm = step[r, :], drive[r, :], keep[r, :], dmix[r, :]
            ds, db, ub, uc = [None] * 8, [None] * 8, [None] * 8, [None] * 8
            for j in reversed(range(8)):
                k = 8 * i + j
                back = cols[N : 2 * N, k : k + 1] * dm[j : j + 1] + flow
                rate = jnp.exp(st[j : j + 1] * base) * kp[j : j + 1]
                hprev = H[pl.ds(pl.multiple_of((t0 + j) * N, N), N), :]
                uc[j] = dm[j : j + 1] * hcur
                ub[j] = back * dr[j : j + 1]
                flow = rate * back
                dlog = flow * hprev
                gacc = gacc + dlog * st[j : j + 1]
                ds[j] = jnp.sum(dlog * base, axis=0, keepdims=True)
                db[j] = jnp.sum(back * cols[0:N, k : k + 1], axis=0, keepdims=True)
                hcur = hprev
            DS[r, :] = jnp.concatenate(ds, axis=0)
            DB[r, :] = jnp.concatenate(db, axis=0)
            sb, sc = lane_sums(ub), lane_sums(uc)
            for j in range(8):
                here = lane == 8 * i + j
                accb = jnp.where(here, sb[j], accb)
                accc = jnp.where(here, sc[j], accc)
        dbct[c, 0:N, :] = accb
        dbct[c, N : 2 * N, :] = accc
        return flow, hcur, gacc

    carry, done = (nothing, H[T * N : (T + 1) * N, :], nothing), 0
    for upto, call in hooks + [(chunks, None)]:
        carry = lax.fori_loop(done, upto, chunk, carry)
        done = upto
        if call is not None:
            call()
    gacc = carry[2]

    def finish(i, carry):
        skip, bias = carry
        r = pl.ds(pl.multiple_of(i * rows, rows), rows)
        a = act[r, :].astype(F32)
        back_b = DB[r, :]
        grad = DS[r, :] + a * back_b
        d = (grad / (1.0 + jnp.exp(-pre[r, :]))).astype(BF16)
        dst[r, :] = d
        wide = d.astype(F32)
        sums = []
        for m in range(M):
            mask = aux[r, m : m + 1]
            masked = wide * mask
            sums.append(jnp.sum(masked, axis=0, keepdims=True))
            dst3[r, m * C : (m + 1) * C] = masked.astype(BF16)
        total = dot(dst3[r, 0:C], wdt[0:R, :], NT)
        for m in range(1, M):
            total = total + dot(dst3[r, m * C : (m + 1) * C], wdt[m * R : (m + 1) * R, :], NT)
        dlow[r, :] = total
        dact[r, :] = dmix[r, :] * ch[K + 1 : K + 2, :] + step[r, :] * back_b
        skip = skip + jnp.sum(dmix[r, :] * a, axis=0, keepdims=True)
        return skip, bias + jnp.concatenate(sums, axis=0)

    skip, bias = lax.fori_loop(
        0, T // rows, finish, (jnp.zeros((1, C), F32), jnp.zeros((M, C), F32))
    )
    gch[0:1, :] = skip
    gch[1 : 1 + M, :] = bias
    gch[1 + M : 1 + M + N, :] = base * gacc
    for m in range(M):
        gdt[m] = dot(low3[:, m * R : (m + 1) * R], dst[...], TN)


def convolve_backward(
    dlow, dbct, act, conv, aux, ch, wxT, dact, dinner, gx, gtap, pad, tail, act3, dpar,
):
    T, C = act.shape
    rows = 128
    tail[T : T + 8, :] = jnp.zeros((8, C), F32)
    blank = jnp.zeros((LANES - 2 * N, LANES), F32)

    def fill(i, _):
        r = pl.ds(pl.multiple_of(i * rows, rows), rows)
        turned = jnp.transpose(jnp.concatenate([dbct[i], blank], axis=0))
        dpar[r, 0:R] = dlow[r, :]
        dpar[r, R : R + 2 * N] = turned[:, 0 : 2 * N].astype(BF16)
        wide = dpar[r, :].astype(F32)
        total = dact[r, :]
        for m in range(M):
            mask = aux[r, m : m + 1]
            total = total + dot((wide * mask).astype(BF16), wxT[m])
        v = conv[r, :]
        sig = 1.0 / (1.0 + jnp.exp(-v))
        tail[r, :] = (total * (sig * (1.0 + v * (1.0 - sig)))).astype(BF16).astype(F32)
        return 0

    lax.fori_loop(0, T // rows, fill, 0)

    def body(i, sums):
        r = pl.ds(pl.multiple_of(i * rows, rows), rows)
        window = pad[pl.ds(pl.multiple_of(i * rows, rows), rows + 8), :]
        d = tail[r, :]
        ahead = tail[pl.ds(pl.multiple_of(i * rows, rows), rows + 8), :]
        same = aux[pl.ds(pl.multiple_of(i * rows, rows), rows + 8), :]
        total = ch[K - 1 : K, :] * d
        new = []
        for k in range(K):
            off = K - 1 - k
            shifted = window[8 - off : 8 - off + rows]
            if k < K - 1:
                shifted = shifted * aux[r, M + k : M + k + 1]
                total = total + ch[k : k + 1, :] * (
                    ahead[off : off + rows] * same[off : off + rows, M + k : M + k + 1]
                )
            new.append(jnp.sum(d * shifted, axis=0, keepdims=True))
        new.append(jnp.sum(d, axis=0, keepdims=True))
        dinner[r, :] = total.astype(BF16)
        return sums + jnp.concatenate(new, axis=0)

    gtap[0 : K + 1, :] = lax.fori_loop(0, T // rows, body, jnp.zeros((K + 1, C), F32))
    for m in range(M):
        gx[m] = dot(dpar[...], act3[:, m * C : (m + 1) * C], TN)


def block_call(S, PN, args, T, C, width):
    dma = pltpu.SemaphoreType.DMA
    TL, DD = args[0].shape
    chunks = T // LANES
    zn = S // 2
    f = lambda *shape: sds(shape)
    b = lambda *shape: sds(shape, BF16)
    vf = lambda *shape: pltpu.VMEM(shape, F32)
    vb = lambda *shape: pltpu.VMEM(shape, BF16)
    n = S * PN
    out = (
        b(S // 2, TL, width), b(S // 2, TL, width), f(PN, 8, width), f(n, 8, LANES),
        f(S, M, R // S, C), f(M, R + 2 * N, C), f(8, C), f(1 + M + N, C),
        f(TL, LANES), f(8, LANES), f(M * width * 2 * S, C), f(M * S * width, C),
    )
    scratch = (
        [vf(8, TL), vb(PN, S, TL, DD // PN), vb(zn, 2, TL, DD // PN), vb(T, DD)]
        + [vb(DD, M * C), vb(zn, 2 * width, M * C), vb(zn, M * C, 2 * width)]
        + [vf(S, 8, TL), vf(S, 8, width)]
        + [vb(S, M, R // S, C)]
        + [vb(zn - 1, T, C)] * 4
        + [vf(T, C)] * 4
        + [vf(T + 8, C), vb(T, M * C), vf(T, R), vf(chunks, 2 * N, LANES)]
        + [vb(T, C), vf(T, C), vb(T, C), vb(T, R), vf(chunks, 2 * N, LANES), vf(T, C)]
        + [vf((T + 1) * N, C), vb(T, C), vb(T, C), vf(T, C), vf(T + 8, 8), vb(T, width)]
        + [vb(T, S * C), vb(T, 2 * S * C), vf(T, C), vf(T, C), vb(T, M * C), vb(T, M * R)]
        + [vb(T, C), vf(T, R), vf(chunks, 2 * N, LANES), vf(T, C), vf(M, R, C)]
        + [vb(T, R), vf(chunks, 2 * N, LANES), vf(T + 8, C), vb(T, R + 2 * N), vb(T, C)]
        + [vb(2, T, width), vf(S, 8, LANES), vf(8, width), vb(M * R, C)]
        + [vb(S, width, M * C), vb(zn, 2, width, M * C), vb(zn, 2, M * C, width)]
        + [vb(M, R // S, S * C)]
        + [vf(8, width), vb(M * C, R), vb(2 * N, M * C), vb(M, R + 2 * N, C), vb(T, width)]
        + [vb(T, width), vf(M, R // S, S * C), vb(S * C // 2, T), vf(2, M, 2, 8, LANES)]
        + [vf(n, 8, LANES), vf(8, LANES), dma((2,)), dma((2, 3)), dma((2,))]
        + [vb(4, T // 2, width), dma((2, 2))]
        + Spread.semaphores(S)
        + FeatureGather.semaphores(S)
        + [dma((zn,))] * 4
        + [dma((S,))] * 12
        + [dma((6,))]
        + sum_scratch(S, PN, T)
        + RowGather.semaphores(S) * 3
        + [dma((S,)), dma((S,)), dma]
        + [dma((S,))] * 4 + [dma((PN,))] * 2 + [dma((n,))] * 4
    )
    vm, hb = pl.BlockSpec(memory_space=pltpu.VMEM), pl.BlockSpec(memory_space=pl.ANY)
    return pl.pallas_call(
        functools.partial(block_kernel, S, PN),
        out_shape=out,
        in_specs=[vm] * (len(args) - 6) + [hb] * 6,
        out_specs=[vm] * (len(out) - 2) + [hb] * 2,
        scratch_shapes=scratch,
        compiler_params=pltpu.CompilerParams(
            collective_id=0, has_side_effects=True, vmem_limit_bytes=VMEM_LIMIT
        ),
    )(*args)


def update_kernel(steps, scale, g, w, m, s, avg, nw, nm, ns, na, which):
    k = lax.div(pl.program_id(0), steps)
    factor = scale[0:1, M * which : M * which + 1]
    for i in range(1, M):
        lane = M * which + i
        factor = jnp.where(k == i, scale[0:1, lane : lane + 1], factor)
    rows = 256

    def body(t, _):
        r = pl.ds(pl.multiple_of(t * rows, rows), rows)
        weight = w[r, :]
        new_m, new_s, ratio = adam_terms(g[r, :], m[r, :], s[r, :])
        new = weight - factor * (ratio + WEIGHT_DECAY * weight)
        nw[r, :] = new
        nm[r, :] = new_m
        ns[r, :] = new_s
        na[r, :] = AVERAGE_KEEP * avg[r, :] + (1.0 - AVERAGE_KEEP) * new
        return 0

    lax.fori_loop(0, w.shape[0] // rows, body, 0)


def update(which, rows, scale, *arrays):
    total, C = arrays[0].shape
    block = pl.BlockSpec((rows, C), lambda i: (i, 0))

    def kernel(*refs):
        update_kernel(total // M // rows, *refs, which)

    return pl.pallas_call(
        kernel,
        out_shape=(sds((total, C)),) * 4,
        grid=(total // rows,),
        in_specs=[pl.BlockSpec((8, LANES), lambda i: (0, 0))] + [block] * 5,
        out_specs=[block] * 4,
        compiler_params=pltpu.CompilerParams(vmem_limit_bytes=VMEM_LIMIT),
    )(scale, *arrays)


def rest_kernel(
    S, PN, tok, og, LO, DN, ROW, INV, scale, gx, more, gtap, gch, GG, wx, mx, sx, ax, wd, md, sd, ad,
    ch, mc, sc, ac, gn, mg, sg, ag,
    layer, grad, nwx, nmx, nsx, nax, nwd, nmd, nsd, nad, nwc, nmc, nsc, nac, nwg, nmg, nsg, nag, gc, gd,
):
    p = lax.axis_index("tp")
    C = more.shape[3]
    width = LO.shape[2]
    out_width = og.shape[1]

    def average(old, new):
        return AVERAGE_KEEP * old + (1.0 - AVERAGE_KEEP) * new

    along = ROW[0, 0:1, :]
    for k in range(1, ROW.shape[0]):
        along = along + ROW[k, 0:1, :]
    column = jnp.transpose(jnp.broadcast_to(along, (LANES, LANES)))[:, 0:1]
    inv = INV[:, 0:1]
    for h in range(out_width // width):
        cols = pl.ds(pl.multiple_of(p * out_width + h * width, LANES), width)
        here = slice(h * width, (h + 1) * width)
        mine = tok[:, cols].astype(F32)
        chips = PN // 2
        total = LO[h * chips].astype(F32)
        back = DN[h * chips].astype(F32)
        for q in range(1, chips):
            total = total + LO[h * chips + q].astype(F32)
            back = back + DN[h * chips + q].astype(F32)
        layer[:, here] = mine + total
        grad[:, here] = og[:, here].astype(F32) + inv * (back - mine * inv * (column / D))
    for t in range(S):
        gd[:, :, t * C : (t + 1) * C] = more[t]
    for m in range(M):
        for k, g, w, mo, sq, av, nw, nm, ns, na in (
            (1, gx, wx, mx, sx, ax, nwx, nmx, nsx, nax),
            (2, gd, wd, md, sd, ad, nwd, nmd, nsd, nad),
        ):
            factor = scale[0:1, M * k + m : M * k + m + 1]
            new_m, new_s, ratio = adam_terms(g[m], mo[m], sq[m])
            new = w[m] - factor * (ratio + WEIGHT_DECAY * w[m])
            nw[m] = new
            nm[m] = new_m
            ns[m] = new_s
            na[m] = average(av[m], new)
    gc[0 : K + 1, :] = gtap[0 : K + 1, :]
    gc[K + 1 :, :] = gch[...]
    new_m, new_s, ratio = adam_terms(gc[...], mc[...], sc[...])
    new = ch[...] - CHANNEL_RATE * ratio
    nwc[...] = new
    nmc[...] = new_m
    nsc[...] = new_s
    nac[...] = average(ac[...], new)
    g = GG[0, 0:1, :]
    for q in range(1, PN):
        g = g + GG[q, 0:1, :]
    new_m, new_s, ratio = adam_terms(g, mg[...], sg[...])
    new = gn[...] - GAIN_RATE * ratio
    nwg[...] = new
    nmg[...] = new_m
    nsg[...] = new_s
    nag[...] = average(ag[...], new)


def to_rows(w, S):
    m, width, two, channels = w.shape
    c = channels // S
    return w.reshape(m, width, two, S, c).transpose(0, 1, 3, 2, 4).reshape(-1, c)


def from_rows(rows, S, shape):
    m, width, two, channels = shape
    c = channels // S
    return rows.reshape(m, width, S, two, c).transpose(0, 1, 3, 2, 4).reshape(shape)


def to_tiles(w):
    m, rows, columns = w.shape
    return w.reshape(m, rows // 8, 8, columns // LANES, LANES).transpose(0, 1, 3, 2, 4).reshape(
        -1, LANES
    )


def from_tiles(flat, shape):
    m, rows, columns = shape
    return flat.reshape(m, rows // 8, columns // LANES, 8, LANES).transpose(0, 1, 3, 2, 4).reshape(
        shape
    )


def local(
    tokens, out_grad, modality, segment,
    w_in, w_x, w_dt, w_out, channel, norm_gain,
    moment_in, moment_x, moment_dt, moment_out, moment_channel, moment_gain,
    square_in, square_x, square_dt, square_out, square_channel, square_gain,
    average_in, average_x, average_dt, average_out, average_channel, average_gain,
):
    S, PN = lax.axis_size("seq"), lax.axis_size("tp")
    TL = tokens.shape[0]
    T = S * TL
    width = D // S
    inner_width = w_out.shape[1]
    C = inner_width // S
    ins = [to_rows(v, S) for v in (w_in, moment_in, square_in, average_in)]
    outs = [to_tiles(v) for v in (w_out, moment_out, square_out, average_out)]
    modrow = jnp.broadcast_to(modality.astype(F32)[None], (8, TL))
    ahead = jnp.concatenate([jnp.full((K - 1,), -1, jnp.int32), segment])
    same = [(ahead[k : k + T] == segment).astype(F32) for k in range(K - 1)]
    zero = jnp.zeros((T,), F32)
    segs = jnp.stack([zero] * M + same + [same[K - 2], zero], axis=1)
    row = lambda v: v[None, :]
    xs = [jnp.transpose(v, (0, 2, 1)) for v in (w_x, moment_x, square_x, average_x)]
    LO, DN, GG, ROW, MORE, gx, gtap, gch, INV, scale, g_in, g_out = block_call(
        S,
        PN,
        (
            tokens, out_grad, modrow, row(norm_gain), segs, channel,
            *xs[:3], w_dt, moment_dt, square_dt, *ins[:3], *outs[:3],
        ),
        T, C, width,
    )
    new_in = [from_rows(v, S, w_in.shape) for v in update(0, 4096, scale, g_in, *ins)]
    new_out = [from_tiles(v, w_out.shape) for v in update(3, 1024, scale, g_out, *outs)]
    like = lambda v: sds(v.shape)
    vec = sds((1, width))
    rest = local_call(
        functools.partial(rest_kernel, S, PN),
        (sds(out_grad.shape),) * 2 + (like(xs[0]),) * 4 + (like(w_dt),) * 4 + (like(channel),) * 4
        + (vec,) * 4,
        28,
        [pltpu.VMEM(channel.shape, F32), pltpu.VMEM(w_dt.shape, F32)],
    )(
        tokens, out_grad, LO, DN, ROW, INV, scale, gx, MORE, gtap, gch, GG,
        *xs, w_dt, moment_dt, square_dt, average_dt,
        channel, moment_channel, square_channel, average_channel,
        row(norm_gain), row(moment_gain), row(square_gain), row(average_gain),
    )
    new_x, new_dt, new_ch, new_g = [rest[2 + 4 * k : 6 + 4 * k] for k in range(4)]
    new_x = [jnp.transpose(v, (0, 2, 1)) for v in new_x]
    groups = [(new_in[k], new_x[k], new_dt[k], new_out[k], new_ch[k], new_g[k][0]) for k in range(4)]
    return (*rest[:2], *groups[0], *groups[1], *groups[2], *groups[3])


def channels_fit(mesh):
    S, PN = mesh.shape["seq"], mesh.shape["tp"]
    n = S * PN
    return PN == 4 and S == 2 * PN and (2 * N) % n == 0 and D * 2 // n == LANES


def solution(mesh):
    placed = (
        P("seq", None),
        P("seq", "tp"),
        P("seq"),
        P(),
        P(None, "seq", None, "tp"),
        P(None, ("tp", "seq"), None),
        P(None, "seq", "tp"),
        P(None, "tp", "seq"),
        P(None, ("tp", "seq")),
        P("seq"),
        P(None, "seq", None, "tp"),
        P(None, ("tp", "seq"), None),
        P(None, "seq", "tp"),
        P(None, "tp", "seq"),
        P(None, ("tp", "seq")),
        P("seq"),
        P(None, "seq", None, "tp"),
        P(None, ("tp", "seq"), None),
        P(None, "seq", "tp"),
        P(None, "tp", "seq"),
        P(None, ("tp", "seq")),
        P("seq"),
        P(None, "seq", None, "tp"),
        P(None, ("tp", "seq"), None),
        P(None, "seq", "tp"),
        P(None, "tp", "seq"),
        P(None, ("tp", "seq")),
        P("seq"),
    )
    return jax.shard_map(
        local if channels_fit(mesh) else generic_local,
        mesh=mesh,
        in_specs=placed,
        out_specs=(
            P("seq", "tp"),
            P("seq", "tp"),
            P(None, "seq", None, "tp"),
            P(None, ("tp", "seq"), None),
            P(None, "seq", "tp"),
            P(None, "tp", "seq"),
            P(None, ("tp", "seq")),
            P("seq"),
            P(None, "seq", None, "tp"),
            P(None, ("tp", "seq"), None),
            P(None, "seq", "tp"),
            P(None, "tp", "seq"),
            P(None, ("tp", "seq")),
            P("seq"),
            P(None, "seq", None, "tp"),
            P(None, ("tp", "seq"), None),
            P(None, "seq", "tp"),
            P(None, "tp", "seq"),
            P(None, ("tp", "seq")),
            P("seq"),
            P(None, "seq", None, "tp"),
            P(None, ("tp", "seq"), None),
            P(None, "seq", "tp"),
            P(None, "tp", "seq"),
            P(None, ("tp", "seq")),
            P("seq"),
        ),
        check_vma=False,
    )
```

```python
import functools

import jax
import jax.numpy as jnp
from jax import lax
from jax.experimental import pallas as pl
from jax.experimental.pallas import tpu as pltpu
from jax.sharding import PartitionSpec as P

D = 2048
R = 128
N = 16
K = 4
M = 3
STEP = 10


EPSILON = 1e-05
BETA_ONE = 0.9
BETA_TWO = 0.999
ADAM_EPSILON = 1e-06
WEIGHT_DECAY = 0.01
MATRIX_RATE = 0.25
CHANNEL_RATE = 0.7
GAIN_RATE = 0.35
AVERAGE_KEEP = 0.8
PRECISE = lax.Precision.HIGHEST


def passed_along(value, axis, steps):
    count = lax.axis_size(axis)
    leading, last = (max(0, -steps), min(count, count - steps))
    return lax.ppermute(value, axis, [(source, source + steps) for source in range(leading, last)])


def prefix(x, axis, combine, identity, reverse):
    devices, place = (lax.axis_size(axis), lax.axis_index(axis))
    everything = jax.tree.map(lambda part: lax.all_gather(part, axis), x)
    start = jax.tree.map(
        lambda part, zero: jnp.broadcast_to(jnp.asarray(zero, part.dtype), part.shape), x, identity
    )

    def lap(k, before):
        at = devices - 1 - k if reverse else k
        reached = at > place if reverse else at < place
        new = combine(before, jax.tree.map(lambda part: part[at], everything))
        return jax.tree.map(lambda a, b: jnp.where(reached, a, b), new, before)

    return lax.fori_loop(0, devices, lap, start)


def silu_grad(operand):
    sigmoid_of = jax.nn.sigmoid(operand)
    return sigmoid_of * (1.0 + operand * (1.0 - sigmoid_of))


def combine(earlier, following):
    return (earlier[0] * following[0], following[0] * earlier[1] + following[1])


def masked_dot(mask_cols, operand, stacked):
    running = mask_cols[:, 0:1] * jnp.dot(operand, stacked[0], preferred_element_type=jnp.float32)
    for modal_index in range(1, M):
        running = running + mask_cols[:, modal_index : modal_index + 1] * jnp.dot(
            operand, stacked[modal_index], preferred_element_type=jnp.float32
        )
    return running


def masked_back(mask_cols, operand, stacked):
    contract = (((1,), (1,)), ((), ()))
    running = mask_cols[:, 0:1] * lax.dot_general(
        operand, stacked[0], contract, preferred_element_type=jnp.float32
    )
    for modal_index in range(1, M):
        running = running + mask_cols[:, modal_index : modal_index + 1] * lax.dot_general(
            operand, stacked[modal_index], contract, preferred_element_type=jnp.float32
        )
    return running


def masked_outer(mask_low, operand, cotangent):
    contract = (((0,), (0,)), ((), ()))
    return jnp.stack(
        [
            lax.dot_general(
                operand * mask_low[:, modal_index : modal_index + 1],
                cotangent,
                contract,
                preferred_element_type=jnp.float32,
            )
            for modal_index in range(M)
        ]
    )


def adam_parts(gradient, moment, square):
    moment_new = BETA_ONE * moment + (1.0 - BETA_ONE) * gradient
    square_new = BETA_TWO * square + (1.0 - BETA_TWO) * gradient * gradient
    adam_ratio = (
        moment_new
        / (1.0 - BETA_ONE**STEP)
        / (jnp.sqrt(square_new / (1.0 - BETA_TWO**STEP)) + ADAM_EPSILON)
    )
    return (moment_new, square_new, adam_ratio)


def generic_local(
    tokens,
    out_grad,
    modality,
    segment,
    w_in,
    w_x,
    w_dt,
    w_out,
    channel,
    norm_gain,
    moment_in,
    moment_x,
    moment_dt,
    moment_out,
    moment_channel,
    moment_gain,
    square_in,
    square_x,
    square_dt,
    square_out,
    square_channel,
    square_gain,
    average_in,
    average_x,
    average_dt,
    average_out,
    average_channel,
    average_gain,
):
    tok_local = tokens.shape[0]
    width_tp = out_grad.shape[1]
    lowered = (
        w_in.astype(jnp.bfloat16),
        w_x.astype(jnp.bfloat16),
        w_dt.astype(jnp.bfloat16),
        w_out.astype(jnp.bfloat16),
    )
    stack_in, stack_x, stack_dt, stack_out = (
        lax.all_gather(lowered[0], "seq", axis=1, tiled=True),
        lax.all_gather(lowered[1], "seq", axis=1, tiled=True),
        lax.all_gather(lowered[2], "seq", axis=1, tiled=True),
        lax.all_gather(lowered[3], "seq", axis=2, tiled=True),
    )
    chan_full, gain_full = (
        lax.all_gather(channel, "seq", axis=1, tiled=True),
        lax.all_gather(norm_gain, "seq", axis=0, tiled=True),
    )
    inner_width = stack_out.shape[1]
    in_flat = stack_in.reshape(M, D, 2 * inner_width)
    seq_index = lax.axis_index("seq")
    tp_index = lax.axis_index("tp")
    start_row = seq_index * tok_local
    seg_local = lax.dynamic_slice(segment, (start_row,), (tok_local,))
    seg_before = lax.dynamic_slice(
        jnp.concatenate([jnp.full((K - 1,), -1, jnp.int32), segment]),
        (start_row,),
        (tok_local + K - 1,),
    )
    seg_after = lax.dynamic_slice(
        jnp.concatenate([segment, jnp.full((K - 1,), -2, jnp.int32)]),
        (start_row,),
        (tok_local + K - 1,),
    )
    mask_cols = (modality[:, None] == jnp.arange(M, dtype=jnp.int32)[None, :]).astype(jnp.float32)
    mask_low = mask_cols.astype(jnp.bfloat16)
    tokens_wide = tokens.astype(jnp.float32)
    inv_root = lax.rsqrt(jnp.mean(tokens_wide * tokens_wide, axis=-1, keepdims=True) + EPSILON)
    scaled = tokens_wide * inv_root
    normed = (scaled * gain_full[None, :]).astype(jnp.bfloat16)
    projected = masked_dot(mask_cols, normed, in_flat)
    inner_act = projected[:, :inner_width].astype(jnp.bfloat16)
    gate_pre = projected[:, inner_width:]
    rim_rows = passed_along(inner_act[tok_local - (K - 1) :], "seq", 1)
    extended = jnp.concatenate([rim_rows, inner_act], axis=0).astype(jnp.float32)
    conv_pre = jnp.broadcast_to(chan_full[K][None, :], (tok_local, inner_width))
    same_docs = []
    for tap_index in range(K):
        same_doc = (seg_before[tap_index : tap_index + tok_local] == seg_local).astype(jnp.float32)[
            :, None
        ]
        same_docs.append(same_doc)
        conv_pre = (
            conv_pre
            + chan_full[tap_index][None, :] * extended[tap_index : tap_index + tok_local] * same_doc
        )
    activated = jax.nn.silu(conv_pre).astype(jnp.bfloat16)
    act_wide = activated.astype(jnp.float32)
    params_x = lax.psum(masked_dot(mask_cols, activated, stack_x), "tp")
    low_rank = params_x[:, :R].astype(jnp.bfloat16)
    input_b = params_x[:, R : R + N]
    output_c = params_x[:, R + N :]
    step_pre = masked_dot(mask_cols, low_rank, stack_dt) + jnp.dot(
        mask_cols, chan_full[K + 2 : K + 2 + M], precision=PRECISE
    )
    step_size = jax.nn.softplus(step_pre)
    decay_base = -jnp.exp(chan_full[K + 2 + M :])
    keep_flag = (seg_before[K - 2 : K - 2 + tok_local] == seg_local).astype(jnp.float32)
    decay_rate = jnp.exp(step_size[:, None, :] * decay_base[None]) * keep_flag[:, None, None]
    drive_term = (step_size * act_wide)[:, None, :] * input_b[:, :, None]
    decay_cum, local_state = lax.associative_scan(combine, (decay_rate, drive_term), axis=0)
    unit_pair = (jnp.ones_like(decay_base), jnp.zeros_like(decay_base))
    carry_in = prefix((decay_cum[-1], local_state[-1]), "seq", combine, unit_pair, False)[1]
    hidden_state = local_state + decay_cum * carry_in[None]
    mixed_out = (
        jnp.einsum("tn,tne->te", output_c, hidden_state, precision=PRECISE)
        + chan_full[K + 1][None, :] * act_wide
    )
    gate_act = jax.nn.silu(gate_pre)
    gated_out = (mixed_out * gate_act).astype(jnp.bfloat16)
    out_share = lax.psum_scatter(
        masked_dot(mask_cols, gated_out, stack_out), "tp", scatter_dimension=1, tiled=True
    )
    layer_out = lax.dynamic_slice_in_dim(tokens_wide, tp_index * width_tp, width_tp, 1) + out_share
    grad_full = lax.all_gather(out_grad, "tp", axis=1, tiled=True)
    d_gated = masked_back(mask_cols, grad_full, stack_out)
    grad_out = masked_outer(mask_low, gated_out, grad_full)
    d_mixed = d_gated * gate_act
    d_gate = d_gated * mixed_out * silu_grad(gate_pre)
    grad_skip = jnp.sum(d_mixed * act_wide, axis=0)
    d_out_c = jnp.einsum("te,tne->tn", d_mixed, hidden_state, precision=PRECISE)
    d_hidden = output_c[:, :, None] * d_mixed[:, None, :]
    decay_next = jnp.concatenate([decay_rate[1:], jnp.ones_like(decay_rate[:1])], axis=0)
    suffix_cum, local_back = lax.associative_scan(
        combine, (decay_next, d_hidden), reverse=True, axis=0
    )
    device_pair = (decay_rate[0] * suffix_cum[0], decay_rate[0] * local_back[0])
    carry_back = prefix(device_pair, "seq", combine, unit_pair, True)[1]
    back_state = local_back + suffix_cum * carry_back[None]
    state_prev = jnp.concatenate([carry_in[None], hidden_state[:-1]], axis=0)
    d_log = back_state * state_prev * decay_rate
    d_drive_sum = jnp.einsum("tne,tn->te", back_state, input_b, precision=PRECISE)
    d_step_size = jnp.sum(d_log * decay_base[None], axis=1) + act_wide * d_drive_sum
    grad_decay = decay_base * jnp.einsum("tne,te->ne", d_log, step_size, precision=PRECISE)
    d_in_b = jnp.einsum("tne,te->tn", back_state, step_size * act_wide, precision=PRECISE)
    d_step = (d_step_size * jax.nn.sigmoid(step_pre)).astype(jnp.bfloat16)
    d_step_wide = d_step.astype(jnp.float32)
    grad_bias = jnp.dot(mask_cols.T, d_step_wide, precision=PRECISE)
    grad_dt = masked_outer(mask_low, low_rank, d_step)
    d_low = masked_back(mask_cols, d_step, stack_dt)
    d_params = lax.psum(jnp.concatenate([d_low, d_in_b, d_out_c], axis=1), "tp").astype(
        jnp.bfloat16
    )
    grad_x = masked_outer(mask_low, activated, d_params)
    d_activ = (
        d_mixed * chan_full[K + 1][None, :]
        + step_size * d_drive_sum
        + masked_back(mask_cols, d_params, stack_x)
    )
    d_conv = (d_activ * silu_grad(conv_pre)).astype(jnp.bfloat16)
    rim_back = passed_along(d_conv[: K - 1], "seq", -1)
    d_conv_wide = d_conv.astype(jnp.float32)
    conv_after = jnp.concatenate([d_conv, rim_back], axis=0).astype(jnp.float32)
    d_inner = jnp.zeros((tok_local, inner_width), jnp.float32)
    grad_taps = []
    for tap_index in range(K):
        grad_taps.append(
            jnp.sum(
                d_conv_wide * extended[tap_index : tap_index + tok_local] * same_docs[tap_index],
                axis=0,
            )
        )
        offset = K - 1 - tap_index
        same_after = (seg_after[offset : offset + tok_local] == seg_local).astype(jnp.float32)[
            :, None
        ]
        d_inner = (
            d_inner
            + chan_full[tap_index][None, :] * conv_after[offset : offset + tok_local] * same_after
        )
    grad_conv_b = jnp.sum(d_conv_wide, axis=0)
    d_proj = jnp.concatenate([d_inner, d_gate], axis=1).astype(jnp.bfloat16)
    grad_in = masked_outer(mask_low, normed, d_proj).reshape(M, D, 2, inner_width)
    d_normed = lax.psum(masked_back(mask_cols, d_proj, in_flat), "tp")
    grad_gain = jnp.sum(d_normed * scaled, axis=0)
    d_scaled = d_normed * gain_full[None, :]
    d_tokens = inv_root * (d_scaled - scaled * jnp.mean(d_scaled * scaled, axis=-1, keepdims=True))
    tokens_grad = out_grad.astype(jnp.float32) + lax.dynamic_slice_in_dim(
        d_tokens, tp_index * width_tp, width_tp, 1
    )
    grad_channel = jnp.concatenate(
        [jnp.stack(grad_taps), grad_conv_b[None], grad_skip[None], grad_bias, grad_decay], axis=0
    )
    reduced = (
        lax.psum_scatter(grad_in, "seq", scatter_dimension=1, tiled=True),
        lax.psum_scatter(grad_x, "seq", scatter_dimension=1, tiled=True),
        lax.psum_scatter(grad_dt, "seq", scatter_dimension=1, tiled=True),
        lax.psum_scatter(grad_out, "seq", scatter_dimension=2, tiled=True),
        lax.psum_scatter(grad_channel, "seq", scatter_dimension=1, tiled=True),
        lax.psum_scatter(grad_gain, "seq", scatter_dimension=0, tiled=True),
    )
    weights = (w_in, w_x, w_dt, w_out, channel, norm_gain)
    moments = (moment_in, moment_x, moment_dt, moment_out, moment_channel, moment_gain)
    squares = (square_in, square_x, square_dt, square_out, square_channel, square_gain)
    averages = (average_in, average_x, average_dt, average_out, average_channel, average_gain)
    adam_all = [
        adam_parts(reduced[position], moments[position], squares[position]) for position in range(6)
    ]
    directions = [adam_all[position][2] + WEIGHT_DECAY * weights[position] for position in range(4)]
    weight_sums = jnp.stack(
        [
            jnp.sum(
                weights[position] * weights[position], axis=tuple(range(1, weights[position].ndim))
            )
            for position in range(4)
        ]
    )
    direction_sums = jnp.stack(
        [
            jnp.sum(
                directions[position] * directions[position],
                axis=tuple(range(1, directions[position].ndim)),
            )
            for position in range(4)
        ]
    )
    totals = lax.psum(jnp.stack([weight_sums, direction_sums]), ("seq", "tp"))
    trust_ratio = jnp.sqrt(totals[0]) / jnp.sqrt(totals[1])
    new_weights = []
    new_averages = []
    for position in range(6):
        weight = weights[position]
        if position < 4:
            updated = (
                weight
                - MATRIX_RATE
                * trust_ratio[position].reshape((M,) + (1,) * (weight.ndim - 1))
                * directions[position]
            )
        elif position == 4:
            updated = weight - CHANNEL_RATE * adam_all[position][2]
        else:
            updated = weight - GAIN_RATE * adam_all[position][2]
        new_weights.append(updated)
        new_averages.append(AVERAGE_KEEP * averages[position] + (1.0 - AVERAGE_KEEP) * updated)
    return (
        layer_out,
        tokens_grad,
        new_weights[0],
        new_weights[1],
        new_weights[2],
        new_weights[3],
        new_weights[4],
        new_weights[5],
        adam_all[0][0],
        adam_all[1][0],
        adam_all[2][0],
        adam_all[3][0],
        adam_all[4][0],
        adam_all[5][0],
        adam_all[0][1],
        adam_all[1][1],
        adam_all[2][1],
        adam_all[3][1],
        adam_all[4][1],
        adam_all[5][1],
        new_averages[0],
        new_averages[1],
        new_averages[2],
        new_averages[3],
        new_averages[4],
        new_averages[5],
    )


MESH = pl.DeviceIdType.MESH
VMEM_LIMIT = 62 * 1024 * 1024
LANES = 128
F32 = jnp.float32
BF16 = jnp.bfloat16
NT = (((1,), (1,)), ((), ()))
TN = (((0,), (0,)), ((), ()))


def dot(a, b, dims=(((1,), (0,)), ((), ()))):
    return lax.dot_general(a, b, dims, preferred_element_type=F32)


def local_call(kernel, out_shape, n_in, scratch=(), cost=None):
    return pl.pallas_call(
        kernel,
        out_shape=out_shape,
        in_specs=[pl.BlockSpec(memory_space=pltpu.VMEM)] * n_in,
        out_specs=jax.tree.map(lambda _: pl.BlockSpec(memory_space=pltpu.VMEM), out_shape),
        scratch_shapes=list(scratch),
        compiler_params=pltpu.CompilerParams(vmem_limit_bytes=VMEM_LIMIT),
        cost_estimate=cost,
    )


def remote_call(kernel, out_shape, n_in, scratch, ident):
    return pl.pallas_call(
        kernel,
        out_shape=out_shape,
        in_specs=[pl.BlockSpec(memory_space=pltpu.VMEM)] * n_in,
        out_specs=jax.tree.map(lambda _: pl.BlockSpec(memory_space=pltpu.VMEM), out_shape),
        scratch_shapes=list(scratch),
        compiler_params=pltpu.CompilerParams(
            collective_id=ident, has_side_effects=True, vmem_limit_bytes=VMEM_LIMIT
        ),
    )


def sds(shape, dtype=F32):
    return jax.ShapeDtypeStruct(shape, dtype)


def seq_copy(src, dst, send, recv, device):
    return pltpu.make_async_remote_copy(
        src_ref=src,
        dst_ref=dst,
        send_sem=send,
        recv_sem=recv,
        device_id=device,
        device_id_type=MESH,
    )


def place(S, PN):
    s, p = lax.axis_index("seq"), lax.axis_index("tp")
    return s, p, lax.div(s, 2), lax.rem(s, 2)


def greet_all(S, PN):
    s, p = lax.axis_index("seq"), lax.axis_index("tp")
    n = S * PN
    me = s * PN + p
    bar = pltpu.get_barrier_semaphore()

    def greet(k, _):
        j = lax.rem(me + k, n)
        pl.semaphore_signal(
            bar,
            inc=1,
            device_id={"seq": lax.div(j, PN), "tp": lax.rem(j, PN)},
            device_id_type=MESH,
        )
        return 0

    lax.fori_loop(1, n, greet, 0)
    pl.semaphore_wait(bar, n - 1)


class Spread:
    def __init__(self, S, PN, own, buf, zs, zr, xs, xr, ys, yr, cs, cr, ls):
        s, p, z, x = place(S, PN)
        self.zn = S // 2
        zn = self.zn
        other_x = {"seq": 2 * z + 1 - x}
        other_y = {"tp": lax.rem(p + 2, PN)}
        other_c = {"tp": p + 1 - 2 * lax.rem(p, 2)}

        def at(k, j):
            return 2 * lax.rem(z - k + zn, zn) + (x if j == 0 else 1 - x)

        self.local = pltpu.make_async_copy(own, buf.at[p, s], ls)
        self.z = [
            seq_copy(own, buf.at[p, s], zs.at[k], zr.at[k], {"seq": 2 * lax.rem(z + k, zn) + x})
            for k in range(1, zn)
        ]
        self.x = []
        self.y = {}
        for k in range(zn):
            src = own if k == 0 else buf.at[p, at(k, 0)]
            self.x.append(seq_copy(src, buf.at[p, at(k, 0)], xs.at[k], xr.at[k], other_x))
            for j in range(2):
                src = own if (k == 0 and j == 0) else buf.at[p, at(k, j)]
                self.y[k, j] = seq_copy(
                    src, buf.at[p, at(k, j)], ys.at[2 * k + j], yr.at[2 * k + j], other_y
                )
        q = lax.rem(p + 2, PN)
        self.c = [
            seq_copy(buf.at[p], buf.at[p], cs.at[0], cr.at[0], other_c),
            seq_copy(buf.at[q], buf.at[q], cs.at[1], cr.at[1], other_c),
        ]

    def start(self):
        self.local.start()
        for cp in self.z:
            cp.start()
        self.x[0].start()
        self.y[0, 0].start()

    def forward(self):
        for k in range(1, self.zn):
            self.z[k - 1].wait_recv()
            self.x[k].start()
            self.y[k, 0].start()
        for k in range(self.zn):
            self.x[k].wait_recv()
            self.y[k, 1].start()
        self.local.wait()
        self.c[0].start()

    def finish(self):
        for cp in self.y.values():
            cp.wait_recv()
        self.c[1].start()
        for cp in self.z + self.x + list(self.y.values()):
            cp.wait_send()
        for cp in self.c:
            cp.wait()

    @staticmethod
    def semaphores(S):
        dma = pltpu.SemaphoreType.DMA
        return [dma((S // 2,))] * 4 + [dma((S,))] * 2 + [dma((2,))] * 2 + [dma]


def row_copies(S, src, dst, send, recv):
    s = lax.axis_index("seq")
    out = []
    for k in range(1, S):
        d = lax.rem(s + k, S)
        out.append(seq_copy(src(d), dst(s), send.at[k], recv.at[k], {"seq": d}))
    return out


def sum_over_all(
    S, PN, lr, bct, LR, BCT, got_l, got_b, core_l, core_b,
    c1s, c1r, ssl, rsl, ssb, rsb, sgl, rgl, sgb, rgb, c2s, c2r, between=(),
):
    n = S * PN // 2
    s, p = lax.axis_index("seq"), lax.axis_index("tp")
    y, c = lax.div(p, 2), lax.rem(p, 2)
    me = s * (PN // 2) + y
    T = lr.shape[0]
    half, rows = T // 2, T // 2 // n
    chunks = bct.shape[0]
    per = n // (chunks // 2)
    high = bct.shape[1] // per
    twin = {"tp": p + 1 - 2 * c}

    def device(j):
        return {"seq": lax.div(j, PN // 2), "tp": 2 * lax.rem(j, PN // 2) + c}

    def half_l(k):
        return pl.ds(pl.multiple_of(k * half, half), half)

    def half_b(k):
        return pl.ds(k * (chunks // 2), chunks // 2)

    def rows_of(j):
        return pl.ds(pl.multiple_of(c * half + j * rows, rows), rows)

    def slab(ref, j):
        at = c * (chunks // 2) + lax.div(j, per)
        return ref.at[at, pl.ds(pl.multiple_of(lax.rem(j, per) * high, 8), high)]

    swap = [
        seq_copy(lr.at[half_l(1 - c)], core_l, c1s.at[0], c1r.at[0], twin),
        seq_copy(bct.at[half_b(1 - c)], core_b, c1s.at[1], c1r.at[1], twin),
    ]
    for cp in swap:
        cp.start()
    for cp in swap:
        cp.wait()
    lr[half_l(c), :] = lr[half_l(c), :] + core_l[...]
    bct[half_b(c)] = bct[half_b(c)] + core_b[...]

    def first(k):
        j = lax.rem(me + k, n)
        return (
            seq_copy(lr.at[rows_of(j)], got_l.at[k], ssl.at[k], rsl.at[k], device(j)),
            seq_copy(slab(bct, j), got_b.at[k], ssb.at[k], rsb.at[k], device(j)),
        )

    def second(k):
        j = lax.rem(me + k, n)
        mine_l, mine_b = LR.at[rows_of(me)], slab(BCT, me)
        return (
            seq_copy(mine_l, mine_l, sgl.at[k], rgl.at[k], device(j)),
            seq_copy(mine_b, mine_b, sgb.at[k], rgb.at[k], device(j)),
        )

    def start(copies, k):
        for cp in copies(k):
            cp.start()
        return 0

    def wait(copies, k):
        for cp in copies(k):
            cp.wait()
        return 0

    lax.fori_loop(1, n, lambda k, _: start(first, k), 0)
    for cp in between[0:1]:
        cp()
    got_l[0] = lr[rows_of(me), :]
    got_b[0] = slab(bct, me)[...]
    lax.fori_loop(1, n, lambda k, _: wait(first, k), 0)
    LR[rows_of(me), :] = jnp.sum(got_l[...], axis=0).astype(LR.dtype)
    slab(BCT, me)[...] = jnp.sum(got_b[...], axis=0)
    lax.fori_loop(1, n, lambda k, _: start(second, k), 0)
    for cp in between[1:2]:
        cp()
    lax.fori_loop(1, n, lambda k, _: wait(second, k), 0)
    swap = [
        seq_copy(LR.at[half_l(c)], LR.at[half_l(c)], c2s.at[0], c2r.at[0], twin),
        seq_copy(BCT.at[half_b(c)], BCT.at[half_b(c)], c2s.at[1], c2r.at[1], twin),
    ]
    for cp in swap:
        cp.start()
    for cp in swap:
        cp.wait()


def sum_scratch(S, PN, T):
    n = S * PN // 2
    dma = pltpu.SemaphoreType.DMA
    chunks = T // LANES
    slabs = chunks * N // n
    return (
        [pltpu.VMEM((n, T // 2 // n, R), F32), pltpu.VMEM((n, slabs, LANES), F32)]
        + [pltpu.VMEM((T // 2, R), F32), pltpu.VMEM((chunks // 2, 2 * N, LANES), F32)]
        + [dma((2,))] * 2 + [dma((n,))] * 8 + [dma((2,))] * 2
    )


class FeatureGather:
    def __init__(self, S, PN, own, buf, s1, r1, s2, r2, cs, cr, ys, yr, ls):
        s, p, z, x = place(S, PN)
        self.zn = zn = S // 2
        self.root = p == z
        self.relay = lax.rem(p + 2, PN) == z
        self.twin_of_root = p + 1 - 2 * lax.rem(p, 2) == z
        self.z = z
        self.moves = z != p
        self.local = pltpu.make_async_copy(own, buf.at[z, x], ls)
        self.first = seq_copy(own, buf.at[z, x], s1, r1.at[z], {"seq": 2 * p + x})
        self.arrive = [
            seq_copy(own, buf.at[t, x], s1, r1.at[t], {"seq": 2 * lax.rem(z + 1, zn) + x})
            for t in range(zn)
        ]
        halves = [buf.at[:, x], buf.at[:, 1 - x]]
        twin = {"tp": p + 1 - 2 * lax.rem(p, 2)}
        far = {"tp": lax.rem(p + 2, PN)}
        self.across = seq_copy(halves[0], halves[0], s2, r2, {"seq": 2 * z + 1 - x})
        self.core = [seq_copy(h, h, cs.at[j], cr.at[j], twin) for j, h in enumerate(halves)]
        self.y = [seq_copy(h, h, ys.at[j], yr.at[j], far) for j, h in enumerate(halves)]

    def start(self):
        @pl.when(self.moves)
        def _():
            self.first.start()

        @pl.when(jnp.logical_not(self.moves))
        def _():
            self.local.start()
            self.local.wait()

    def near(self):
        @pl.when(self.root)
        def _():
            for t in range(self.zn):

                @pl.when(self.z != t)
                def _():
                    self.arrive[t].wait_recv()

            self.across.start()
            self.core[0].start()
            self.y[0].start()

    def far(self):
        @pl.when(self.root)
        def _():
            self.across.wait_recv()
            self.core[1].start()
            self.y[1].start()

        self.pass_on(0)

    def pass_on(self, j):
        @pl.when(self.relay)
        def _():
            self.y[j].wait_recv()
            self.core[j].start()

    def finish(self):
        self.pass_on(1)

        @pl.when(self.moves)
        def _():
            self.first.wait_send()

        @pl.when(self.root)
        def _():
            self.across.wait_send()
            for cp in self.core + self.y:
                cp.wait_send()

        @pl.when(self.relay)
        def _():
            for cp in self.core:
                cp.wait_send()

        @pl.when(jnp.logical_not(jnp.logical_or(self.root, self.relay)))
        def _():
            for cp in self.core:
                cp.wait_recv()

    @staticmethod
    def semaphores(S):
        dma = pltpu.SemaphoreType.DMA
        return [dma, dma((S // 2,)), dma, dma] + [dma((2,))] * 4 + [dma]


class RowGather:
    PARTS = 2

    def __init__(self, S, own, place_of, us, ur, ds, dr, xs, xr, ls):
        s, p, z, x = place(S, 1)
        self.zn, self.z, self.x, self.own, self.place_of = S // 2, z, x, own, place_of
        self.up_sems, self.down_sems, self.x_sems = (us, ur), (ds, dr), (xs, xr)
        self.every = pl.ds(0, own.shape[0])
        self.local = pltpu.make_async_copy(own, place_of(self.every, s), ls)

    def hop(self, t, d, h, up, toward=1):
        size = self.own.shape[0] // self.PARTS
        r = pl.ds(h * size, size)
        there = self.place_of(r, 2 * t + self.x)
        send, recv = self.up_sems if up else self.down_sems
        chip = self.z + (toward if up else -toward)
        src = self.own.at[r] if d == 1 else there
        return seq_copy(src, there, send.at[d, h], recv.at[d, h], {"seq": 2 * chip + self.x})

    def across(self, t):
        block = self.place_of(self.every, 2 * t + self.x)
        send, recv = self.x_sems
        other = {"seq": 2 * self.z + 1 - self.x}
        return seq_copy(block, block, send.at[t], recv.at[t], other)

    def can(self, d, up):
        z, last = self.z, self.zn - 1
        if up:
            return jnp.logical_and(z >= d - 1, z < last)
        return jnp.logical_and(z + d - 1 <= last, z > 0)

    def start(self):
        self.local.start()
        for h in range(self.PARTS):
            for up in (True, False):

                @pl.when(self.can(1, up))
                def _():
                    self.hop(self.z, 1, h, up).start()

        self.local.wait()
        self.across(self.z).start()

    def step(self, d):
        if d >= self.zn:
            return
        for up in (True, False):
            t = self.z - d if up else self.z + d
            there = self.z >= d if up else self.z + d < self.zn

            @pl.when(there)
            def _():
                for h in range(self.PARTS):
                    self.hop(t, d, h, up, -1).wait_recv()
                    if d + 1 < self.zn:

                        @pl.when(self.can(d + 1, up))
                        def _():
                            self.hop(t, d + 1, h, up).start()

                self.across(t).start()

    def finish(self):
        for d in range(1, self.zn):
            for h in range(self.PARTS):
                for up in (True, False):

                    @pl.when(self.can(d, up))
                    def _():
                        t = self.z - (d - 1) if up else self.z + (d - 1)
                        self.hop(t, d, h, up).wait_send()

        for t in range(self.zn):
            self.across(t).wait()

    @staticmethod
    def semaphores(S):
        dma = pltpu.SemaphoreType.DMA
        return [dma((S // 2, RowGather.PARTS))] * 4 + [dma((S // 2,))] * 2 + [dma]


def adam_terms(g, m, s):
    new_m = BETA_ONE * m + (1.0 - BETA_ONE) * g
    new_s = BETA_TWO * s + (1.0 - BETA_TWO) * (g * g)
    root = jnp.sqrt(new_s * (1.0 / (1.0 - BETA_TWO**STEP))) + ADAM_EPSILON
    return new_m, new_s, (new_m * (1.0 / (1.0 - BETA_ONE**STEP))) / root


def softplus(v):
    u = jnp.exp(-jnp.abs(v))
    w = 1.0 + u
    small = jnp.where(w == 1.0, u, jnp.log(w) * (u / jnp.where(w == 1.0, 1.0, w - 1.0)))
    return jnp.maximum(v, 0.0) + small


def masked_sum(acc, aux, r, C):
    total = acc[:, 0:C] * aux[r, 0:1]
    for m in range(1, M):
        total = total + acc[:, m * C : (m + 1) * C] * aux[r, m : m + 1]
    return total


def block_kernel(S, PN, *refs):
    rest = list(refs)
    take = lambda k: [rest.pop(0) for _ in range(k)]
    tok, og, modrow, gain, segs, ch, w_x, m_x, s_x, w_dt, m_dt, s_dt = take(12)
    w_in, m_in, s_in, w_out, m_out, s_out = take(6)
    LO, DN, GG, ROW, MORE, gx, gtap, gch, INV, SCALE, g_in, g_out = take(12)
    tile, toks, ogz, nrm, Wi, Wg, Wo, AUX, GAIN, WD = take(10)
    gsend, grecv, osend, orecv = take(4)
    step, drive, keep, Y, pad, act3, lr, bcp = take(8)
    act, conv, inner, low, bct, pre, H, gated, dgate, dmix, aux, X = take(12)
    gall, dall, DS, DB, dst3, low3, dst, dlow, dbct, dact, gdt = take(11)
    LR2, BCT2, tail, dpar, dinner, part, rowdot, ggs, wdt = take(9)
    wi, wg, wo, wdt_mine, gain_mine, wlr, wbc, wxT, NR, G = take(10)
    gdt_mine, turned, sums_ref, TILE, total_tile = take(5)
    stage, load, store, pair, swaps = take(5)
    ag1, ag2 = take(9), take(9)
    parts_sems = take(4)
    ws = take(12)
    ls = take(1)[0]
    sums = take(16)
    rows_g, rows_d, rows_i = take(7), take(7), take(7)
    mx, mr, ml = take(3)
    last = take(10)
    s, p, z, x = place(S, PN)
    TL, DD = tok.shape
    T = S * TL
    width = DD // S
    quarter = DD // PN
    C = act.shape[1]
    rows = 128

    load_in = pltpu.make_async_copy(w_in, H.at[0 : w_in.shape[0]], stage.at[0])
    load_in.start()
    wide = tok[...].astype(F32)
    inv = lax.rsqrt(jnp.mean(wide * wide, axis=1, keepdims=True) + EPSILON)
    row = jnp.transpose(jnp.broadcast_to(inv, (TL, LANES)))[0:8]
    tile[...] = jnp.where(
        lax.broadcasted_iota(jnp.int32, row.shape, 0) == 0, modrow[...], row
    )
    gain_mine[...] = jnp.broadcast_to(gain[...], gain_mine.shape)
    wdt_mine[...] = w_dt[...].astype(BF16)
    greet_all(S, PN)
    chans = lambda d: pl.ds(pl.multiple_of(d * C, LANES), C)
    block = lambda d: pl.ds(pl.multiple_of(d * width, width), width)
    tokens = Spread(
        S, PN, tok.at[:, pl.ds(pl.multiple_of(p * quarter, LANES), quarter)], toks, *ag1
    )
    small = (
        row_copies(S, lambda d: tile, lambda t: AUX.at[t], ws[0], ws[1])
        + row_copies(S, lambda d: gain_mine, lambda t: GAIN.at[t], ws[2], ws[3])
    )
    dts = row_copies(S, lambda d: wdt_mine.at[:, :, chans(d)], lambda t: WD.at[t], ws[4], ws[5])
    inners = row_copies(S, lambda d: wi.at[d], lambda t: Wi.at[block(t)], ws[6], ws[7])
    zn = S // 2
    across = {"seq": 2 * z + 1 - x}
    pair_rows = pl.ds(pl.multiple_of(x * width, width), width)
    gate_swap = seq_copy(wg.at[:, 1 - x], Wg.at[:, pair_rows], ws[8].at[0], ws[9].at[0], across)
    out_swap = seq_copy(
        wo.at[:, 1 - x], Wo.at[:, :, pair_rows], ws[10].at[0], ws[11].at[0], across
    )

    def along(k, send, recv, sems):
        return seq_copy(
            send.at[k - 1],
            recv.at[k - 1],
            sems[0].at[k],
            sems[1].at[k],
            {"seq": 2 * lax.rem(z + k, zn) + x},
        )

    gates = [along(k, gsend, grecv, parts_sems[0:2]) for k in range(1, zn)]
    backs = [along(k, osend, orecv, parts_sems[2:4]) for k in range(1, zn)]
    cotangent = FeatureGather(S, PN, og, ogz, *ag2)
    for cp in small:
        cp.start()
    tokens.start()
    load_in.wait()
    stride = 2 * S
    for m in range(M):
        for b in range(S):
            r = pl.ds(m * width * stride + 2 * b, width, stride=stride)
            wi[b, :, m * C : (m + 1) * C] = H[r, :].astype(BF16)
    for cp in inners + dts:
        cp.start()
    cotangent.start()
    for m in range(M):
        for b in range(S):
            r = pl.ds(m * width * stride + 2 * b + 1, width, stride=stride)
            wg[b // 2, b % 2, :, m * C : (m + 1) * C] = H[r, :].astype(BF16)
    gate_swap.start()
    load_out = pltpu.make_async_copy(w_out, H.at[0 : w_out.shape[0]], stage.at[1])
    load_out.start()
    own = [
        pltpu.make_async_copy(tile, AUX.at[s], ls.at[0]),
        pltpu.make_async_copy(gain_mine, GAIN.at[s], ls.at[1]),
        pltpu.make_async_copy(wdt_mine.at[:, :, chans(s)], WD.at[s], ls.at[2]),
        pltpu.make_async_copy(wi.at[s], Wi.at[block(s)], ls.at[3]),
        pltpu.make_async_copy(wg.at[:, x], Wg.at[:, pair_rows], ls.at[4]),
    ]
    for cp in own:
        cp.start()
    for m in range(M):
        wlr[m * C : (m + 1) * C, :] = jnp.transpose(w_x[m, 0:R, :]).astype(BF16)
        wbc[:, m * C : (m + 1) * C] = w_x[m, R : R + 2 * N, :].astype(BF16)
        wxT[m] = w_x[m].astype(BF16)
    load_out.wait()
    tiles = width // LANES
    for m in range(M):
        for b in range(S):
            rows_b = H[(m * S + b) * C * tiles : (m * S + b + 1) * C * tiles, :]
            pieces = rows_b.reshape(C // 8, tiles, 8, LANES)
            for t in range(tiles):
                wo[b // 2, b % 2, m * C : (m + 1) * C, t * LANES : (t + 1) * LANES] = (
                    pieces[:, t].reshape(C, LANES).astype(BF16)
                )
    out_swap.start()
    own.append(pltpu.make_async_copy(wo.at[:, x], Wo.at[:, :, pair_rows], ls.at[5]))
    own[-1].start()
    for cp in own:
        cp.wait()
    tokens.forward()
    cotangent.near()
    for cp in small:
        cp.wait()
    lane = lax.broadcasted_iota(jnp.int32, (TL, 8), 1)

    def columns(t, _):
        r = pl.ds(pl.multiple_of(t * TL, TL), TL)
        turned = jnp.transpose(jnp.concatenate([AUX[t]] * (LANES // 8), axis=0))
        mask = (turned[:, 0:1] == lane.astype(F32)).astype(F32)
        aux[r, :] = jnp.where(
            lane < M, mask, jnp.where(lane == 7, turned[:, 1:2], segs[r, :])
        )
        return 0

    lax.fori_loop(0, S, columns, 0)
    aux[T : T + 8, :] = jnp.zeros((8, 8), F32)
    tokens.finish()
    per = quarter // width

    def norm(t, _):
        r = pl.ds(pl.multiple_of(t * TL, TL), TL)
        scale = aux[r, 7:8]
        for q in range(PN):
            scaled = toks[q, t].astype(F32) * scale
            for j in range(per):
                part = scaled[:, j * width : (j + 1) * width] * GAIN[q * per + j, 0:1, :]
                nrm[r, q * quarter + j * width : q * quarter + (j + 1) * width] = part.astype(BF16)
        return 0

    lax.fori_loop(0, S, norm, 0)
    big = 256
    features = pl.ds(pl.multiple_of(z * 2 * width, 2 * width), 2 * width)

    def gate_part(k):
        def body(i, _):
            r = pl.ds(pl.multiple_of(i * big, big), big)
            w = Wg[lax.rem(z + k, zn)]
            value = masked_sum(dot(nrm[r, features], w), aux, r, C)
            if k == 0:
                DS[r, :] = value
            else:
                gsend[k - 1, r, :] = value.astype(BF16)
            return 0

        lax.fori_loop(0, T // big, body, 0)

    def back_part(k):
        def body(i, _):
            r = pl.ds(pl.multiple_of(i * big, big), big)
            w = Wo[lax.rem(z + k, zn)]
            chips = big // TL // 2
            g = ogz[pl.ds(i * chips, chips)].reshape(big, 2 * width)
            value = masked_sum(dot(g, w, NT), aux, r, C)
            if k == 0:
                DB[r, :] = value
            else:
                osend[k - 1, r, :] = value.astype(BF16)
            return 0

        lax.fori_loop(0, T // big, body, 0)

    gate_swap.wait()
    gate_part(1)
    gates[0].start()
    gate_part(2)
    gates[1].start()
    gate_part(3)
    gates[2].start()
    gate_part(0)
    for cp in inners:
        cp.wait()

    pad[0:8, :] = jnp.zeros((8, C), F32)

    def first(i, _):
        r = pl.ds(pl.multiple_of(i * big, big), big)
        value = masked_sum(dot(nrm[r, :], Wi[...]), aux, r, C).astype(BF16)
        inner[r, :] = value
        pad[pl.ds(pl.multiple_of(i * big + 8, 8), big), :] = value.astype(F32)
        return 0

    lax.fori_loop(0, T // big, first, 0)

    def convolve(i, _):
        r = pl.ds(pl.multiple_of(i * rows, rows), rows)
        window = pad[pl.ds(pl.multiple_of(i * rows, rows), rows + 8), :]
        v = jnp.broadcast_to(ch[K : K + 1, :], (rows, C))
        for k in range(K):
            term = ch[k : k + 1, :] * window[8 - (K - 1) + k : 8 - (K - 1) + k + rows]
            v = v + (term * aux[r, M + k : M + k + 1] if k < K - 1 else term)
        conv[r, :] = v
        a = (v / (1.0 + jnp.exp(-v))).astype(BF16)
        act[r, :] = a
        a_wide = a.astype(F32)
        for m in range(M):
            act3[r, m * C : (m + 1) * C] = (a_wide * aux[r, m : m + 1]).astype(BF16)
        lr[r, :] = dot(act3[r, :], wlr[...])
        bcp[i] = dot(wbc[...], act3[r, :], NT)
        return 0

    lax.fori_loop(0, T // rows, convolve, 0)
    cotangent.far()

    def during_first():
        cotangent.finish()
        out_swap.wait()
        back_part(1)
        back_part(2)
        back_part(3)

    def during_second():
        backs[0].start()
        backs[1].start()
        back_part(0)

    sum_over_all(
        S, PN, lr, bcp, low, bct, *sums, between=(during_first, during_second)
    )
    backs[2].start()
    for cp in dts:
        cp.wait()
    for m in range(M):
        for t in range(S):
            h = R // S
            wdt[m * R + t * h : m * R + (t + 1) * h, :] = WD[t, m]

    def prepare(i, _):
        r = pl.ds(pl.multiple_of(i * rows, rows), rows)
        low_wide = low[r, :].astype(F32)
        bias = jnp.zeros((rows, C), F32)
        for m in range(M):
            mask = aux[r, m : m + 1]
            masked = (low_wide * mask).astype(BF16)
            bias = bias + mask * ch[K + 2 + m : K + 3 + m, :]
            low3[r, m * R : (m + 1) * R] = masked
        bias = bias + dot(low3[r, :], wdt[...])
        pre[r, :] = bias
        st = softplus(bias)
        step[r, :] = st
        drive[r, :] = st * act[r, :].astype(F32)
        keep[r, :] = jnp.broadcast_to(aux[r, 6:7], (rows, C))
        return 0

    lax.fori_loop(0, T // rows, prepare, 0)
    scan_forward(T, C, bct, ch, step, drive, keep, H, Y)
    for cp in gates + backs:
        cp.wait()

    def finish(i, _):
        r = pl.ds(pl.multiple_of(i * rows, rows), rows)
        mixed = Y[r, :] + ch[K + 1 : K + 2, :] * act[r, :].astype(F32)
        g, d = DS[r, :], DB[r, :]
        for k in range(zn - 1):
            g = g + grecv[k, r, :].astype(F32)
            d = d + orecv[k, r, :].astype(F32)
        sig = 1.0 / (1.0 + jnp.exp(-g))
        gated[r, :] = (mixed * (g * sig)).astype(BF16)
        dmix[r, :] = d * (g * sig)
        dgate[r, :] = (d * mixed * (sig * (1.0 + g * (1.0 - sig)))).astype(BF16)
        return 0

    lax.fori_loop(0, T // rows, finish, 0)
    half = lambda t, k: pl.ds(pl.multiple_of((2 * t + k) * C, LANES), C)
    gathers = [
        RowGather(S, gated, lambda r, t: gall.at[r, chans(t)], *rows_g),
        RowGather(S, dgate, lambda r, t: dall.at[r, half(t, 1)], *rows_d),
        RowGather(S, dinner, lambda r, t: dall.at[r, half(t, 0)], *rows_i),
    ]
    gathers[0].start()
    gathers[1].start()
    mine = pl.ds(pl.multiple_of(lax.rem(s, per) * width, width), width)
    NR[...] = nrm[:, pl.ds(pl.multiple_of(s * width, width), width)]

    def own_features(t, _):
        r = pl.ds(pl.multiple_of(t * TL, TL), TL)
        X[r, :] = toks[lax.div(s, per), t, :, mine]
        G[r, :] = ogz[lax.div(t, 2), lax.rem(t, 2), :, mine]
        return 0

    lax.fori_loop(0, S, own_features, 0)
    INV[...] = jnp.broadcast_to(inv, INV.shape)
    scan_backward(
        pre, H, dmix, act, bct, aux, ch, wdt, low,
        dlow, dbct, gdt, gch, dact, step, drive, keep, DS, DB, dst3, low3, dst,
        [(T // LANES * 3 // 4, lambda: gathers[0].step(1))],
    )
    h = R // S
    part_dt = lambda d: gdt.at[:, pl.ds(pl.multiple_of(d * h, 8), h), :]
    more = row_copies(S, part_dt, lambda t: MORE.at[t], mx, mr)
    more_own = pltpu.make_async_copy(part_dt(s), MORE.at[s], ml)
    for cp in more + [more_own]:
        cp.start()
    def during_second_sum():
        gathers[1].step(1)
        gathers[0].step(3)

    sum_over_all(
        S, PN, dlow, dbct, LR2, BCT2, *sums,
        between=(lambda: gathers[0].step(2), during_second_sum),
    )
    convolve_backward(
        LR2, BCT2, act, conv, aux, ch, wxT, dact, dinner, gx, gtap, pad, tail, act3, dpar
    )
    gathers[2].start()
    for cp in more + [more_own]:
        cp.wait()
    gathers[0].finish()

    large = 512

    def layer(i, _):
        r = pl.ds(pl.multiple_of(i * large, large), large)

        total = jnp.zeros((large, width), F32)
        for m in range(M):
            w = jnp.concatenate(
                [wo[b // 2, b % 2, m * C : (m + 1) * C, :] for b in range(S)], axis=0
            )
            total = total + dot(gall[r, :], w) * aux[r, m : m + 1]
        part[0, r, :] = total.astype(BF16)
        return 0

    lax.fori_loop(0, T // large, layer, 0)
    stream = Stream(H, load, (w_out, m_out, s_out), 6, sums_ref.at[1])
    stream.start(0)

    def out_gradient(i, rows_of):
        m, k = i // 2, i % 2
        wide = gall[:, k * (S // 2) * C : (k + 1) * (S // 2) * C].astype(F32)
        turned[...] = jnp.transpose((wide * aux[0:T, m : m + 1]).astype(BF16))
        g = dot(turned[...], G[...])
        parts = [
            g[:, t * LANES : (t + 1) * LANES].reshape(-1, 8, LANES) for t in range(tiles)
        ]
        H[rows_of, :] = jnp.stack(parts, axis=1).reshape(-1, LANES)

    to_out = LastBlocks(
        S, PN, part.at[0], LO, pair.at[0], pair.at[1], last[0], last[1], swaps.at[0], ls.at[1]
    )
    to_out.start()
    gathers[1].step(2)
    stores = [None, None]
    for i in range(6):
        k = i % 2
        if stores[k] is not None:
            stores[k].wait()
        rows_of = pl.ds((6 + k) * 1024, 1024)
        out_gradient(i, rows_of)
        stores[k] = pltpu.make_async_copy(
            H.at[rows_of], g_out.at[i * 1024 : (i + 1) * 1024], store.at[k]
        )
        stores[k].start()
        stream.norms(i, i // 2, (6 + k) * 1024)
        if i == 0:
            gathers[2].step(1)
        elif i == 1:
            gathers[1].step(3)
        elif i == 3:
            gathers[2].step(2)
        elif i == 5:
            gathers[2].step(3)
    for cp in stores:
        cp.wait()
    stream = Stream(H, load, (w_in, m_in, s_in), 12, sums_ref.at[0])
    stream.start(0)
    gathers[1].finish()
    spare = 6 * 1024 + 2 * width * stride

    def half_product(r, h, m):
        cols = slice(m * C, (m + 1) * C)
        v = jnp.concatenate(
            [dall[r, (2 * b + h) * C : (2 * b + h + 1) * C] for b in range(S)], axis=1
        )
        pieces = [wg[b // 2, b % 2, :, cols] if h else wi[b, :, cols] for b in range(S)]
        return dot(v, jnp.concatenate(pieces, axis=1), NT)

    def gate_back(i, _):
        r = pl.ds(pl.multiple_of(i * large, large), large)
        d = half_product(r, 1, 0) * aux[r, 0:1]
        for m in range(1, M):
            d = d + half_product(r, 1, m) * aux[r, m : m + 1]
        for t in range(tiles):
            at = pl.ds(pl.multiple_of(spare + t * T + i * large, large), large)
            H[at, :] = d[:, t * LANES : (t + 1) * LANES]
        return 0

    lax.fori_loop(0, T // large, gate_back, 0)
    gathers[2].finish()

    def normed_back(i, total):
        r = pl.ds(pl.multiple_of(i * large, large), large)

        d = jnp.concatenate(
            [
                H[pl.ds(pl.multiple_of(spare + t * T + i * large, large), large), :]
                for t in range(tiles)
            ],
            axis=1,
        )
        for m in range(M):
            d = d + half_product(r, 0, m) * aux[r, m : m + 1]
        scaled = X[r, :].astype(F32) * aux[r, 7:8]
        gained = d * gain_mine[0:1, :]
        part[1, r, :] = gained.astype(BF16)
        along = jnp.sum(gained * scaled, axis=1, keepdims=True)
        for j in range(large // TL):
            turned = jnp.transpose(jnp.broadcast_to(along[j * TL : (j + 1) * TL], (TL, LANES)))
            rowdot[i * (large // TL) + j] = turned[0:8]
        return total + jnp.sum(d * scaled, axis=0, keepdims=True)

    total = lax.fori_loop(0, T // large, normed_back, jnp.zeros((1, width), F32))
    ggs[...] = jnp.broadcast_to(total, ggs.shape)
    to_in = LastBlocks(
        S, PN, part.at[1], DN, pair.at[2], pair.at[3], last[2], last[3], swaps.at[1], ls.at[3]
    )
    to_in.start()
    gains = [
        seq_copy(ggs, GG.at[k], last[4].at[k], last[5].at[k], {"tp": lax.rem(p + k, PN)})
        for k in range(1, PN)
    ]
    for cp in gains:
        cp.start()
    n = S * PN
    me = s * PN + p

    def to_all(src, dst, send, recv):
        def copy(k):
            j = lax.rem(me + k, n)
            device = {"seq": lax.div(j, PN), "tp": lax.rem(j, PN)}
            return seq_copy(src(lax.div(j, PN)), dst.at[k], send.at[k], recv.at[k], device)

        def start(k, _):
            copy(k).start()
            return 0

        def wait(k, _):
            copy(k).wait()
            return 0

        return (
            lambda: lax.fori_loop(1, n, start, 0),
            lambda: lax.fori_loop(1, n, wait, 0),
        )

    send_row, wait_row = to_all(lambda t: rowdot.at[t], ROW, last[6], last[7])
    send_row()
    GG[0] = ggs[...]
    ROW[0] = rowdot[s]

    stores = [None, None]
    per_m = width * stride
    for m in range(M):
        k = m % 2
        if stores[k] is not None:
            stores[k].wait()
        first_row = 6 * 1024 + k * per_m
        turned[0:width, :] = jnp.transpose(
            (NR[...].astype(F32) * aux[0:T, m : m + 1]).astype(BF16)
        )
        for b in range(S):
            g = dot(turned[0:width, :], dall[:, 2 * b * C : 2 * (b + 1) * C])
            H[pl.ds(first_row + 2 * b, width, stride=stride), :] = g[:, 0:C]
            H[pl.ds(first_row + 2 * b + 1, width, stride=stride), :] = g[:, C : 2 * C]
        stores[k] = pltpu.make_async_copy(
            H.at[first_row : first_row + per_m], g_in.at[m * per_m : (m + 1) * per_m], store.at[k]
        )
        stores[k].start()
        for q in range(per_m // 1024):
            stream.norms(m * (per_m // 1024) + q, m, first_row + q * 1024)
    lane = lax.broadcasted_iota(jnp.int32, (8, LANES), 1)
    total = jnp.zeros((8, LANES), F32)
    square = lambda v: jnp.sum(v * v)
    for t in range(S):
        gdt_mine[:, :, t * C : (t + 1) * C] = MORE[t]
    for m in range(M):
        x = adam_terms(gx[m], m_x[m], s_x[m])[2] + WEIGHT_DECAY * w_x[m]
        d = adam_terms(gdt_mine[m], m_dt[m], s_dt[m])[2] + WEIGHT_DECAY * w_dt[m]
        for k, value in enumerate((
            jnp.sum(sums_ref[0, m, 0]), square(w_x[m]), square(w_dt[m]), jnp.sum(sums_ref[1, m, 0]),
            jnp.sum(sums_ref[0, m, 1]), square(x), square(d), jnp.sum(sums_ref[1, m, 1]),
        )):
            total = jnp.where(lane == k * M + m, value, total)
    total_tile[...] = total
    send_tile, wait_tile = to_all(lambda t: total_tile, TILE, last[8], last[9])
    send_tile()
    TILE[0] = total
    for cp in gains:
        cp.wait()
    wait_row()
    wait_tile()
    total = jnp.sum(TILE[...], axis=0)
    below = pltpu.roll(total, LANES - 4 * M, 1)
    SCALE[...] = MATRIX_RATE * (jnp.sqrt(total) / jnp.sqrt(below))
    for cp in stores:
        cp.wait()
    to_out.finish()
    to_in.finish()


class Stream:
    def __init__(self, H, sems, refs, steps, sums):
        self.H, self.sems, self.refs, self.steps, self.sums = H, sems, refs, steps, sums
        sums[...] = jnp.zeros(sums.shape, F32)

    def copies(self, i):
        k = i % 2
        return [
            pltpu.make_async_copy(
                ref.at[i * 1024 : (i + 1) * 1024],
                self.H.at[pl.ds((3 * k + a) * 1024, 1024)],
                self.sems.at[k, a],
            )
            for a, ref in enumerate(self.refs)
        ]

    def start(self, i):
        for cp in self.copies(i):
            cp.start()

    def norms(self, i, m, g_row):
        for cp in self.copies(i):
            cp.wait()
        if i + 1 < self.steps:
            self.start(i + 1)
        H, k, rows = self.H, i % 2, 128

        def body(t, sums):
            at = lambda first: pl.ds(pl.multiple_of(first + t * rows, rows), rows)
            weight = H[at(3 * k * 1024), :]
            ratio = adam_terms(
                H[at(g_row), :], H[at((3 * k + 1) * 1024), :], H[at((3 * k + 2) * 1024), :]
            )[2]
            direction = ratio + WEIGHT_DECAY * weight
            fold = lambda v: jnp.sum((v * v).reshape(rows // 8, 8, LANES), axis=0)
            return sums[0] + fold(weight), sums[1] + fold(direction)

        a, b = lax.fori_loop(0, 1024 // rows, body, (self.sums[m, 0], self.sums[m, 1]))
        self.sums[m, 0] = a
        self.sums[m, 1] = b


class LastBlocks:
    def __init__(self, S, PN, part, out, other, both, send, recv, swap, ls):
        s, p = lax.axis_index("seq"), lax.axis_index("tp")
        ratio = S // PN
        self.S, self.PN, self.ratio = S, PN, ratio
        self.s, self.p, self.home = s, p, lax.div(s, ratio)
        self.y, self.c = lax.div(p, 2), lax.rem(p, 2)
        self.slot = lax.rem(s, ratio) * (PN // 2) + self.y
        self.part, self.out, self.other, self.both = part, out, other, both
        self.send, self.recv, self.ls = send, recv, ls
        self.half = part.shape[0] // 2
        self.TL = part.shape[0] // S
        self.swap = seq_copy(
            part.at[self.rows(1 - self.c)],
            other,
            swap.at[0],
            swap.at[1],
            {"tp": p + 1 - 2 * self.c},
        )

    def rows(self, c):
        return pl.ds(pl.multiple_of(c * self.half, self.half), self.half)

    def seq(self, k):
        return self.c * (self.S // 2) + k

    def away(self, k):
        return jnp.logical_or(self.s != self.seq(k), self.home != self.p)

    def copy(self, k):
        return seq_copy(
            self.both.at[k * self.TL : (k + 1) * self.TL],
            self.out.at[self.slot],
            self.send.at[k],
            self.recv.at[self.slot],
            {"seq": self.seq(k), "tp": self.home},
        )

    def own(self, k):
        return pltpu.make_async_copy(
            self.both.at[k * self.TL : (k + 1) * self.TL], self.out.at[self.slot], self.ls
        )

    def start(self):
        self.swap.start()
        self.swap.wait()
        mine = self.part[self.rows(self.c), :].astype(F32)
        self.both[...] = (mine + self.other[...].astype(F32)).astype(BF16)
        for k in range(self.S // 2):

            @pl.when(self.away(k))
            def _():
                self.copy(k).start()

            @pl.when(jnp.logical_not(self.away(k)))
            def _():
                self.own(k).start()

    def finish(self):
        for k in range(self.S // 2):

            @pl.when(self.away(k))
            def _():
                self.copy(k).wait_send()

            @pl.when(jnp.logical_not(self.away(k)))
            def _():
                self.own(k).wait()

        core = lax.div(self.s, self.S // 2)
        for h in range(self.ratio):
            for y in range(self.PN // 2):
                t, q = self.ratio * self.p + h, 2 * y + core
                i = h * (self.PN // 2) + y

                @pl.when(jnp.logical_or(t != self.s, self.p != q))
                def _():
                    seq_copy(
                        self.both.at[0 : self.TL],
                        self.out.at[i],
                        self.send.at[0],
                        self.recv.at[i],
                        {"seq": t, "tp": q},
                    ).wait_recv()


def scan_forward(T, C, bct, ch, step, drive, keep, H, Y):
    base = -jnp.exp(ch[K + 2 + M : K + 2 + M + N, :])
    H[0:N, :] = jnp.zeros((N, C), F32)

    def chunk(c, h):
        cols = bct[c]
        for i in range(LANES // 8):
            t0 = pl.multiple_of(c * LANES + 8 * i, 8)
            r = pl.ds(t0, 8)
            st, dr, kp = step[r, :], drive[r, :], keep[r, :]
            ys = []
            for j in range(8):
                k = 8 * i + j
                rate = jnp.exp(st[j : j + 1] * base) * kp[j : j + 1]
                h = rate * h + dr[j : j + 1] * cols[0:N, k : k + 1]
                H[pl.ds(pl.multiple_of((t0 + j + 1) * N, N), N), :] = h
                ys.append(jnp.sum(cols[N : 2 * N, k : k + 1] * h, axis=0, keepdims=True))
            Y[r, :] = jnp.concatenate(ys, axis=0)
        return h

    lax.fori_loop(0, T // LANES, chunk, jnp.zeros((N, C), F32))


def lane_sums(values):
    v = jnp.concatenate(values, axis=0)
    high = v.astype(BF16)
    low = (v - high.astype(F32)).astype(BF16)
    sums = dot(jnp.concatenate([high, low], axis=1), jnp.ones((2 * v.shape[1], LANES), BF16))
    return [sums[k * N : (k + 1) * N] for k in range(len(values))]


def scan_backward(
    pre, H, dmix, act, bct, aux, ch, wdt, low,
    dlow, dbct, gdt, gch, dact, step, drive, keep, DS, DB, dst3, low3, dst, hooks,
):
    T, C = act.shape
    rows = 128

    base = -jnp.exp(ch[K + 2 + M : K + 2 + M + N, :])
    lane = lax.broadcasted_iota(jnp.int32, (N, LANES), 1)
    nothing = jnp.zeros((N, C), F32)
    chunks = T // LANES

    def chunk(cc, carry):
        c = chunks - 1 - cc
        cols = bct[c]
        flow, hcur, gacc = carry
        accb = accc = jnp.zeros((N, LANES), F32)
        for i in reversed(range(LANES // 8)):
            t0 = pl.multiple_of(c * LANES + 8 * i, 8)
            r = pl.ds(t0, 8)
            st, dr, kp, dm = step[r, :], drive[r, :], keep[r, :], dmix[r, :]
            ds, db, ub, uc = [None] * 8, [None] * 8, [None] * 8, [None] * 8
            for j in reversed(range(8)):
                k = 8 * i + j
                back = cols[N : 2 * N, k : k + 1] * dm[j : j + 1] + flow
                rate = jnp.exp(st[j : j + 1] * base) * kp[j : j + 1]
                hprev = H[pl.ds(pl.multiple_of((t0 + j) * N, N), N), :]
                uc[j] = dm[j : j + 1] * hcur
                ub[j] = back * dr[j : j + 1]
                flow = rate * back
                dlog = flow * hprev
                gacc = gacc + dlog * st[j : j + 1]
                ds[j] = jnp.sum(dlog * base, axis=0, keepdims=True)
                db[j] = jnp.sum(back * cols[0:N, k : k + 1], axis=0, keepdims=True)
                hcur = hprev
            DS[r, :] = jnp.concatenate(ds, axis=0)
            DB[r, :] = jnp.concatenate(db, axis=0)
            sb, sc = lane_sums(ub), lane_sums(uc)
            for j in range(8):
                here = lane == 8 * i + j
                accb = jnp.where(here, sb[j], accb)
                accc = jnp.where(here, sc[j], accc)
        dbct[c, 0:N, :] = accb
        dbct[c, N : 2 * N, :] = accc
        return flow, hcur, gacc

    carry, done = (nothing, H[T * N : (T + 1) * N, :], nothing), 0
    for upto, call in hooks + [(chunks, None)]:
        carry = lax.fori_loop(done, upto, chunk, carry)
        done = upto
        if call is not None:
            call()
    gacc = carry[2]

    def finish(i, carry):
        skip, bias = carry
        r = pl.ds(pl.multiple_of(i * rows, rows), rows)
        a = act[r, :].astype(F32)
        back_b = DB[r, :]
        grad = DS[r, :] + a * back_b
        d = (grad / (1.0 + jnp.exp(-pre[r, :]))).astype(BF16)
        dst[r, :] = d
        wide = d.astype(F32)
        sums = []
        for m in range(M):
            mask = aux[r, m : m + 1]
            masked = wide * mask
            sums.append(jnp.sum(masked, axis=0, keepdims=True))
            dst3[r, m * C : (m + 1) * C] = masked.astype(BF16)
        total = dot(dst3[r, 0:C], wdt[0:R, :], NT)
        for m in range(1, M):
            total = total + dot(dst3[r, m * C : (m + 1) * C], wdt[m * R : (m + 1) * R, :], NT)
        dlow[r, :] = total
        dact[r, :] = dmix[r, :] * ch[K + 1 : K + 2, :] + step[r, :] * back_b
        skip = skip + jnp.sum(dmix[r, :] * a, axis=0, keepdims=True)
        return skip, bias + jnp.concatenate(sums, axis=0)

    skip, bias = lax.fori_loop(
        0, T // rows, finish, (jnp.zeros((1, C), F32), jnp.zeros((M, C), F32))
    )
    gch[0:1, :] = skip
    gch[1 : 1 + M, :] = bias
    gch[1 + M : 1 + M + N, :] = base * gacc
    for m in range(M):
        gdt[m] = dot(low3[:, m * R : (m + 1) * R], dst[...], TN)


def convolve_backward(
    dlow, dbct, act, conv, aux, ch, wxT, dact, dinner, gx, gtap, pad, tail, act3, dpar,
):
    T, C = act.shape
    rows = 128
    tail[T : T + 8, :] = jnp.zeros((8, C), F32)
    blank = jnp.zeros((LANES - 2 * N, LANES), F32)

    def fill(i, _):
        r = pl.ds(pl.multiple_of(i * rows, rows), rows)
        turned = jnp.transpose(jnp.concatenate([dbct[i], blank], axis=0))
        dpar[r, 0:R] = dlow[r, :]
        dpar[r, R : R + 2 * N] = turned[:, 0 : 2 * N].astype(BF16)
        wide = dpar[r, :].astype(F32)
        total = dact[r, :]
        for m in range(M):
            mask = aux[r, m : m + 1]
            total = total + dot((wide * mask).astype(BF16), wxT[m])
        v = conv[r, :]
        sig = 1.0 / (1.0 + jnp.exp(-v))
        tail[r, :] = (total * (sig * (1.0 + v * (1.0 - sig)))).astype(BF16).astype(F32)
        return 0

    lax.fori_loop(0, T // rows, fill, 0)

    def body(i, sums):
        r = pl.ds(pl.multiple_of(i * rows, rows), rows)
        window = pad[pl.ds(pl.multiple_of(i * rows, rows), rows + 8), :]
        d = tail[r, :]
        ahead = tail[pl.ds(pl.multiple_of(i * rows, rows), rows + 8), :]
        same = aux[pl.ds(pl.multiple_of(i * rows, rows), rows + 8), :]
        total = ch[K - 1 : K, :] * d
        new = []
        for k in range(K):
            off = K - 1 - k
            shifted = window[8 - off : 8 - off + rows]
            if k < K - 1:
                shifted = shifted * aux[r, M + k : M + k + 1]
                total = total + ch[k : k + 1, :] * (
                    ahead[off : off + rows] * same[off : off + rows, M + k : M + k + 1]
                )
            new.append(jnp.sum(d * shifted, axis=0, keepdims=True))
        new.append(jnp.sum(d, axis=0, keepdims=True))
        dinner[r, :] = total.astype(BF16)
        return sums + jnp.concatenate(new, axis=0)

    gtap[0 : K + 1, :] = lax.fori_loop(0, T // rows, body, jnp.zeros((K + 1, C), F32))
    for m in range(M):
        gx[m] = dot(dpar[...], act3[:, m * C : (m + 1) * C], TN)


def block_call(S, PN, args, T, C, width):
    dma = pltpu.SemaphoreType.DMA
    TL, DD = args[0].shape
    chunks = T // LANES
    zn = S // 2
    f = lambda *shape: sds(shape)
    b = lambda *shape: sds(shape, BF16)
    vf = lambda *shape: pltpu.VMEM(shape, F32)
    vb = lambda *shape: pltpu.VMEM(shape, BF16)
    n = S * PN
    out = (
        b(S // 2, TL, width), b(S // 2, TL, width), f(PN, 8, width), f(n, 8, LANES),
        f(S, M, R // S, C), f(M, R + 2 * N, C), f(8, C), f(1 + M + N, C),
        f(TL, LANES), f(8, LANES), f(M * width * 2 * S, C), f(M * S * width, C),
    )
    scratch = (
        [vf(8, TL), vb(PN, S, TL, DD // PN), vb(zn, 2, TL, DD // PN), vb(T, DD)]
        + [vb(DD, M * C), vb(zn, 2 * width, M * C), vb(zn, M * C, 2 * width)]
        + [vf(S, 8, TL), vf(S, 8, width)]
        + [vb(S, M, R // S, C)]
        + [vb(zn - 1, T, C)] * 4
        + [vf(T, C)] * 4
        + [vf(T + 8, C), vb(T, M * C), vf(T, R), vf(chunks, 2 * N, LANES)]
        + [vb(T, C), vf(T, C), vb(T, C), vb(T, R), vf(chunks, 2 * N, LANES), vf(T, C)]
        + [vf((T + 1) * N, C), vb(T, C), vb(T, C), vf(T, C), vf(T + 8, 8), vb(T, width)]
        + [vb(T, S * C), vb(T, 2 * S * C), vf(T, C), vf(T, C), vb(T, M * C), vb(T, M * R)]
        + [vb(T, C), vf(T, R), vf(chunks, 2 * N, LANES), vf(T, C), vf(M, R, C)]
        + [vb(T, R), vf(chunks, 2 * N, LANES), vf(T + 8, C), vb(T, R + 2 * N), vb(T, C)]
        + [vb(2, T, width), vf(S, 8, LANES), vf(8, width), vb(M * R, C)]
        + [vb(S, width, M * C), vb(zn, 2, width, M * C), vb(zn, 2, M * C, width)]
        + [vb(M, R // S, S * C)]
        + [vf(8, width), vb(M * C, R), vb(2 * N, M * C), vb(M, R + 2 * N, C), vb(T, width)]
        + [vb(T, width), vf(M, R // S, S * C), vb(S * C // 2, T), vf(2, M, 2, 8, LANES)]
        + [vf(n, 8, LANES), vf(8, LANES), dma((2,)), dma((2, 3)), dma((2,))]
        + [vb(4, T // 2, width), dma((2, 2))]
        + Spread.semaphores(S)
        + FeatureGather.semaphores(S)
        + [dma((zn,))] * 4
        + [dma((S,))] * 12
        + [dma((6,))]
        + sum_scratch(S, PN, T)
        + RowGather.semaphores(S) * 3
        + [dma((S,)), dma((S,)), dma]
        + [dma((S,))] * 4 + [dma((PN,))] * 2 + [dma((n,))] * 4
    )
    vm, hb = pl.BlockSpec(memory_space=pltpu.VMEM), pl.BlockSpec(memory_space=pl.ANY)
    return pl.pallas_call(
        functools.partial(block_kernel, S, PN),
        out_shape=out,
        in_specs=[vm] * (len(args) - 6) + [hb] * 6,
        out_specs=[vm] * (len(out) - 2) + [hb] * 2,
        scratch_shapes=scratch,
        compiler_params=pltpu.CompilerParams(
            collective_id=0, has_side_effects=True, vmem_limit_bytes=VMEM_LIMIT
        ),
    )(*args)


def update_rows(scale, which, k, g, w, m, s, avg, nw, nm, ns, na):
    factor = scale[0:1, M * which : M * which + 1]
    for i in range(1, M):
        lane = M * which + i
        factor = jnp.where(k == i, scale[0:1, lane : lane + 1], factor)
    rows = 128

    def body(t, _):
        r = pl.ds(pl.multiple_of(t * rows, rows), rows)
        weight = w[r, :]
        new_m, new_s, ratio = adam_terms(g[r, :], m[r, :], s[r, :])
        new = weight - factor * (ratio + WEIGHT_DECAY * weight)
        nw[r, :] = new
        nm[r, :] = new_m
        ns[r, :] = new_s
        na[r, :] = AVERAGE_KEEP * avg[r, :] + (1.0 - AVERAGE_KEEP) * new
        return 0

    lax.fori_loop(0, w.shape[0] // rows, body, 0)


def update_kernel(S, PN, count, outs, *refs):
    ins, outputs, scratch = refs[: 10 + count], refs[10 + count : 18 + count + outs], refs[18 + count + outs :]
    scale = ins[10 + 6]
    step = pl.program_id(0)
    k = lax.div(step, pl.num_programs(0) // M)
    update_rows(scale, 0, k, *ins[0:5], *outputs[0:4])
    update_rows(scale, 3, k, *ins[5:10], *outputs[4:8])

    @pl.when(step == 2)
    def _():
        rest_kernel(S, PN, *ins[10:], *outputs[8:], *scratch)


def update_all(S, PN, in_rows, out_rows, rest, rest_out, scratch):
    steps = 2 * M

    def piece(v):
        return pl.BlockSpec((v.shape[0] // steps, v.shape[1]), lambda i: (i, 0))

    def whole(v):
        return pl.BlockSpec(v.shape, lambda i: (0,) * len(v.shape))

    arrays = (*in_rows, *out_rows)
    new = (sds(in_rows[0].shape),) * 4 + (sds(out_rows[0].shape),) * 4
    return pl.pallas_call(
        functools.partial(update_kernel, S, PN, len(rest), len(rest_out)),
        out_shape=new + tuple(rest_out),
        grid=(steps,),
        in_specs=[piece(v) for v in arrays] + [whole(v) for v in rest],
        out_specs=[piece(v) for v in new] + [whole(v) for v in rest_out],
        scratch_shapes=scratch,
        compiler_params=pltpu.CompilerParams(vmem_limit_bytes=VMEM_LIMIT),
    )(*arrays, *rest)


def rest_kernel(
    S, PN, tok, og, LO, DN, ROW, INV, scale, gx, more, gtap, gch, GG, wx, mx, sx, ax, wd, md, sd, ad,
    ch, mc, sc, ac, gn, mg, sg, ag,
    layer, grad, nwx, nmx, nsx, nax, nwd, nmd, nsd, nad, nwc, nmc, nsc, nac, nwg, nmg, nsg, nag, gc, gd,
):
    p = lax.axis_index("tp")
    C = more.shape[3]
    width = LO.shape[2]
    out_width = og.shape[1]

    def average(old, new):
        return AVERAGE_KEEP * old + (1.0 - AVERAGE_KEEP) * new

    along = ROW[0, 0:1, :]
    for k in range(1, ROW.shape[0]):
        along = along + ROW[k, 0:1, :]
    column = jnp.transpose(jnp.broadcast_to(along, (LANES, LANES)))[:, 0:1]
    inv = INV[:, 0:1]
    for h in range(out_width // width):
        cols = pl.ds(pl.multiple_of(p * out_width + h * width, LANES), width)
        here = slice(h * width, (h + 1) * width)
        mine = tok[:, cols].astype(F32)
        chips = PN // 2
        total = LO[h * chips].astype(F32)
        back = DN[h * chips].astype(F32)
        for q in range(1, chips):
            total = total + LO[h * chips + q].astype(F32)
            back = back + DN[h * chips + q].astype(F32)
        layer[:, here] = mine + total
        grad[:, here] = og[:, here].astype(F32) + inv * (back - mine * inv * (column / D))
    for t in range(S):
        gd[:, :, t * C : (t + 1) * C] = more[t]
    for m in range(M):
        for k, g, w, mo, sq, av, nw, nm, ns, na in (
            (1, gx, wx, mx, sx, ax, nwx, nmx, nsx, nax),
            (2, gd, wd, md, sd, ad, nwd, nmd, nsd, nad),
        ):
            factor = scale[0:1, M * k + m : M * k + m + 1]
            new_m, new_s, ratio = adam_terms(g[m], mo[m], sq[m])
            new = w[m] - factor * (ratio + WEIGHT_DECAY * w[m])
            nw[m] = new
            nm[m] = new_m
            ns[m] = new_s
            na[m] = average(av[m], new)
    gc[0 : K + 1, :] = gtap[0 : K + 1, :]
    gc[K + 1 :, :] = gch[...]
    new_m, new_s, ratio = adam_terms(gc[...], mc[...], sc[...])
    new = ch[...] - CHANNEL_RATE * ratio
    nwc[...] = new
    nmc[...] = new_m
    nsc[...] = new_s
    nac[...] = average(ac[...], new)
    g = GG[0, 0:1, :]
    for q in range(1, PN):
        g = g + GG[q, 0:1, :]
    new_m, new_s, ratio = adam_terms(g, mg[...], sg[...])
    new = gn[...] - GAIN_RATE * ratio
    nwg[...] = new
    nmg[...] = new_m
    nsg[...] = new_s
    nag[...] = average(ag[...], new)


def to_rows(w, S):
    m, width, two, channels = w.shape
    c = channels // S
    return w.reshape(m, width, two, S, c).transpose(0, 1, 3, 2, 4).reshape(-1, c)


def from_rows(rows, S, shape):
    m, width, two, channels = shape
    c = channels // S
    return rows.reshape(m, width, S, two, c).transpose(0, 1, 3, 2, 4).reshape(shape)


def to_tiles(w):
    m, rows, columns = w.shape
    return w.reshape(m, rows // 8, 8, columns // LANES, LANES).transpose(0, 1, 3, 2, 4).reshape(
        -1, LANES
    )


def from_tiles(flat, shape):
    m, rows, columns = shape
    return flat.reshape(m, rows // 8, columns // LANES, 8, LANES).transpose(0, 1, 3, 2, 4).reshape(
        shape
    )


def local(
    tokens, out_grad, modality, segment,
    w_in, w_x, w_dt, w_out, channel, norm_gain,
    moment_in, moment_x, moment_dt, moment_out, moment_channel, moment_gain,
    square_in, square_x, square_dt, square_out, square_channel, square_gain,
    average_in, average_x, average_dt, average_out, average_channel, average_gain,
):
    S, PN = lax.axis_size("seq"), lax.axis_size("tp")
    TL = tokens.shape[0]
    T = S * TL
    width = D // S
    inner_width = w_out.shape[1]
    C = inner_width // S
    ins = [to_rows(v, S) for v in (w_in, moment_in, square_in, average_in)]
    outs = [to_tiles(v) for v in (w_out, moment_out, square_out, average_out)]
    modrow = jnp.broadcast_to(modality.astype(F32)[None], (8, TL))
    ahead = jnp.concatenate([jnp.full((K - 1,), -1, jnp.int32), segment])
    same = [(ahead[k : k + T] == segment).astype(F32) for k in range(K - 1)]
    zero = jnp.zeros((T,), F32)
    segs = jnp.stack([zero] * M + same + [same[K - 2], zero], axis=1)
    row = lambda v: v[None, :]
    xs = [jnp.transpose(v, (0, 2, 1)) for v in (w_x, moment_x, square_x, average_x)]
    LO, DN, GG, ROW, MORE, gx, gtap, gch, INV, scale, g_in, g_out = block_call(
        S,
        PN,
        (
            tokens, out_grad, modrow, row(norm_gain), segs, channel,
            *xs[:3], w_dt, moment_dt, square_dt, *ins[:3], *outs[:3],
        ),
        T, C, width,
    )
    like = lambda v: sds(v.shape)
    vec = sds((1, width))
    everything = update_all(
        S,
        PN,
        (g_in, *ins),
        (g_out, *outs),
        (
            tokens, out_grad, LO, DN, ROW, INV, scale, gx, MORE, gtap, gch, GG,
            *xs, w_dt, moment_dt, square_dt, average_dt,
            channel, moment_channel, square_channel, average_channel,
            row(norm_gain), row(moment_gain), row(square_gain), row(average_gain),
        ),
        (sds(out_grad.shape),) * 2 + (like(xs[0]),) * 4 + (like(w_dt),) * 4 + (like(channel),) * 4
        + (vec,) * 4,
        [pltpu.VMEM(channel.shape, F32), pltpu.VMEM(w_dt.shape, F32)],
    )
    new_in = [from_rows(v, S, w_in.shape) for v in everything[0:4]]
    new_out = [from_tiles(v, w_out.shape) for v in everything[4:8]]
    rest = everything[8:]
    new_x, new_dt, new_ch, new_g = [rest[2 + 4 * k : 6 + 4 * k] for k in range(4)]
    new_x = [jnp.transpose(v, (0, 2, 1)) for v in new_x]
    groups = [(new_in[k], new_x[k], new_dt[k], new_out[k], new_ch[k], new_g[k][0]) for k in range(4)]
    return (*rest[:2], *groups[0], *groups[1], *groups[2], *groups[3])


def channels_fit(mesh):
    S, PN = mesh.shape["seq"], mesh.shape["tp"]
    n = S * PN
    return PN == 4 and S == 2 * PN and (2 * N) % n == 0 and D * 2 // n == LANES


def solution(mesh):
    placed = (
        P("seq", None),
        P("seq", "tp"),
        P("seq"),
        P(),
        P(None, "seq", None, "tp"),
        P(None, ("tp", "seq"), None),
        P(None, "seq", "tp"),
        P(None, "tp", "seq"),
        P(None, ("tp", "seq")),
        P("seq"),
        P(None, "seq", None, "tp"),
        P(None, ("tp", "seq"), None),
        P(None, "seq", "tp"),
        P(None, "tp", "seq"),
        P(None, ("tp", "seq")),
        P("seq"),
        P(None, "seq", None, "tp"),
        P(None, ("tp", "seq"), None),
        P(None, "seq", "tp"),
        P(None, "tp", "seq"),
        P(None, ("tp", "seq")),
        P("seq"),
        P(None, "seq", None, "tp"),
        P(None, ("tp", "seq"), None),
        P(None, "seq", "tp"),
        P(None, "tp", "seq"),
        P(None, ("tp", "seq")),
        P("seq"),
    )
    return jax.shard_map(
        local if channels_fit(mesh) else generic_local,
        mesh=mesh,
        in_specs=placed,
        out_specs=(
            P("seq", "tp"),
            P("seq", "tp"),
            P(None, "seq", None, "tp"),
            P(None, ("tp", "seq"), None),
            P(None, "seq", "tp"),
            P(None, "tp", "seq"),
            P(None, ("tp", "seq")),
            P("seq"),
            P(None, "seq", None, "tp"),
            P(None, ("tp", "seq"), None),
            P(None, "seq", "tp"),
            P(None, "tp", "seq"),
            P(None, ("tp", "seq")),
            P("seq"),
            P(None, "seq", None, "tp"),
            P(None, ("tp", "seq"), None),
            P(None, "seq", "tp"),
            P(None, "tp", "seq"),
            P(None, ("tp", "seq")),
            P("seq"),
            P(None, "seq", None, "tp"),
            P(None, ("tp", "seq"), None),
            P(None, "seq", "tp"),
            P(None, "tp", "seq"),
            P(None, ("tp", "seq")),
            P("seq"),
        ),
        check_vma=False,
    )
```

```python
import functools

import jax
import jax.numpy as jnp
from jax import lax
from jax.experimental import pallas as pl
from jax.experimental.pallas import tpu as pltpu
from jax.sharding import PartitionSpec as P

D = 2048
R = 128
N = 16
K = 4
M = 3
STEP = 10


EPSILON = 1e-05
BETA_ONE = 0.9
BETA_TWO = 0.999
ADAM_EPSILON = 1e-06
WEIGHT_DECAY = 0.01
MATRIX_RATE = 0.25
CHANNEL_RATE = 0.7
GAIN_RATE = 0.35
AVERAGE_KEEP = 0.8
PRECISE = lax.Precision.HIGHEST


def passed_along(value, axis, steps):
    count = lax.axis_size(axis)
    leading, last = (max(0, -steps), min(count, count - steps))
    return lax.ppermute(value, axis, [(source, source + steps) for source in range(leading, last)])


def prefix(x, axis, combine, identity, reverse):
    devices, place = (lax.axis_size(axis), lax.axis_index(axis))
    everything = jax.tree.map(lambda part: lax.all_gather(part, axis), x)
    start = jax.tree.map(
        lambda part, zero: jnp.broadcast_to(jnp.asarray(zero, part.dtype), part.shape), x, identity
    )

    def lap(k, before):
        at = devices - 1 - k if reverse else k
        reached = at > place if reverse else at < place
        new = combine(before, jax.tree.map(lambda part: part[at], everything))
        return jax.tree.map(lambda a, b: jnp.where(reached, a, b), new, before)

    return lax.fori_loop(0, devices, lap, start)


def silu_grad(operand):
    sigmoid_of = jax.nn.sigmoid(operand)
    return sigmoid_of * (1.0 + operand * (1.0 - sigmoid_of))


def combine(earlier, following):
    return (earlier[0] * following[0], following[0] * earlier[1] + following[1])


def masked_dot(mask_cols, operand, stacked):
    running = mask_cols[:, 0:1] * jnp.dot(operand, stacked[0], preferred_element_type=jnp.float32)
    for modal_index in range(1, M):
        running = running + mask_cols[:, modal_index : modal_index + 1] * jnp.dot(
            operand, stacked[modal_index], preferred_element_type=jnp.float32
        )
    return running


def masked_back(mask_cols, operand, stacked):
    contract = (((1,), (1,)), ((), ()))
    running = mask_cols[:, 0:1] * lax.dot_general(
        operand, stacked[0], contract, preferred_element_type=jnp.float32
    )
    for modal_index in range(1, M):
        running = running + mask_cols[:, modal_index : modal_index + 1] * lax.dot_general(
            operand, stacked[modal_index], contract, preferred_element_type=jnp.float32
        )
    return running


def masked_outer(mask_low, operand, cotangent):
    contract = (((0,), (0,)), ((), ()))
    return jnp.stack(
        [
            lax.dot_general(
                operand * mask_low[:, modal_index : modal_index + 1],
                cotangent,
                contract,
                preferred_element_type=jnp.float32,
            )
            for modal_index in range(M)
        ]
    )


def adam_parts(gradient, moment, square):
    moment_new = BETA_ONE * moment + (1.0 - BETA_ONE) * gradient
    square_new = BETA_TWO * square + (1.0 - BETA_TWO) * gradient * gradient
    adam_ratio = (
        moment_new
        / (1.0 - BETA_ONE**STEP)
        / (jnp.sqrt(square_new / (1.0 - BETA_TWO**STEP)) + ADAM_EPSILON)
    )
    return (moment_new, square_new, adam_ratio)


def generic_local(
    tokens,
    out_grad,
    modality,
    segment,
    w_in,
    w_x,
    w_dt,
    w_out,
    channel,
    norm_gain,
    moment_in,
    moment_x,
    moment_dt,
    moment_out,
    moment_channel,
    moment_gain,
    square_in,
    square_x,
    square_dt,
    square_out,
    square_channel,
    square_gain,
    average_in,
    average_x,
    average_dt,
    average_out,
    average_channel,
    average_gain,
):
    tok_local = tokens.shape[0]
    width_tp = out_grad.shape[1]
    lowered = (
        w_in.astype(jnp.bfloat16),
        w_x.astype(jnp.bfloat16),
        w_dt.astype(jnp.bfloat16),
        w_out.astype(jnp.bfloat16),
    )
    stack_in, stack_x, stack_dt, stack_out = (
        lax.all_gather(lowered[0], "seq", axis=1, tiled=True),
        lax.all_gather(lowered[1], "seq", axis=1, tiled=True),
        lax.all_gather(lowered[2], "seq", axis=1, tiled=True),
        lax.all_gather(lowered[3], "seq", axis=2, tiled=True),
    )
    chan_full, gain_full = (
        lax.all_gather(channel, "seq", axis=1, tiled=True),
        lax.all_gather(norm_gain, "seq", axis=0, tiled=True),
    )
    inner_width = stack_out.shape[1]
    in_flat = stack_in.reshape(M, D, 2 * inner_width)
    seq_index = lax.axis_index("seq")
    tp_index = lax.axis_index("tp")
    start_row = seq_index * tok_local
    seg_local = lax.dynamic_slice(segment, (start_row,), (tok_local,))
    seg_before = lax.dynamic_slice(
        jnp.concatenate([jnp.full((K - 1,), -1, jnp.int32), segment]),
        (start_row,),
        (tok_local + K - 1,),
    )
    seg_after = lax.dynamic_slice(
        jnp.concatenate([segment, jnp.full((K - 1,), -2, jnp.int32)]),
        (start_row,),
        (tok_local + K - 1,),
    )
    mask_cols = (modality[:, None] == jnp.arange(M, dtype=jnp.int32)[None, :]).astype(jnp.float32)
    mask_low = mask_cols.astype(jnp.bfloat16)
    tokens_wide = tokens.astype(jnp.float32)
    inv_root = lax.rsqrt(jnp.mean(tokens_wide * tokens_wide, axis=-1, keepdims=True) + EPSILON)
    scaled = tokens_wide * inv_root
    normed = (scaled * gain_full[None, :]).astype(jnp.bfloat16)
    projected = masked_dot(mask_cols, normed, in_flat)
    inner_act = projected[:, :inner_width].astype(jnp.bfloat16)
    gate_pre = projected[:, inner_width:]
    rim_rows = passed_along(inner_act[tok_local - (K - 1) :], "seq", 1)
    extended = jnp.concatenate([rim_rows, inner_act], axis=0).astype(jnp.float32)
    conv_pre = jnp.broadcast_to(chan_full[K][None, :], (tok_local, inner_width))
    same_docs = []
    for tap_index in range(K):
        same_doc = (seg_before[tap_index : tap_index + tok_local] == seg_local).astype(jnp.float32)[
            :, None
        ]
        same_docs.append(same_doc)
        conv_pre = (
            conv_pre
            + chan_full[tap_index][None, :] * extended[tap_index : tap_index + tok_local] * same_doc
        )
    activated = jax.nn.silu(conv_pre).astype(jnp.bfloat16)
    act_wide = activated.astype(jnp.float32)
    params_x = lax.psum(masked_dot(mask_cols, activated, stack_x), "tp")
    low_rank = params_x[:, :R].astype(jnp.bfloat16)
    input_b = params_x[:, R : R + N]
    output_c = params_x[:, R + N :]
    step_pre = masked_dot(mask_cols, low_rank, stack_dt) + jnp.dot(
        mask_cols, chan_full[K + 2 : K + 2 + M], precision=PRECISE
    )
    step_size = jax.nn.softplus(step_pre)
    decay_base = -jnp.exp(chan_full[K + 2 + M :])
    keep_flag = (seg_before[K - 2 : K - 2 + tok_local] == seg_local).astype(jnp.float32)
    decay_rate = jnp.exp(step_size[:, None, :] * decay_base[None]) * keep_flag[:, None, None]
    drive_term = (step_size * act_wide)[:, None, :] * input_b[:, :, None]
    decay_cum, local_state = lax.associative_scan(combine, (decay_rate, drive_term), axis=0)
    unit_pair = (jnp.ones_like(decay_base), jnp.zeros_like(decay_base))
    carry_in = prefix((decay_cum[-1], local_state[-1]), "seq", combine, unit_pair, False)[1]
    hidden_state = local_state + decay_cum * carry_in[None]
    mixed_out = (
        jnp.einsum("tn,tne->te", output_c, hidden_state, precision=PRECISE)
        + chan_full[K + 1][None, :] * act_wide
    )
    gate_act = jax.nn.silu(gate_pre)
    gated_out = (mixed_out * gate_act).astype(jnp.bfloat16)
    out_share = lax.psum_scatter(
        masked_dot(mask_cols, gated_out, stack_out), "tp", scatter_dimension=1, tiled=True
    )
    layer_out = lax.dynamic_slice_in_dim(tokens_wide, tp_index * width_tp, width_tp, 1) + out_share
    grad_full = lax.all_gather(out_grad, "tp", axis=1, tiled=True)
    d_gated = masked_back(mask_cols, grad_full, stack_out)
    grad_out = masked_outer(mask_low, gated_out, grad_full)
    d_mixed = d_gated * gate_act
    d_gate = d_gated * mixed_out * silu_grad(gate_pre)
    grad_skip = jnp.sum(d_mixed * act_wide, axis=0)
    d_out_c = jnp.einsum("te,tne->tn", d_mixed, hidden_state, precision=PRECISE)
    d_hidden = output_c[:, :, None] * d_mixed[:, None, :]
    decay_next = jnp.concatenate([decay_rate[1:], jnp.ones_like(decay_rate[:1])], axis=0)
    suffix_cum, local_back = lax.associative_scan(
        combine, (decay_next, d_hidden), reverse=True, axis=0
    )
    device_pair = (decay_rate[0] * suffix_cum[0], decay_rate[0] * local_back[0])
    carry_back = prefix(device_pair, "seq", combine, unit_pair, True)[1]
    back_state = local_back + suffix_cum * carry_back[None]
    state_prev = jnp.concatenate([carry_in[None], hidden_state[:-1]], axis=0)
    d_log = back_state * state_prev * decay_rate
    d_drive_sum = jnp.einsum("tne,tn->te", back_state, input_b, precision=PRECISE)
    d_step_size = jnp.sum(d_log * decay_base[None], axis=1) + act_wide * d_drive_sum
    grad_decay = decay_base * jnp.einsum("tne,te->ne", d_log, step_size, precision=PRECISE)
    d_in_b = jnp.einsum("tne,te->tn", back_state, step_size * act_wide, precision=PRECISE)
    d_step = (d_step_size * jax.nn.sigmoid(step_pre)).astype(jnp.bfloat16)
    d_step_wide = d_step.astype(jnp.float32)
    grad_bias = jnp.dot(mask_cols.T, d_step_wide, precision=PRECISE)
    grad_dt = masked_outer(mask_low, low_rank, d_step)
    d_low = masked_back(mask_cols, d_step, stack_dt)
    d_params = lax.psum(jnp.concatenate([d_low, d_in_b, d_out_c], axis=1), "tp").astype(
        jnp.bfloat16
    )
    grad_x = masked_outer(mask_low, activated, d_params)
    d_activ = (
        d_mixed * chan_full[K + 1][None, :]
        + step_size * d_drive_sum
        + masked_back(mask_cols, d_params, stack_x)
    )
    d_conv = (d_activ * silu_grad(conv_pre)).astype(jnp.bfloat16)
    rim_back = passed_along(d_conv[: K - 1], "seq", -1)
    d_conv_wide = d_conv.astype(jnp.float32)
    conv_after = jnp.concatenate([d_conv, rim_back], axis=0).astype(jnp.float32)
    d_inner = jnp.zeros((tok_local, inner_width), jnp.float32)
    grad_taps = []
    for tap_index in range(K):
        grad_taps.append(
            jnp.sum(
                d_conv_wide * extended[tap_index : tap_index + tok_local] * same_docs[tap_index],
                axis=0,
            )
        )
        offset = K - 1 - tap_index
        same_after = (seg_after[offset : offset + tok_local] == seg_local).astype(jnp.float32)[
            :, None
        ]
        d_inner = (
            d_inner
            + chan_full[tap_index][None, :] * conv_after[offset : offset + tok_local] * same_after
        )
    grad_conv_b = jnp.sum(d_conv_wide, axis=0)
    d_proj = jnp.concatenate([d_inner, d_gate], axis=1).astype(jnp.bfloat16)
    grad_in = masked_outer(mask_low, normed, d_proj).reshape(M, D, 2, inner_width)
    d_normed = lax.psum(masked_back(mask_cols, d_proj, in_flat), "tp")
    grad_gain = jnp.sum(d_normed * scaled, axis=0)
    d_scaled = d_normed * gain_full[None, :]
    d_tokens = inv_root * (d_scaled - scaled * jnp.mean(d_scaled * scaled, axis=-1, keepdims=True))
    tokens_grad = out_grad.astype(jnp.float32) + lax.dynamic_slice_in_dim(
        d_tokens, tp_index * width_tp, width_tp, 1
    )
    grad_channel = jnp.concatenate(
        [jnp.stack(grad_taps), grad_conv_b[None], grad_skip[None], grad_bias, grad_decay], axis=0
    )
    reduced = (
        lax.psum_scatter(grad_in, "seq", scatter_dimension=1, tiled=True),
        lax.psum_scatter(grad_x, "seq", scatter_dimension=1, tiled=True),
        lax.psum_scatter(grad_dt, "seq", scatter_dimension=1, tiled=True),
        lax.psum_scatter(grad_out, "seq", scatter_dimension=2, tiled=True),
        lax.psum_scatter(grad_channel, "seq", scatter_dimension=1, tiled=True),
        lax.psum_scatter(grad_gain, "seq", scatter_dimension=0, tiled=True),
    )
    weights = (w_in, w_x, w_dt, w_out, channel, norm_gain)
    moments = (moment_in, moment_x, moment_dt, moment_out, moment_channel, moment_gain)
    squares = (square_in, square_x, square_dt, square_out, square_channel, square_gain)
    averages = (average_in, average_x, average_dt, average_out, average_channel, average_gain)
    adam_all = [
        adam_parts(reduced[position], moments[position], squares[position]) for position in range(6)
    ]
    directions = [adam_all[position][2] + WEIGHT_DECAY * weights[position] for position in range(4)]
    weight_sums = jnp.stack(
        [
            jnp.sum(
                weights[position] * weights[position], axis=tuple(range(1, weights[position].ndim))
            )
            for position in range(4)
        ]
    )
    direction_sums = jnp.stack(
        [
            jnp.sum(
                directions[position] * directions[position],
                axis=tuple(range(1, directions[position].ndim)),
            )
            for position in range(4)
        ]
    )
    totals = lax.psum(jnp.stack([weight_sums, direction_sums]), ("seq", "tp"))
    trust_ratio = jnp.sqrt(totals[0]) / jnp.sqrt(totals[1])
    new_weights = []
    new_averages = []
    for position in range(6):
        weight = weights[position]
        if position < 4:
            updated = (
                weight
                - MATRIX_RATE
                * trust_ratio[position].reshape((M,) + (1,) * (weight.ndim - 1))
                * directions[position]
            )
        elif position == 4:
            updated = weight - CHANNEL_RATE * adam_all[position][2]
        else:
            updated = weight - GAIN_RATE * adam_all[position][2]
        new_weights.append(updated)
        new_averages.append(AVERAGE_KEEP * averages[position] + (1.0 - AVERAGE_KEEP) * updated)
    return (
        layer_out,
        tokens_grad,
        new_weights[0],
        new_weights[1],
        new_weights[2],
        new_weights[3],
        new_weights[4],
        new_weights[5],
        adam_all[0][0],
        adam_all[1][0],
        adam_all[2][0],
        adam_all[3][0],
        adam_all[4][0],
        adam_all[5][0],
        adam_all[0][1],
        adam_all[1][1],
        adam_all[2][1],
        adam_all[3][1],
        adam_all[4][1],
        adam_all[5][1],
        new_averages[0],
        new_averages[1],
        new_averages[2],
        new_averages[3],
        new_averages[4],
        new_averages[5],
    )


MESH = pl.DeviceIdType.MESH
VMEM_LIMIT = 62 * 1024 * 1024
LANES = 128
F32 = jnp.float32
BF16 = jnp.bfloat16
NT = (((1,), (1,)), ((), ()))
TN = (((0,), (0,)), ((), ()))


def dot(a, b, dims=(((1,), (0,)), ((), ()))):
    return lax.dot_general(a, b, dims, preferred_element_type=F32)


def local_call(kernel, out_shape, n_in, scratch=(), cost=None):
    return pl.pallas_call(
        kernel,
        out_shape=out_shape,
        in_specs=[pl.BlockSpec(memory_space=pltpu.VMEM)] * n_in,
        out_specs=jax.tree.map(lambda _: pl.BlockSpec(memory_space=pltpu.VMEM), out_shape),
        scratch_shapes=list(scratch),
        compiler_params=pltpu.CompilerParams(vmem_limit_bytes=VMEM_LIMIT),
        cost_estimate=cost,
    )


def remote_call(kernel, out_shape, n_in, scratch, ident):
    return pl.pallas_call(
        kernel,
        out_shape=out_shape,
        in_specs=[pl.BlockSpec(memory_space=pltpu.VMEM)] * n_in,
        out_specs=jax.tree.map(lambda _: pl.BlockSpec(memory_space=pltpu.VMEM), out_shape),
        scratch_shapes=list(scratch),
        compiler_params=pltpu.CompilerParams(
            collective_id=ident, has_side_effects=True, vmem_limit_bytes=VMEM_LIMIT
        ),
    )


def sds(shape, dtype=F32):
    return jax.ShapeDtypeStruct(shape, dtype)


def seq_copy(src, dst, send, recv, device):
    return pltpu.make_async_remote_copy(
        src_ref=src,
        dst_ref=dst,
        send_sem=send,
        recv_sem=recv,
        device_id=device,
        device_id_type=MESH,
    )


def place(S, PN):
    s, p = lax.axis_index("seq"), lax.axis_index("tp")
    return s, p, lax.div(s, 2), lax.rem(s, 2)


def greet_all(S, PN):
    s, p = lax.axis_index("seq"), lax.axis_index("tp")
    n = S * PN
    me = s * PN + p
    bar = pltpu.get_barrier_semaphore()

    def greet(k, _):
        j = lax.rem(me + k, n)
        pl.semaphore_signal(
            bar,
            inc=1,
            device_id={"seq": lax.div(j, PN), "tp": lax.rem(j, PN)},
            device_id_type=MESH,
        )
        return 0

    lax.fori_loop(1, n, greet, 0)
    return lambda: pl.semaphore_wait(bar, n - 1)


class Spread:
    def __init__(self, S, PN, own, buf, zs, zr, xs, xr, ys, yr, cs, cr, ls):
        s, p, z, x = place(S, PN)
        self.zn = S // 2
        zn = self.zn
        other_x = {"seq": 2 * z + 1 - x}
        other_y = {"tp": lax.rem(p + 2, PN)}
        other_c = {"tp": p + 1 - 2 * lax.rem(p, 2)}

        def at(k, j):
            return 2 * lax.rem(z - k + zn, zn) + (x if j == 0 else 1 - x)

        self.local = pltpu.make_async_copy(own, buf.at[p, s], ls)
        self.z = [
            seq_copy(own, buf.at[p, s], zs.at[k], zr.at[k], {"seq": 2 * lax.rem(z + k, zn) + x})
            for k in range(1, zn)
        ]
        self.x = []
        self.y = {}
        for k in range(zn):
            src = own if k == 0 else buf.at[p, at(k, 0)]
            self.x.append(seq_copy(src, buf.at[p, at(k, 0)], xs.at[k], xr.at[k], other_x))
            for j in range(2):
                src = own if (k == 0 and j == 0) else buf.at[p, at(k, j)]
                self.y[k, j] = seq_copy(
                    src, buf.at[p, at(k, j)], ys.at[2 * k + j], yr.at[2 * k + j], other_y
                )
        q = lax.rem(p + 2, PN)
        self.c = [
            seq_copy(buf.at[p], buf.at[p], cs.at[0], cr.at[0], other_c),
            seq_copy(buf.at[q], buf.at[q], cs.at[1], cr.at[1], other_c),
        ]

    def start(self):
        self.local.start()
        for cp in self.z:
            cp.start()
        self.x[0].start()
        self.y[0, 0].start()

    def forward(self):
        for k in range(1, self.zn):
            self.z[k - 1].wait_recv()
            self.x[k].start()
            self.y[k, 0].start()
        for k in range(self.zn):
            self.x[k].wait_recv()
            self.y[k, 1].start()
        self.local.wait()
        self.c[0].start()

    def finish(self):
        for cp in self.y.values():
            cp.wait_recv()
        self.c[1].start()
        for cp in self.z + self.x + list(self.y.values()):
            cp.wait_send()
        for cp in self.c:
            cp.wait()

    @staticmethod
    def semaphores(S):
        dma = pltpu.SemaphoreType.DMA
        return [dma((S // 2,))] * 4 + [dma((S,))] * 2 + [dma((2,))] * 2 + [dma]


def row_copies(S, src, dst, send, recv):
    s = lax.axis_index("seq")
    out = []
    for k in range(1, S):
        d = lax.rem(s + k, S)
        out.append(seq_copy(src(d), dst(s), send.at[k], recv.at[k], {"seq": d}))
    return out


def sum_over_all(
    S, PN, lr, bct, LR, BCT, got_l, got_b, core_l, core_b,
    c1s, c1r, ssl, rsl, ssb, rsb, sgl, rgl, sgb, rgb, c2s, c2r, between=(),
):
    n = S * PN // 2
    s, p = lax.axis_index("seq"), lax.axis_index("tp")
    y, c = lax.div(p, 2), lax.rem(p, 2)
    me = s * (PN // 2) + y
    T = lr.shape[0]
    half, rows = T // 2, T // 2 // n
    chunks = bct.shape[0]
    per = n // (chunks // 2)
    high = bct.shape[1] // per
    twin = {"tp": p + 1 - 2 * c}

    def device(j):
        return {"seq": lax.div(j, PN // 2), "tp": 2 * lax.rem(j, PN // 2) + c}

    def half_l(k):
        return pl.ds(pl.multiple_of(k * half, half), half)

    def half_b(k):
        return pl.ds(k * (chunks // 2), chunks // 2)

    def rows_of(j):
        return pl.ds(pl.multiple_of(c * half + j * rows, rows), rows)

    def slab(ref, j):
        at = c * (chunks // 2) + lax.div(j, per)
        return ref.at[at, pl.ds(pl.multiple_of(lax.rem(j, per) * high, 8), high)]

    swap = [
        seq_copy(lr.at[half_l(1 - c)], core_l, c1s.at[0], c1r.at[0], twin),
        seq_copy(bct.at[half_b(1 - c)], core_b, c1s.at[1], c1r.at[1], twin),
    ]
    for cp in swap:
        cp.start()
    for cp in swap:
        cp.wait()
    lr[half_l(c), :] = lr[half_l(c), :] + core_l[...]
    bct[half_b(c)] = bct[half_b(c)] + core_b[...]

    def first(k):
        j = lax.rem(me + k, n)
        return (
            seq_copy(lr.at[rows_of(j)], got_l.at[k], ssl.at[k], rsl.at[k], device(j)),
            seq_copy(slab(bct, j), got_b.at[k], ssb.at[k], rsb.at[k], device(j)),
        )

    def second(k):
        j = lax.rem(me + k, n)
        mine_l, mine_b = LR.at[rows_of(me)], slab(BCT, me)
        return (
            seq_copy(mine_l, mine_l, sgl.at[k], rgl.at[k], device(j)),
            seq_copy(mine_b, mine_b, sgb.at[k], rgb.at[k], device(j)),
        )

    def start(copies, k):
        for cp in copies(k):
            cp.start()
        return 0

    def wait(copies, k):
        for cp in copies(k):
            cp.wait()
        return 0

    lax.fori_loop(1, n, lambda k, _: start(first, k), 0)
    for cp in between[0:1]:
        cp()
    got_l[0] = lr[rows_of(me), :]
    got_b[0] = slab(bct, me)[...]
    lax.fori_loop(1, n, lambda k, _: wait(first, k), 0)
    LR[rows_of(me), :] = jnp.sum(got_l[...], axis=0).astype(LR.dtype)
    slab(BCT, me)[...] = jnp.sum(got_b[...], axis=0)
    lax.fori_loop(1, n, lambda k, _: start(second, k), 0)
    for cp in between[1:2]:
        cp()
    lax.fori_loop(1, n, lambda k, _: wait(second, k), 0)
    swap = [
        seq_copy(LR.at[half_l(c)], LR.at[half_l(c)], c2s.at[0], c2r.at[0], twin),
        seq_copy(BCT.at[half_b(c)], BCT.at[half_b(c)], c2s.at[1], c2r.at[1], twin),
    ]
    for cp in swap:
        cp.start()
    for cp in swap:
        cp.wait()


def sum_scratch(S, PN, T):
    n = S * PN // 2
    dma = pltpu.SemaphoreType.DMA
    chunks = T // LANES
    slabs = chunks * N // n
    return (
        [pltpu.VMEM((n, T // 2 // n, R), F32), pltpu.VMEM((n, slabs, LANES), F32)]
        + [pltpu.VMEM((T // 2, R), F32), pltpu.VMEM((chunks // 2, 2 * N, LANES), F32)]
        + [dma((2,))] * 2 + [dma((n,))] * 8 + [dma((2,))] * 2
    )


class FeatureGather:
    def __init__(self, S, PN, own, buf, s1, r1, s2, r2, cs, cr, ys, yr, ls):
        s, p, z, x = place(S, PN)
        self.zn = zn = S // 2
        self.root = p == z
        self.relay = lax.rem(p + 2, PN) == z
        self.twin_of_root = p + 1 - 2 * lax.rem(p, 2) == z
        self.z = z
        self.moves = z != p
        self.local = pltpu.make_async_copy(own, buf.at[z, x], ls)
        self.first = seq_copy(own, buf.at[z, x], s1, r1.at[z], {"seq": 2 * p + x})
        self.arrive = [
            seq_copy(own, buf.at[t, x], s1, r1.at[t], {"seq": 2 * lax.rem(z + 1, zn) + x})
            for t in range(zn)
        ]
        halves = [buf.at[:, x], buf.at[:, 1 - x]]
        twin = {"tp": p + 1 - 2 * lax.rem(p, 2)}
        far = {"tp": lax.rem(p + 2, PN)}
        self.across = seq_copy(halves[0], halves[0], s2, r2, {"seq": 2 * z + 1 - x})
        self.core = [seq_copy(h, h, cs.at[j], cr.at[j], twin) for j, h in enumerate(halves)]
        self.y = [seq_copy(h, h, ys.at[j], yr.at[j], far) for j, h in enumerate(halves)]

    def start(self):
        @pl.when(self.moves)
        def _():
            self.first.start()

        @pl.when(jnp.logical_not(self.moves))
        def _():
            self.local.start()
            self.local.wait()

    def near(self):
        @pl.when(self.root)
        def _():
            for t in range(self.zn):

                @pl.when(self.z != t)
                def _():
                    self.arrive[t].wait_recv()

            self.across.start()
            self.core[0].start()
            self.y[0].start()

    def far(self):
        @pl.when(self.root)
        def _():
            self.across.wait_recv()
            self.core[1].start()
            self.y[1].start()

        self.pass_on(0)

    def pass_on(self, j):
        @pl.when(self.relay)
        def _():
            self.y[j].wait_recv()
            self.core[j].start()

    def finish(self):
        self.pass_on(1)

        @pl.when(self.moves)
        def _():
            self.first.wait_send()

        @pl.when(self.root)
        def _():
            self.across.wait_send()
            for cp in self.core + self.y:
                cp.wait_send()

        @pl.when(self.relay)
        def _():
            for cp in self.core:
                cp.wait_send()

        @pl.when(jnp.logical_not(jnp.logical_or(self.root, self.relay)))
        def _():
            for cp in self.core:
                cp.wait_recv()

    @staticmethod
    def semaphores(S):
        dma = pltpu.SemaphoreType.DMA
        return [dma, dma((S // 2,)), dma, dma] + [dma((2,))] * 4 + [dma]


class RowGather:
    PARTS = 2

    def __init__(self, S, own, place_of, us, ur, ds, dr, xs, xr, ls):
        s, p, z, x = place(S, 1)
        self.zn, self.z, self.x, self.own, self.place_of = S // 2, z, x, own, place_of
        self.up_sems, self.down_sems, self.x_sems = (us, ur), (ds, dr), (xs, xr)
        self.every = pl.ds(0, own.shape[0])
        self.local = pltpu.make_async_copy(own, place_of(self.every, s), ls)

    def hop(self, t, d, h, up, toward=1):
        size = self.own.shape[0] // self.PARTS
        r = pl.ds(h * size, size)
        there = self.place_of(r, 2 * t + self.x)
        send, recv = self.up_sems if up else self.down_sems
        chip = self.z + (toward if up else -toward)
        src = self.own.at[r] if d == 1 else there
        return seq_copy(src, there, send.at[d, h], recv.at[d, h], {"seq": 2 * chip + self.x})

    def across(self, t):
        block = self.place_of(self.every, 2 * t + self.x)
        send, recv = self.x_sems
        other = {"seq": 2 * self.z + 1 - self.x}
        return seq_copy(block, block, send.at[t], recv.at[t], other)

    def can(self, d, up):
        z, last = self.z, self.zn - 1
        if up:
            return jnp.logical_and(z >= d - 1, z < last)
        return jnp.logical_and(z + d - 1 <= last, z > 0)

    def start(self):
        self.local.start()
        for h in range(self.PARTS):
            for up in (True, False):

                @pl.when(self.can(1, up))
                def _():
                    self.hop(self.z, 1, h, up).start()

        self.local.wait()
        self.across(self.z).start()

    def step(self, d):
        if d >= self.zn:
            return
        for up in (True, False):
            t = self.z - d if up else self.z + d
            there = self.z >= d if up else self.z + d < self.zn

            @pl.when(there)
            def _():
                for h in range(self.PARTS):
                    self.hop(t, d, h, up, -1).wait_recv()
                    if d + 1 < self.zn:

                        @pl.when(self.can(d + 1, up))
                        def _():
                            self.hop(t, d + 1, h, up).start()

                self.across(t).start()

    def finish(self):
        for d in range(1, self.zn):
            for h in range(self.PARTS):
                for up in (True, False):

                    @pl.when(self.can(d, up))
                    def _():
                        t = self.z - (d - 1) if up else self.z + (d - 1)
                        self.hop(t, d, h, up).wait_send()

        for t in range(self.zn):
            self.across(t).wait()

    @staticmethod
    def semaphores(S):
        dma = pltpu.SemaphoreType.DMA
        return [dma((S // 2, RowGather.PARTS))] * 4 + [dma((S // 2,))] * 2 + [dma]


def adam_terms(g, m, s):
    new_m = BETA_ONE * m + (1.0 - BETA_ONE) * g
    new_s = BETA_TWO * s + (1.0 - BETA_TWO) * (g * g)
    root = jnp.sqrt(new_s * (1.0 / (1.0 - BETA_TWO**STEP))) + ADAM_EPSILON
    return new_m, new_s, (new_m * (1.0 / (1.0 - BETA_ONE**STEP))) / root


def softplus(v):
    u = jnp.exp(-jnp.abs(v))
    w = 1.0 + u
    small = jnp.where(w == 1.0, u, jnp.log(w) * (u / jnp.where(w == 1.0, 1.0, w - 1.0)))
    return jnp.maximum(v, 0.0) + small


def masked_sum(acc, aux, r, C):
    total = acc[:, 0:C] * aux[r, 0:1]
    for m in range(1, M):
        total = total + acc[:, m * C : (m + 1) * C] * aux[r, m : m + 1]
    return total


def block_kernel(S, PN, *refs):
    rest = list(refs)
    take = lambda k: [rest.pop(0) for _ in range(k)]
    tok, og, modrow, gain, segs, ch, w_x, m_x, s_x, w_dt, m_dt, s_dt = take(12)
    w_in, m_in, s_in, w_out, m_out, s_out = take(6)
    LO, DN, GG, ROW, MORE, gx, gtap, gch, INV, SCALE, g_in, g_out = take(12)
    tile, toks, ogz, nrm, Wi, Wg, Wo, AUX, GAIN, WD = take(10)
    gsend, grecv, osend, orecv = take(4)
    step, drive, keep, Y, pad, act3, lr, bcp = take(8)
    act, conv, inner, low, bct, pre, H, gated, dgate, dmix, aux, X = take(12)
    gall, dall, DS, DB, dst3, low3, dst, dlow, dbct, dact, gdt = take(11)
    LR2, BCT2, tail, dpar, dinner, part, rowdot, ggs, wdt = take(9)
    wi, wg, wo, wdt_mine, gain_mine, wlr, wbc, wxT, NR, G = take(10)
    gdt_mine, turned, sums_ref, TILE, total_tile = take(5)
    stage, load, store, pair, swaps = take(5)
    ag1, ag2 = take(9), take(9)
    parts_sems = take(4)
    ws = take(12)
    ls = take(1)[0]
    sums = take(16)
    rows_g, rows_d, rows_i = take(7), take(7), take(7)
    mx, mr, ml = take(3)
    last = take(10)
    s, p, z, x = place(S, PN)
    TL, DD = tok.shape
    T = S * TL
    width = DD // S
    quarter = DD // PN
    C = act.shape[1]
    rows = 128

    wait_for_all = greet_all(S, PN)
    load_in = pltpu.make_async_copy(w_in, H.at[0 : w_in.shape[0]], stage.at[0])
    load_in.start()
    wide = tok[...].astype(F32)
    inv = lax.rsqrt(jnp.mean(wide * wide, axis=1, keepdims=True) + EPSILON)
    row = jnp.transpose(jnp.broadcast_to(inv, (TL, LANES)))[0:8]
    tile[...] = jnp.where(
        lax.broadcasted_iota(jnp.int32, row.shape, 0) == 0, modrow[...], row
    )
    gain_mine[...] = jnp.broadcast_to(gain[...], gain_mine.shape)
    wdt_mine[...] = w_dt[...].astype(BF16)
    chans = lambda d: pl.ds(pl.multiple_of(d * C, LANES), C)
    block = lambda d: pl.ds(pl.multiple_of(d * width, width), width)
    tokens = Spread(
        S, PN, tok.at[:, pl.ds(pl.multiple_of(p * quarter, LANES), quarter)], toks, *ag1
    )
    small = (
        row_copies(S, lambda d: tile, lambda t: AUX.at[t], ws[0], ws[1])
        + row_copies(S, lambda d: gain_mine, lambda t: GAIN.at[t], ws[2], ws[3])
    )
    dts = row_copies(S, lambda d: wdt_mine.at[:, :, chans(d)], lambda t: WD.at[t], ws[4], ws[5])
    inners = row_copies(S, lambda d: wi.at[d], lambda t: Wi.at[block(t)], ws[6], ws[7])
    zn = S // 2
    across = {"seq": 2 * z + 1 - x}
    pair_rows = pl.ds(pl.multiple_of(x * width, width), width)
    gate_swap = seq_copy(wg.at[:, 1 - x], Wg.at[:, pair_rows], ws[8].at[0], ws[9].at[0], across)
    out_swap = seq_copy(
        wo.at[:, 1 - x], Wo.at[:, :, pair_rows], ws[10].at[0], ws[11].at[0], across
    )

    def along(k, send, recv, sems):
        return seq_copy(
            send.at[k - 1],
            recv.at[k - 1],
            sems[0].at[k],
            sems[1].at[k],
            {"seq": 2 * lax.rem(z + k, zn) + x},
        )

    gates = [along(k, gsend, grecv, parts_sems[0:2]) for k in range(1, zn)]
    backs = [along(k, osend, orecv, parts_sems[2:4]) for k in range(1, zn)]
    cotangent = FeatureGather(S, PN, og, ogz, *ag2)
    wait_for_all()
    for cp in small:
        cp.start()
    tokens.start()
    load_in.wait()
    stride = 2 * S
    for m in range(M):
        for b in range(S):
            r = pl.ds(m * width * stride + 2 * b, width, stride=stride)
            wi[b, :, m * C : (m + 1) * C] = H[r, :].astype(BF16)
    for cp in inners[::-1] + dts:
        cp.start()
    cotangent.start()
    for m in range(M):
        for b in range(S):
            r = pl.ds(m * width * stride + 2 * b + 1, width, stride=stride)
            wg[b // 2, b % 2, :, m * C : (m + 1) * C] = H[r, :].astype(BF16)
    gate_swap.start()
    load_out = pltpu.make_async_copy(w_out, H.at[0 : w_out.shape[0]], stage.at[1])
    load_out.start()
    own = [
        pltpu.make_async_copy(tile, AUX.at[s], ls.at[0]),
        pltpu.make_async_copy(gain_mine, GAIN.at[s], ls.at[1]),
        pltpu.make_async_copy(wdt_mine.at[:, :, chans(s)], WD.at[s], ls.at[2]),
        pltpu.make_async_copy(wi.at[s], Wi.at[block(s)], ls.at[3]),
        pltpu.make_async_copy(wg.at[:, x], Wg.at[:, pair_rows], ls.at[4]),
    ]
    for cp in own:
        cp.start()
    for m in range(M):
        wlr[m * C : (m + 1) * C, :] = jnp.transpose(w_x[m, 0:R, :]).astype(BF16)
        wbc[:, m * C : (m + 1) * C] = w_x[m, R : R + 2 * N, :].astype(BF16)
        wxT[m] = w_x[m].astype(BF16)
    load_out.wait()
    tiles = width // LANES
    for m in range(M):
        for b in range(S):
            rows_b = H[(m * S + b) * C * tiles : (m * S + b + 1) * C * tiles, :]
            pieces = rows_b.reshape(C // 8, tiles, 8, LANES)
            for t in range(tiles):
                wo[b // 2, b % 2, m * C : (m + 1) * C, t * LANES : (t + 1) * LANES] = (
                    pieces[:, t].reshape(C, LANES).astype(BF16)
                )
    out_swap.start()
    own.append(pltpu.make_async_copy(wo.at[:, x], Wo.at[:, :, pair_rows], ls.at[5]))
    own[-1].start()
    for cp in own:
        cp.wait()
    tokens.forward()
    cotangent.near()
    for cp in small:
        cp.wait()
    lane = lax.broadcasted_iota(jnp.int32, (TL, 8), 1)

    def columns(t, _):
        r = pl.ds(pl.multiple_of(t * TL, TL), TL)
        turned = jnp.transpose(jnp.concatenate([AUX[t]] * (LANES // 8), axis=0))
        mask = (turned[:, 0:1] == lane.astype(F32)).astype(F32)
        aux[r, :] = jnp.where(
            lane < M, mask, jnp.where(lane == 7, turned[:, 1:2], segs[r, :])
        )
        return 0

    lax.fori_loop(0, S, columns, 0)
    aux[T : T + 8, :] = jnp.zeros((8, 8), F32)
    tokens.finish()
    per = quarter // width

    def norm(t, _):
        r = pl.ds(pl.multiple_of(t * TL, TL), TL)
        scale = aux[r, 7:8]
        for q in range(PN):
            scaled = toks[q, t].astype(F32) * scale
            for j in range(per):
                part = scaled[:, j * width : (j + 1) * width] * GAIN[q * per + j, 0:1, :]
                nrm[r, q * quarter + j * width : q * quarter + (j + 1) * width] = part.astype(BF16)
        return 0

    lax.fori_loop(0, S, norm, 0)
    big = 512
    features = pl.ds(pl.multiple_of(z * 2 * width, 2 * width), 2 * width)

    def gate_part(k):
        def body(i, _):
            r = pl.ds(pl.multiple_of(i * big, big), big)
            w = Wg[lax.rem(z + k, zn)]
            value = masked_sum(dot(nrm[r, features], w), aux, r, C)
            if k == 0:
                DS[r, :] = value
            else:
                gsend[k - 1, r, :] = value.astype(BF16)
            return 0

        lax.fori_loop(0, T // big, body, 0)

    def back_part(k):
        def body(i, _):
            r = pl.ds(pl.multiple_of(i * big, big), big)
            w = Wo[lax.rem(z + k, zn)]
            chips = big // TL // 2
            g = ogz[pl.ds(i * chips, chips)].reshape(big, 2 * width)
            value = masked_sum(dot(g, w, NT), aux, r, C)
            if k == 0:
                DB[r, :] = value
            else:
                osend[k - 1, r, :] = value.astype(BF16)
            return 0

        lax.fori_loop(0, T // big, body, 0)

    gate_swap.wait()
    gate_part(1)
    gates[0].start()
    gate_part(2)
    gates[1].start()
    gate_part(3)
    gates[2].start()
    gate_part(0)
    for cp in inners:
        cp.wait()

    pad[0:8, :] = jnp.zeros((8, C), F32)

    def first(i, _):
        r = pl.ds(pl.multiple_of(i * big, big), big)
        value = masked_sum(dot(nrm[r, :], Wi[...]), aux, r, C).astype(BF16)
        inner[r, :] = value
        pad[pl.ds(pl.multiple_of(i * big + 8, 8), big), :] = value.astype(F32)
        return 0

    lax.fori_loop(0, T // big, first, 0)

    def convolve(i, _):
        r = pl.ds(pl.multiple_of(i * rows, rows), rows)
        window = pad[pl.ds(pl.multiple_of(i * rows, rows), rows + 8), :]
        v = jnp.broadcast_to(ch[K : K + 1, :], (rows, C))
        for k in range(K):
            term = ch[k : k + 1, :] * window[8 - (K - 1) + k : 8 - (K - 1) + k + rows]
            v = v + (term * aux[r, M + k : M + k + 1] if k < K - 1 else term)
        conv[r, :] = v
        a = (v / (1.0 + jnp.exp(-v))).astype(BF16)
        act[r, :] = a
        a_wide = a.astype(F32)
        for m in range(M):
            act3[r, m * C : (m + 1) * C] = (a_wide * aux[r, m : m + 1]).astype(BF16)
        lr[r, :] = dot(act3[r, :], wlr[...])
        bcp[i] = dot(wbc[...], act3[r, :], NT)
        return 0

    lax.fori_loop(0, T // rows, convolve, 0)
    cotangent.far()

    def during_first():
        cotangent.finish()
        out_swap.wait()
        back_part(1)
        back_part(2)
        back_part(3)

    def during_second():
        backs[0].start()
        backs[1].start()
        back_part(0)

    sum_over_all(
        S, PN, lr, bcp, low, bct, *sums, between=(during_first, during_second)
    )
    backs[2].start()
    for cp in dts:
        cp.wait()
    for m in range(M):
        for t in range(S):
            h = R // S
            wdt[m * R + t * h : m * R + (t + 1) * h, :] = WD[t, m]

    def prepare(i, _):
        r = pl.ds(pl.multiple_of(i * rows, rows), rows)
        low_wide = low[r, :].astype(F32)
        bias = jnp.zeros((rows, C), F32)
        for m in range(M):
            mask = aux[r, m : m + 1]
            masked = (low_wide * mask).astype(BF16)
            bias = bias + mask * ch[K + 2 + m : K + 3 + m, :]
            low3[r, m * R : (m + 1) * R] = masked
        bias = bias + dot(low3[r, :], wdt[...])
        pre[r, :] = bias
        st = softplus(bias)
        step[r, :] = st
        drive[r, :] = st * act[r, :].astype(F32)
        keep[r, :] = jnp.broadcast_to(aux[r, 6:7], (rows, C))
        return 0

    lax.fori_loop(0, T // rows, prepare, 0)
    scan_forward(T, C, bct, ch, step, drive, keep, H, Y)
    for cp in gates + backs:
        cp.wait()

    def finish(i, _):
        r = pl.ds(pl.multiple_of(i * rows, rows), rows)
        mixed = Y[r, :] + ch[K + 1 : K + 2, :] * act[r, :].astype(F32)
        g, d = DS[r, :], DB[r, :]
        for k in range(zn - 1):
            g = g + grecv[k, r, :].astype(F32)
            d = d + orecv[k, r, :].astype(F32)
        sig = 1.0 / (1.0 + jnp.exp(-g))
        gated[r, :] = (mixed * (g * sig)).astype(BF16)
        dmix[r, :] = d * (g * sig)
        dgate[r, :] = (d * mixed * (sig * (1.0 + g * (1.0 - sig)))).astype(BF16)
        return 0

    lax.fori_loop(0, T // rows, finish, 0)
    half = lambda t, k: pl.ds(pl.multiple_of((2 * t + k) * C, LANES), C)
    gathers = [
        RowGather(S, gated, lambda r, t: gall.at[r, chans(t)], *rows_g),
        RowGather(S, dgate, lambda r, t: dall.at[r, half(t, 1)], *rows_d),
        RowGather(S, dinner, lambda r, t: dall.at[r, half(t, 0)], *rows_i),
    ]
    gathers[0].start()
    gathers[1].start()
    mine = pl.ds(pl.multiple_of(lax.rem(s, per) * width, width), width)
    NR[...] = nrm[:, pl.ds(pl.multiple_of(s * width, width), width)]

    def own_features(t, _):
        r = pl.ds(pl.multiple_of(t * TL, TL), TL)
        X[r, :] = toks[lax.div(s, per), t, :, mine]
        G[r, :] = ogz[lax.div(t, 2), lax.rem(t, 2), :, mine]
        return 0

    lax.fori_loop(0, S, own_features, 0)
    INV[...] = jnp.broadcast_to(inv, INV.shape)
    scan_backward(
        pre, H, dmix, act, bct, aux, ch, wdt, low,
        dlow, dbct, gdt, gch, dact, step, drive, keep, DS, DB, dst3, low3, dst,
        [(T // LANES * 3 // 4, lambda: gathers[0].step(1))],
    )
    h = R // S
    part_dt = lambda d: gdt.at[:, pl.ds(pl.multiple_of(d * h, 8), h), :]
    more = row_copies(S, part_dt, lambda t: MORE.at[t], mx, mr)
    more_own = pltpu.make_async_copy(part_dt(s), MORE.at[s], ml)
    for cp in more + [more_own]:
        cp.start()
    def during_second_sum():
        gathers[1].step(1)
        gathers[0].step(3)

    sum_over_all(
        S, PN, dlow, dbct, LR2, BCT2, *sums,
        between=(lambda: gathers[0].step(2), during_second_sum),
    )
    convolve_backward(
        LR2, BCT2, act, conv, aux, ch, wxT, dact, dinner, gx, gtap, pad, tail, act3, dpar
    )
    gathers[2].start()
    for cp in more + [more_own]:
        cp.wait()
    gathers[0].finish()

    large = 512

    def layer(i, _):
        r = pl.ds(pl.multiple_of(i * large, large), large)

        total = jnp.zeros((large, width), F32)
        for m in range(M):
            w = jnp.concatenate(
                [wo[b // 2, b % 2, m * C : (m + 1) * C, :] for b in range(S)], axis=0
            )
            total = total + dot(gall[r, :], w) * aux[r, m : m + 1]
        part[0, r, :] = total.astype(BF16)
        return 0

    lax.fori_loop(0, T // large, layer, 0)
    stream = Stream(H, load, (w_out, m_out, s_out), 6, sums_ref.at[1])
    stream.start(0)

    def out_gradient(i, rows_of):
        m, k = i // 2, i % 2
        wide = gall[:, k * (S // 2) * C : (k + 1) * (S // 2) * C].astype(F32)
        turned[...] = jnp.transpose((wide * aux[0:T, m : m + 1]).astype(BF16))
        g = dot(turned[...], G[...])
        parts = [
            g[:, t * LANES : (t + 1) * LANES].reshape(-1, 8, LANES) for t in range(tiles)
        ]
        H[rows_of, :] = jnp.stack(parts, axis=1).reshape(-1, LANES)

    to_out = LastBlocks(
        S, PN, part.at[0], LO, pair.at[0], pair.at[1], last[0], last[1], swaps.at[0], ls.at[1]
    )
    to_out.start()
    gathers[1].step(2)
    stores = [None, None]
    for i in range(6):
        k = i % 2
        if stores[k] is not None:
            stores[k].wait()
        rows_of = pl.ds((6 + k) * 1024, 1024)
        out_gradient(i, rows_of)
        stores[k] = pltpu.make_async_copy(
            H.at[rows_of], g_out.at[i * 1024 : (i + 1) * 1024], store.at[k]
        )
        stores[k].start()
        stream.norms(i, i // 2, (6 + k) * 1024)
        if i == 0:
            gathers[2].step(1)
        elif i == 1:
            gathers[1].step(3)
        elif i == 3:
            gathers[2].step(2)
        elif i == 5:
            gathers[2].step(3)
    for cp in stores:
        cp.wait()
    stream = Stream(H, load, (w_in, m_in, s_in), 12, sums_ref.at[0])
    stream.start(0)
    gathers[1].finish()
    spare = 6 * 1024 + 2 * width * stride

    def half_product(r, h, m):
        cols = slice(m * C, (m + 1) * C)
        v = jnp.concatenate(
            [dall[r, (2 * b + h) * C : (2 * b + h + 1) * C] for b in range(S)], axis=1
        )
        pieces = [wg[b // 2, b % 2, :, cols] if h else wi[b, :, cols] for b in range(S)]
        return dot(v, jnp.concatenate(pieces, axis=1), NT)

    def gate_back(i, _):
        r = pl.ds(pl.multiple_of(i * large, large), large)
        d = half_product(r, 1, 0) * aux[r, 0:1]
        for m in range(1, M):
            d = d + half_product(r, 1, m) * aux[r, m : m + 1]
        for t in range(tiles):
            at = pl.ds(pl.multiple_of(spare + t * T + i * large, large), large)
            H[at, :] = d[:, t * LANES : (t + 1) * LANES]
        return 0

    lax.fori_loop(0, T // large, gate_back, 0)
    gathers[2].finish()

    def normed_back(i, total):
        r = pl.ds(pl.multiple_of(i * large, large), large)

        d = jnp.concatenate(
            [
                H[pl.ds(pl.multiple_of(spare + t * T + i * large, large), large), :]
                for t in range(tiles)
            ],
            axis=1,
        )
        for m in range(M):
            d = d + half_product(r, 0, m) * aux[r, m : m + 1]
        scaled = X[r, :].astype(F32) * aux[r, 7:8]
        gained = d * gain_mine[0:1, :]
        part[1, r, :] = gained.astype(BF16)
        along = jnp.sum(gained * scaled, axis=1, keepdims=True)
        for j in range(large // TL):
            turned = jnp.transpose(jnp.broadcast_to(along[j * TL : (j + 1) * TL], (TL, LANES)))
            rowdot[i * (large // TL) + j] = turned[0:8]
        return total + jnp.sum(d * scaled, axis=0, keepdims=True)

    total = lax.fori_loop(0, T // large, normed_back, jnp.zeros((1, width), F32))
    ggs[...] = jnp.broadcast_to(total, ggs.shape)
    to_in = LastBlocks(
        S, PN, part.at[1], DN, pair.at[2], pair.at[3], last[2], last[3], swaps.at[1], ls.at[3]
    )
    to_in.start()
    gains = [
        seq_copy(ggs, GG.at[k], last[4].at[k], last[5].at[k], {"tp": lax.rem(p + k, PN)})
        for k in range(1, PN)
    ]
    for cp in gains:
        cp.start()
    n = S * PN
    me = s * PN + p

    def to_all(src, dst, send, recv):
        def copy(k):
            j = lax.rem(me + k, n)
            device = {"seq": lax.div(j, PN), "tp": lax.rem(j, PN)}
            return seq_copy(src(lax.div(j, PN)), dst.at[k], send.at[k], recv.at[k], device)

        def start(k, _):
            copy(k).start()
            return 0

        def wait(k, _):
            copy(k).wait()
            return 0

        return (
            lambda: lax.fori_loop(1, n, start, 0),
            lambda: lax.fori_loop(1, n, wait, 0),
        )

    send_row, wait_row = to_all(lambda t: rowdot.at[t], ROW, last[6], last[7])
    send_row()
    GG[0] = ggs[...]
    ROW[0] = rowdot[s]

    stores = [None, None]
    per_m = width * stride
    for m in range(M):
        k = m % 2
        if stores[k] is not None:
            stores[k].wait()
        first_row = 6 * 1024 + k * per_m
        turned[0:width, :] = jnp.transpose(
            (NR[...].astype(F32) * aux[0:T, m : m + 1]).astype(BF16)
        )
        for b in range(S):
            g = dot(turned[0:width, :], dall[:, 2 * b * C : 2 * (b + 1) * C])
            H[pl.ds(first_row + 2 * b, width, stride=stride), :] = g[:, 0:C]
            H[pl.ds(first_row + 2 * b + 1, width, stride=stride), :] = g[:, C : 2 * C]
        stores[k] = pltpu.make_async_copy(
            H.at[first_row : first_row + per_m], g_in.at[m * per_m : (m + 1) * per_m], store.at[k]
        )
        stores[k].start()
        for q in range(per_m // 1024):
            stream.norms(m * (per_m // 1024) + q, m, first_row + q * 1024)
    lane = lax.broadcasted_iota(jnp.int32, (8, LANES), 1)
    total = jnp.zeros((8, LANES), F32)
    square = lambda v: jnp.sum(v * v)
    for t in range(S):
        gdt_mine[:, :, t * C : (t + 1) * C] = MORE[t]
    for m in range(M):
        x = adam_terms(gx[m], m_x[m], s_x[m])[2] + WEIGHT_DECAY * w_x[m]
        d = adam_terms(gdt_mine[m], m_dt[m], s_dt[m])[2] + WEIGHT_DECAY * w_dt[m]
        for k, value in enumerate((
            jnp.sum(sums_ref[0, m, 0]), square(w_x[m]), square(w_dt[m]), jnp.sum(sums_ref[1, m, 0]),
            jnp.sum(sums_ref[0, m, 1]), square(x), square(d), jnp.sum(sums_ref[1, m, 1]),
        )):
            total = jnp.where(lane == k * M + m, value, total)
    total_tile[...] = total
    send_tile, wait_tile = to_all(lambda t: total_tile, TILE, last[8], last[9])
    send_tile()
    TILE[0] = total
    for cp in gains:
        cp.wait()
    wait_row()
    wait_tile()
    total = jnp.sum(TILE[...], axis=0)
    below = pltpu.roll(total, LANES - 4 * M, 1)
    SCALE[...] = MATRIX_RATE * (jnp.sqrt(total) / jnp.sqrt(below))
    for cp in stores:
        cp.wait()
    to_out.finish()
    to_in.finish()


class Stream:
    def __init__(self, H, sems, refs, steps, sums):
        self.H, self.sems, self.refs, self.steps, self.sums = H, sems, refs, steps, sums
        sums[...] = jnp.zeros(sums.shape, F32)

    def copies(self, i):
        k = i % 2
        return [
            pltpu.make_async_copy(
                ref.at[i * 1024 : (i + 1) * 1024],
                self.H.at[pl.ds((3 * k + a) * 1024, 1024)],
                self.sems.at[k, a],
            )
            for a, ref in enumerate(self.refs)
        ]

    def start(self, i):
        for cp in self.copies(i):
            cp.start()

    def norms(self, i, m, g_row):
        for cp in self.copies(i):
            cp.wait()
        if i + 1 < self.steps:
            self.start(i + 1)
        H, k, rows = self.H, i % 2, 128

        def body(t, sums):
            at = lambda first: pl.ds(pl.multiple_of(first + t * rows, rows), rows)
            weight = H[at(3 * k * 1024), :]
            ratio = adam_terms(
                H[at(g_row), :], H[at((3 * k + 1) * 1024), :], H[at((3 * k + 2) * 1024), :]
            )[2]
            direction = ratio + WEIGHT_DECAY * weight
            fold = lambda v: jnp.sum((v * v).reshape(rows // 8, 8, LANES), axis=0)
            return sums[0] + fold(weight), sums[1] + fold(direction)

        a, b = lax.fori_loop(0, 1024 // rows, body, (self.sums[m, 0], self.sums[m, 1]))
        self.sums[m, 0] = a
        self.sums[m, 1] = b


class LastBlocks:
    def __init__(self, S, PN, part, out, other, both, send, recv, swap, ls):
        s, p = lax.axis_index("seq"), lax.axis_index("tp")
        ratio = S // PN
        self.S, self.PN, self.ratio = S, PN, ratio
        self.s, self.p, self.home = s, p, lax.div(s, ratio)
        self.y, self.c = lax.div(p, 2), lax.rem(p, 2)
        self.slot = lax.rem(s, ratio) * (PN // 2) + self.y
        self.part, self.out, self.other, self.both = part, out, other, both
        self.send, self.recv, self.ls = send, recv, ls
        self.half = part.shape[0] // 2
        self.TL = part.shape[0] // S
        self.swap = seq_copy(
            part.at[self.rows(1 - self.c)],
            other,
            swap.at[0],
            swap.at[1],
            {"tp": p + 1 - 2 * self.c},
        )

    def rows(self, c):
        return pl.ds(pl.multiple_of(c * self.half, self.half), self.half)

    def seq(self, k):
        return self.c * (self.S // 2) + k

    def away(self, k):
        return jnp.logical_or(self.s != self.seq(k), self.home != self.p)

    def copy(self, k):
        return seq_copy(
            self.both.at[k * self.TL : (k + 1) * self.TL],
            self.out.at[self.slot],
            self.send.at[k],
            self.recv.at[self.slot],
            {"seq": self.seq(k), "tp": self.home},
        )

    def own(self, k):
        return pltpu.make_async_copy(
            self.both.at[k * self.TL : (k + 1) * self.TL], self.out.at[self.slot], self.ls
        )

    def start(self):
        self.swap.start()
        self.swap.wait()
        mine = self.part[self.rows(self.c), :].astype(F32)
        self.both[...] = (mine + self.other[...].astype(F32)).astype(BF16)
        for k in range(self.S // 2):

            @pl.when(self.away(k))
            def _():
                self.copy(k).start()

            @pl.when(jnp.logical_not(self.away(k)))
            def _():
                self.own(k).start()

    def finish(self):
        for k in range(self.S // 2):

            @pl.when(self.away(k))
            def _():
                self.copy(k).wait_send()

            @pl.when(jnp.logical_not(self.away(k)))
            def _():
                self.own(k).wait()

        core = lax.div(self.s, self.S // 2)
        for h in range(self.ratio):
            for y in range(self.PN // 2):
                t, q = self.ratio * self.p + h, 2 * y + core
                i = h * (self.PN // 2) + y

                @pl.when(jnp.logical_or(t != self.s, self.p != q))
                def _():
                    seq_copy(
                        self.both.at[0 : self.TL],
                        self.out.at[i],
                        self.send.at[0],
                        self.recv.at[i],
                        {"seq": t, "tp": q},
                    ).wait_recv()


def scan_forward(T, C, bct, ch, step, drive, keep, H, Y):
    base = -jnp.exp(ch[K + 2 + M : K + 2 + M + N, :])
    H[0:N, :] = jnp.zeros((N, C), F32)

    def chunk(c, h):
        cols = bct[c]
        for i in range(LANES // 8):
            t0 = pl.multiple_of(c * LANES + 8 * i, 8)
            r = pl.ds(t0, 8)
            st, dr, kp = step[r, :], drive[r, :], keep[r, :]
            ys = []
            for j in range(8):
                k = 8 * i + j
                rate = jnp.exp(st[j : j + 1] * base) * kp[j : j + 1]
                h = rate * h + dr[j : j + 1] * cols[0:N, k : k + 1]
                H[pl.ds(pl.multiple_of((t0 + j + 1) * N, N), N), :] = h
                ys.append(jnp.sum(cols[N : 2 * N, k : k + 1] * h, axis=0, keepdims=True))
            Y[r, :] = jnp.concatenate(ys, axis=0)
        return h

    lax.fori_loop(0, T // LANES, chunk, jnp.zeros((N, C), F32))


def lane_sums(values):
    v = jnp.concatenate(values, axis=0)
    high = v.astype(BF16)
    low = (v - high.astype(F32)).astype(BF16)
    sums = dot(jnp.concatenate([high, low], axis=1), jnp.ones((2 * v.shape[1], LANES), BF16))
    return [sums[k * N : (k + 1) * N] for k in range(len(values))]


def scan_backward(
    pre, H, dmix, act, bct, aux, ch, wdt, low,
    dlow, dbct, gdt, gch, dact, step, drive, keep, DS, DB, dst3, low3, dst, hooks,
):
    T, C = act.shape
    rows = 128

    base = -jnp.exp(ch[K + 2 + M : K + 2 + M + N, :])
    lane = lax.broadcasted_iota(jnp.int32, (N, LANES), 1)
    nothing = jnp.zeros((N, C), F32)
    chunks = T // LANES

    def chunk(cc, carry):
        c = chunks - 1 - cc
        cols = bct[c]
        flow, hcur, gacc = carry
        accb = accc = jnp.zeros((N, LANES), F32)
        for i in reversed(range(LANES // 8)):
            t0 = pl.multiple_of(c * LANES + 8 * i, 8)
            r = pl.ds(t0, 8)
            st, dr, kp, dm = step[r, :], drive[r, :], keep[r, :], dmix[r, :]
            ds, db, ub, uc = [None] * 8, [None] * 8, [None] * 8, [None] * 8
            for j in reversed(range(8)):
                k = 8 * i + j
                back = cols[N : 2 * N, k : k + 1] * dm[j : j + 1] + flow
                rate = jnp.exp(st[j : j + 1] * base) * kp[j : j + 1]
                hprev = H[pl.ds(pl.multiple_of((t0 + j) * N, N), N), :]
                uc[j] = dm[j : j + 1] * hcur
                ub[j] = back * dr[j : j + 1]
                flow = rate * back
                dlog = flow * hprev
                gacc = gacc + dlog * st[j : j + 1]
                ds[j] = jnp.sum(dlog * base, axis=0, keepdims=True)
                db[j] = jnp.sum(back * cols[0:N, k : k + 1], axis=0, keepdims=True)
                hcur = hprev
            DS[r, :] = jnp.concatenate(ds, axis=0)
            DB[r, :] = jnp.concatenate(db, axis=0)
            sb, sc = lane_sums(ub), lane_sums(uc)
            for j in range(8):
                here = lane == 8 * i + j
                accb = jnp.where(here, sb[j], accb)
                accc = jnp.where(here, sc[j], accc)
        dbct[c, 0:N, :] = accb
        dbct[c, N : 2 * N, :] = accc
        return flow, hcur, gacc

    carry, done = (nothing, H[T * N : (T + 1) * N, :], nothing), 0
    for upto, call in hooks + [(chunks, None)]:
        carry = lax.fori_loop(done, upto, chunk, carry)
        done = upto
        if call is not None:
            call()
    gacc = carry[2]

    def finish(i, carry):
        skip, bias = carry
        r = pl.ds(pl.multiple_of(i * rows, rows), rows)
        a = act[r, :].astype(F32)
        back_b = DB[r, :]
        grad = DS[r, :] + a * back_b
        d = (grad / (1.0 + jnp.exp(-pre[r, :]))).astype(BF16)
        dst[r, :] = d
        wide = d.astype(F32)
        sums = []
        for m in range(M):
            mask = aux[r, m : m + 1]
            masked = wide * mask
            sums.append(jnp.sum(masked, axis=0, keepdims=True))
            dst3[r, m * C : (m + 1) * C] = masked.astype(BF16)
        total = dot(dst3[r, 0:C], wdt[0:R, :], NT)
        for m in range(1, M):
            total = total + dot(dst3[r, m * C : (m + 1) * C], wdt[m * R : (m + 1) * R, :], NT)
        dlow[r, :] = total
        dact[r, :] = dmix[r, :] * ch[K + 1 : K + 2, :] + step[r, :] * back_b
        skip = skip + jnp.sum(dmix[r, :] * a, axis=0, keepdims=True)
        return skip, bias + jnp.concatenate(sums, axis=0)

    skip, bias = lax.fori_loop(
        0, T // rows, finish, (jnp.zeros((1, C), F32), jnp.zeros((M, C), F32))
    )
    gch[0:1, :] = skip
    gch[1 : 1 + M, :] = bias
    gch[1 + M : 1 + M + N, :] = base * gacc
    for m in range(M):
        gdt[m] = dot(low3[:, m * R : (m + 1) * R], dst[...], TN)


def convolve_backward(
    dlow, dbct, act, conv, aux, ch, wxT, dact, dinner, gx, gtap, pad, tail, act3, dpar,
):
    T, C = act.shape
    rows = 128
    tail[T : T + 8, :] = jnp.zeros((8, C), F32)
    blank = jnp.zeros((LANES - 2 * N, LANES), F32)

    def fill(i, _):
        r = pl.ds(pl.multiple_of(i * rows, rows), rows)
        turned = jnp.transpose(jnp.concatenate([dbct[i], blank], axis=0))
        dpar[r, 0:R] = dlow[r, :]
        dpar[r, R : R + 2 * N] = turned[:, 0 : 2 * N].astype(BF16)
        wide = dpar[r, :].astype(F32)
        total = dact[r, :]
        for m in range(M):
            mask = aux[r, m : m + 1]
            total = total + dot((wide * mask).astype(BF16), wxT[m])
        v = conv[r, :]
        sig = 1.0 / (1.0 + jnp.exp(-v))
        tail[r, :] = (total * (sig * (1.0 + v * (1.0 - sig)))).astype(BF16).astype(F32)
        return 0

    lax.fori_loop(0, T // rows, fill, 0)

    def body(i, sums):
        r = pl.ds(pl.multiple_of(i * rows, rows), rows)
        window = pad[pl.ds(pl.multiple_of(i * rows, rows), rows + 8), :]
        d = tail[r, :]
        ahead = tail[pl.ds(pl.multiple_of(i * rows, rows), rows + 8), :]
        same = aux[pl.ds(pl.multiple_of(i * rows, rows), rows + 8), :]
        total = ch[K - 1 : K, :] * d
        new = []
        for k in range(K):
            off = K - 1 - k
            shifted = window[8 - off : 8 - off + rows]
            if k < K - 1:
                shifted = shifted * aux[r, M + k : M + k + 1]
                total = total + ch[k : k + 1, :] * (
                    ahead[off : off + rows] * same[off : off + rows, M + k : M + k + 1]
                )
            new.append(jnp.sum(d * shifted, axis=0, keepdims=True))
        new.append(jnp.sum(d, axis=0, keepdims=True))
        dinner[r, :] = total.astype(BF16)
        return sums + jnp.concatenate(new, axis=0)

    gtap[0 : K + 1, :] = lax.fori_loop(0, T // rows, body, jnp.zeros((K + 1, C), F32))
    for m in range(M):
        gx[m] = dot(dpar[...], act3[:, m * C : (m + 1) * C], TN)


def block_call(S, PN, args, T, C, width):
    dma = pltpu.SemaphoreType.DMA
    TL, DD = args[0].shape
    chunks = T // LANES
    zn = S // 2
    f = lambda *shape: sds(shape)
    b = lambda *shape: sds(shape, BF16)
    vf = lambda *shape: pltpu.VMEM(shape, F32)
    vb = lambda *shape: pltpu.VMEM(shape, BF16)
    n = S * PN
    out = (
        b(S // 2, TL, width), b(S // 2, TL, width), f(PN, 8, width), f(n, 8, LANES),
        f(S, M, R // S, C), f(M, R + 2 * N, C), f(8, C), f(1 + M + N, C),
        f(TL, LANES), f(8, LANES), f(M * width * 2 * S, C), f(M * S * width, C),
    )
    scratch = (
        [vf(8, TL), vb(PN, S, TL, DD // PN), vb(zn, 2, TL, DD // PN), vb(T, DD)]
        + [vb(DD, M * C), vb(zn, 2 * width, M * C), vb(zn, M * C, 2 * width)]
        + [vf(S, 8, TL), vf(S, 8, width)]
        + [vb(S, M, R // S, C)]
        + [vb(zn - 1, T, C)] * 4
        + [vf(T, C)] * 4
        + [vf(T + 8, C), vb(T, M * C), vf(T, R), vf(chunks, 2 * N, LANES)]
        + [vb(T, C), vf(T, C), vb(T, C), vb(T, R), vf(chunks, 2 * N, LANES), vf(T, C)]
        + [vf((T + 1) * N, C), vb(T, C), vb(T, C), vf(T, C), vf(T + 8, 8), vb(T, width)]
        + [vb(T, S * C), vb(T, 2 * S * C), vf(T, C), vf(T, C), vb(T, M * C), vb(T, M * R)]
        + [vb(T, C), vf(T, R), vf(chunks, 2 * N, LANES), vf(T, C), vf(M, R, C)]
        + [vb(T, R), vf(chunks, 2 * N, LANES), vf(T + 8, C), vb(T, R + 2 * N), vb(T, C)]
        + [vb(2, T, width), vf(S, 8, LANES), vf(8, width), vb(M * R, C)]
        + [vb(S, width, M * C), vb(zn, 2, width, M * C), vb(zn, 2, M * C, width)]
        + [vb(M, R // S, S * C)]
        + [vf(8, width), vb(M * C, R), vb(2 * N, M * C), vb(M, R + 2 * N, C), vb(T, width)]
        + [vb(T, width), vf(M, R // S, S * C), vb(S * C // 2, T), vf(2, M, 2, 8, LANES)]
        + [vf(n, 8, LANES), vf(8, LANES), dma((2,)), dma((2, 3)), dma((2,))]
        + [vb(4, T // 2, width), dma((2, 2))]
        + Spread.semaphores(S)
        + FeatureGather.semaphores(S)
        + [dma((zn,))] * 4
        + [dma((S,))] * 12
        + [dma((6,))]
        + sum_scratch(S, PN, T)
        + RowGather.semaphores(S) * 3
        + [dma((S,)), dma((S,)), dma]
        + [dma((S,))] * 4 + [dma((PN,))] * 2 + [dma((n,))] * 4
    )
    vm, hb = pl.BlockSpec(memory_space=pltpu.VMEM), pl.BlockSpec(memory_space=pl.ANY)
    return pl.pallas_call(
        functools.partial(block_kernel, S, PN),
        out_shape=out,
        in_specs=[vm] * (len(args) - 6) + [hb] * 6,
        out_specs=[vm] * (len(out) - 2) + [hb] * 2,
        scratch_shapes=scratch,
        compiler_params=pltpu.CompilerParams(
            collective_id=0, has_side_effects=True, vmem_limit_bytes=VMEM_LIMIT
        ),
    )(*args)


def update_rows(scale, which, k, g, w, m, s, avg, nw, nm, ns, na):
    factor = scale[0:1, M * which : M * which + 1]
    for i in range(1, M):
        lane = M * which + i
        factor = jnp.where(k == i, scale[0:1, lane : lane + 1], factor)
    rows = 128

    def body(t, _):
        r = pl.ds(pl.multiple_of(t * rows, rows), rows)
        weight = w[r, :]
        new_m, new_s, ratio = adam_terms(g[r, :], m[r, :], s[r, :])
        new = weight - factor * (ratio + WEIGHT_DECAY * weight)
        nw[r, :] = new
        nm[r, :] = new_m
        ns[r, :] = new_s
        na[r, :] = AVERAGE_KEEP * avg[r, :] + (1.0 - AVERAGE_KEEP) * new
        return 0

    lax.fori_loop(0, w.shape[0] // rows, body, 0)


def update_kernel(S, PN, count, outs, *refs):
    ins, outputs, scratch = refs[: 10 + count], refs[10 + count : 18 + count + outs], refs[18 + count + outs :]
    scale = ins[10 + 6]
    step = pl.program_id(0)
    k = lax.div(step, pl.num_programs(0) // M)
    update_rows(scale, 0, k, *ins[0:5], *outputs[0:4])
    update_rows(scale, 3, k, *ins[5:10], *outputs[4:8])

    @pl.when(step == 2)
    def _():
        rest_kernel(S, PN, *ins[10:], *outputs[8:], *scratch)


def update_all(S, PN, in_rows, out_rows, rest, rest_out, scratch):
    steps = 2 * M

    def piece(v):
        return pl.BlockSpec((v.shape[0] // steps, v.shape[1]), lambda i: (i, 0))

    def whole(v):
        return pl.BlockSpec(v.shape, lambda i: (0,) * len(v.shape))

    arrays = (*in_rows, *out_rows)
    new = (sds(in_rows[0].shape),) * 4 + (sds(out_rows[0].shape),) * 4
    return pl.pallas_call(
        functools.partial(update_kernel, S, PN, len(rest), len(rest_out)),
        out_shape=new + tuple(rest_out),
        grid=(steps,),
        in_specs=[piece(v) for v in arrays] + [whole(v) for v in rest],
        out_specs=[piece(v) for v in new] + [whole(v) for v in rest_out],
        scratch_shapes=scratch,
        compiler_params=pltpu.CompilerParams(vmem_limit_bytes=VMEM_LIMIT),
    )(*arrays, *rest)


def rest_kernel(
    S, PN, tok, og, LO, DN, ROW, INV, scale, gx, more, gtap, gch, GG, wx, mx, sx, ax, wd, md, sd, ad,
    ch, mc, sc, ac, gn, mg, sg, ag,
    layer, grad, nwx, nmx, nsx, nax, nwd, nmd, nsd, nad, nwc, nmc, nsc, nac, nwg, nmg, nsg, nag, gc, gd,
):
    p = lax.axis_index("tp")
    C = more.shape[3]
    width = LO.shape[2]
    out_width = og.shape[1]

    def average(old, new):
        return AVERAGE_KEEP * old + (1.0 - AVERAGE_KEEP) * new

    along = ROW[0, 0:1, :]
    for k in range(1, ROW.shape[0]):
        along = along + ROW[k, 0:1, :]
    column = jnp.transpose(jnp.broadcast_to(along, (LANES, LANES)))[:, 0:1]
    inv = INV[:, 0:1]
    for h in range(out_width // width):
        cols = pl.ds(pl.multiple_of(p * out_width + h * width, LANES), width)
        here = slice(h * width, (h + 1) * width)
        mine = tok[:, cols].astype(F32)
        chips = PN // 2
        total = LO[h * chips].astype(F32)
        back = DN[h * chips].astype(F32)
        for q in range(1, chips):
            total = total + LO[h * chips + q].astype(F32)
            back = back + DN[h * chips + q].astype(F32)
        layer[:, here] = mine + total
        grad[:, here] = og[:, here].astype(F32) + inv * (back - mine * inv * (column / D))
    for t in range(S):
        gd[:, :, t * C : (t + 1) * C] = more[t]
    for m in range(M):
        for k, g, w, mo, sq, av, nw, nm, ns, na in (
            (1, gx, wx, mx, sx, ax, nwx, nmx, nsx, nax),
            (2, gd, wd, md, sd, ad, nwd, nmd, nsd, nad),
        ):
            factor = scale[0:1, M * k + m : M * k + m + 1]
            new_m, new_s, ratio = adam_terms(g[m], mo[m], sq[m])
            new = w[m] - factor * (ratio + WEIGHT_DECAY * w[m])
            nw[m] = new
            nm[m] = new_m
            ns[m] = new_s
            na[m] = average(av[m], new)
    gc[0 : K + 1, :] = gtap[0 : K + 1, :]
    gc[K + 1 :, :] = gch[...]
    new_m, new_s, ratio = adam_terms(gc[...], mc[...], sc[...])
    new = ch[...] - CHANNEL_RATE * ratio
    nwc[...] = new
    nmc[...] = new_m
    nsc[...] = new_s
    nac[...] = average(ac[...], new)
    g = GG[0, 0:1, :]
    for q in range(1, PN):
        g = g + GG[q, 0:1, :]
    new_m, new_s, ratio = adam_terms(g, mg[...], sg[...])
    new = gn[...] - GAIN_RATE * ratio
    nwg[...] = new
    nmg[...] = new_m
    nsg[...] = new_s
    nag[...] = average(ag[...], new)


def to_rows(w, S):
    m, width, two, channels = w.shape
    c = channels // S
    return w.reshape(m, width, two, S, c).transpose(0, 1, 3, 2, 4).reshape(-1, c)


def from_rows(rows, S, shape):
    m, width, two, channels = shape
    c = channels // S
    return rows.reshape(m, width, S, two, c).transpose(0, 1, 3, 2, 4).reshape(shape)


def to_tiles(w):
    m, rows, columns = w.shape
    return w.reshape(m, rows // 8, 8, columns // LANES, LANES).transpose(0, 1, 3, 2, 4).reshape(
        -1, LANES
    )


def from_tiles(flat, shape):
    m, rows, columns = shape
    return flat.reshape(m, rows // 8, columns // LANES, 8, LANES).transpose(0, 1, 3, 2, 4).reshape(
        shape
    )


def local(
    tokens, out_grad, modality, segment,
    w_in, w_x, w_dt, w_out, channel, norm_gain,
    moment_in, moment_x, moment_dt, moment_out, moment_channel, moment_gain,
    square_in, square_x, square_dt, square_out, square_channel, square_gain,
    average_in, average_x, average_dt, average_out, average_channel, average_gain,
):
    S, PN = lax.axis_size("seq"), lax.axis_size("tp")
    TL = tokens.shape[0]
    T = S * TL
    width = D // S
    inner_width = w_out.shape[1]
    C = inner_width // S
    ins = [to_rows(v, S) for v in (w_in, moment_in, square_in, average_in)]
    outs = [to_tiles(v) for v in (w_out, moment_out, square_out, average_out)]
    modrow = jnp.broadcast_to(modality.astype(F32)[None], (8, TL))
    ahead = jnp.concatenate([jnp.full((K - 1,), -1, jnp.int32), segment])
    same = [(ahead[k : k + T] == segment).astype(F32) for k in range(K - 1)]
    zero = jnp.zeros((T,), F32)
    segs = jnp.stack([zero] * M + same + [same[K - 2], zero], axis=1)
    row = lambda v: v[None, :]
    xs = [jnp.transpose(v, (0, 2, 1)) for v in (w_x, moment_x, square_x, average_x)]
    LO, DN, GG, ROW, MORE, gx, gtap, gch, INV, scale, g_in, g_out = block_call(
        S,
        PN,
        (
            tokens, out_grad, modrow, row(norm_gain), segs, channel,
            *xs[:3], w_dt, moment_dt, square_dt, *ins[:3], *outs[:3],
        ),
        T, C, width,
    )
    like = lambda v: sds(v.shape)
    vec = sds((1, width))
    everything = update_all(
        S,
        PN,
        (g_in, *ins),
        (g_out, *outs),
        (
            tokens, out_grad, LO, DN, ROW, INV, scale, gx, MORE, gtap, gch, GG,
            *xs, w_dt, moment_dt, square_dt, average_dt,
            channel, moment_channel, square_channel, average_channel,
            row(norm_gain), row(moment_gain), row(square_gain), row(average_gain),
        ),
        (sds(out_grad.shape),) * 2 + (like(xs[0]),) * 4 + (like(w_dt),) * 4 + (like(channel),) * 4
        + (vec,) * 4,
        [pltpu.VMEM(channel.shape, F32), pltpu.VMEM(w_dt.shape, F32)],
    )
    new_in = [from_rows(v, S, w_in.shape) for v in everything[0:4]]
    new_out = [from_tiles(v, w_out.shape) for v in everything[4:8]]
    rest = everything[8:]
    new_x, new_dt, new_ch, new_g = [rest[2 + 4 * k : 6 + 4 * k] for k in range(4)]
    new_x = [jnp.transpose(v, (0, 2, 1)) for v in new_x]
    groups = [(new_in[k], new_x[k], new_dt[k], new_out[k], new_ch[k], new_g[k][0]) for k in range(4)]
    return (*rest[:2], *groups[0], *groups[1], *groups[2], *groups[3])


def channels_fit(mesh):
    S, PN = mesh.shape["seq"], mesh.shape["tp"]
    n = S * PN
    return PN == 4 and S == 2 * PN and (2 * N) % n == 0 and D * 2 // n == LANES


def solution(mesh):
    placed = (
        P("seq", None),
        P("seq", "tp"),
        P("seq"),
        P(),
        P(None, "seq", None, "tp"),
        P(None, ("tp", "seq"), None),
        P(None, "seq", "tp"),
        P(None, "tp", "seq"),
        P(None, ("tp", "seq")),
        P("seq"),
        P(None, "seq", None, "tp"),
        P(None, ("tp", "seq"), None),
        P(None, "seq", "tp"),
        P(None, "tp", "seq"),
        P(None, ("tp", "seq")),
        P("seq"),
        P(None, "seq", None, "tp"),
        P(None, ("tp", "seq"), None),
        P(None, "seq", "tp"),
        P(None, "tp", "seq"),
        P(None, ("tp", "seq")),
        P("seq"),
        P(None, "seq", None, "tp"),
        P(None, ("tp", "seq"), None),
        P(None, "seq", "tp"),
        P(None, "tp", "seq"),
        P(None, ("tp", "seq")),
        P("seq"),
    )
    return jax.shard_map(
        local if channels_fit(mesh) else generic_local,
        mesh=mesh,
        in_specs=placed,
        out_specs=(
            P("seq", "tp"),
            P("seq", "tp"),
            P(None, "seq", None, "tp"),
            P(None, ("tp", "seq"), None),
            P(None, "seq", "tp"),
            P(None, "tp", "seq"),
            P(None, ("tp", "seq")),
            P("seq"),
            P(None, "seq", None, "tp"),
            P(None, ("tp", "seq"), None),
            P(None, "seq", "tp"),
            P(None, "tp", "seq"),
            P(None, ("tp", "seq")),
            P("seq"),
            P(None, "seq", None, "tp"),
            P(None, ("tp", "seq"), None),
            P(None, "seq", "tp"),
            P(None, "tp", "seq"),
            P(None, ("tp", "seq")),
            P("seq"),
            P(None, "seq", None, "tp"),
            P(None, ("tp", "seq"), None),
            P(None, "seq", "tp"),
            P(None, "tp", "seq"),
            P(None, ("tp", "seq")),
            P("seq"),
        ),
        check_vma=False,
    )
```
